32 devices in a mesh: group: 4 (over z), member: 8 (over y, x, core).
Axes of the slice: x: 2, y: 2, z: 4, core: 2. Of those that a mesh axis runs over, the one named last changes fastest.
Arguments:
- tokens: bfloat16 [32, 3584], P(('group', 'member')), may hold values from -6 to 6
- grad_out: bfloat16 [32, 3584], P(('group', 'member')), may hold values from -6 to 6
- route_token: int32 [4, 4, 1, 8], P('group'), may hold values from 0 to 7, as said below
- route_count: int32 [4, 4, 1], P('group'), may hold values from 0 to 8, as said below
- route_prob: float32 [4, 4, 1, 8], P('group'), may hold values from 0.05 to 0.6
- w_gate: bfloat16 [32, 128, 3584], P(('group', 'member')), may hold values from -0.09375 to 0.09375
- w_up: bfloat16 [32, 128, 3584], P(('group', 'member')), may hold values from -0.09375 to 0.09375
- w_down: bfloat16 [32, 128, 3584], P(('group', 'member')), may hold values from -0.1875 to 0.1875
Outputs:
- grad_tokens: bfloat16 [32, 3584], P(('group', 'member'))
- grad_gate: bfloat16 [32, 128, 3584], P(('group', 'member'))
- grad_up: bfloat16 [32, 128, 3584], P(('group', 'member'))
- grad_down: bfloat16 [32, 128, 3584], P(('group', 'member'))
The draws below stay inside these ranges and needn't reach their ends.
Inputs may be any that keep to these rules, and one draw needn't show every extreme that they name: Each token of a source group is routed to 1 different experts in each of 2 different groups. An expert keeps, for each source group, the first 8 of the tokens routed to it in token order and drops the rest; route_token lists the kept tokens in that order, all different, and slots at or past route_count hold 0. In every draw one expert keeps 8 tokens from every source group. `route_count`: the number of kept tokens of each source group for each expert; 8 is reached in every draw.
All inputs are finite; a program needn't handle non-finite values.
Results may differ from the reference program's by a relative error of at most 0.0058.
Values may be sent and summed in bfloat16 or wider, within the bound.
No kernel may reach another device: no remote copies, remote signals or barrier semaphores. Data moves between devices by JAX's collectives and lax.ppermute only.
A program may use at most 64 MiB of HBM per device.

```python
import math
import jax
import jax.numpy as jnp
from jax import lax

D = 3584
FFN = 1024
SPLIT = 8
HS = 128
EPG = 1
SLICES = 32
LIMIT = 2
PER_GROUP = 1
TOK_GROUP = 8
TOKENS = 32
CAP = 8
N_GROUP = 4


def routing_tables(key):
    key_groups, key_experts, key_hot_group, key_hot_expert = jax.random.split(key, 4)
    hot_group = jax.random.randint(key_hot_group, (), 0, N_GROUP)
    hot_expert = jax.random.randint(key_hot_expert, (), 0, EPG)
    forced = (jnp.arange(TOK_GROUP, dtype=jnp.int32) < CAP)[None, :]
    group_scores = jax.random.randint(key_groups, (N_GROUP, TOK_GROUP, N_GROUP), 0, 1 << 20)
    group_scores = group_scores * N_GROUP + jnp.arange(N_GROUP, dtype=jnp.int32)
    group_hot = (jnp.arange(N_GROUP, dtype=jnp.int32) == hot_group)[None, None, :]
    group_scores = jnp.where(forced[:, :, None] & group_hot, -1, group_scores)
    group_rank = jnp.argsort(jnp.argsort(group_scores, axis=-1), axis=-1)
    chosen_group = group_rank < LIMIT
    expert_scores = jax.random.randint(key_experts, (N_GROUP, TOK_GROUP, N_GROUP, EPG), 0, 1 << 20)
    expert_scores = expert_scores * EPG + jnp.arange(EPG, dtype=jnp.int32)
    expert_hot = (jnp.arange(EPG, dtype=jnp.int32) == hot_expert)[None, None, None, :]
    expert_scores = jnp.where(forced[:, :, None, None] & group_hot[:, :, :, None] & expert_hot, -1, expert_scores)
    expert_rank = jnp.argsort(jnp.argsort(expert_scores, axis=-1), axis=-1)
    chosen = ((expert_rank < PER_GROUP) & chosen_group[:, :, :, None]).astype(jnp.int32)
    position = jnp.cumsum(chosen, axis=1) - 1
    kept = (chosen > 0) & (position < CAP)
    counts = jnp.minimum(jnp.sum(chosen, axis=1), CAP).astype(jnp.int32)
    slot_match = kept[..., None] & (position[..., None] == jnp.arange(CAP, dtype=jnp.int32))
    token_numbers = jnp.arange(TOK_GROUP, dtype=jnp.int32)[None, :, None, None, None]
    table = jnp.sum(jnp.where(slot_match, token_numbers, 0), axis=1).astype(jnp.int32)
    return (table, counts)


def draw_route_token(key, part):
    tables = routing_tables(key)
    return tables[0]


def draw_route_count(key, part):
    tables = routing_tables(key)
    return tables[1]


def level_of(own_key, shape, cuts, least, largest):
    def one(dim, blocks):
        steps = jax.random.uniform(jax.random.fold_in(jax.random.fold_in(own_key, 6), dim), (blocks,), jnp.float32, least / len(cuts), largest / len(cuts))
        return jnp.repeat(jnp.exp(steps), shape[dim] // blocks).reshape((-1,) + (1,) * (len(shape) - dim - 1))

    factor_of = one(*cuts[0])
    for cut in cuts[1:]:
        factor_of = factor_of * one(*cut)
    return factor_of


def normal_values(stream_key, extent, deviation, limit, cuts=(), held_as=jnp.bfloat16):
    gain = level_of(stream_key, extent, cuts, -0.22, 0.18) if cuts else 1.0
    drawn = jax.random.normal(stream_key, extent, jnp.float32) * deviation * gain
    return jnp.minimum(jnp.maximum(drawn, -limit), limit).astype(held_as)


def setup_inputs(seed: int = 0) -> dict:
    keys = jax.random.split(jax.random.key(seed), 9)
    return {
        "tokens": normal_values(keys[0], (TOKENS, D), 1.0, 6.0, ((0, 32),)),
        "grad_out": normal_values(keys[1], (TOKENS, D), 1.0, 6.0, ((0, 32),)),
        "route_token": draw_route_token(jax.random.fold_in(keys[8], 71), 0),
        "route_count": draw_route_count(jax.random.fold_in(keys[8], 71), 0),
        "route_prob": jnp.clip(jnp.exp(math.log(0.6) - 2.4849067 * jax.random.uniform(keys[4], (N_GROUP, N_GROUP, EPG, CAP), jnp.float32) ** level_of(keys[4], (N_GROUP, N_GROUP, EPG, CAP), ((0, 4),), -0.2, 0.2)), 0.05, 0.6),
        "w_gate": normal_values(keys[5], (SLICES, HS, D), D ** -0.5, 0.09375, ((0, 32),)),
        "w_up": normal_values(keys[6], (SLICES, HS, D), D ** -0.5, 0.09375, ((0, 32),)),
        "w_down": normal_values(keys[7], (SLICES, HS, D), FFN ** -0.5, 0.1875, ((0, 32),)),
    }


def slice_backward(rows_x, rows_scaled, gate_weight, up_weight, down_weight):
    gate_value = jnp.dot(rows_x, gate_weight.T, preferred_element_type=jnp.float32)
    up_value = jnp.dot(rows_x, up_weight.T, preferred_element_type=jnp.float32)
    sigma_gate = jax.nn.sigmoid(gate_value)
    active = gate_value * sigma_gate
    hidden = (active * up_value).astype(jnp.bfloat16)
    d_hidden = jnp.dot(rows_scaled, down_weight.T, preferred_element_type=jnp.float32)
    d_gate = (d_hidden * up_value * sigma_gate * (1.0 + gate_value * (1.0 - sigma_gate))).astype(jnp.bfloat16)
    d_up = (d_hidden * active).astype(jnp.bfloat16)
    grad_down = jnp.dot(hidden.T, rows_scaled, preferred_element_type=jnp.float32).astype(jnp.bfloat16)
    grad_gate = jnp.dot(d_gate.T, rows_x, preferred_element_type=jnp.float32).astype(jnp.bfloat16)
    grad_up = jnp.dot(d_up.T, rows_x, preferred_element_type=jnp.float32).astype(jnp.bfloat16)
    partial_rows = jnp.dot(d_gate, gate_weight, preferred_element_type=jnp.float32)
    partial_rows = partial_rows + jnp.dot(d_up, up_weight, preferred_element_type=jnp.float32)
    return grad_gate, grad_up, grad_down, partial_rows


def reference(tokens, grad_out, route_token, route_count, route_prob, w_gate, w_up, w_down):
    source_base = jnp.arange(N_GROUP, dtype=jnp.int32)[:, None] * TOK_GROUP
    slot_index = jnp.arange(CAP, dtype=jnp.int32)[None, :]

    def step_fn(running, inputs):
        gate_weight, up_weight, down_weight, slice_id = inputs
        expert_id = slice_id // SPLIT
        dest_group = expert_id // EPG
        local_expert = expert_id % EPG
        slot_tokens = route_token[:, dest_group, local_expert, :].astype(jnp.int32)
        slot_counts = route_count[:, dest_group, local_expert].astype(jnp.int32)
        live = (slot_index < slot_counts[:, None]).astype(jnp.float32)
        slot_weights = (route_prob[:, dest_group, local_expert, :] * live).reshape(-1)
        global_rows = (source_base + slot_tokens).reshape(-1).astype(jnp.int32)
        rows_x = tokens[global_rows]
        rows_scaled = (slot_weights[:, None] * grad_out[global_rows].astype(jnp.float32)).astype(jnp.bfloat16)
        grad_gate, grad_up, grad_down, partial_rows = slice_backward(rows_x, rows_scaled, gate_weight, up_weight, down_weight)
        running = running.at[global_rows].add(partial_rows)
        return running, (grad_gate, grad_up, grad_down)

    zero_grad = jnp.zeros((TOKENS, D), jnp.float32)
    slice_ids = jnp.arange(SLICES, dtype=jnp.int32)
    summed, outputs = lax.scan(step_fn, zero_grad, (w_gate, w_up, w_down, slice_ids))
    return summed.astype(jnp.bfloat16), outputs[0], outputs[1], outputs[2]
```

```python
import functools

import jax
import jax.numpy as jnp
from jax import lax
from jax.experimental import pallas as pl
from jax.experimental.pallas import tpu as pltpu
from jax.sharding import PartitionSpec as P

LANES = 128
AXES = ("group", "member")
VMEM = pl.BlockSpec(memory_space=pltpu.VMEM)
SMEM = pl.BlockSpec(memory_space=pltpu.SMEM)
NT = (((1,), (1,)), ((), ()))
TN = (((0,), (0,)), ((), ()))


def round_up(value, step):
    return (value + step - 1) // step * step


def pack_kernel(chunks, tokens_ref, grad_ref, token_ref, count_ref, prob_ref, out_ref, rows_ref):
    me = lax.axis_index("member")
    groups, experts, capacity = token_ref.shape[1:]
    token_row = tokens_ref[...].astype(jnp.float32)
    grad_row = grad_ref[...].astype(jnp.float32)
    for k in range(chunks):
        part = slice(k * LANES, (k + 1) * LANES)
        rows_ref[k : k + 1, :] = token_row[:, part]
        rows_ref[chunks + k : chunks + k + 1, :] = grad_row[:, part]
    lane = lax.broadcasted_iota(jnp.int32, (1, LANES), 1)
    third = lax.rem(lane, 32)
    weights = jnp.zeros((1, LANES), jnp.float32)
    for g in range(groups):
        for j in range(experts):
            weight = jnp.float32(0)
            for p in range(capacity):
                live = (token_ref[0, g, j, p] == me) & (p < count_ref[0, g, j])
                weight = weight + jnp.where(live, prob_ref[0, g, j, p], 0.0)
            weights = jnp.where(third == g * experts + j, weight, weights)
    high = weights.astype(jnp.bfloat16).astype(jnp.float32)
    middle = (weights - high).astype(jnp.bfloat16).astype(jnp.float32)
    low = weights - high - middle
    parts = jnp.where(lane < 32, high, jnp.where(lane < 64, middle, jnp.where(lane < 96, low, 0.0)))
    rows_ref[2 * chunks : 2 * chunks + 1, :] = parts
    used = 2 * chunks + 1
    rows_ref[used:, :] = jnp.zeros((rows_ref.shape[0] - used, LANES), jnp.float32)
    out_ref[...] = rows_ref[...].astype(jnp.bfloat16)


def partial_kernel(
    chunks,
    gathered_ref,
    gate_ref,
    up_ref,
    down_ref,
    sent_ref,
    x_ref,
    scaled_ref,
    acts_ref,
    wide_ref,
    spread_ref,
):
    tokens, rows, _ = gathered_ref.shape
    expert = lax.axis_index("group")
    wide_ref[...] = gathered_ref[...].reshape(tokens * rows, LANES).astype(jnp.float32)

    def column(k):
        return wide_ref[pl.ds(k, tokens, stride=rows), :]

    lane = lax.broadcasted_iota(jnp.int32, (tokens, LANES), 1)
    mine = (lane < 96) & (lax.rem(lane, 32) == expert)
    weight = jnp.sum(jnp.where(mine, column(2 * chunks), 0.0), axis=1, keepdims=True)
    for k in range(chunks):
        part = slice(k * LANES, (k + 1) * LANES)
        x_ref[:, part] = column(k).astype(jnp.bfloat16)
        scaled_ref[:, part] = (weight * column(chunks + k)).astype(jnp.bfloat16)

    x = x_ref[...]
    gate_value = lax.dot_general(x, gate_ref[0], NT, preferred_element_type=jnp.float32)
    up_value = lax.dot_general(x, up_ref[0], NT, preferred_element_type=jnp.float32)
    d_hidden = lax.dot_general(scaled_ref[...], down_ref[0], NT, preferred_element_type=jnp.float32)
    sigma_gate = jax.nn.sigmoid(gate_value)
    active = gate_value * sigma_gate
    hidden = (active * up_value).astype(jnp.bfloat16)
    d_gate = (d_hidden * up_value * sigma_gate * (1.0 + gate_value * (1.0 - sigma_gate))).astype(
        jnp.bfloat16
    )
    d_up = (d_hidden * active).astype(jnp.bfloat16)
    acts_ref[0] = d_gate
    acts_ref[1] = d_up
    acts_ref[2] = hidden
    sent_rows = sent_ref.shape[1]
    partial = jnp.dot(d_gate, gate_ref[0], preferred_element_type=jnp.float32)
    partial = partial + jnp.dot(d_up, up_ref[0], preferred_element_type=jnp.float32)
    for k in range(chunks):
        spread_ref[pl.ds(k, tokens, stride=sent_rows), :] = partial[:, k * LANES : (k + 1) * LANES]
    for k in range(chunks, sent_rows):
        spread_ref[pl.ds(k, tokens, stride=sent_rows), :] = jnp.zeros((tokens, LANES), jnp.float32)
    sent_ref[...] = spread_ref[...].reshape(tokens, sent_rows, LANES).astype(jnp.bfloat16)


def grads_kernel(x_ref, scaled_ref, acts_ref, gate_out, up_out, down_out):
    x = x_ref[...]
    gate_out[0] = lax.dot_general(
        acts_ref[0], x, TN, preferred_element_type=jnp.float32
    ).astype(jnp.bfloat16)
    up_out[0] = lax.dot_general(
        acts_ref[1], x, TN, preferred_element_type=jnp.float32
    ).astype(jnp.bfloat16)
    down_out[0] = lax.dot_general(
        acts_ref[2], scaled_ref[...], TN, preferred_element_type=jnp.float32
    ).astype(jnp.bfloat16)


def sum_kernel(chunks, back_ref, out_ref, total_ref):
    total_ref[...] = jnp.sum(back_ref[...].astype(jnp.float32), axis=0)
    for k in range(chunks):
        out_ref[:, k * LANES : (k + 1) * LANES] = total_ref[k : k + 1, :].astype(jnp.bfloat16)


def dense_shards(tokens, grad_out, route_token, route_count, route_prob, w_gate, w_up, w_down):
    features = tokens.shape[1]
    hidden_units = w_gate.shape[1]
    chunks = features // LANES
    count = lax.axis_size("group") * lax.axis_size("member")
    rows = round_up(2 * chunks + 1, 16)
    sent_rows = round_up(chunks, 16)
    packed = pl.pallas_call(
        functools.partial(pack_kernel, chunks),
        out_shape=jax.ShapeDtypeStruct((rows, LANES), jnp.bfloat16),
        in_specs=[VMEM, VMEM, SMEM, SMEM, SMEM],
        out_specs=VMEM,
        scratch_shapes=[pltpu.VMEM((rows, LANES), jnp.float32)],
        name="pack_rows",
    )(tokens, grad_out, route_token, route_count, route_prob)
    gathered = lax.all_gather(packed, AXES, axis=0, tiled=False)
    sent, x, scaled, acts = pl.pallas_call(
        functools.partial(partial_kernel, chunks),
        out_shape=(
            jax.ShapeDtypeStruct((count, sent_rows, LANES), jnp.bfloat16),
            jax.ShapeDtypeStruct((count, features), jnp.bfloat16),
            jax.ShapeDtypeStruct((count, features), jnp.bfloat16),
            jax.ShapeDtypeStruct((3, count, hidden_units), jnp.bfloat16),
        ),
        in_specs=[VMEM] * 4,
        out_specs=(VMEM,) * 4,
        scratch_shapes=[
            pltpu.VMEM((count * rows, LANES), jnp.float32),
            pltpu.VMEM((count * sent_rows, LANES), jnp.float32),
        ],
        compiler_params=pltpu.CompilerParams(vmem_limit_bytes=24 * 1024 * 1024),
        name="partial_rows",
    )(gathered, w_gate, w_up, w_down)
    back = lax.all_to_all(sent, AXES, split_axis=0, concat_axis=0, tiled=True)
    grad_shape = jax.ShapeDtypeStruct((1, hidden_units, features), jnp.bfloat16)
    grad_gate, grad_up, grad_down = pl.pallas_call(
        grads_kernel,
        out_shape=(grad_shape,) * 3,
        in_specs=[VMEM] * 3,
        out_specs=(VMEM,) * 3,
        compiler_params=pltpu.CompilerParams(vmem_limit_bytes=24 * 1024 * 1024),
        cost_estimate=pl.CostEstimate(
            flops=6 * count * hidden_units * features,
            bytes_accessed=6 * hidden_units * features,
            transcendentals=0,
        ),
        name="weight_grads",
    )(x, scaled, acts)
    grad_tokens = pl.pallas_call(
        functools.partial(sum_kernel, chunks),
        out_shape=jax.ShapeDtypeStruct((1, features), jnp.bfloat16),
        in_specs=[VMEM],
        out_specs=VMEM,
        scratch_shapes=[pltpu.VMEM((sent_rows, LANES), jnp.float32)],
        name="sum_rows",
    )(back)
    return grad_tokens, grad_gate, grad_up, grad_down


def slice_backward(rows_x, rows_scaled, gate_weight, up_weight, down_weight):
    gate_value = jnp.dot(rows_x, gate_weight.T, preferred_element_type=jnp.float32)
    up_value = jnp.dot(rows_x, up_weight.T, preferred_element_type=jnp.float32)
    sigma_gate = jax.nn.sigmoid(gate_value)
    active = gate_value * sigma_gate
    hidden = (active * up_value).astype(jnp.bfloat16)
    d_hidden = jnp.dot(rows_scaled, down_weight.T, preferred_element_type=jnp.float32)
    d_gate = (d_hidden * up_value * sigma_gate * (1.0 + gate_value * (1.0 - sigma_gate))).astype(
        jnp.bfloat16
    )
    d_up = (d_hidden * active).astype(jnp.bfloat16)
    grad_down = jnp.dot(hidden.T, rows_scaled, preferred_element_type=jnp.float32).astype(
        jnp.bfloat16
    )
    grad_gate = jnp.dot(d_gate.T, rows_x, preferred_element_type=jnp.float32).astype(jnp.bfloat16)
    grad_up = jnp.dot(d_up.T, rows_x, preferred_element_type=jnp.float32).astype(jnp.bfloat16)
    partial_rows = jnp.dot(d_gate, gate_weight, preferred_element_type=jnp.float32)
    partial_rows = partial_rows + jnp.dot(d_up, up_weight, preferred_element_type=jnp.float32)
    return (grad_gate, grad_up, grad_down, partial_rows)


def routed_shards(tokens, grad_out, route_token, route_count, route_prob, w_gate, w_up, w_down):
    groups = route_token.shape[1]
    capacity = route_token.shape[3]
    features = tokens.shape[1]
    block_rows = groups * capacity
    split_count = max(8, lax.axis_size("member") // 8)
    expert_local = lax.axis_index("member") // split_count
    slot_tokens = lax.dynamic_index_in_dim(route_token[0], expert_local, 1, keepdims=False)
    slot_counts = lax.dynamic_index_in_dim(route_count[0], expert_local, 1, keepdims=False)
    slot_probs = lax.dynamic_index_in_dim(route_prob[0], expert_local, 1, keepdims=False)
    slot_index = jnp.arange(capacity, dtype=jnp.int32)[None, :]
    live = (slot_index < slot_counts[:, None]).astype(jnp.float32)
    slot_weights = (slot_probs * live).reshape(-1)
    flat_slots = slot_tokens.reshape(-1)
    group_x, group_dy = (
        lax.all_gather(tokens, "member", axis=0, tiled=True),
        lax.all_gather(grad_out, "member", axis=0, tiled=True),
    )
    picked_x = jnp.take(group_x, flat_slots, axis=0)
    picked_dy = jnp.take(group_dy, flat_slots, axis=0)
    scaled = (slot_weights[:, None] * picked_dy.astype(jnp.float32)).astype(jnp.bfloat16)
    send_x = picked_x.reshape(groups, capacity, features)
    send_scaled = scaled.reshape(groups, capacity, features)
    rows_x, rows_scaled = (
        lax.all_to_all(send_x, "group", split_axis=0, concat_axis=0, tiled=True),
        lax.all_to_all(send_scaled, "group", split_axis=0, concat_axis=0, tiled=True),
    )
    grad_gate, grad_up, grad_down, partial_rows = slice_backward(
        rows_x.reshape(block_rows, features),
        rows_scaled.reshape(block_rows, features),
        w_gate[0],
        w_up[0],
        w_down[0],
    )
    returned = lax.all_to_all(
        partial_rows.reshape(groups, capacity, features),
        "group",
        split_axis=0,
        concat_axis=0,
        tiled=True,
    )
    returned = returned.reshape(block_rows, features)
    row_numbers = jnp.arange(tokens.shape[0] * lax.axis_size("member"), dtype=jnp.int32)
    selector = (row_numbers[:, None] == flat_slots[None, :]).astype(jnp.float32)
    summed = lax.psum_scatter(
        jnp.dot(
            selector, returned, precision=lax.Precision.HIGHEST, preferred_element_type=jnp.float32
        ),
        "member",
        scatter_dimension=0,
        tiled=True,
    )
    return (summed.astype(jnp.bfloat16), grad_gate[None], grad_up[None], grad_down[None])


def shards(tokens, grad_out, route_token, *rest):
    devices = lax.axis_size("group") * lax.axis_size("member")
    _, groups, experts, capacity = route_token.shape
    dense = devices * tokens.shape[0] <= groups * capacity and experts == 1 and groups <= 32
    body = dense_shards if dense and tokens.shape[0] == 1 else routed_shards
    return body(tokens, grad_out, route_token, *rest)


def solution(mesh):
    placed = (
        P(("group", "member"), None),
        P(("group", "member"), None),
        P("group", None, None, None),
        P("group", None, None),
        P("group", None, None, None),
        P(("group", "member"), None, None),
        P(("group", "member"), None, None),
        P(("group", "member"), None, None),
    )
    return jax.shard_map(
        shards,
        mesh=mesh,
        in_specs=placed,
        out_specs=(
            P(("group", "member"), None),
            P(("group", "member"), None, None),
            P(("group", "member"), None, None),
            P(("group", "member"), None, None),
        ),
        check_vma=False,
    )
```

```python
import functools

import jax
import jax.numpy as jnp
from jax import lax
from jax.experimental import pallas as pl
from jax.experimental.pallas import tpu as pltpu
from jax.sharding import PartitionSpec as P

LANES = 128
PIECES = 4
AXES = ("group", "member")
VMEM = pl.BlockSpec(memory_space=pltpu.VMEM)
HBM = pl.BlockSpec(memory_space=pltpu.HBM)
SMEM = pl.BlockSpec(memory_space=pltpu.SMEM)
NT = (((1,), (1,)), ((), ()))
TN = (((0,), (0,)), ((), ()))


def round_up(value, step):
    return (value + step - 1) // step * step


def pack_kernel(chunks, tokens_ref, grad_ref, token_ref, count_ref, prob_ref, out_ref, rows_ref):
    me = lax.axis_index("member")
    groups, experts, capacity = token_ref.shape[1:]
    token_row = tokens_ref[...].astype(jnp.float32)
    grad_row = grad_ref[...].astype(jnp.float32)
    for k in range(chunks):
        part = slice(k * LANES, (k + 1) * LANES)
        rows_ref[k : k + 1, :] = token_row[:, part]
        rows_ref[chunks + k : chunks + k + 1, :] = grad_row[:, part]
    lane = lax.broadcasted_iota(jnp.int32, (1, LANES), 1)
    third = lax.rem(lane, 32)
    weights = jnp.zeros((1, LANES), jnp.float32)
    for g in range(groups):
        for j in range(experts):
            weight = jnp.float32(0)
            for p in range(capacity):
                live = (token_ref[0, g, j, p] == me) & (p < count_ref[0, j, g])
                weight = weight + jnp.where(live, prob_ref[0, g, j, p], 0.0)
            weights = jnp.where(third == g * experts + j, weight, weights)
    high = weights.astype(jnp.bfloat16).astype(jnp.float32)
    middle = (weights - high).astype(jnp.bfloat16).astype(jnp.float32)
    low = weights - high - middle
    parts = jnp.where(lane < 32, high, jnp.where(lane < 64, middle, jnp.where(lane < 96, low, 0.0)))
    rows_ref[2 * chunks : 2 * chunks + 1, :] = parts
    used = 2 * chunks + 1
    rows_ref[used:, :] = jnp.zeros((rows_ref.shape[0] - used, LANES), jnp.float32)
    out_ref[...] = rows_ref[...].astype(jnp.bfloat16)


def load_kernel(after_ref, gate_ref, up_ref, down_ref, gate_out, up_out, down_out, sems):
    del after_ref
    copies = []
    for n, (source, target) in enumerate(
        ((gate_ref, gate_out), (up_ref, up_out), (down_ref, down_out))
    ):
        height = source.shape[1] // PIECES
        for k in range(PIECES):
            part = pl.ds(k * height, height)
            copies.append(
                pltpu.make_async_copy(source.at[0, part], target.at[part], sems.at[n * PIECES + k])
            )
    for copy in copies:
        copy.start()
    for copy in copies:
        copy.wait()


def partial_kernel(chunks, pieces, *refs):
    piece_refs = refs[:pieces]
    gate_ref, up_ref, down_ref, sent_ref, x_ref, scaled_ref, acts_ref, wide_ref, spread_ref = refs[
        pieces:
    ]
    count, rows, _ = piece_refs[0].shape
    tokens = count * pieces
    expert = lax.axis_index("group")
    me = expert * lax.axis_size("member") + lax.axis_index("member")
    for n, piece_ref in enumerate(piece_refs):
        block = pl.ds(n * count * rows, count * rows)
        wide_ref[block, :] = piece_ref[...].reshape(count * rows, LANES).astype(jnp.float32)

    def column(k):
        return wide_ref[pl.ds(k, tokens, stride=rows), :]

    lane = lax.broadcasted_iota(jnp.int32, (tokens, LANES), 1)
    mine = (lane < 96) & (lax.rem(lane, 32) == expert)
    weight = jnp.sum(jnp.where(mine, column(2 * chunks), 0.0), axis=1, keepdims=True)
    for k in range(chunks):
        part = slice(k * LANES, (k + 1) * LANES)
        x_ref[:, part] = column(k).astype(jnp.bfloat16)
        scaled_ref[:, part] = (weight * column(chunks + k)).astype(jnp.bfloat16)

    x = x_ref[...]
    gate_value = lax.dot_general(x, gate_ref[...], NT, preferred_element_type=jnp.float32)
    up_value = lax.dot_general(x, up_ref[...], NT, preferred_element_type=jnp.float32)
    d_hidden = lax.dot_general(
        scaled_ref[...], down_ref[...], NT, preferred_element_type=jnp.float32
    )
    sigma_gate = jax.nn.sigmoid(gate_value)
    active = gate_value * sigma_gate
    hidden = (active * up_value).astype(jnp.bfloat16)
    d_gate = (d_hidden * up_value * sigma_gate * (1.0 + gate_value * (1.0 - sigma_gate))).astype(
        jnp.bfloat16
    )
    d_up = (d_hidden * active).astype(jnp.bfloat16)
    acts_ref[0] = d_gate
    acts_ref[1] = d_up
    acts_ref[2] = hidden
    sent_rows = sent_ref.shape[1]
    partial = jnp.dot(d_gate, gate_ref[...], preferred_element_type=jnp.float32)
    partial = partial + jnp.dot(d_up, up_ref[...], preferred_element_type=jnp.float32)
    for k in range(chunks):
        spread_ref[pl.ds(k, tokens, stride=sent_rows), :] = partial[:, k * LANES : (k + 1) * LANES]
    for k in range(chunks, sent_rows):
        spread_ref[pl.ds(k, tokens, stride=sent_rows), :] = jnp.zeros((tokens, LANES), jnp.float32)
    for n in range(pieces):
        for z in range(count):
            source = pl.ds((n * count + z) * sent_rows, sent_rows)
            owner = me ^ (z * lax.axis_size("member") + n)
            sent_ref[owner] = spread_ref[source, :].astype(jnp.bfloat16)


def grads_kernel(x_ref, scaled_ref, acts_ref, gate_out, up_out, down_out):
    x = x_ref[...]
    gate_out[0] = lax.dot_general(
        acts_ref[0], x, TN, preferred_element_type=jnp.float32
    ).astype(jnp.bfloat16)
    up_out[0] = lax.dot_general(
        acts_ref[1], x, TN, preferred_element_type=jnp.float32
    ).astype(jnp.bfloat16)
    down_out[0] = lax.dot_general(
        acts_ref[2], scaled_ref[...], TN, preferred_element_type=jnp.float32
    ).astype(jnp.bfloat16)


def sum_kernel(chunks, back_ref, out_ref, total_ref):
    total_ref[...] = jnp.sum(back_ref[...].astype(jnp.float32), axis=0)
    for k in range(chunks):
        out_ref[:, k * LANES : (k + 1) * LANES] = total_ref[k : k + 1, :].astype(jnp.bfloat16)


def exchange(value, distance):
    count = lax.axis_size("group") * lax.axis_size("member")
    return lax.ppermute(value, AXES, [(i, i ^ distance) for i in range(count)])


def dense_shards(tokens, grad_out, route_token, route_count, route_prob, w_gate, w_up, w_down):
    features = tokens.shape[1]
    hidden_units = w_gate.shape[1]
    chunks = features // LANES
    groups, members = lax.axis_size("group"), lax.axis_size("member")
    count = groups * members
    rows = round_up(2 * chunks + 1, 16)
    sent_rows = round_up(chunks, 16)
    packed = pl.pallas_call(
        functools.partial(pack_kernel, chunks),
        out_shape=jax.ShapeDtypeStruct((rows, LANES), jnp.bfloat16),
        in_specs=[VMEM, VMEM, SMEM, SMEM, SMEM],
        out_specs=VMEM,
        scratch_shapes=[pltpu.VMEM((rows, LANES), jnp.float32)],
        compiler_params=pltpu.CompilerParams(vmem_limit_bytes=1024 * 1024),
        name="pack_rows",
    )(tokens, grad_out, route_token, jnp.swapaxes(route_count, 1, 2), route_prob)
    gate, up, down = pl.pallas_call(
        load_kernel,
        out_shape=(pltpu.VMEM(w_gate.shape[1:], jnp.bfloat16),) * 3,
        in_specs=[HBM] * 4,
        out_specs=(VMEM,) * 3,
        scratch_shapes=[pltpu.SemaphoreType.DMA((3 * PIECES,))],
        compiler_params=pltpu.CompilerParams(vmem_limit_bytes=8 * 1024 * 1024),
        cost_estimate=pl.CostEstimate(
            flops=0, bytes_accessed=6 * hidden_units * features, transcendentals=0
        ),
        name="load_weights",
    )(packed, w_gate, w_up, w_down)
    column = jnp.stack([packed] + [exchange(packed, z * members) for z in range(1, groups)])
    plane = {0: column}
    for n in range(2, members, 2):
        plane[n] = exchange(column, n)
    for n in range(0, members, 2):
        plane[n + 1] = exchange(plane[n], 1)
    sent, x, scaled, acts = pl.pallas_call(
        functools.partial(partial_kernel, chunks, members),
        out_shape=(
            jax.ShapeDtypeStruct((count, sent_rows, LANES), jnp.bfloat16),
            pltpu.VMEM((count, features), jnp.bfloat16),
            pltpu.VMEM((count, features), jnp.bfloat16),
            pltpu.VMEM((3, count, hidden_units), jnp.bfloat16),
        ),
        in_specs=[VMEM] * (members + 3),
        out_specs=(VMEM,) * 4,
        scratch_shapes=[
            pltpu.VMEM((count * rows, LANES), jnp.float32),
            pltpu.VMEM((count * sent_rows, LANES), jnp.float32),
        ],
        compiler_params=pltpu.CompilerParams(vmem_limit_bytes=16 * 1024 * 1024),
        name="partial_rows",
    )(*[plane[n] for n in range(members)], gate, up, down)
    back = lax.all_to_all(sent, AXES, split_axis=0, concat_axis=0, tiled=True)
    grad_shape = jax.ShapeDtypeStruct((1, hidden_units, features), jnp.bfloat16)
    grad_gate, grad_up, grad_down = pl.pallas_call(
        grads_kernel,
        out_shape=(grad_shape,) * 3,
        in_specs=[VMEM] * 3,
        out_specs=(VMEM,) * 3,
        compiler_params=pltpu.CompilerParams(vmem_limit_bytes=16 * 1024 * 1024),
        cost_estimate=pl.CostEstimate(
            flops=6 * count * hidden_units * features,
            bytes_accessed=6 * hidden_units * features,
            transcendentals=0,
        ),
        name="weight_grads",
    )(x, scaled, acts)
    grad_tokens = pl.pallas_call(
        functools.partial(sum_kernel, chunks),
        out_shape=jax.ShapeDtypeStruct((1, features), jnp.bfloat16),
        in_specs=[VMEM],
        out_specs=VMEM,
        scratch_shapes=[pltpu.VMEM((sent_rows, LANES), jnp.float32)],
        compiler_params=pltpu.CompilerParams(vmem_limit_bytes=4 * 1024 * 1024),
        name="sum_rows",
    )(back)
    return grad_tokens, grad_gate, grad_up, grad_down


def slice_backward(rows_x, rows_scaled, gate_weight, up_weight, down_weight):
    gate_value = jnp.dot(rows_x, gate_weight.T, preferred_element_type=jnp.float32)
    up_value = jnp.dot(rows_x, up_weight.T, preferred_element_type=jnp.float32)
    sigma_gate = jax.nn.sigmoid(gate_value)
    active = gate_value * sigma_gate
    hidden = (active * up_value).astype(jnp.bfloat16)
    d_hidden = jnp.dot(rows_scaled, down_weight.T, preferred_element_type=jnp.float32)
    d_gate = (d_hidden * up_value * sigma_gate * (1.0 + gate_value * (1.0 - sigma_gate))).astype(
        jnp.bfloat16
    )
    d_up = (d_hidden * active).astype(jnp.bfloat16)
    grad_down = jnp.dot(hidden.T, rows_scaled, preferred_element_type=jnp.float32).astype(
        jnp.bfloat16
    )
    grad_gate = jnp.dot(d_gate.T, rows_x, preferred_element_type=jnp.float32).astype(jnp.bfloat16)
    grad_up = jnp.dot(d_up.T, rows_x, preferred_element_type=jnp.float32).astype(jnp.bfloat16)
    partial_rows = jnp.dot(d_gate, gate_weight, preferred_element_type=jnp.float32)
    partial_rows = partial_rows + jnp.dot(d_up, up_weight, preferred_element_type=jnp.float32)
    return (grad_gate, grad_up, grad_down, partial_rows)


def routed_shards(tokens, grad_out, route_token, route_count, route_prob, w_gate, w_up, w_down):
    groups = route_token.shape[1]
    capacity = route_token.shape[3]
    features = tokens.shape[1]
    block_rows = groups * capacity
    split_count = max(8, lax.axis_size("member") // 8)
    expert_local = lax.axis_index("member") // split_count
    slot_tokens = lax.dynamic_index_in_dim(route_token[0], expert_local, 1, keepdims=False)
    slot_counts = lax.dynamic_index_in_dim(route_count[0], expert_local, 1, keepdims=False)
    slot_probs = lax.dynamic_index_in_dim(route_prob[0], expert_local, 1, keepdims=False)
    slot_index = jnp.arange(capacity, dtype=jnp.int32)[None, :]
    live = (slot_index < slot_counts[:, None]).astype(jnp.float32)
    slot_weights = (slot_probs * live).reshape(-1)
    flat_slots = slot_tokens.reshape(-1)
    group_x, group_dy = (
        lax.all_gather(tokens, "member", axis=0, tiled=True),
        lax.all_gather(grad_out, "member", axis=0, tiled=True),
    )
    picked_x = jnp.take(group_x, flat_slots, axis=0)
    picked_dy = jnp.take(group_dy, flat_slots, axis=0)
    scaled = (slot_weights[:, None] * picked_dy.astype(jnp.float32)).astype(jnp.bfloat16)
    send_x = picked_x.reshape(groups, capacity, features)
    send_scaled = scaled.reshape(groups, capacity, features)
    rows_x, rows_scaled = (
        lax.all_to_all(send_x, "group", split_axis=0, concat_axis=0, tiled=True),
        lax.all_to_all(send_scaled, "group", split_axis=0, concat_axis=0, tiled=True),
    )
    grad_gate, grad_up, grad_down, partial_rows = slice_backward(
        rows_x.reshape(block_rows, features),
        rows_scaled.reshape(block_rows, features),
        w_gate[0],
        w_up[0],
        w_down[0],
    )
    returned = lax.all_to_all(
        partial_rows.reshape(groups, capacity, features),
        "group",
        split_axis=0,
        concat_axis=0,
        tiled=True,
    )
    returned = returned.reshape(block_rows, features)
    row_numbers = jnp.arange(tokens.shape[0] * lax.axis_size("member"), dtype=jnp.int32)
    selector = (row_numbers[:, None] == flat_slots[None, :]).astype(jnp.float32)
    summed = lax.psum_scatter(
        jnp.dot(
            selector, returned, precision=lax.Precision.HIGHEST, preferred_element_type=jnp.float32
        ),
        "member",
        scatter_dimension=0,
        tiled=True,
    )
    return (summed.astype(jnp.bfloat16), grad_gate[None], grad_up[None], grad_down[None])


def shards(tokens, grad_out, route_token, *rest):
    devices = lax.axis_size("group") * lax.axis_size("member")
    _, groups, experts, capacity = route_token.shape
    dense = devices * tokens.shape[0] <= groups * capacity and experts == 1 and groups <= 32
    paired = tokens.shape[0] == 1 and devices & (devices - 1) == 0
    body = dense_shards if dense and paired else routed_shards
    return body(tokens, grad_out, route_token, *rest)


def solution(mesh):
    placed = (
        P(("group", "member"), None),
        P(("group", "member"), None),
        P("group", None, None, None),
        P("group", None, None),
        P("group", None, None, None),
        P(("group", "member"), None, None),
        P(("group", "member"), None, None),
        P(("group", "member"), None, None),
    )
    return jax.shard_map(
        shards,
        mesh=mesh,
        in_specs=placed,
        out_specs=(
            P(("group", "member"), None),
            P(("group", "member"), None, None),
            P(("group", "member"), None, None),
            P(("group", "member"), None, None),
        ),
        check_vma=False,
    )
```

```python
import functools

import jax
import jax.numpy as jnp
from jax import lax
from jax.experimental import pallas as pl
from jax.experimental.pallas import tpu as pltpu
from jax.sharding import PartitionSpec as P

LANES = 128
PIECES = 4
AXES = ("group", "member")
VMEM = pl.BlockSpec(memory_space=pltpu.VMEM)
HBM = pl.BlockSpec(memory_space=pltpu.HBM)
SMEM = pl.BlockSpec(memory_space=pltpu.SMEM)
NT = (((1,), (1,)), ((), ()))
TN = (((0,), (0,)), ((), ()))


def round_up(value, step):
    return (value + step - 1) // step * step


def pack_kernel(chunks, tokens_ref, grad_ref, token_ref, count_ref, prob_ref, out_ref, rows_ref):
    me = lax.axis_index("member")
    groups, experts, capacity = token_ref.shape[1:]
    token_row = tokens_ref[...].astype(jnp.float32)
    grad_row = grad_ref[...].astype(jnp.float32)
    for k in range(chunks):
        part = slice(k * LANES, (k + 1) * LANES)
        rows_ref[k : k + 1, :] = token_row[:, part]
        rows_ref[chunks + k : chunks + k + 1, :] = grad_row[:, part]
    lane = lax.broadcasted_iota(jnp.int32, (1, LANES), 1)
    third = lax.rem(lane, 32)
    weights = jnp.zeros((1, LANES), jnp.float32)
    for g in range(groups):
        for j in range(experts):
            weight = jnp.float32(0)
            for p in range(capacity):
                live = (token_ref[0, g, j, p] == me) & (p < count_ref[0, j, g])
                weight = weight + jnp.where(live, prob_ref[0, g, j, p], 0.0)
            weights = jnp.where(third == g * experts + j, weight, weights)
    high = weights.astype(jnp.bfloat16).astype(jnp.float32)
    middle = (weights - high).astype(jnp.bfloat16).astype(jnp.float32)
    low = weights - high - middle
    parts = jnp.where(lane < 32, high, jnp.where(lane < 64, middle, jnp.where(lane < 96, low, 0.0)))
    rows_ref[2 * chunks : 2 * chunks + 1, :] = parts
    used = 2 * chunks + 1
    rows_ref[used:, :] = jnp.zeros((rows_ref.shape[0] - used, LANES), jnp.float32)
    out_ref[...] = rows_ref[...].astype(jnp.bfloat16)


def load_kernel(gate_ref, up_ref, down_ref, gate_out, up_out, down_out, sems):
    copies = []
    for n, (source, target) in enumerate(
        ((gate_ref, gate_out), (up_ref, up_out), (down_ref, down_out))
    ):
        height = source.shape[1] // PIECES
        for k in range(PIECES):
            part = pl.ds(k * height, height)
            copies.append(
                pltpu.make_async_copy(
                    source.at[:, part], target.at[:, part], sems.at[n * PIECES + k]
                )
            )
    for copy in copies:
        copy.start()
    for copy in copies:
        copy.wait()


def partial_kernel(chunks, pieces, *refs):
    piece_refs, refs = refs[:pieces], refs[pieces:]
    weight_refs, refs = refs[:6], refs[6:]
    sent_ref, acts_ref, rows_ref, wide_ref, spread_ref = refs
    groups, rows, _ = piece_refs[0].shape
    tokens = groups * pieces
    features = chunks * LANES
    expert = lax.axis_index("group")
    place = expert * pieces + lax.axis_index("member") // 2
    for n, piece_ref in enumerate(piece_refs):
        block = pl.ds(n * groups * rows, groups * rows)
        wide_ref[block, :] = piece_ref[...].reshape(groups * rows, LANES).astype(jnp.float32)

    def column(k):
        return wide_ref[pl.ds(k, tokens, stride=rows), :]

    lane = lax.broadcasted_iota(jnp.int32, (tokens, LANES), 1)
    mine = (lane < 96) & (lax.rem(lane, 32) == expert)
    weight = jnp.sum(jnp.where(mine, column(2 * chunks), 0.0), axis=1, keepdims=True)
    for k in range(chunks):
        rows_ref[:, k * LANES : (k + 1) * LANES] = column(k).astype(jnp.bfloat16)
        rows_ref[:, features + k * LANES : features + (k + 1) * LANES] = (
            weight * column(chunks + k)
        ).astype(jnp.bfloat16)

    x = rows_ref[:, :features]
    scaled = rows_ref[:, features : 2 * features]
    partial = None
    for core in range(2):
        gate, up, down = (ref[0] for ref in weight_refs[3 * core : 3 * core + 3])
        gate_value = lax.dot_general(x, gate, NT, preferred_element_type=jnp.float32)
        up_value = lax.dot_general(x, up, NT, preferred_element_type=jnp.float32)
        d_hidden = lax.dot_general(scaled, down, NT, preferred_element_type=jnp.float32)
        sigma_gate = jax.nn.sigmoid(gate_value)
        active = gate_value * sigma_gate
        hidden = (active * up_value).astype(jnp.bfloat16)
        d_gate = (
            d_hidden * up_value * sigma_gate * (1.0 + gate_value * (1.0 - sigma_gate))
        ).astype(jnp.bfloat16)
        d_up = (d_hidden * active).astype(jnp.bfloat16)
        for k, value in enumerate((d_gate, d_up, hidden)):
            if core == 0:
                acts_ref[k] = value
            else:
                first = 2 * features + k * value.shape[1]
                rows_ref[:, first : first + value.shape[1]] = value
        term = jnp.dot(d_gate, gate, preferred_element_type=jnp.float32)
        term = term + jnp.dot(d_up, up, preferred_element_type=jnp.float32)
        partial = term if core == 0 else partial + term
    sent_rows = sent_ref.shape[1]
    for k in range(chunks):
        spread_ref[pl.ds(k, tokens, stride=sent_rows), :] = partial[:, k * LANES : (k + 1) * LANES]
    for k in range(chunks, sent_rows):
        spread_ref[pl.ds(k, tokens, stride=sent_rows), :] = jnp.zeros((tokens, LANES), jnp.float32)
    for n in range(pieces):
        for z in range(groups):
            source = pl.ds((n * groups + z) * sent_rows, sent_rows)
            sent_ref[place ^ (z * pieces + n)] = spread_ref[source, :].astype(jnp.bfloat16)


def grads_kernel(features, rows_ref, other_ref, acts_ref, gate_out, up_out, down_out):
    units = acts_ref.shape[2]
    for k, (out, first) in enumerate(((gate_out, 0), (up_out, 0), (down_out, features))):
        part = slice(first, first + features)
        acts = slice(2 * features + k * units, 2 * features + (k + 1) * units)
        left = jnp.concatenate([acts_ref[k], other_ref[:, acts]], axis=0)
        right = jnp.concatenate([rows_ref[:, part], other_ref[:, part]], axis=0)
        out[0] = lax.dot_general(left, right, TN, preferred_element_type=jnp.float32).astype(
            jnp.bfloat16
        )


def sum_kernel(chunks, back_ref, out_ref, total_ref):
    total_ref[...] = jnp.sum(back_ref[...].astype(jnp.float32), axis=0)
    for k in range(chunks):
        out_ref[:, k * LANES : (k + 1) * LANES] = total_ref[k : k + 1, :].astype(jnp.bfloat16)


def exchange(value, distance):
    count = lax.axis_size("group") * lax.axis_size("member")
    return lax.ppermute(value, AXES, [(i, i ^ distance) for i in range(count)])


def in_hbm(value):
    return pltpu.with_memory_space_constraint(value, pltpu.HBM)


def dense_shards(tokens, grad_out, route_token, route_count, route_prob, w_gate, w_up, w_down):
    features = tokens.shape[1]
    units = w_gate.shape[1]
    chunks = features // LANES
    groups, members = lax.axis_size("group"), lax.axis_size("member")
    count = groups * members
    half = count // 2
    rows = round_up(2 * chunks + 1, 16)
    sent_rows = round_up(chunks, 16)
    packed = pl.pallas_call(
        functools.partial(pack_kernel, chunks),
        out_shape=jax.ShapeDtypeStruct((rows, LANES), jnp.bfloat16),
        in_specs=[VMEM, VMEM, SMEM, SMEM, SMEM],
        out_specs=VMEM,
        scratch_shapes=[pltpu.VMEM((rows, LANES), jnp.float32)],
        name="pack_rows",
    )(tokens, grad_out, route_token, jnp.swapaxes(route_count, 1, 2), route_prob)
    weights = (w_gate, w_up, w_down)
    swapped = [exchange(w, 1) for w in weights]
    loaded = pl.pallas_call(
        load_kernel,
        out_shape=(pltpu.VMEM(w_gate.shape, jnp.bfloat16),) * 3,
        in_specs=[HBM] * 3,
        out_specs=(VMEM,) * 3,
        scratch_shapes=[pltpu.SemaphoreType.DMA((3 * PIECES,))],
        compiler_params=pltpu.CompilerParams(vmem_limit_bytes=8 * 1024 * 1024),
        cost_estimate=pl.CostEstimate(
            flops=0, bytes_accessed=6 * units * features, transcendentals=0
        ),
        name="load_weights",
    )(*[in_hbm(w) for w in weights])
    column = jnp.stack([packed] + [exchange(packed, z * members) for z in range(1, groups)])
    pieces = [column] + [exchange(column, n) for n in range(2, members, 2)]
    sent, acts, mine = pl.pallas_call(
        functools.partial(partial_kernel, chunks, members // 2),
        out_shape=(
            jax.ShapeDtypeStruct((half, sent_rows, LANES), jnp.bfloat16),
            pltpu.VMEM((3, half, units), jnp.bfloat16),
            pltpu.VMEM((half, 2 * features + 3 * units), jnp.bfloat16),
        ),
        in_specs=[VMEM] * (members // 2 + 6),
        out_specs=(VMEM,) * 3,
        scratch_shapes=[
            pltpu.VMEM((half * rows, LANES), jnp.float32),
            pltpu.VMEM((half * sent_rows, LANES), jnp.float32),
        ],
        compiler_params=pltpu.CompilerParams(vmem_limit_bytes=16 * 1024 * 1024),
        name="partial_rows",
    )(*pieces, *loaded, *swapped)
    cores = [list(range(c, count, 2)) for c in range(2)]
    back = lax.all_to_all(
        sent, AXES, split_axis=0, concat_axis=0, tiled=True, axis_index_groups=cores
    )
    other = exchange(mine, 1)
    grad_shape = jax.ShapeDtypeStruct((1, units, features), jnp.bfloat16)
    grad_gate, grad_up, grad_down = pl.pallas_call(
        functools.partial(grads_kernel, features),
        out_shape=(grad_shape,) * 3,
        in_specs=[VMEM] * 3,
        out_specs=(VMEM,) * 3,
        compiler_params=pltpu.CompilerParams(vmem_limit_bytes=16 * 1024 * 1024),
        cost_estimate=pl.CostEstimate(
            flops=6 * count * units * features,
            bytes_accessed=6 * units * features,
            transcendentals=0,
        ),
        name="weight_grads",
    )(mine, other, acts)
    grad_tokens = pl.pallas_call(
        functools.partial(sum_kernel, chunks),
        out_shape=jax.ShapeDtypeStruct((1, features), jnp.bfloat16),
        in_specs=[VMEM],
        out_specs=VMEM,
        scratch_shapes=[pltpu.VMEM((sent_rows, LANES), jnp.float32)],
        compiler_params=pltpu.CompilerParams(vmem_limit_bytes=4 * 1024 * 1024),
        name="sum_rows",
    )(back)
    return grad_tokens, grad_gate, grad_up, grad_down


def slice_backward(rows_x, rows_scaled, gate_weight, up_weight, down_weight):
    gate_value = jnp.dot(rows_x, gate_weight.T, preferred_element_type=jnp.float32)
    up_value = jnp.dot(rows_x, up_weight.T, preferred_element_type=jnp.float32)
    sigma_gate = jax.nn.sigmoid(gate_value)
    active = gate_value * sigma_gate
    hidden = (active * up_value).astype(jnp.bfloat16)
    d_hidden = jnp.dot(rows_scaled, down_weight.T, preferred_element_type=jnp.float32)
    d_gate = (d_hidden * up_value * sigma_gate * (1.0 + gate_value * (1.0 - sigma_gate))).astype(
        jnp.bfloat16
    )
    d_up = (d_hidden * active).astype(jnp.bfloat16)
    grad_down = jnp.dot(hidden.T, rows_scaled, preferred_element_type=jnp.float32).astype(
        jnp.bfloat16
    )
    grad_gate = jnp.dot(d_gate.T, rows_x, preferred_element_type=jnp.float32).astype(jnp.bfloat16)
    grad_up = jnp.dot(d_up.T, rows_x, preferred_element_type=jnp.float32).astype(jnp.bfloat16)
    partial_rows = jnp.dot(d_gate, gate_weight, preferred_element_type=jnp.float32)
    partial_rows = partial_rows + jnp.dot(d_up, up_weight, preferred_element_type=jnp.float32)
    return (grad_gate, grad_up, grad_down, partial_rows)


def routed_shards(tokens, grad_out, route_token, route_count, route_prob, w_gate, w_up, w_down):
    groups = route_token.shape[1]
    capacity = route_token.shape[3]
    features = tokens.shape[1]
    block_rows = groups * capacity
    split_count = max(8, lax.axis_size("member") // 8)
    expert_local = lax.axis_index("member") // split_count
    slot_tokens = lax.dynamic_index_in_dim(route_token[0], expert_local, 1, keepdims=False)
    slot_counts = lax.dynamic_index_in_dim(route_count[0], expert_local, 1, keepdims=False)
    slot_probs = lax.dynamic_index_in_dim(route_prob[0], expert_local, 1, keepdims=False)
    slot_index = jnp.arange(capacity, dtype=jnp.int32)[None, :]
    live = (slot_index < slot_counts[:, None]).astype(jnp.float32)
    slot_weights = (slot_probs * live).reshape(-1)
    flat_slots = slot_tokens.reshape(-1)
    group_x, group_dy = (
        lax.all_gather(tokens, "member", axis=0, tiled=True),
        lax.all_gather(grad_out, "member", axis=0, tiled=True),
    )
    picked_x = jnp.take(group_x, flat_slots, axis=0)
    picked_dy = jnp.take(group_dy, flat_slots, axis=0)
    scaled = (slot_weights[:, None] * picked_dy.astype(jnp.float32)).astype(jnp.bfloat16)
    send_x = picked_x.reshape(groups, capacity, features)
    send_scaled = scaled.reshape(groups, capacity, features)
    rows_x, rows_scaled = (
        lax.all_to_all(send_x, "group", split_axis=0, concat_axis=0, tiled=True),
        lax.all_to_all(send_scaled, "group", split_axis=0, concat_axis=0, tiled=True),
    )
    grad_gate, grad_up, grad_down, partial_rows = slice_backward(
        rows_x.reshape(block_rows, features),
        rows_scaled.reshape(block_rows, features),
        w_gate[0],
        w_up[0],
        w_down[0],
    )
    returned = lax.all_to_all(
        partial_rows.reshape(groups, capacity, features),
        "group",
        split_axis=0,
        concat_axis=0,
        tiled=True,
    )
    returned = returned.reshape(block_rows, features)
    row_numbers = jnp.arange(tokens.shape[0] * lax.axis_size("member"), dtype=jnp.int32)
    selector = (row_numbers[:, None] == flat_slots[None, :]).astype(jnp.float32)
    summed = lax.psum_scatter(
        jnp.dot(
            selector, returned, precision=lax.Precision.HIGHEST, preferred_element_type=jnp.float32
        ),
        "member",
        scatter_dimension=0,
        tiled=True,
    )
    return (summed.astype(jnp.bfloat16), grad_gate[None], grad_up[None], grad_down[None])


def shards(tokens, grad_out, route_token, *rest):
    devices = lax.axis_size("group") * lax.axis_size("member")
    _, groups, experts, capacity = route_token.shape
    dense = devices * tokens.shape[0] <= groups * capacity and experts == 1 and groups <= 32
    paired = tokens.shape[0] == 1 and devices & (devices - 1) == 0
    body = dense_shards if dense and paired else routed_shards
    return body(tokens, grad_out, route_token, *rest)


def solution(mesh):
    placed = (
        P(("group", "member"), None),
        P(("group", "member"), None),
        P("group", None, None, None),
        P("group", None, None),
        P("group", None, None, None),
        P(("group", "member"), None, None),
        P(("group", "member"), None, None),
        P(("group", "member"), None, None),
    )
    return jax.shard_map(
        shards,
        mesh=mesh,
        in_specs=placed,
        out_specs=(
            P(("group", "member"), None),
            P(("group", "member"), None, None),
            P(("group", "member"), None, None),
            P(("group", "member"), None, None),
        ),
        check_vma=False,
    )
```

```python
import functools

import jax
import jax.numpy as jnp
from jax import lax
from jax.experimental import pallas as pl
from jax.experimental.pallas import tpu as pltpu
from jax.sharding import PartitionSpec as P

LANES = 128
PIECES = 4
AXES = ("group", "member")
VMEM = pl.BlockSpec(memory_space=pltpu.VMEM)
HBM = pl.BlockSpec(memory_space=pltpu.HBM)
SMEM = pl.BlockSpec(memory_space=pltpu.SMEM)
NT = (((1,), (1,)), ((), ()))
TN = (((0,), (0,)), ((), ()))


def round_up(value, step):
    return (value + step - 1) // step * step


def pack_kernel(chunks, tokens_ref, grad_ref, token_ref, count_ref, prob_ref, out_ref, rows_ref):
    me = lax.axis_index("member")
    groups, experts, capacity = token_ref.shape[1:]
    token_row = tokens_ref[...].astype(jnp.float32)
    grad_row = grad_ref[...].astype(jnp.float32)
    for k in range(chunks):
        part = slice(k * LANES, (k + 1) * LANES)
        rows_ref[k : k + 1, :] = token_row[:, part]
        rows_ref[chunks + k : chunks + k + 1, :] = grad_row[:, part]
    lane = lax.broadcasted_iota(jnp.int32, (1, LANES), 1)
    third = lax.rem(lane, 32)
    weights = jnp.zeros((1, LANES), jnp.float32)
    for g in range(groups):
        for j in range(experts):
            weight = jnp.float32(0)
            for p in range(capacity):
                live = (token_ref[0, g, j, p] == me) & (p < count_ref[0, j, g])
                weight = weight + jnp.where(live, prob_ref[0, g, j, p], 0.0)
            weights = jnp.where(third == g * experts + j, weight, weights)
    high = weights.astype(jnp.bfloat16).astype(jnp.float32)
    middle = (weights - high).astype(jnp.bfloat16).astype(jnp.float32)
    low = weights - high - middle
    parts = jnp.where(lane < 32, high, jnp.where(lane < 64, middle, jnp.where(lane < 96, low, 0.0)))
    rows_ref[2 * chunks : 2 * chunks + 1, :] = parts
    used = 2 * chunks + 1
    rows_ref[used:, :] = jnp.zeros((rows_ref.shape[0] - used, LANES), jnp.float32)
    packed = rows_ref[...].astype(jnp.bfloat16)
    for n in range(out_ref.shape[0]):
        out_ref[n] = packed


def load_kernel(gate_ref, up_ref, down_ref, gate_out, up_out, down_out, sems):
    copies = []
    for n, (source, target) in enumerate(
        ((gate_ref, gate_out), (up_ref, up_out), (down_ref, down_out))
    ):
        height = source.shape[1] // PIECES
        for k in range(PIECES):
            part = pl.ds(k * height, height)
            copies.append(
                pltpu.make_async_copy(
                    source.at[:, part], target.at[:, part], sems.at[n * PIECES + k]
                )
            )
    for copy in copies:
        copy.start()
    for copy in copies:
        copy.wait()


def unpack_rows(chunks, packed_ref, wide_ref, rows_ref):
    tokens, rows, _ = packed_ref.shape
    features = chunks * LANES
    wide_ref[...] = packed_ref[...].reshape(tokens * rows, LANES).astype(jnp.float32)

    def column(k):
        return wide_ref[pl.ds(k, tokens, stride=rows), :]

    lane = lax.broadcasted_iota(jnp.int32, (tokens, LANES), 1)
    mine = (lane < 96) & (lax.rem(lane, 32) == lax.axis_index("group"))
    weight = jnp.sum(jnp.where(mine, column(2 * chunks), 0.0), axis=1, keepdims=True)
    for k in range(chunks):
        rows_ref[:, k * LANES : (k + 1) * LANES] = column(k).astype(jnp.bfloat16)
        rows_ref[:, features + k * LANES : features + (k + 1) * LANES] = (
            weight * column(chunks + k)
        ).astype(jnp.bfloat16)
    return rows_ref[:, :features], rows_ref[:, features : 2 * features]


def activations(x, scaled, gate, up, down):
    gate_value = lax.dot_general(x, gate, NT, preferred_element_type=jnp.float32)
    up_value = lax.dot_general(x, up, NT, preferred_element_type=jnp.float32)
    d_hidden = lax.dot_general(scaled, down, NT, preferred_element_type=jnp.float32)
    sigma_gate = jax.nn.sigmoid(gate_value)
    active = gate_value * sigma_gate
    hidden = (active * up_value).astype(jnp.bfloat16)
    d_gate = (d_hidden * up_value * sigma_gate * (1.0 + gate_value * (1.0 - sigma_gate))).astype(
        jnp.bfloat16
    )
    d_up = (d_hidden * active).astype(jnp.bfloat16)
    return d_gate, d_up, hidden


def partial_kernel(chunks, packed_ref, *refs):
    weight_refs = refs[:6]
    sent_ref, acts_ref, rows_ref, wide_ref, spread_ref = refs[6:]
    tokens = packed_ref.shape[0]
    x, scaled = unpack_rows(chunks, packed_ref, wide_ref, rows_ref)
    partial = None
    for core in range(2):
        gate, up, down = (ref[0] for ref in weight_refs[3 * core : 3 * core + 3])
        acts = activations(x, scaled, gate, up, down)
        if core == 0:
            for k, value in enumerate(acts):
                acts_ref[k] = value
        term = jnp.dot(acts[0], gate, preferred_element_type=jnp.float32)
        term = term + jnp.dot(acts[1], up, preferred_element_type=jnp.float32)
        partial = term if core == 0 else partial + term
    sent_rows = sent_ref.shape[1]
    for k in range(chunks):
        spread_ref[pl.ds(k, tokens, stride=sent_rows), :] = partial[:, k * LANES : (k + 1) * LANES]
    for k in range(chunks, sent_rows):
        spread_ref[pl.ds(k, tokens, stride=sent_rows), :] = jnp.zeros((tokens, LANES), jnp.float32)
    sent_ref[...] = spread_ref[...].reshape(sent_ref.shape).astype(jnp.bfloat16)


def grads_kernel(
    chunks,
    rows_ref,
    acts_ref,
    packed_ref,
    gate_ref,
    up_ref,
    down_ref,
    gate_out,
    up_out,
    down_out,
    wide_ref,
    other_ref,
):
    other_x, other_scaled = unpack_rows(chunks, packed_ref, wide_ref, other_ref)
    acts = activations(other_x, other_scaled, gate_ref[0], up_ref[0], down_ref[0])
    features = chunks * LANES
    x = jnp.concatenate([rows_ref[:, :features], other_x], axis=0)
    scaled = jnp.concatenate([rows_ref[:, features:], other_scaled], axis=0)
    for k, (out, right) in enumerate(((gate_out, x), (up_out, x), (down_out, scaled))):
        left = jnp.concatenate([acts_ref[k], acts[k]], axis=0)
        out[0] = lax.dot_general(left, right, TN, preferred_element_type=jnp.float32).astype(
            jnp.bfloat16
        )


def sum_kernel(chunks, back_ref, out_ref, total_ref):
    total_ref[...] = jnp.sum(back_ref[...].astype(jnp.float32), axis=0)
    for k in range(chunks):
        out_ref[:, k * LANES : (k + 1) * LANES] = total_ref[k : k + 1, :].astype(jnp.bfloat16)


def exchange(value, distance):
    count = lax.axis_size("group") * lax.axis_size("member")
    return lax.ppermute(value, AXES, [(i, i ^ distance) for i in range(count)])


def in_hbm(value):
    return pltpu.with_memory_space_constraint(value, pltpu.HBM)


def dense_shards(tokens, grad_out, route_token, route_count, route_prob, w_gate, w_up, w_down):
    features = tokens.shape[1]
    units = w_gate.shape[1]
    chunks = features // LANES
    groups, members = lax.axis_size("group"), lax.axis_size("member")
    count = groups * members
    half = count // 2
    rows = round_up(2 * chunks + 1, 16)
    sent_rows = round_up(chunks, 16)
    copies = pl.pallas_call(
        functools.partial(pack_kernel, chunks),
        out_shape=jax.ShapeDtypeStruct((half, rows, LANES), jnp.bfloat16),
        in_specs=[VMEM, VMEM, SMEM, SMEM, SMEM],
        out_specs=VMEM,
        scratch_shapes=[pltpu.VMEM((rows, LANES), jnp.float32)],
        name="pack_rows",
    )(tokens, grad_out, route_token, jnp.swapaxes(route_count, 1, 2), route_prob)
    weights = (w_gate, w_up, w_down)
    swapped = [exchange(w, 1) for w in weights]
    loaded = pl.pallas_call(
        load_kernel,
        out_shape=(pltpu.VMEM(w_gate.shape, jnp.bfloat16),) * 3,
        in_specs=[HBM] * 3,
        out_specs=(VMEM,) * 3,
        scratch_shapes=[pltpu.SemaphoreType.DMA((3 * PIECES,))],
        compiler_params=pltpu.CompilerParams(vmem_limit_bytes=8 * 1024 * 1024),
        cost_estimate=pl.CostEstimate(
            flops=0, bytes_accessed=6 * units * features, transcendentals=0
        ),
        name="load_weights",
    )(*[in_hbm(w) for w in weights])
    cores = [list(range(c, count, 2)) for c in range(2)]
    trade = functools.partial(
        lax.all_to_all,
        axis_name=AXES,
        split_axis=0,
        concat_axis=0,
        tiled=True,
        axis_index_groups=cores,
    )
    gathered = trade(copies)
    other = exchange(gathered, 1)
    wide = pltpu.VMEM((half * rows, LANES), jnp.float32)
    sent, acts, mine = pl.pallas_call(
        functools.partial(partial_kernel, chunks),
        out_shape=(
            jax.ShapeDtypeStruct((half, sent_rows, LANES), jnp.bfloat16),
            pltpu.VMEM((3, half, units), jnp.bfloat16),
            pltpu.VMEM((half, 2 * features), jnp.bfloat16),
        ),
        in_specs=[VMEM] * 7,
        out_specs=(VMEM,) * 3,
        scratch_shapes=[wide, pltpu.VMEM((half * sent_rows, LANES), jnp.float32)],
        compiler_params=pltpu.CompilerParams(vmem_limit_bytes=16 * 1024 * 1024),
        name="partial_rows",
    )(gathered, *loaded, *swapped)
    back = trade(sent)
    grad_shape = jax.ShapeDtypeStruct((1, units, features), jnp.bfloat16)
    grad_gate, grad_up, grad_down = pl.pallas_call(
        functools.partial(grads_kernel, chunks),
        out_shape=(grad_shape,) * 3,
        in_specs=[VMEM] * 6,
        out_specs=(VMEM,) * 3,
        scratch_shapes=[wide, pltpu.VMEM((half, 2 * features), jnp.bfloat16)],
        compiler_params=pltpu.CompilerParams(vmem_limit_bytes=16 * 1024 * 1024),
        cost_estimate=pl.CostEstimate(
            flops=6 * count * units * features,
            bytes_accessed=6 * units * features,
            transcendentals=0,
        ),
        name="weight_grads",
    )(mine, acts, other, *loaded)
    grad_tokens = pl.pallas_call(
        functools.partial(sum_kernel, chunks),
        out_shape=jax.ShapeDtypeStruct((1, features), jnp.bfloat16),
        in_specs=[VMEM],
        out_specs=VMEM,
        scratch_shapes=[pltpu.VMEM((sent_rows, LANES), jnp.float32)],
        compiler_params=pltpu.CompilerParams(vmem_limit_bytes=4 * 1024 * 1024),
        name="sum_rows",
    )(back)
    return grad_tokens, grad_gate, grad_up, grad_down


def slice_backward(rows_x, rows_scaled, gate_weight, up_weight, down_weight):
    gate_value = jnp.dot(rows_x, gate_weight.T, preferred_element_type=jnp.float32)
    up_value = jnp.dot(rows_x, up_weight.T, preferred_element_type=jnp.float32)
    sigma_gate = jax.nn.sigmoid(gate_value)
    active = gate_value * sigma_gate
    hidden = (active * up_value).astype(jnp.bfloat16)
    d_hidden = jnp.dot(rows_scaled, down_weight.T, preferred_element_type=jnp.float32)
    d_gate = (d_hidden * up_value * sigma_gate * (1.0 + gate_value * (1.0 - sigma_gate))).astype(
        jnp.bfloat16
    )
    d_up = (d_hidden * active).astype(jnp.bfloat16)
    grad_down = jnp.dot(hidden.T, rows_scaled, preferred_element_type=jnp.float32).astype(
        jnp.bfloat16
    )
    grad_gate = jnp.dot(d_gate.T, rows_x, preferred_element_type=jnp.float32).astype(jnp.bfloat16)
    grad_up = jnp.dot(d_up.T, rows_x, preferred_element_type=jnp.float32).astype(jnp.bfloat16)
    partial_rows = jnp.dot(d_gate, gate_weight, preferred_element_type=jnp.float32)
    partial_rows = partial_rows + jnp.dot(d_up, up_weight, preferred_element_type=jnp.float32)
    return (grad_gate, grad_up, grad_down, partial_rows)


def routed_shards(tokens, grad_out, route_token, route_count, route_prob, w_gate, w_up, w_down):
    groups = route_token.shape[1]
    capacity = route_token.shape[3]
    features = tokens.shape[1]
    block_rows = groups * capacity
    split_count = max(8, lax.axis_size("member") // 8)
    expert_local = lax.axis_index("member") // split_count
    slot_tokens = lax.dynamic_index_in_dim(route_token[0], expert_local, 1, keepdims=False)
    slot_counts = lax.dynamic_index_in_dim(route_count[0], expert_local, 1, keepdims=False)
    slot_probs = lax.dynamic_index_in_dim(route_prob[0], expert_local, 1, keepdims=False)
    slot_index = jnp.arange(capacity, dtype=jnp.int32)[None, :]
    live = (slot_index < slot_counts[:, None]).astype(jnp.float32)
    slot_weights = (slot_probs * live).reshape(-1)
    flat_slots = slot_tokens.reshape(-1)
    group_x, group_dy = (
        lax.all_gather(tokens, "member", axis=0, tiled=True),
        lax.all_gather(grad_out, "member", axis=0, tiled=True),
    )
    picked_x = jnp.take(group_x, flat_slots, axis=0)
    picked_dy = jnp.take(group_dy, flat_slots, axis=0)
    scaled = (slot_weights[:, None] * picked_dy.astype(jnp.float32)).astype(jnp.bfloat16)
    send_x = picked_x.reshape(groups, capacity, features)
    send_scaled = scaled.reshape(groups, capacity, features)
    rows_x, rows_scaled = (
        lax.all_to_all(send_x, "group", split_axis=0, concat_axis=0, tiled=True),
        lax.all_to_all(send_scaled, "group", split_axis=0, concat_axis=0, tiled=True),
    )
    grad_gate, grad_up, grad_down, partial_rows = slice_backward(
        rows_x.reshape(block_rows, features),
        rows_scaled.reshape(block_rows, features),
        w_gate[0],
        w_up[0],
        w_down[0],
    )
    returned = lax.all_to_all(
        partial_rows.reshape(groups, capacity, features),
        "group",
        split_axis=0,
        concat_axis=0,
        tiled=True,
    )
    returned = returned.reshape(block_rows, features)
    row_numbers = jnp.arange(tokens.shape[0] * lax.axis_size("member"), dtype=jnp.int32)
    selector = (row_numbers[:, None] == flat_slots[None, :]).astype(jnp.float32)
    summed = lax.psum_scatter(
        jnp.dot(
            selector, returned, precision=lax.Precision.HIGHEST, preferred_element_type=jnp.float32
        ),
        "member",
        scatter_dimension=0,
        tiled=True,
    )
    return (summed.astype(jnp.bfloat16), grad_gate[None], grad_up[None], grad_down[None])


def shards(tokens, grad_out, route_token, *rest):
    devices = lax.axis_size("group") * lax.axis_size("member")
    _, groups, experts, capacity = route_token.shape
    dense = devices * tokens.shape[0] <= groups * capacity and experts == 1 and groups <= 32
    paired = tokens.shape[0] == 1 and devices & (devices - 1) == 0
    body = dense_shards if dense and paired else routed_shards
    return body(tokens, grad_out, route_token, *rest)


def solution(mesh):
    placed = (
        P(("group", "member"), None),
        P(("group", "member"), None),
        P("group", None, None, None),
        P("group", None, None),
        P("group", None, None, None),
        P(("group", "member"), None, None),
        P(("group", "member"), None, None),
        P(("group", "member"), None, None),
    )
    return jax.shard_map(
        shards,
        mesh=mesh,
        in_specs=placed,
        out_specs=(
            P(("group", "member"), None),
            P(("group", "member"), None, None),
            P(("group", "member"), None, None),
            P(("group", "member"), None, None),
        ),
        check_vma=False,
    )
```

```python
import functools

import jax
import jax.numpy as jnp
from jax import lax
from jax.experimental import pallas as pl
from jax.experimental.pallas import tpu as pltpu
from jax.sharding import PartitionSpec as P

LANES = 128
PIECES = 4
AXES = ("group", "member")
VMEM = pl.BlockSpec(memory_space=pltpu.VMEM)
HBM = pl.BlockSpec(memory_space=pltpu.HBM)
SMEM = pl.BlockSpec(memory_space=pltpu.SMEM)
NT = (((1,), (1,)), ((), ()))
TN = (((0,), (0,)), ((), ()))


def round_up(value, step):
    return (value + step - 1) // step * step


def pack_kernel(tokens_ref, grad_ref, token_ref, count_ref, prob_ref, out_ref):
    me = lax.axis_index("member")
    groups, experts, capacity = token_ref.shape[1:]
    features = tokens_ref.shape[1]
    row = lax.broadcasted_iota(jnp.int32, (2, LANES), 0)
    lane = lax.broadcasted_iota(jnp.int32, (2, LANES), 1)
    third = lax.rem(lane, 32)
    weights = jnp.zeros((2, LANES), jnp.float32)
    for g in range(groups):
        for j in range(experts):
            weight = jnp.float32(0)
            for p in range(capacity):
                live = (token_ref[0, g, j, p] == me) & (p < count_ref[0, j, g])
                weight = weight + jnp.where(live, prob_ref[0, g, j, p], 0.0)
            weights = jnp.where(third == g * experts + j, weight, weights)
    high = weights.astype(jnp.bfloat16).astype(jnp.float32)
    middle = (weights - high).astype(jnp.bfloat16).astype(jnp.float32)
    low = weights - high - middle
    parts = jnp.where(lane < 32, high, jnp.where(lane < 64, middle, jnp.where(lane < 96, low, 0.0)))
    rows = (tokens_ref[...].astype(jnp.float32), grad_ref[...].astype(jnp.float32))
    out_ref[:, :features] = jnp.concatenate(rows, axis=0).astype(jnp.bfloat16)
    out_ref[:, features:] = jnp.where(row == 0, parts, 0.0).astype(jnp.bfloat16)


def unpack_rows(packed_ref, wide_ref, x_ref, scaled_ref):
    tokens, features = x_ref.shape
    expert = lax.axis_index("group")
    lane = lax.broadcasted_iota(jnp.int32, (tokens, LANES), 1)
    mine = (lane < 96) & (lax.rem(lane, 32) == expert)
    chunks = features // LANES
    weight = None
    for k in [chunks] + list(range(chunks)):
        part = slice(k * LANES, (k + 1) * LANES)
        first = 2 * tokens * k
        wide_ref[first : first + 2 * tokens, :] = packed_ref[:, part].astype(jnp.float32)
        x = wide_ref[pl.ds(first, tokens, stride=2), :]
        if k == chunks:
            weight = jnp.sum(jnp.where(mine, x, 0.0), axis=1, keepdims=True)
            continue
        x_ref[:, part] = x.astype(jnp.bfloat16)
        grad = wide_ref[pl.ds(first + 1, tokens, stride=2), :]
        scaled_ref[:, part] = (weight * grad).astype(jnp.bfloat16)


def partial_kernel(
    packed_ref,
    gate_hbm,
    up_hbm,
    down_hbm,
    sent_ref,
    x_ref,
    scaled_ref,
    acts_ref,
    wide_ref,
    spread_ref,
    weights_ref,
    sems,
):
    copies = []
    for n, source in enumerate((gate_hbm, up_hbm, down_hbm)):
        height = source.shape[1] // PIECES
        for k in range(PIECES):
            part = pl.ds(k * height, height)
            copies.append(
                pltpu.make_async_copy(
                    source.at[0, part], weights_ref.at[n, part], sems.at[n * PIECES + k]
                )
            )
    for copy in copies:
        copy.start()
    unpack_rows(packed_ref, wide_ref, x_ref, scaled_ref)
    for copy in copies:
        copy.wait()
    tokens, features = x_ref.shape
    chunks = features // LANES
    x = x_ref[...]
    gate_value = lax.dot_general(x, weights_ref[0], NT, preferred_element_type=jnp.float32)
    up_value = lax.dot_general(x, weights_ref[1], NT, preferred_element_type=jnp.float32)
    d_hidden = lax.dot_general(
        scaled_ref[...], weights_ref[2], NT, preferred_element_type=jnp.float32
    )
    sigma_gate = jax.nn.sigmoid(gate_value)
    active = gate_value * sigma_gate
    hidden = (active * up_value).astype(jnp.bfloat16)
    d_gate = (d_hidden * up_value * sigma_gate * (1.0 + gate_value * (1.0 - sigma_gate))).astype(
        jnp.bfloat16
    )
    d_up = (d_hidden * active).astype(jnp.bfloat16)
    acts_ref[0] = d_gate
    acts_ref[1] = d_up
    acts_ref[2] = hidden
    partial = jnp.dot(d_gate, weights_ref[0], preferred_element_type=jnp.float32)
    partial = partial + jnp.dot(d_up, weights_ref[1], preferred_element_type=jnp.float32)
    sent_rows = sent_ref.shape[1]
    for k in range(chunks):
        spread_ref[pl.ds(k, tokens, stride=sent_rows), :] = partial[:, k * LANES : (k + 1) * LANES]
    for k in range(chunks, sent_rows):
        spread_ref[pl.ds(k, tokens, stride=sent_rows), :] = jnp.zeros((tokens, LANES), jnp.float32)
    sent_ref[...] = spread_ref[...].reshape(sent_ref.shape).astype(jnp.bfloat16)


def grads_kernel(x_ref, scaled_ref, acts_ref, gate_out, up_out, down_out):
    for k, (out, right) in enumerate(((gate_out, x_ref), (up_out, x_ref), (down_out, scaled_ref))):
        out[0] = lax.dot_general(
            acts_ref[k], right[...], TN, preferred_element_type=jnp.float32
        ).astype(jnp.bfloat16)


def sum_kernel(chunks, back_ref, out_ref, total_ref):
    total_ref[...] = jnp.sum(back_ref[...].astype(jnp.float32), axis=0)
    for k in range(chunks):
        out_ref[:, k * LANES : (k + 1) * LANES] = total_ref[k : k + 1, :].astype(jnp.bfloat16)


def in_hbm(value):
    return pltpu.with_memory_space_constraint(value, pltpu.HBM)


def dense_shards(tokens, grad_out, route_token, route_count, route_prob, w_gate, w_up, w_down):
    features = tokens.shape[1]
    units = w_gate.shape[1]
    chunks = features // LANES
    count = lax.axis_size("group") * lax.axis_size("member")
    sent_rows = round_up(chunks, 16)
    packed = pl.pallas_call(
        pack_kernel,
        out_shape=jax.ShapeDtypeStruct((2, features + LANES), jnp.bfloat16),
        in_specs=[VMEM, VMEM, SMEM, SMEM, SMEM],
        out_specs=VMEM,
        name="pack_rows",
    )(tokens, grad_out, route_token, jnp.swapaxes(route_count, 1, 2), route_prob)
    gathered = lax.all_gather(packed, AXES, axis=0, tiled=True)
    sent, x, scaled, acts = pl.pallas_call(
        partial_kernel,
        out_shape=(
            jax.ShapeDtypeStruct((count, sent_rows, LANES), jnp.bfloat16),
            pltpu.VMEM((count, features), jnp.bfloat16),
            pltpu.VMEM((count, features), jnp.bfloat16),
            pltpu.VMEM((3, count, units), jnp.bfloat16),
        ),
        in_specs=[VMEM, HBM, HBM, HBM],
        out_specs=(VMEM,) * 4,
        scratch_shapes=[
            pltpu.VMEM((2 * count * (chunks + 1), LANES), jnp.float32),
            pltpu.VMEM((count * sent_rows, LANES), jnp.float32),
            pltpu.VMEM((3, units, features), jnp.bfloat16),
            pltpu.SemaphoreType.DMA((3 * PIECES,)),
        ],
        compiler_params=pltpu.CompilerParams(vmem_limit_bytes=16 * 1024 * 1024),
        name="partial_rows",
    )(gathered, *[in_hbm(w) for w in (w_gate, w_up, w_down)])
    back = lax.all_to_all(sent, AXES, split_axis=0, concat_axis=0, tiled=True)
    grad_shape = jax.ShapeDtypeStruct((1, units, features), jnp.bfloat16)
    grad_gate, grad_up, grad_down = pl.pallas_call(
        grads_kernel,
        out_shape=(grad_shape,) * 3,
        in_specs=[VMEM] * 3,
        out_specs=(VMEM,) * 3,
        compiler_params=pltpu.CompilerParams(vmem_limit_bytes=16 * 1024 * 1024),
        cost_estimate=pl.CostEstimate(
            flops=6 * count * units * features,
            bytes_accessed=6 * units * features,
            transcendentals=0,
        ),
        name="weight_grads",
    )(x, scaled, acts)
    grad_tokens = pl.pallas_call(
        functools.partial(sum_kernel, chunks),
        out_shape=jax.ShapeDtypeStruct((1, features), jnp.bfloat16),
        in_specs=[VMEM],
        out_specs=VMEM,
        scratch_shapes=[pltpu.VMEM((sent_rows, LANES), jnp.float32)],
        compiler_params=pltpu.CompilerParams(vmem_limit_bytes=4 * 1024 * 1024),
        name="sum_rows",
    )(back)
    return grad_tokens, grad_gate, grad_up, grad_down


def slice_backward(rows_x, rows_scaled, gate_weight, up_weight, down_weight):
    gate_value = jnp.dot(rows_x, gate_weight.T, preferred_element_type=jnp.float32)
    up_value = jnp.dot(rows_x, up_weight.T, preferred_element_type=jnp.float32)
    sigma_gate = jax.nn.sigmoid(gate_value)
    active = gate_value * sigma_gate
    hidden = (active * up_value).astype(jnp.bfloat16)
    d_hidden = jnp.dot(rows_scaled, down_weight.T, preferred_element_type=jnp.float32)
    d_gate = (d_hidden * up_value * sigma_gate * (1.0 + gate_value * (1.0 - sigma_gate))).astype(
        jnp.bfloat16
    )
    d_up = (d_hidden * active).astype(jnp.bfloat16)
    grad_down = jnp.dot(hidden.T, rows_scaled, preferred_element_type=jnp.float32).astype(
        jnp.bfloat16
    )
    grad_gate = jnp.dot(d_gate.T, rows_x, preferred_element_type=jnp.float32).astype(jnp.bfloat16)
    grad_up = jnp.dot(d_up.T, rows_x, preferred_element_type=jnp.float32).astype(jnp.bfloat16)
    partial_rows = jnp.dot(d_gate, gate_weight, preferred_element_type=jnp.float32)
    partial_rows = partial_rows + jnp.dot(d_up, up_weight, preferred_element_type=jnp.float32)
    return (grad_gate, grad_up, grad_down, partial_rows)


def routed_shards(tokens, grad_out, route_token, route_count, route_prob, w_gate, w_up, w_down):
    groups = route_token.shape[1]
    capacity = route_token.shape[3]
    features = tokens.shape[1]
    block_rows = groups * capacity
    split_count = max(8, lax.axis_size("member") // 8)
    expert_local = lax.axis_index("member") // split_count
    slot_tokens = lax.dynamic_index_in_dim(route_token[0], expert_local, 1, keepdims=False)
    slot_counts = lax.dynamic_index_in_dim(route_count[0], expert_local, 1, keepdims=False)
    slot_probs = lax.dynamic_index_in_dim(route_prob[0], expert_local, 1, keepdims=False)
    slot_index = jnp.arange(capacity, dtype=jnp.int32)[None, :]
    live = (slot_index < slot_counts[:, None]).astype(jnp.float32)
    slot_weights = (slot_probs * live).reshape(-1)
    flat_slots = slot_tokens.reshape(-1)
    group_x, group_dy = (
        lax.all_gather(tokens, "member", axis=0, tiled=True),
        lax.all_gather(grad_out, "member", axis=0, tiled=True),
    )
    picked_x = jnp.take(group_x, flat_slots, axis=0)
    picked_dy = jnp.take(group_dy, flat_slots, axis=0)
    scaled = (slot_weights[:, None] * picked_dy.astype(jnp.float32)).astype(jnp.bfloat16)
    send_x = picked_x.reshape(groups, capacity, features)
    send_scaled = scaled.reshape(groups, capacity, features)
    rows_x, rows_scaled = (
        lax.all_to_all(send_x, "group", split_axis=0, concat_axis=0, tiled=True),
        lax.all_to_all(send_scaled, "group", split_axis=0, concat_axis=0, tiled=True),
    )
    grad_gate, grad_up, grad_down, partial_rows = slice_backward(
        rows_x.reshape(block_rows, features),
        rows_scaled.reshape(block_rows, features),
        w_gate[0],
        w_up[0],
        w_down[0],
    )
    returned = lax.all_to_all(
        partial_rows.reshape(groups, capacity, features),
        "group",
        split_axis=0,
        concat_axis=0,
        tiled=True,
    )
    returned = returned.reshape(block_rows, features)
    row_numbers = jnp.arange(tokens.shape[0] * lax.axis_size("member"), dtype=jnp.int32)
    selector = (row_numbers[:, None] == flat_slots[None, :]).astype(jnp.float32)
    summed = lax.psum_scatter(
        jnp.dot(
            selector, returned, precision=lax.Precision.HIGHEST, preferred_element_type=jnp.float32
        ),
        "member",
        scatter_dimension=0,
        tiled=True,
    )
    return (summed.astype(jnp.bfloat16), grad_gate[None], grad_up[None], grad_down[None])


def shards(tokens, grad_out, route_token, *rest):
    devices = lax.axis_size("group") * lax.axis_size("member")
    _, groups, experts, capacity = route_token.shape
    dense = devices * tokens.shape[0] <= groups * capacity and experts == 1 and groups <= 32
    body = dense_shards if dense and tokens.shape[0] == 1 else routed_shards
    return body(tokens, grad_out, route_token, *rest)


def solution(mesh):
    placed = (
        P(("group", "member"), None),
        P(("group", "member"), None),
        P("group", None, None, None),
        P("group", None, None),
        P("group", None, None, None),
        P(("group", "member"), None, None),
        P(("group", "member"), None, None),
        P(("group", "member"), None, None),
    )
    return jax.shard_map(
        shards,
        mesh=mesh,
        in_specs=placed,
        out_specs=(
            P(("group", "member"), None),
            P(("group", "member"), None, None),
            P(("group", "member"), None, None),
            P(("group", "member"), None, None),
        ),
        check_vma=False,
    )
```

```python
import functools

import jax
import jax.numpy as jnp
from jax import lax
from jax.experimental import pallas as pl
from jax.experimental.pallas import tpu as pltpu
from jax.sharding import PartitionSpec as P

LANES = 128
PIECES = 4
AXES = ("group", "member")
VMEM = pl.BlockSpec(memory_space=pltpu.VMEM)
HBM = pl.BlockSpec(memory_space=pltpu.HBM)
SMEM = pl.BlockSpec(memory_space=pltpu.SMEM)
NT = (((1,), (1,)), ((), ()))
TN = (((0,), (0,)), ((), ()))


def round_up(value, step):
    return (value + step - 1) // step * step


def pack_kernel(chunks, tokens_ref, grad_ref, token_ref, count_ref, prob_ref, out_ref, rows_ref):
    me = lax.axis_index("member")
    groups, experts, capacity = token_ref.shape[1:]
    token_row = tokens_ref[...].astype(jnp.float32)
    grad_row = grad_ref[...].astype(jnp.float32)
    for k in range(chunks):
        part = slice(k * LANES, (k + 1) * LANES)
        rows_ref[k : k + 1, :] = token_row[:, part]
        rows_ref[chunks + k : chunks + k + 1, :] = grad_row[:, part]
    lane = lax.broadcasted_iota(jnp.int32, (1, LANES), 1)
    third = lax.rem(lane, 32)
    weights = jnp.zeros((1, LANES), jnp.float32)
    for g in range(groups):
        for j in range(experts):
            weight = jnp.float32(0)
            for p in range(capacity):
                live = (token_ref[0, g, j, p] == me) & (p < count_ref[0, j, g])
                weight = weight + jnp.where(live, prob_ref[0, g, j, p], 0.0)
            weights = jnp.where(third == g * experts + j, weight, weights)
    high = weights.astype(jnp.bfloat16).astype(jnp.float32)
    middle = (weights - high).astype(jnp.bfloat16).astype(jnp.float32)
    low = weights - high - middle
    parts = jnp.where(lane < 32, high, jnp.where(lane < 64, middle, jnp.where(lane < 96, low, 0.0)))
    rows_ref[2 * chunks : 2 * chunks + 1, :] = parts
    used = 2 * chunks + 1
    rows_ref[used:, :] = jnp.zeros((rows_ref.shape[0] - used, LANES), jnp.float32)
    out_ref[...] = rows_ref[...].astype(jnp.bfloat16)


def load_kernel(gate_ref, up_ref, down_ref, gate_out, up_out, down_out, sems):
    copies = []
    for n, (source, target) in enumerate(
        ((gate_ref, gate_out), (up_ref, up_out), (down_ref, down_out))
    ):
        height = source.shape[1] // PIECES
        for k in range(PIECES):
            part = pl.ds(k * height, height)
            copies.append(
                pltpu.make_async_copy(
                    source.at[:, part], target.at[:, part], sems.at[n * PIECES + k]
                )
            )
    for copy in copies:
        copy.start()
    for copy in copies:
        copy.wait()


def unpack_rows(chunks, packed_ref, wide_ref, rows_ref):
    tokens, rows, _ = packed_ref.shape
    features = chunks * LANES
    wide_ref[...] = packed_ref[...].reshape(tokens * rows, LANES).astype(jnp.float32)

    def column(k):
        return wide_ref[pl.ds(k, tokens, stride=rows), :]

    lane = lax.broadcasted_iota(jnp.int32, (tokens, LANES), 1)
    mine = (lane < 96) & (lax.rem(lane, 32) == lax.axis_index("group"))
    weight = jnp.sum(jnp.where(mine, column(2 * chunks), 0.0), axis=1, keepdims=True)
    for k in range(chunks):
        rows_ref[:, k * LANES : (k + 1) * LANES] = column(k).astype(jnp.bfloat16)
        rows_ref[:, features + k * LANES : features + (k + 1) * LANES] = (
            weight * column(chunks + k)
        ).astype(jnp.bfloat16)
    return rows_ref[:, :features], rows_ref[:, features : 2 * features]


def activations(x, scaled, gate, up, down):
    gate_value = lax.dot_general(x, gate, NT, preferred_element_type=jnp.float32)
    up_value = lax.dot_general(x, up, NT, preferred_element_type=jnp.float32)
    d_hidden = lax.dot_general(scaled, down, NT, preferred_element_type=jnp.float32)
    sigma_gate = jax.nn.sigmoid(gate_value)
    active = gate_value * sigma_gate
    hidden = (active * up_value).astype(jnp.bfloat16)
    d_gate = (d_hidden * up_value * sigma_gate * (1.0 + gate_value * (1.0 - sigma_gate))).astype(
        jnp.bfloat16
    )
    d_up = (d_hidden * active).astype(jnp.bfloat16)
    return d_gate, d_up, hidden


def partial_kernel(
    chunks,
    mine_ref,
    other_ref,
    gate_ref,
    up_ref,
    down_ref,
    sent_ref,
    rows_ref,
    acts_ref,
    wide_ref,
    spread_ref,
):
    count = mine_ref.shape[0]
    tokens = 2 * count
    features = chunks * LANES
    for n, ref in enumerate((mine_ref, other_ref)):
        unpack_rows(chunks, ref, wide_ref, rows_ref.at[pl.ds(n * count, count)])
    x, scaled = rows_ref[:, :features], rows_ref[:, features:]
    acts = activations(x, scaled, gate_ref[0], up_ref[0], down_ref[0])
    for k, value in enumerate(acts):
        acts_ref[k] = value
    partial = jnp.dot(acts[0], gate_ref[0], preferred_element_type=jnp.float32)
    partial = partial + jnp.dot(acts[1], up_ref[0], preferred_element_type=jnp.float32)
    members, groups, sent_rows, _ = sent_ref.shape
    for k in range(chunks):
        spread_ref[pl.ds(k, tokens, stride=sent_rows), :] = partial[:, k * LANES : (k + 1) * LANES]
    for k in range(chunks, sent_rows):
        spread_ref[pl.ds(k, tokens, stride=sent_rows), :] = jnp.zeros((tokens, LANES), jnp.float32)
    core = lax.rem(lax.axis_index("member"), 2)
    for n in range(2):
        for m in range(members // 2):
            first = (n * count + m * groups) * sent_rows
            rows = spread_ref[first : first + groups * sent_rows, :].astype(jnp.bfloat16)
            sent_ref[2 * m + (core ^ n)] = rows.reshape(groups, sent_rows, LANES)


def grads_kernel(features, rows_ref, acts_ref, gate_out, up_out, down_out):
    for k, (out, first) in enumerate(((gate_out, 0), (up_out, 0), (down_out, features))):
        out[0] = lax.dot_general(
            acts_ref[k], rows_ref[:, first : first + features], TN, preferred_element_type=jnp.float32
        ).astype(jnp.bfloat16)


def plane_sum_kernel(back_ref, out_ref):
    out_ref[...] = jnp.sum(back_ref[...].astype(jnp.float32), axis=0).astype(jnp.bfloat16)


def sum_kernel(chunks, back_ref, out_ref, total_ref):
    total_ref[...] = jnp.sum(back_ref[...].astype(jnp.float32), axis=0)
    for k in range(chunks):
        out_ref[:, k * LANES : (k + 1) * LANES] = total_ref[k : k + 1, :].astype(jnp.bfloat16)


def exchange(value, distance):
    count = lax.axis_size("group") * lax.axis_size("member")
    return lax.ppermute(value, AXES, [(i, i ^ distance) for i in range(count)])


def in_hbm(value):
    return pltpu.with_memory_space_constraint(value, pltpu.HBM)


def dense_shards(tokens, grad_out, route_token, route_count, route_prob, w_gate, w_up, w_down):
    features = tokens.shape[1]
    units = w_gate.shape[1]
    chunks = features // LANES
    groups, members = lax.axis_size("group"), lax.axis_size("member")
    count = groups * members
    half = count // 2
    rows = round_up(2 * chunks + 1, 16)
    sent_rows = round_up(chunks, 16)
    packed = pl.pallas_call(
        functools.partial(pack_kernel, chunks),
        out_shape=jax.ShapeDtypeStruct((rows, LANES), jnp.bfloat16),
        in_specs=[VMEM, VMEM, SMEM, SMEM, SMEM],
        out_specs=VMEM,
        scratch_shapes=[pltpu.VMEM((rows, LANES), jnp.float32)],
        name="pack_rows",
    )(tokens, grad_out, route_token, jnp.swapaxes(route_count, 1, 2), route_prob)
    loaded = pl.pallas_call(
        load_kernel,
        out_shape=(pltpu.VMEM(w_gate.shape, jnp.bfloat16),) * 3,
        in_specs=[HBM] * 3,
        out_specs=(VMEM,) * 3,
        scratch_shapes=[pltpu.SemaphoreType.DMA((3 * PIECES,))],
        compiler_params=pltpu.CompilerParams(vmem_limit_bytes=8 * 1024 * 1024),
        cost_estimate=pl.CostEstimate(
            flops=0, bytes_accessed=6 * units * features, transcendentals=0
        ),
        name="load_weights",
    )(*[in_hbm(w) for w in (w_gate, w_up, w_down)])
    column = lax.all_gather(packed, "group", axis=0, tiled=False)
    cores = [list(range(c, members, 2)) for c in range(2)]
    mine = lax.all_gather(column, "member", axis=0, tiled=True, axis_index_groups=cores)
    other = exchange(mine, 1)
    sent, both, acts = pl.pallas_call(
        functools.partial(partial_kernel, chunks),
        out_shape=(
            jax.ShapeDtypeStruct((members, groups, sent_rows, LANES), jnp.bfloat16),
            pltpu.VMEM((count, 2 * features), jnp.bfloat16),
            pltpu.VMEM((3, count, units), jnp.bfloat16),
        ),
        in_specs=[VMEM] * 5,
        out_specs=(VMEM,) * 3,
        scratch_shapes=[
            pltpu.VMEM((half * rows, LANES), jnp.float32),
            pltpu.VMEM((count * sent_rows, LANES), jnp.float32),
        ],
        compiler_params=pltpu.CompilerParams(vmem_limit_bytes=16 * 1024 * 1024),
        name="partial_rows",
    )(mine, other, *loaded)
    back = lax.all_to_all(sent, "member", split_axis=0, concat_axis=0, tiled=True)
    summed = pl.pallas_call(
        plane_sum_kernel,
        out_shape=jax.ShapeDtypeStruct(sent.shape[1:], jnp.bfloat16),
        in_specs=[VMEM],
        out_specs=VMEM,
        compiler_params=pltpu.CompilerParams(vmem_limit_bytes=4 * 1024 * 1024),
        name="plane_sum",
    )(back)
    back = lax.all_to_all(summed, "group", split_axis=0, concat_axis=0, tiled=True)
    grad_shape = jax.ShapeDtypeStruct((1, units, features), jnp.bfloat16)
    grad_gate, grad_up, grad_down = pl.pallas_call(
        functools.partial(grads_kernel, features),
        out_shape=(grad_shape,) * 3,
        in_specs=[VMEM] * 2,
        out_specs=(VMEM,) * 3,
        compiler_params=pltpu.CompilerParams(vmem_limit_bytes=16 * 1024 * 1024),
        cost_estimate=pl.CostEstimate(
            flops=6 * count * units * features,
            bytes_accessed=6 * units * features,
            transcendentals=0,
        ),
        name="weight_grads",
    )(both, acts)
    grad_tokens = pl.pallas_call(
        functools.partial(sum_kernel, chunks),
        out_shape=jax.ShapeDtypeStruct((1, features), jnp.bfloat16),
        in_specs=[VMEM],
        out_specs=VMEM,
        scratch_shapes=[pltpu.VMEM((sent_rows, LANES), jnp.float32)],
        compiler_params=pltpu.CompilerParams(vmem_limit_bytes=4 * 1024 * 1024),
        name="sum_rows",
    )(back)
    return grad_tokens, grad_gate, grad_up, grad_down


def slice_backward(rows_x, rows_scaled, gate_weight, up_weight, down_weight):
    gate_value = jnp.dot(rows_x, gate_weight.T, preferred_element_type=jnp.float32)
    up_value = jnp.dot(rows_x, up_weight.T, preferred_element_type=jnp.float32)
    sigma_gate = jax.nn.sigmoid(gate_value)
    active = gate_value * sigma_gate
    hidden = (active * up_value).astype(jnp.bfloat16)
    d_hidden = jnp.dot(rows_scaled, down_weight.T, preferred_element_type=jnp.float32)
    d_gate = (d_hidden * up_value * sigma_gate * (1.0 + gate_value * (1.0 - sigma_gate))).astype(
        jnp.bfloat16
    )
    d_up = (d_hidden * active).astype(jnp.bfloat16)
    grad_down = jnp.dot(hidden.T, rows_scaled, preferred_element_type=jnp.float32).astype(
        jnp.bfloat16
    )
    grad_gate = jnp.dot(d_gate.T, rows_x, preferred_element_type=jnp.float32).astype(jnp.bfloat16)
    grad_up = jnp.dot(d_up.T, rows_x, preferred_element_type=jnp.float32).astype(jnp.bfloat16)
    partial_rows = jnp.dot(d_gate, gate_weight, preferred_element_type=jnp.float32)
    partial_rows = partial_rows + jnp.dot(d_up, up_weight, preferred_element_type=jnp.float32)
    return (grad_gate, grad_up, grad_down, partial_rows)


def routed_shards(tokens, grad_out, route_token, route_count, route_prob, w_gate, w_up, w_down):
    groups = route_token.shape[1]
    capacity = route_token.shape[3]
    features = tokens.shape[1]
    block_rows = groups * capacity
    split_count = max(8, lax.axis_size("member") // 8)
    expert_local = lax.axis_index("member") // split_count
    slot_tokens = lax.dynamic_index_in_dim(route_token[0], expert_local, 1, keepdims=False)
    slot_counts = lax.dynamic_index_in_dim(route_count[0], expert_local, 1, keepdims=False)
    slot_probs = lax.dynamic_index_in_dim(route_prob[0], expert_local, 1, keepdims=False)
    slot_index = jnp.arange(capacity, dtype=jnp.int32)[None, :]
    live = (slot_index < slot_counts[:, None]).astype(jnp.float32)
    slot_weights = (slot_probs * live).reshape(-1)
    flat_slots = slot_tokens.reshape(-1)
    group_x, group_dy = (
        lax.all_gather(tokens, "member", axis=0, tiled=True),
        lax.all_gather(grad_out, "member", axis=0, tiled=True),
    )
    picked_x = jnp.take(group_x, flat_slots, axis=0)
    picked_dy = jnp.take(group_dy, flat_slots, axis=0)
    scaled = (slot_weights[:, None] * picked_dy.astype(jnp.float32)).astype(jnp.bfloat16)
    send_x = picked_x.reshape(groups, capacity, features)
    send_scaled = scaled.reshape(groups, capacity, features)
    rows_x, rows_scaled = (
        lax.all_to_all(send_x, "group", split_axis=0, concat_axis=0, tiled=True),
        lax.all_to_all(send_scaled, "group", split_axis=0, concat_axis=0, tiled=True),
    )
    grad_gate, grad_up, grad_down, partial_rows = slice_backward(
        rows_x.reshape(block_rows, features),
        rows_scaled.reshape(block_rows, features),
        w_gate[0],
        w_up[0],
        w_down[0],
    )
    returned = lax.all_to_all(
        partial_rows.reshape(groups, capacity, features),
        "group",
        split_axis=0,
        concat_axis=0,
        tiled=True,
    )
    returned = returned.reshape(block_rows, features)
    row_numbers = jnp.arange(tokens.shape[0] * lax.axis_size("member"), dtype=jnp.int32)
    selector = (row_numbers[:, None] == flat_slots[None, :]).astype(jnp.float32)
    summed = lax.psum_scatter(
        jnp.dot(
            selector, returned, precision=lax.Precision.HIGHEST, preferred_element_type=jnp.float32
        ),
        "member",
        scatter_dimension=0,
        tiled=True,
    )
    return (summed.astype(jnp.bfloat16), grad_gate[None], grad_up[None], grad_down[None])


def shards(tokens, grad_out, route_token, *rest):
    devices = lax.axis_size("group") * lax.axis_size("member")
    _, groups, experts, capacity = route_token.shape
    dense = devices * tokens.shape[0] <= groups * capacity and experts == 1 and groups <= 32
    paired = tokens.shape[0] == 1 and devices & (devices - 1) == 0
    body = dense_shards if dense and paired else routed_shards
    return body(tokens, grad_out, route_token, *rest)


def solution(mesh):
    placed = (
        P(("group", "member"), None),
        P(("group", "member"), None),
        P("group", None, None, None),
        P("group", None, None),
        P("group", None, None, None),
        P(("group", "member"), None, None),
        P(("group", "member"), None, None),
        P(("group", "member"), None, None),
    )
    return jax.shard_map(
        shards,
        mesh=mesh,
        in_specs=placed,
        out_specs=(
            P(("group", "member"), None),
            P(("group", "member"), None, None),
            P(("group", "member"), None, None),
            P(("group", "member"), None, None),
        ),
        check_vma=False,
    )
```

```python
import functools

import jax
import jax.numpy as jnp
from jax import lax
from jax.experimental import pallas as pl
from jax.experimental.pallas import tpu as pltpu
from jax.sharding import PartitionSpec as P

LANES = 128
PIECES = 4
AXES = ("group", "member")
VMEM = pl.BlockSpec(memory_space=pltpu.VMEM)
HBM = pl.BlockSpec(memory_space=pltpu.HBM)
SMEM = pl.BlockSpec(memory_space=pltpu.SMEM)
NT = (((1,), (1,)), ((), ()))
TN = (((0,), (0,)), ((), ()))


def round_up(value, step):
    return (value + step - 1) // step * step


def pack_kernel(chunks, tokens_ref, grad_ref, token_ref, count_ref, prob_ref, out_ref, rows_ref):
    me = lax.axis_index("member")
    groups, experts, capacity = token_ref.shape[1:]
    token_row = tokens_ref[...].astype(jnp.float32)
    grad_row = grad_ref[...].astype(jnp.float32)
    for k in range(chunks):
        part = slice(k * LANES, (k + 1) * LANES)
        rows_ref[k : k + 1, :] = token_row[:, part]
        rows_ref[chunks + k : chunks + k + 1, :] = grad_row[:, part]
    lane = lax.broadcasted_iota(jnp.int32, (1, LANES), 1)
    third = lax.rem(lane, 32)
    weights = jnp.zeros((1, LANES), jnp.float32)
    for g in range(groups):
        for j in range(experts):
            weight = jnp.float32(0)
            for p in range(capacity):
                live = (token_ref[0, g, j, p] == me) & (p < count_ref[0, j, g])
                weight = weight + jnp.where(live, prob_ref[0, g, j, p], 0.0)
            weights = jnp.where(third == g * experts + j, weight, weights)
    high = weights.astype(jnp.bfloat16).astype(jnp.float32)
    middle = (weights - high).astype(jnp.bfloat16).astype(jnp.float32)
    low = weights - high - middle
    parts = jnp.where(lane < 32, high, jnp.where(lane < 64, middle, jnp.where(lane < 96, low, 0.0)))
    rows_ref[2 * chunks : 2 * chunks + 1, :] = parts
    used = 2 * chunks + 1
    rows_ref[used:, :] = jnp.zeros((rows_ref.shape[0] - used, LANES), jnp.float32)
    packed = rows_ref[...].astype(jnp.bfloat16)
    for n in range(out_ref.shape[0]):
        out_ref[n] = packed


def load_kernel(gate_ref, up_ref, down_ref, gate_out, up_out, down_out, sems):
    copies = []
    for n, (source, target) in enumerate(
        ((gate_ref, gate_out), (up_ref, up_out), (down_ref, down_out))
    ):
        height = source.shape[1] // PIECES
        for k in range(PIECES):
            part = pl.ds(k * height, height)
            copies.append(
                pltpu.make_async_copy(
                    source.at[:, part], target.at[:, part], sems.at[n * PIECES + k]
                )
            )
    for copy in copies:
        copy.start()
    for copy in copies:
        copy.wait()


def unpack_rows(chunks, packed_ref, wide_ref, rows_ref):
    tokens, rows, _ = packed_ref.shape
    features = chunks * LANES
    wide_ref[...] = packed_ref[...].reshape(tokens * rows, LANES).astype(jnp.float32)

    def column(k):
        return wide_ref[pl.ds(k, tokens, stride=rows), :]

    lane = lax.broadcasted_iota(jnp.int32, (tokens, LANES), 1)
    mine = (lane < 96) & (lax.rem(lane, 32) == lax.axis_index("group"))
    weight = jnp.sum(jnp.where(mine, column(2 * chunks), 0.0), axis=1, keepdims=True)
    for k in range(chunks):
        rows_ref[:, k * LANES : (k + 1) * LANES] = column(k).astype(jnp.bfloat16)
        rows_ref[:, features + k * LANES : features + (k + 1) * LANES] = (
            weight * column(chunks + k)
        ).astype(jnp.bfloat16)
    return rows_ref[:, :features], rows_ref[:, features : 2 * features]


def activations(x, scaled, gate, up, down):
    gate_value = lax.dot_general(x, gate, NT, preferred_element_type=jnp.float32)
    up_value = lax.dot_general(x, up, NT, preferred_element_type=jnp.float32)
    d_hidden = lax.dot_general(scaled, down, NT, preferred_element_type=jnp.float32)
    sigma_gate = jax.nn.sigmoid(gate_value)
    active = gate_value * sigma_gate
    hidden = (active * up_value).astype(jnp.bfloat16)
    d_gate = (d_hidden * up_value * sigma_gate * (1.0 + gate_value * (1.0 - sigma_gate))).astype(
        jnp.bfloat16
    )
    d_up = (d_hidden * active).astype(jnp.bfloat16)
    return d_gate, d_up, hidden


def partial_kernel(
    chunks,
    mine_ref,
    other_ref,
    gate_ref,
    up_ref,
    down_ref,
    sent_ref,
    rows_ref,
    acts_ref,
    wide_ref,
    spread_ref,
):
    count = mine_ref.shape[0]
    tokens = 2 * count
    features = chunks * LANES
    for n, ref in enumerate((mine_ref, other_ref)):
        unpack_rows(chunks, ref, wide_ref, rows_ref.at[pl.ds(n * count, count)])
    x, scaled = rows_ref[:, :features], rows_ref[:, features:]
    acts = activations(x, scaled, gate_ref[0], up_ref[0], down_ref[0])
    for k, value in enumerate(acts):
        acts_ref[k] = value
    partial = jnp.dot(acts[0], gate_ref[0], preferred_element_type=jnp.float32)
    partial = partial + jnp.dot(acts[1], up_ref[0], preferred_element_type=jnp.float32)
    sent_rows = sent_ref.shape[2]
    for k in range(chunks):
        spread_ref[pl.ds(k, tokens, stride=sent_rows), :] = partial[:, k * LANES : (k + 1) * LANES]
    for k in range(chunks, sent_rows):
        spread_ref[pl.ds(k, tokens, stride=sent_rows), :] = jnp.zeros((tokens, LANES), jnp.float32)
    core = lax.rem(lax.axis_index("member"), 2)
    for n in range(2):
        first = n * count * sent_rows
        block = spread_ref[first : first + count * sent_rows, :].astype(jnp.bfloat16)
        sent_ref[:, core ^ n] = block.reshape(count, sent_rows, LANES)


def grads_kernel(features, rows_ref, acts_ref, gate_out, up_out, down_out):
    for k, (out, first) in enumerate(((gate_out, 0), (up_out, 0), (down_out, features))):
        out[0] = lax.dot_general(
            acts_ref[k], rows_ref[:, first : first + features], TN, preferred_element_type=jnp.float32
        ).astype(jnp.bfloat16)


def sum_kernel(chunks, back_ref, out_ref, total_ref):
    total_ref[...] = jnp.sum(back_ref[...].astype(jnp.float32), axis=0)
    for k in range(chunks):
        out_ref[:, k * LANES : (k + 1) * LANES] = total_ref[k : k + 1, :].astype(jnp.bfloat16)


def exchange(value, distance):
    count = lax.axis_size("group") * lax.axis_size("member")
    return lax.ppermute(value, AXES, [(i, i ^ distance) for i in range(count)])


def in_hbm(value):
    return pltpu.with_memory_space_constraint(value, pltpu.HBM)


def dense_shards(tokens, grad_out, route_token, route_count, route_prob, w_gate, w_up, w_down):
    features = tokens.shape[1]
    units = w_gate.shape[1]
    chunks = features // LANES
    count = lax.axis_size("group") * lax.axis_size("member")
    half = count // 2
    rows = round_up(2 * chunks + 1, 16)
    sent_rows = round_up(chunks, 16)
    copies = pl.pallas_call(
        functools.partial(pack_kernel, chunks),
        out_shape=jax.ShapeDtypeStruct((half, rows, LANES), jnp.bfloat16),
        in_specs=[VMEM, VMEM, SMEM, SMEM, SMEM],
        out_specs=VMEM,
        scratch_shapes=[pltpu.VMEM((rows, LANES), jnp.float32)],
        name="pack_rows",
    )(tokens, grad_out, route_token, jnp.swapaxes(route_count, 1, 2), route_prob)
    loaded = pl.pallas_call(
        load_kernel,
        out_shape=(pltpu.VMEM(w_gate.shape, jnp.bfloat16),) * 3,
        in_specs=[HBM] * 3,
        out_specs=(VMEM,) * 3,
        scratch_shapes=[pltpu.SemaphoreType.DMA((3 * PIECES,))],
        compiler_params=pltpu.CompilerParams(vmem_limit_bytes=8 * 1024 * 1024),
        cost_estimate=pl.CostEstimate(
            flops=0, bytes_accessed=6 * units * features, transcendentals=0
        ),
        name="load_weights",
    )(*[in_hbm(w) for w in (w_gate, w_up, w_down)])
    cores = [list(range(c, count, 2)) for c in range(2)]
    trade = functools.partial(
        lax.all_to_all, axis_name=AXES, split_axis=0, concat_axis=0, tiled=True
    )
    mine = trade(copies, axis_index_groups=cores)
    other = exchange(mine, 1)
    sent, both, acts = pl.pallas_call(
        functools.partial(partial_kernel, chunks),
        out_shape=(
            jax.ShapeDtypeStruct((half, 2, sent_rows, LANES), jnp.bfloat16),
            pltpu.VMEM((count, 2 * features), jnp.bfloat16),
            pltpu.VMEM((3, count, units), jnp.bfloat16),
        ),
        in_specs=[VMEM] * 5,
        out_specs=(VMEM,) * 3,
        scratch_shapes=[
            pltpu.VMEM((half * rows, LANES), jnp.float32),
            pltpu.VMEM((count * sent_rows, LANES), jnp.float32),
        ],
        compiler_params=pltpu.CompilerParams(vmem_limit_bytes=16 * 1024 * 1024),
        name="partial_rows",
    )(mine, other, *loaded)
    back = trade(sent.reshape(count, sent_rows, LANES))
    grad_shape = jax.ShapeDtypeStruct((1, units, features), jnp.bfloat16)
    grad_gate, grad_up, grad_down = pl.pallas_call(
        functools.partial(grads_kernel, features),
        out_shape=(grad_shape,) * 3,
        in_specs=[VMEM] * 2,
        out_specs=(VMEM,) * 3,
        compiler_params=pltpu.CompilerParams(vmem_limit_bytes=16 * 1024 * 1024),
        cost_estimate=pl.CostEstimate(
            flops=6 * count * units * features,
            bytes_accessed=6 * units * features,
            transcendentals=0,
        ),
        name="weight_grads",
    )(both, acts)
    grad_tokens = pl.pallas_call(
        functools.partial(sum_kernel, chunks),
        out_shape=jax.ShapeDtypeStruct((1, features), jnp.bfloat16),
        in_specs=[VMEM],
        out_specs=VMEM,
        scratch_shapes=[pltpu.VMEM((sent_rows, LANES), jnp.float32)],
        compiler_params=pltpu.CompilerParams(vmem_limit_bytes=4 * 1024 * 1024),
        name="sum_rows",
    )(back)
    return grad_tokens, grad_gate, grad_up, grad_down


def slice_backward(rows_x, rows_scaled, gate_weight, up_weight, down_weight):
    gate_value = jnp.dot(rows_x, gate_weight.T, preferred_element_type=jnp.float32)
    up_value = jnp.dot(rows_x, up_weight.T, preferred_element_type=jnp.float32)
    sigma_gate = jax.nn.sigmoid(gate_value)
    active = gate_value * sigma_gate
    hidden = (active * up_value).astype(jnp.bfloat16)
    d_hidden = jnp.dot(rows_scaled, down_weight.T, preferred_element_type=jnp.float32)
    d_gate = (d_hidden * up_value * sigma_gate * (1.0 + gate_value * (1.0 - sigma_gate))).astype(
        jnp.bfloat16
    )
    d_up = (d_hidden * active).astype(jnp.bfloat16)
    grad_down = jnp.dot(hidden.T, rows_scaled, preferred_element_type=jnp.float32).astype(
        jnp.bfloat16
    )
    grad_gate = jnp.dot(d_gate.T, rows_x, preferred_element_type=jnp.float32).astype(jnp.bfloat16)
    grad_up = jnp.dot(d_up.T, rows_x, preferred_element_type=jnp.float32).astype(jnp.bfloat16)
    partial_rows = jnp.dot(d_gate, gate_weight, preferred_element_type=jnp.float32)
    partial_rows = partial_rows + jnp.dot(d_up, up_weight, preferred_element_type=jnp.float32)
    return (grad_gate, grad_up, grad_down, partial_rows)


def routed_shards(tokens, grad_out, route_token, route_count, route_prob, w_gate, w_up, w_down):
    groups = route_token.shape[1]
    capacity = route_token.shape[3]
    features = tokens.shape[1]
    block_rows = groups * capacity
    split_count = max(8, lax.axis_size("member") // 8)
    expert_local = lax.axis_index("member") // split_count
    slot_tokens = lax.dynamic_index_in_dim(route_token[0], expert_local, 1, keepdims=False)
    slot_counts = lax.dynamic_index_in_dim(route_count[0], expert_local, 1, keepdims=False)
    slot_probs = lax.dynamic_index_in_dim(route_prob[0], expert_local, 1, keepdims=False)
    slot_index = jnp.arange(capacity, dtype=jnp.int32)[None, :]
    live = (slot_index < slot_counts[:, None]).astype(jnp.float32)
    slot_weights = (slot_probs * live).reshape(-1)
    flat_slots = slot_tokens.reshape(-1)
    group_x, group_dy = (
        lax.all_gather(tokens, "member", axis=0, tiled=True),
        lax.all_gather(grad_out, "member", axis=0, tiled=True),
    )
    picked_x = jnp.take(group_x, flat_slots, axis=0)
    picked_dy = jnp.take(group_dy, flat_slots, axis=0)
    scaled = (slot_weights[:, None] * picked_dy.astype(jnp.float32)).astype(jnp.bfloat16)
    send_x = picked_x.reshape(groups, capacity, features)
    send_scaled = scaled.reshape(groups, capacity, features)
    rows_x, rows_scaled = (
        lax.all_to_all(send_x, "group", split_axis=0, concat_axis=0, tiled=True),
        lax.all_to_all(send_scaled, "group", split_axis=0, concat_axis=0, tiled=True),
    )
    grad_gate, grad_up, grad_down, partial_rows = slice_backward(
        rows_x.reshape(block_rows, features),
        rows_scaled.reshape(block_rows, features),
        w_gate[0],
        w_up[0],
        w_down[0],
    )
    returned = lax.all_to_all(
        partial_rows.reshape(groups, capacity, features),
        "group",
        split_axis=0,
        concat_axis=0,
        tiled=True,
    )
    returned = returned.reshape(block_rows, features)
    row_numbers = jnp.arange(tokens.shape[0] * lax.axis_size("member"), dtype=jnp.int32)
    selector = (row_numbers[:, None] == flat_slots[None, :]).astype(jnp.float32)
    summed = lax.psum_scatter(
        jnp.dot(
            selector, returned, precision=lax.Precision.HIGHEST, preferred_element_type=jnp.float32
        ),
        "member",
        scatter_dimension=0,
        tiled=True,
    )
    return (summed.astype(jnp.bfloat16), grad_gate[None], grad_up[None], grad_down[None])


def shards(tokens, grad_out, route_token, *rest):
    devices = lax.axis_size("group") * lax.axis_size("member")
    _, groups, experts, capacity = route_token.shape
    dense = devices * tokens.shape[0] <= groups * capacity and experts == 1 and groups <= 32
    paired = tokens.shape[0] == 1 and devices & (devices - 1) == 0
    body = dense_shards if dense and paired else routed_shards
    return body(tokens, grad_out, route_token, *rest)


def solution(mesh):
    placed = (
        P(("group", "member"), None),
        P(("group", "member"), None),
        P("group", None, None, None),
        P("group", None, None),
        P("group", None, None, None),
        P(("group", "member"), None, None),
        P(("group", "member"), None, None),
        P(("group", "member"), None, None),
    )
    return jax.shard_map(
        shards,
        mesh=mesh,
        in_specs=placed,
        out_specs=(
            P(("group", "member"), None),
            P(("group", "member"), None, None),
            P(("group", "member"), None, None),
            P(("group", "member"), None, None),
        ),
        check_vma=False,
    )
```

```python
import functools

import jax
import jax.numpy as jnp
from jax import lax
from jax.experimental import pallas as pl
from jax.experimental.pallas import tpu as pltpu
from jax.sharding import PartitionSpec as P

LANES = 128
PIECES = 4
AXES = ("group", "member")
VMEM = pl.BlockSpec(memory_space=pltpu.VMEM)
HBM = pl.BlockSpec(memory_space=pltpu.HBM)
SMEM = pl.BlockSpec(memory_space=pltpu.SMEM)
NT = (((1,), (1,)), ((), ()))
TN = (((0,), (0,)), ((), ()))


def round_up(value, step):
    return (value + step - 1) // step * step


def pack_kernel(chunks, tokens_ref, grad_ref, token_ref, count_ref, prob_ref, out_ref, rows_ref):
    me = lax.axis_index("member")
    groups, experts, capacity = token_ref.shape[1:]
    token_row = tokens_ref[...].astype(jnp.float32)
    grad_row = grad_ref[...].astype(jnp.float32)
    for k in range(chunks):
        part = slice(k * LANES, (k + 1) * LANES)
        rows_ref[k : k + 1, :] = token_row[:, part]
        rows_ref[chunks + k : chunks + k + 1, :] = grad_row[:, part]
    lane = lax.broadcasted_iota(jnp.int32, (1, LANES), 1)
    third = lax.rem(lane, 32)
    weights = jnp.zeros((1, LANES), jnp.float32)
    for g in range(groups):
        for j in range(experts):
            weight = jnp.float32(0)
            for p in range(capacity):
                live = (token_ref[0, g, j, p] == me) & (p < count_ref[0, j, g])
                weight = weight + jnp.where(live, prob_ref[0, g, j, p], 0.0)
            weights = jnp.where(third == g * experts + j, weight, weights)
    high = weights.astype(jnp.bfloat16).astype(jnp.float32)
    middle = (weights - high).astype(jnp.bfloat16).astype(jnp.float32)
    low = weights - high - middle
    parts = jnp.where(lane < 32, high, jnp.where(lane < 64, middle, jnp.where(lane < 96, low, 0.0)))
    rows_ref[2 * chunks : 2 * chunks + 1, :] = parts
    used = 2 * chunks + 1
    rows_ref[used:, :] = jnp.zeros((rows_ref.shape[0] - used, LANES), jnp.float32)
    packed = rows_ref[...].astype(jnp.bfloat16)
    for n in range(out_ref.shape[0]):
        out_ref[n] = packed


def load_kernel(gate_ref, up_ref, down_ref, gate_out, up_out, down_out, sems):
    copies = []
    for n, (source, target) in enumerate(
        ((gate_ref, gate_out), (up_ref, up_out), (down_ref, down_out))
    ):
        height = source.shape[1] // PIECES
        for k in range(PIECES):
            part = pl.ds(k * height, height)
            copies.append(
                pltpu.make_async_copy(
                    source.at[:, part], target.at[:, part], sems.at[n * PIECES + k]
                )
            )
    for copy in copies:
        copy.start()
    for copy in copies:
        copy.wait()


def unpack_rows(chunks, packed_ref, wide_ref, rows_ref):
    tokens, rows, _ = packed_ref.shape
    features = chunks * LANES
    wide_ref[...] = packed_ref[...].reshape(tokens * rows, LANES).astype(jnp.float32)

    def column(k):
        return wide_ref[pl.ds(k, tokens, stride=rows), :]

    lane = lax.broadcasted_iota(jnp.int32, (tokens, LANES), 1)
    mine = (lane < 96) & (lax.rem(lane, 32) == lax.axis_index("group"))
    weight = jnp.sum(jnp.where(mine, column(2 * chunks), 0.0), axis=1, keepdims=True)
    for k in range(chunks):
        rows_ref[:, k * LANES : (k + 1) * LANES] = column(k).astype(jnp.bfloat16)
        rows_ref[:, features + k * LANES : features + (k + 1) * LANES] = (
            weight * column(chunks + k)
        ).astype(jnp.bfloat16)
    return rows_ref[:, :features], rows_ref[:, features : 2 * features]


def activations(x, scaled, gate, up, down):
    gate_value = lax.dot_general(x, gate, NT, preferred_element_type=jnp.float32)
    up_value = lax.dot_general(x, up, NT, preferred_element_type=jnp.float32)
    d_hidden = lax.dot_general(scaled, down, NT, preferred_element_type=jnp.float32)
    sigma_gate = jax.nn.sigmoid(gate_value)
    active = gate_value * sigma_gate
    hidden = (active * up_value).astype(jnp.bfloat16)
    d_gate = (d_hidden * up_value * sigma_gate * (1.0 + gate_value * (1.0 - sigma_gate))).astype(
        jnp.bfloat16
    )
    d_up = (d_hidden * active).astype(jnp.bfloat16)
    return d_gate, d_up, hidden


def partial_kernel(
    chunks,
    mine_ref,
    other_ref,
    gate_ref,
    up_ref,
    down_ref,
    keep_ref,
    give_ref,
    rows_ref,
    acts_ref,
    wide_ref,
    spread_ref,
):
    count = mine_ref.shape[0]
    tokens = 2 * count
    features = chunks * LANES
    for n, ref in enumerate((mine_ref, other_ref)):
        unpack_rows(chunks, ref, wide_ref, rows_ref.at[pl.ds(n * count, count)])
    x, scaled = rows_ref[:, :features], rows_ref[:, features:]
    acts = activations(x, scaled, gate_ref[0], up_ref[0], down_ref[0])
    for k, value in enumerate(acts):
        acts_ref[k] = value
    partial = jnp.dot(acts[0], gate_ref[0], preferred_element_type=jnp.float32)
    partial = partial + jnp.dot(acts[1], up_ref[0], preferred_element_type=jnp.float32)
    sent_rows = keep_ref.shape[1]
    for k in range(chunks):
        spread_ref[pl.ds(k, tokens, stride=sent_rows), :] = partial[:, k * LANES : (k + 1) * LANES]
    for k in range(chunks, sent_rows):
        spread_ref[pl.ds(k, tokens, stride=sent_rows), :] = jnp.zeros((tokens, LANES), jnp.float32)
    half = count * sent_rows
    keep_ref[...] = spread_ref[:half, :].reshape(keep_ref.shape)
    give_ref[...] = spread_ref[half:, :].reshape(give_ref.shape).astype(jnp.bfloat16)


def grads_kernel(features, rows_ref, acts_ref, gate_out, up_out, down_out, done_out):
    for k, (out, first) in enumerate(((gate_out, 0), (up_out, 0), (down_out, features))):
        out[0] = lax.dot_general(
            acts_ref[k], rows_ref[:, first : first + features], TN, preferred_element_type=jnp.float32
        ).astype(jnp.bfloat16)
    done_out[...] = jnp.zeros_like(done_out)


def add_kernel(keep_ref, got_ref, after_ref, sent_ref):
    del after_ref
    sent_ref[...] = (keep_ref[...] + got_ref[...].astype(jnp.float32)).astype(jnp.bfloat16)


def sum_kernel(chunks, back_ref, out_ref, total_ref):
    total_ref[...] = jnp.sum(back_ref[...].astype(jnp.float32), axis=0)
    for k in range(chunks):
        out_ref[:, k * LANES : (k + 1) * LANES] = total_ref[k : k + 1, :].astype(jnp.bfloat16)


def exchange(value, distance):
    count = lax.axis_size("group") * lax.axis_size("member")
    return lax.ppermute(value, AXES, [(i, i ^ distance) for i in range(count)])


def in_hbm(value):
    return pltpu.with_memory_space_constraint(value, pltpu.HBM)


def dense_shards(tokens, grad_out, route_token, route_count, route_prob, w_gate, w_up, w_down):
    features = tokens.shape[1]
    units = w_gate.shape[1]
    chunks = features // LANES
    count = lax.axis_size("group") * lax.axis_size("member")
    half = count // 2
    rows = round_up(2 * chunks + 1, 16)
    sent_rows = round_up(chunks, 16)
    copies = pl.pallas_call(
        functools.partial(pack_kernel, chunks),
        out_shape=jax.ShapeDtypeStruct((half, rows, LANES), jnp.bfloat16),
        in_specs=[VMEM, VMEM, SMEM, SMEM, SMEM],
        out_specs=VMEM,
        scratch_shapes=[pltpu.VMEM((rows, LANES), jnp.float32)],
        name="pack_rows",
    )(tokens, grad_out, route_token, jnp.swapaxes(route_count, 1, 2), route_prob)
    loaded = pl.pallas_call(
        load_kernel,
        out_shape=(pltpu.VMEM(w_gate.shape, jnp.bfloat16),) * 3,
        in_specs=[HBM] * 3,
        out_specs=(VMEM,) * 3,
        scratch_shapes=[pltpu.SemaphoreType.DMA((3 * PIECES,))],
        compiler_params=pltpu.CompilerParams(vmem_limit_bytes=8 * 1024 * 1024),
        cost_estimate=pl.CostEstimate(
            flops=0, bytes_accessed=6 * units * features, transcendentals=0
        ),
        name="load_weights",
    )(*[in_hbm(w) for w in (w_gate, w_up, w_down)])
    cores = [list(range(c, count, 2)) for c in range(2)]
    trade = functools.partial(
        lax.all_to_all,
        axis_name=AXES,
        split_axis=0,
        concat_axis=0,
        tiled=True,
        axis_index_groups=cores,
    )
    mine = trade(copies)
    other = exchange(mine, 1)
    keep, give, both, acts = pl.pallas_call(
        functools.partial(partial_kernel, chunks),
        out_shape=(
            pltpu.VMEM((half, sent_rows, LANES), jnp.float32),
            pltpu.VMEM((half, sent_rows, LANES), jnp.bfloat16),
            pltpu.VMEM((count, 2 * features), jnp.bfloat16),
            pltpu.VMEM((3, count, units), jnp.bfloat16),
        ),
        in_specs=[VMEM] * 5,
        out_specs=(VMEM,) * 4,
        scratch_shapes=[
            pltpu.VMEM((half * rows, LANES), jnp.float32),
            pltpu.VMEM((count * sent_rows, LANES), jnp.float32),
        ],
        compiler_params=pltpu.CompilerParams(vmem_limit_bytes=16 * 1024 * 1024),
        name="partial_rows",
    )(mine, other, *loaded)
    got = exchange(give, 1)
    grad_shape = jax.ShapeDtypeStruct((1, units, features), jnp.bfloat16)
    grad_gate, grad_up, grad_down, done = pl.pallas_call(
        functools.partial(grads_kernel, features),
        out_shape=(grad_shape,) * 3 + (pltpu.VMEM((8, LANES), jnp.float32),),
        in_specs=[VMEM] * 2,
        out_specs=(VMEM,) * 4,
        compiler_params=pltpu.CompilerParams(vmem_limit_bytes=16 * 1024 * 1024),
        cost_estimate=pl.CostEstimate(
            flops=6 * count * units * features,
            bytes_accessed=6 * units * features,
            transcendentals=0,
        ),
        name="weight_grads",
    )(both, acts)
    sent = pl.pallas_call(
        add_kernel,
        out_shape=pltpu.VMEM((half, sent_rows, LANES), jnp.bfloat16),
        in_specs=[VMEM] * 3,
        out_specs=VMEM,
        compiler_params=pltpu.CompilerParams(vmem_limit_bytes=4 * 1024 * 1024),
        name="add_cores",
    )(keep, got, done)
    back = trade(sent)
    grad_tokens = pl.pallas_call(
        functools.partial(sum_kernel, chunks),
        out_shape=jax.ShapeDtypeStruct((1, features), jnp.bfloat16),
        in_specs=[VMEM],
        out_specs=VMEM,
        scratch_shapes=[pltpu.VMEM((sent_rows, LANES), jnp.float32)],
        compiler_params=pltpu.CompilerParams(vmem_limit_bytes=4 * 1024 * 1024),
        name="sum_rows",
    )(back)
    return grad_tokens, grad_gate, grad_up, grad_down


def slice_backward(rows_x, rows_scaled, gate_weight, up_weight, down_weight):
    gate_value = jnp.dot(rows_x, gate_weight.T, preferred_element_type=jnp.float32)
    up_value = jnp.dot(rows_x, up_weight.T, preferred_element_type=jnp.float32)
    sigma_gate = jax.nn.sigmoid(gate_value)
    active = gate_value * sigma_gate
    hidden = (active * up_value).astype(jnp.bfloat16)
    d_hidden = jnp.dot(rows_scaled, down_weight.T, preferred_element_type=jnp.float32)
    d_gate = (d_hidden * up_value * sigma_gate * (1.0 + gate_value * (1.0 - sigma_gate))).astype(
        jnp.bfloat16
    )
    d_up = (d_hidden * active).astype(jnp.bfloat16)
    grad_down = jnp.dot(hidden.T, rows_scaled, preferred_element_type=jnp.float32).astype(
        jnp.bfloat16
    )
    grad_gate = jnp.dot(d_gate.T, rows_x, preferred_element_type=jnp.float32).astype(jnp.bfloat16)
    grad_up = jnp.dot(d_up.T, rows_x, preferred_element_type=jnp.float32).astype(jnp.bfloat16)
    partial_rows = jnp.dot(d_gate, gate_weight, preferred_element_type=jnp.float32)
    partial_rows = partial_rows + jnp.dot(d_up, up_weight, preferred_element_type=jnp.float32)
    return (grad_gate, grad_up, grad_down, partial_rows)


def routed_shards(tokens, grad_out, route_token, route_count, route_prob, w_gate, w_up, w_down):
    groups = route_token.shape[1]
    capacity = route_token.shape[3]
    features = tokens.shape[1]
    block_rows = groups * capacity
    split_count = max(8, lax.axis_size("member") // 8)
    expert_local = lax.axis_index("member") // split_count
    slot_tokens = lax.dynamic_index_in_dim(route_token[0], expert_local, 1, keepdims=False)
    slot_counts = lax.dynamic_index_in_dim(route_count[0], expert_local, 1, keepdims=False)
    slot_probs = lax.dynamic_index_in_dim(route_prob[0], expert_local, 1, keepdims=False)
    slot_index = jnp.arange(capacity, dtype=jnp.int32)[None, :]
    live = (slot_index < slot_counts[:, None]).astype(jnp.float32)
    slot_weights = (slot_probs * live).reshape(-1)
    flat_slots = slot_tokens.reshape(-1)
    group_x, group_dy = (
        lax.all_gather(tokens, "member", axis=0, tiled=True),
        lax.all_gather(grad_out, "member", axis=0, tiled=True),
    )
    picked_x = jnp.take(group_x, flat_slots, axis=0)
    picked_dy = jnp.take(group_dy, flat_slots, axis=0)
    scaled = (slot_weights[:, None] * picked_dy.astype(jnp.float32)).astype(jnp.bfloat16)
    send_x = picked_x.reshape(groups, capacity, features)
    send_scaled = scaled.reshape(groups, capacity, features)
    rows_x, rows_scaled = (
        lax.all_to_all(send_x, "group", split_axis=0, concat_axis=0, tiled=True),
        lax.all_to_all(send_scaled, "group", split_axis=0, concat_axis=0, tiled=True),
    )
    grad_gate, grad_up, grad_down, partial_rows = slice_backward(
        rows_x.reshape(block_rows, features),
        rows_scaled.reshape(block_rows, features),
        w_gate[0],
        w_up[0],
        w_down[0],
    )
    returned = lax.all_to_all(
        partial_rows.reshape(groups, capacity, features),
        "group",
        split_axis=0,
        concat_axis=0,
        tiled=True,
    )
    returned = returned.reshape(block_rows, features)
    row_numbers = jnp.arange(tokens.shape[0] * lax.axis_size("member"), dtype=jnp.int32)
    selector = (row_numbers[:, None] == flat_slots[None, :]).astype(jnp.float32)
    summed = lax.psum_scatter(
        jnp.dot(
            selector, returned, precision=lax.Precision.HIGHEST, preferred_element_type=jnp.float32
        ),
        "member",
        scatter_dimension=0,
        tiled=True,
    )
    return (summed.astype(jnp.bfloat16), grad_gate[None], grad_up[None], grad_down[None])


def shards(tokens, grad_out, route_token, *rest):
    devices = lax.axis_size("group") * lax.axis_size("member")
    _, groups, experts, capacity = route_token.shape
    dense = devices * tokens.shape[0] <= groups * capacity and experts == 1 and groups <= 32
    paired = tokens.shape[0] == 1 and devices & (devices - 1) == 0
    body = dense_shards if dense and paired else routed_shards
    return body(tokens, grad_out, route_token, *rest)


def solution(mesh):
    placed = (
        P(("group", "member"), None),
        P(("group", "member"), None),
        P("group", None, None, None),
        P("group", None, None),
        P("group", None, None, None),
        P(("group", "member"), None, None),
        P(("group", "member"), None, None),
        P(("group", "member"), None, None),
    )
    return jax.shard_map(
        shards,
        mesh=mesh,
        in_specs=placed,
        out_specs=(
            P(("group", "member"), None),
            P(("group", "member"), None, None),
            P(("group", "member"), None, None),
            P(("group", "member"), None, None),
        ),
        check_vma=False,
    )
```

```python
import functools

import jax
import jax.numpy as jnp
from jax import lax
from jax.experimental import pallas as pl
from jax.experimental.pallas import tpu as pltpu
from jax.sharding import PartitionSpec as P

LANES = 128
PIECES = 4
AXES = ("group", "member")
VMEM = pl.BlockSpec(memory_space=pltpu.VMEM)
HBM = pl.BlockSpec(memory_space=pltpu.HBM)
SMEM = pl.BlockSpec(memory_space=pltpu.SMEM)
NT = (((1,), (1,)), ((), ()))
TN = (((0,), (0,)), ((), ()))


def round_up(value, step):
    return (value + step - 1) // step * step


def pack_kernel(chunks, tokens_ref, grad_ref, token_ref, count_ref, prob_ref, out_ref, rows_ref):
    me = lax.axis_index("member")
    groups, experts, capacity = token_ref.shape[1:]
    token_row = tokens_ref[...].astype(jnp.float32)
    grad_row = grad_ref[...].astype(jnp.float32)
    for k in range(chunks):
        part = slice(k * LANES, (k + 1) * LANES)
        rows_ref[k : k + 1, :] = token_row[:, part]
        rows_ref[chunks + k : chunks + k + 1, :] = grad_row[:, part]
    lane = lax.broadcasted_iota(jnp.int32, (1, LANES), 1)
    third = lax.rem(lane, 32)
    weights = jnp.zeros((1, LANES), jnp.float32)
    for g in range(groups):
        for j in range(experts):
            weight = jnp.float32(0)
            for p in range(capacity):
                live = (token_ref[0, g, j, p] == me) & (p < count_ref[0, j, g])
                weight = weight + jnp.where(live, prob_ref[0, g, j, p], 0.0)
            weights = jnp.where(third == g * experts + j, weight, weights)
    high = weights.astype(jnp.bfloat16).astype(jnp.float32)
    middle = (weights - high).astype(jnp.bfloat16).astype(jnp.float32)
    low = weights - high - middle
    parts = jnp.where(lane < 32, high, jnp.where(lane < 64, middle, jnp.where(lane < 96, low, 0.0)))
    rows_ref[2 * chunks : 2 * chunks + 1, :] = parts
    used = 2 * chunks + 1
    rows_ref[used:, :] = jnp.zeros((rows_ref.shape[0] - used, LANES), jnp.float32)
    packed = rows_ref[...].astype(jnp.bfloat16)
    for n in range(out_ref.shape[0]):
        out_ref[n] = packed


def load_kernel(gate_ref, up_ref, down_ref, gate_out, up_out, down_out, sems):
    copies = []
    for n, (source, target) in enumerate(
        ((gate_ref, gate_out), (up_ref, up_out), (down_ref, down_out))
    ):
        height = source.shape[1] // PIECES
        for k in range(PIECES):
            part = pl.ds(k * height, height)
            copies.append(
                pltpu.make_async_copy(
                    source.at[:, part], target.at[:, part], sems.at[n * PIECES + k]
                )
            )
    for copy in copies:
        copy.start()
    for copy in copies:
        copy.wait()


def unpack_rows(chunks, packed_ref, wide_ref, rows_ref):
    tokens, rows, _ = packed_ref.shape
    features = chunks * LANES
    wide_ref[...] = packed_ref[...].reshape(tokens * rows, LANES).astype(jnp.float32)

    def column(k):
        return wide_ref[pl.ds(k, tokens, stride=rows), :]

    lane = lax.broadcasted_iota(jnp.int32, (tokens, LANES), 1)
    mine = (lane < 96) & (lax.rem(lane, 32) == lax.axis_index("group"))
    weight = jnp.sum(jnp.where(mine, column(2 * chunks), 0.0), axis=1, keepdims=True)
    for k in range(chunks):
        rows_ref[:, k * LANES : (k + 1) * LANES] = column(k).astype(jnp.bfloat16)
        rows_ref[:, features + k * LANES : features + (k + 1) * LANES] = (
            weight * column(chunks + k)
        ).astype(jnp.bfloat16)
    return rows_ref[:, :features], rows_ref[:, features : 2 * features]


def activations(x, scaled, gate, up, down):
    gate_value = lax.dot_general(x, gate, NT, preferred_element_type=jnp.float32)
    up_value = lax.dot_general(x, up, NT, preferred_element_type=jnp.float32)
    d_hidden = lax.dot_general(scaled, down, NT, preferred_element_type=jnp.float32)
    sigma_gate = jax.nn.sigmoid(gate_value)
    active = gate_value * sigma_gate
    hidden = (active * up_value).astype(jnp.bfloat16)
    d_gate = (d_hidden * up_value * sigma_gate * (1.0 + gate_value * (1.0 - sigma_gate))).astype(
        jnp.bfloat16
    )
    d_up = (d_hidden * active).astype(jnp.bfloat16)
    return d_gate, d_up, hidden


def partial_kernel(
    chunks,
    mine_ref,
    other_ref,
    gate_ref,
    up_ref,
    down_ref,
    keep_ref,
    give_ref,
    rows_ref,
    acts_ref,
    wide_ref,
    spread_ref,
):
    count = mine_ref.shape[0]
    tokens = 2 * count
    features = chunks * LANES
    for n, ref in enumerate((mine_ref, other_ref)):
        unpack_rows(chunks, ref, wide_ref, rows_ref.at[pl.ds(n * count, count)])
    x, scaled = rows_ref[:, :features], rows_ref[:, features:]
    acts = activations(x, scaled, gate_ref[0], up_ref[0], down_ref[0])
    for k, value in enumerate(acts):
        acts_ref[k] = value
    partial = jnp.dot(acts[0], gate_ref[0], preferred_element_type=jnp.float32)
    partial = partial + jnp.dot(acts[1], up_ref[0], preferred_element_type=jnp.float32)
    sent_rows = keep_ref.shape[1]
    for k in range(chunks):
        spread_ref[pl.ds(k, tokens, stride=sent_rows), :] = partial[:, k * LANES : (k + 1) * LANES]
    for k in range(chunks, sent_rows):
        spread_ref[pl.ds(k, tokens, stride=sent_rows), :] = jnp.zeros((tokens, LANES), jnp.float32)
    half = count * sent_rows
    keep_ref[...] = spread_ref[:half, :].reshape(keep_ref.shape)
    give_ref[...] = spread_ref[half:, :].reshape(give_ref.shape).astype(jnp.bfloat16)


def grads_kernel(features, rows_ref, acts_ref, gate_out, up_out, down_out, done_out):
    for k, (out, first) in enumerate(((gate_out, 0), (up_out, 0), (down_out, features))):
        out[0] = lax.dot_general(
            acts_ref[k], rows_ref[:, first : first + features], TN, preferred_element_type=jnp.float32
        ).astype(jnp.bfloat16)
    done_out[...] = jnp.zeros_like(done_out)


def add_kernel(keep_ref, got_ref, after_ref, sent_ref):
    del after_ref
    sent_ref[...] = (keep_ref[...] + got_ref[...].astype(jnp.float32)).astype(jnp.bfloat16)


def plane_sum_kernel(back_ref, out_ref):
    out_ref[...] = jnp.sum(back_ref[...].astype(jnp.float32), axis=0).astype(jnp.bfloat16)


def sum_kernel(chunks, back_ref, out_ref, total_ref):
    total_ref[...] = jnp.sum(back_ref[...].astype(jnp.float32), axis=0)
    for k in range(chunks):
        out_ref[:, k * LANES : (k + 1) * LANES] = total_ref[k : k + 1, :].astype(jnp.bfloat16)


def exchange(value, distance):
    count = lax.axis_size("group") * lax.axis_size("member")
    return lax.ppermute(value, AXES, [(i, i ^ distance) for i in range(count)])


def trade(value, axis, index_groups=None):
    return lax.all_to_all(value, axis, 0, 0, tiled=True, axis_index_groups=index_groups)


def in_hbm(value):
    return pltpu.with_memory_space_constraint(value, pltpu.HBM)


def dense_shards(tokens, grad_out, route_token, route_count, route_prob, w_gate, w_up, w_down):
    features = tokens.shape[1]
    units = w_gate.shape[1]
    chunks = features // LANES
    groups, members = lax.axis_size("group"), lax.axis_size("member")
    count = groups * members
    half = count // 2
    rows = round_up(2 * chunks + 1, 16)
    sent_rows = round_up(chunks, 16)
    copies = pl.pallas_call(
        functools.partial(pack_kernel, chunks),
        out_shape=jax.ShapeDtypeStruct((groups, rows, LANES), jnp.bfloat16),
        in_specs=[VMEM, VMEM, SMEM, SMEM, SMEM],
        out_specs=VMEM,
        scratch_shapes=[pltpu.VMEM((rows, LANES), jnp.float32)],
        name="pack_rows",
    )(tokens, grad_out, route_token, jnp.swapaxes(route_count, 1, 2), route_prob)
    loaded = pl.pallas_call(
        load_kernel,
        out_shape=(pltpu.VMEM(w_gate.shape, jnp.bfloat16),) * 3,
        in_specs=[HBM] * 3,
        out_specs=(VMEM,) * 3,
        scratch_shapes=[pltpu.SemaphoreType.DMA((3 * PIECES,))],
        compiler_params=pltpu.CompilerParams(vmem_limit_bytes=8 * 1024 * 1024),
        cost_estimate=pl.CostEstimate(
            flops=0, bytes_accessed=6 * units * features, transcendentals=0
        ),
        name="load_weights",
    )(*[in_hbm(w) for w in (w_gate, w_up, w_down)])
    cores = [list(range(c, members, 2)) for c in range(2)]
    column = trade(copies, "group")
    mine = lax.all_gather(column, "member", axis=0, tiled=True, axis_index_groups=cores)
    other = exchange(mine, 1)
    keep, give, both, acts = pl.pallas_call(
        functools.partial(partial_kernel, chunks),
        out_shape=(
            pltpu.VMEM((half, sent_rows, LANES), jnp.float32),
            pltpu.VMEM((half, sent_rows, LANES), jnp.bfloat16),
            pltpu.VMEM((count, 2 * features), jnp.bfloat16),
            pltpu.VMEM((3, count, units), jnp.bfloat16),
        ),
        in_specs=[VMEM] * 5,
        out_specs=(VMEM,) * 4,
        scratch_shapes=[
            pltpu.VMEM((half * rows, LANES), jnp.float32),
            pltpu.VMEM((count * sent_rows, LANES), jnp.float32),
        ],
        compiler_params=pltpu.CompilerParams(vmem_limit_bytes=16 * 1024 * 1024),
        name="partial_rows",
    )(mine, other, *loaded)
    got = exchange(give, 1)
    grad_shape = jax.ShapeDtypeStruct((1, units, features), jnp.bfloat16)
    grad_gate, grad_up, grad_down, done = pl.pallas_call(
        functools.partial(grads_kernel, features),
        out_shape=(grad_shape,) * 3 + (pltpu.VMEM((8, LANES), jnp.float32),),
        in_specs=[VMEM] * 2,
        out_specs=(VMEM,) * 4,
        compiler_params=pltpu.CompilerParams(vmem_limit_bytes=16 * 1024 * 1024),
        cost_estimate=pl.CostEstimate(
            flops=6 * count * units * features,
            bytes_accessed=6 * units * features,
            transcendentals=0,
        ),
        name="weight_grads",
    )(both, acts)
    sent = pl.pallas_call(
        add_kernel,
        out_shape=pltpu.VMEM((half, sent_rows, LANES), jnp.bfloat16),
        in_specs=[VMEM] * 3,
        out_specs=VMEM,
        compiler_params=pltpu.CompilerParams(vmem_limit_bytes=4 * 1024 * 1024),
        name="add_cores",
    )(keep, got, done)
    back = trade(sent.reshape(members // 2, groups, sent_rows, LANES), "member", cores)
    summed = pl.pallas_call(
        plane_sum_kernel,
        out_shape=pltpu.VMEM((groups, sent_rows, LANES), jnp.bfloat16),
        in_specs=[VMEM],
        out_specs=VMEM,
        compiler_params=pltpu.CompilerParams(vmem_limit_bytes=4 * 1024 * 1024),
        name="plane_sum",
    )(back)
    back = trade(summed, "group")
    grad_tokens = pl.pallas_call(
        functools.partial(sum_kernel, chunks),
        out_shape=jax.ShapeDtypeStruct((1, features), jnp.bfloat16),
        in_specs=[VMEM],
        out_specs=VMEM,
        scratch_shapes=[pltpu.VMEM((sent_rows, LANES), jnp.float32)],
        compiler_params=pltpu.CompilerParams(vmem_limit_bytes=4 * 1024 * 1024),
        name="sum_rows",
    )(back)
    return grad_tokens, grad_gate, grad_up, grad_down


def slice_backward(rows_x, rows_scaled, gate_weight, up_weight, down_weight):
    gate_value = jnp.dot(rows_x, gate_weight.T, preferred_element_type=jnp.float32)
    up_value = jnp.dot(rows_x, up_weight.T, preferred_element_type=jnp.float32)
    sigma_gate = jax.nn.sigmoid(gate_value)
    active = gate_value * sigma_gate
    hidden = (active * up_value).astype(jnp.bfloat16)
    d_hidden = jnp.dot(rows_scaled, down_weight.T, preferred_element_type=jnp.float32)
    d_gate = (d_hidden * up_value * sigma_gate * (1.0 + gate_value * (1.0 - sigma_gate))).astype(
        jnp.bfloat16
    )
    d_up = (d_hidden * active).astype(jnp.bfloat16)
    grad_down = jnp.dot(hidden.T, rows_scaled, preferred_element_type=jnp.float32).astype(
        jnp.bfloat16
    )
    grad_gate = jnp.dot(d_gate.T, rows_x, preferred_element_type=jnp.float32).astype(jnp.bfloat16)
    grad_up = jnp.dot(d_up.T, rows_x, preferred_element_type=jnp.float32).astype(jnp.bfloat16)
    partial_rows = jnp.dot(d_gate, gate_weight, preferred_element_type=jnp.float32)
    partial_rows = partial_rows + jnp.dot(d_up, up_weight, preferred_element_type=jnp.float32)
    return (grad_gate, grad_up, grad_down, partial_rows)


def routed_shards(tokens, grad_out, route_token, route_count, route_prob, w_gate, w_up, w_down):
    groups = route_token.shape[1]
    capacity = route_token.shape[3]
    features = tokens.shape[1]
    block_rows = groups * capacity
    split_count = max(8, lax.axis_size("member") // 8)
    expert_local = lax.axis_index("member") // split_count
    slot_tokens = lax.dynamic_index_in_dim(route_token[0], expert_local, 1, keepdims=False)
    slot_counts = lax.dynamic_index_in_dim(route_count[0], expert_local, 1, keepdims=False)
    slot_probs = lax.dynamic_index_in_dim(route_prob[0], expert_local, 1, keepdims=False)
    slot_index = jnp.arange(capacity, dtype=jnp.int32)[None, :]
    live = (slot_index < slot_counts[:, None]).astype(jnp.float32)
    slot_weights = (slot_probs * live).reshape(-1)
    flat_slots = slot_tokens.reshape(-1)
    group_x, group_dy = (
        lax.all_gather(tokens, "member", axis=0, tiled=True),
        lax.all_gather(grad_out, "member", axis=0, tiled=True),
    )
    picked_x = jnp.take(group_x, flat_slots, axis=0)
    picked_dy = jnp.take(group_dy, flat_slots, axis=0)
    scaled = (slot_weights[:, None] * picked_dy.astype(jnp.float32)).astype(jnp.bfloat16)
    send_x = picked_x.reshape(groups, capacity, features)
    send_scaled = scaled.reshape(groups, capacity, features)
    rows_x, rows_scaled = (
        lax.all_to_all(send_x, "group", split_axis=0, concat_axis=0, tiled=True),
        lax.all_to_all(send_scaled, "group", split_axis=0, concat_axis=0, tiled=True),
    )
    grad_gate, grad_up, grad_down, partial_rows = slice_backward(
        rows_x.reshape(block_rows, features),
        rows_scaled.reshape(block_rows, features),
        w_gate[0],
        w_up[0],
        w_down[0],
    )
    returned = lax.all_to_all(
        partial_rows.reshape(groups, capacity, features),
        "group",
        split_axis=0,
        concat_axis=0,
        tiled=True,
    )
    returned = returned.reshape(block_rows, features)
    row_numbers = jnp.arange(tokens.shape[0] * lax.axis_size("member"), dtype=jnp.int32)
    selector = (row_numbers[:, None] == flat_slots[None, :]).astype(jnp.float32)
    summed = lax.psum_scatter(
        jnp.dot(
            selector, returned, precision=lax.Precision.HIGHEST, preferred_element_type=jnp.float32
        ),
        "member",
        scatter_dimension=0,
        tiled=True,
    )
    return (summed.astype(jnp.bfloat16), grad_gate[None], grad_up[None], grad_down[None])


def shards(tokens, grad_out, route_token, *rest):
    devices = lax.axis_size("group") * lax.axis_size("member")
    _, groups, experts, capacity = route_token.shape
    dense = devices * tokens.shape[0] <= groups * capacity and experts == 1 and groups <= 32
    paired = tokens.shape[0] == 1 and devices & (devices - 1) == 0
    body = dense_shards if dense and paired else routed_shards
    return body(tokens, grad_out, route_token, *rest)


def solution(mesh):
    placed = (
        P(("group", "member"), None),
        P(("group", "member"), None),
        P("group", None, None, None),
        P("group", None, None),
        P("group", None, None, None),
        P(("group", "member"), None, None),
        P(("group", "member"), None, None),
        P(("group", "member"), None, None),
    )
    return jax.shard_map(
        shards,
        mesh=mesh,
        in_specs=placed,
        out_specs=(
            P(("group", "member"), None),
            P(("group", "member"), None, None),
            P(("group", "member"), None, None),
            P(("group", "member"), None, None),
        ),
        check_vma=False,
    )
```

```python
import functools

import jax
import jax.numpy as jnp
from jax import lax
from jax.experimental import pallas as pl
from jax.experimental.pallas import tpu as pltpu
from jax.sharding import PartitionSpec as P

LANES = 128
PIECES = 4
AXES = ("group", "member")
VMEM = pl.BlockSpec(memory_space=pltpu.VMEM)
HBM = pl.BlockSpec(memory_space=pltpu.HBM)
SMEM = pl.BlockSpec(memory_space=pltpu.SMEM)
NT = (((1,), (1,)), ((), ()))
TN = (((0,), (0,)), ((), ()))


def round_up(value, step):
    return (value + step - 1) // step * step


def pack_kernel(
    chunks,
    tokens_hbm,
    grad_hbm,
    token_hbm,
    count_hbm,
    prob_hbm,
    out_ref,
    rows_ref,
    tokens_ref,
    grad_ref,
    token_ref,
    count_ref,
    prob_ref,
    sems,
):
    pairs = (
        (token_hbm, token_ref),
        (count_hbm, count_ref),
        (prob_hbm, prob_ref),
        (tokens_hbm, tokens_ref),
        (grad_hbm, grad_ref),
    )
    copies = [pltpu.make_async_copy(*pair, sems.at[n]) for n, pair in enumerate(pairs)]
    for copy in copies:
        copy.start()
    for copy in copies:
        copy.wait()
    me = lax.axis_index("member")
    groups, experts, capacity = token_ref.shape[1:]
    token_row = tokens_ref[...].astype(jnp.float32)
    grad_row = grad_ref[...].astype(jnp.float32)
    for k in range(chunks):
        part = slice(k * LANES, (k + 1) * LANES)
        rows_ref[k : k + 1, :] = token_row[:, part]
        rows_ref[chunks + k : chunks + k + 1, :] = grad_row[:, part]
    lane = lax.broadcasted_iota(jnp.int32, (1, LANES), 1)
    third = lax.rem(lane, 32)
    weights = jnp.zeros((1, LANES), jnp.float32)
    for g in range(groups):
        for j in range(experts):
            weight = jnp.float32(0)
            for p in range(capacity):
                live = (token_ref[0, g, j, p] == me) & (p < count_ref[0, j, g])
                weight = weight + jnp.where(live, prob_ref[0, g, j, p], 0.0)
            weights = jnp.where(third == g * experts + j, weight, weights)
    high = weights.astype(jnp.bfloat16).astype(jnp.float32)
    middle = (weights - high).astype(jnp.bfloat16).astype(jnp.float32)
    low = weights - high - middle
    parts = jnp.where(lane < 32, high, jnp.where(lane < 64, middle, jnp.where(lane < 96, low, 0.0)))
    rows_ref[2 * chunks : 2 * chunks + 1, :] = parts
    used = 2 * chunks + 1
    rows_ref[used:, :] = jnp.zeros((rows_ref.shape[0] - used, LANES), jnp.float32)
    out_ref[0] = rows_ref[...].astype(jnp.bfloat16)


def load_kernel(source, target, sems):
    height = source.shape[1] // PIECES
    copies = []
    for k in range(PIECES):
        part = pl.ds(k * height, height)
        copies.append(pltpu.make_async_copy(source.at[:, part], target.at[:, part], sems.at[k]))
    for copy in copies:
        copy.start()
    for copy in copies:
        copy.wait()


def join_kernel(first_ref, second_ref, after_ref, out_ref):
    del after_ref
    count = first_ref.shape[0]
    out_ref[:count] = first_ref[...]
    out_ref[count:] = second_ref[...]


def unpack_rows(chunks, packed_ref, wide_ref, rows_ref):
    tokens, rows, _ = packed_ref.shape
    features = chunks * LANES
    wide_ref[...] = packed_ref[...].reshape(tokens * rows, LANES).astype(jnp.float32)

    def column(k):
        return wide_ref[pl.ds(k, tokens, stride=rows), :]

    lane = lax.broadcasted_iota(jnp.int32, (tokens, LANES), 1)
    mine = (lane < 96) & (lax.rem(lane, 32) == lax.axis_index("group"))
    weight = jnp.sum(jnp.where(mine, column(2 * chunks), 0.0), axis=1, keepdims=True)
    for k in range(chunks):
        rows_ref[:, k * LANES : (k + 1) * LANES] = column(k).astype(jnp.bfloat16)
        rows_ref[:, features + k * LANES : features + (k + 1) * LANES] = (
            weight * column(chunks + k)
        ).astype(jnp.bfloat16)
    return rows_ref[:, :features], rows_ref[:, features : 2 * features]


def activations(x, scaled, gate, up, down):
    gate_value = lax.dot_general(x, gate, NT, preferred_element_type=jnp.float32)
    up_value = lax.dot_general(x, up, NT, preferred_element_type=jnp.float32)
    d_hidden = lax.dot_general(scaled, down, NT, preferred_element_type=jnp.float32)
    sigma_gate = jax.nn.sigmoid(gate_value)
    active = gate_value * sigma_gate
    hidden = (active * up_value).astype(jnp.bfloat16)
    d_gate = (d_hidden * up_value * sigma_gate * (1.0 + gate_value * (1.0 - sigma_gate))).astype(
        jnp.bfloat16
    )
    d_up = (d_hidden * active).astype(jnp.bfloat16)
    return d_gate, d_up, hidden


def partial_kernel(
    chunks,
    mine_ref,
    other_ref,
    gate_ref,
    up_ref,
    down_ref,
    keep_ref,
    give_ref,
    rows_ref,
    acts_ref,
    wide_ref,
    spread_ref,
):
    count = mine_ref.shape[0]
    tokens = 2 * count
    features = chunks * LANES
    for n, ref in enumerate((mine_ref, other_ref)):
        unpack_rows(chunks, ref, wide_ref, rows_ref.at[pl.ds(n * count, count)])
    x, scaled = rows_ref[:, :features], rows_ref[:, features:]
    acts = activations(x, scaled, gate_ref[0], up_ref[0], down_ref[0])
    for k, value in enumerate(acts):
        acts_ref[k] = value
    partial = jnp.dot(acts[0], gate_ref[0], preferred_element_type=jnp.float32)
    partial = partial + jnp.dot(acts[1], up_ref[0], preferred_element_type=jnp.float32)
    sent_rows = keep_ref.shape[1]
    for k in range(chunks):
        spread_ref[pl.ds(k, tokens, stride=sent_rows), :] = partial[:, k * LANES : (k + 1) * LANES]
    for k in range(chunks, sent_rows):
        spread_ref[pl.ds(k, tokens, stride=sent_rows), :] = jnp.zeros((tokens, LANES), jnp.float32)
    half = count * sent_rows
    keep_ref[...] = spread_ref[:half, :].reshape(keep_ref.shape)
    give_ref[...] = spread_ref[half:, :].reshape(give_ref.shape).astype(jnp.bfloat16)


def grads_kernel(features, rows_ref, acts_ref, gate_out, up_out, down_out, done_out):
    for k, (out, first) in enumerate(((gate_out, 0), (up_out, 0), (down_out, features))):
        out[0] = lax.dot_general(
            acts_ref[k], rows_ref[:, first : first + features], TN, preferred_element_type=jnp.float32
        ).astype(jnp.bfloat16)
    done_out[...] = jnp.zeros_like(done_out)


def add_kernel(groups, keep_ref, got_ref, after_ref, sent_ref):
    del after_ref
    plane = keep_ref.shape[0] // groups
    for z in range(groups):
        for n in range(plane):
            value = keep_ref[n * groups + z] + got_ref[n * groups + z].astype(jnp.float32)
            sent_ref[(lax.axis_index("group") ^ z) * plane + n] = value.astype(jnp.bfloat16)


def sum_kernel(chunks, back_ref, out_ref, total_ref):
    total_ref[...] = jnp.sum(back_ref[...].astype(jnp.float32), axis=0)
    for k in range(chunks):
        out_ref[:, k * LANES : (k + 1) * LANES] = total_ref[k : k + 1, :].astype(jnp.bfloat16)


def exchange(value, distance):
    count = lax.axis_size("group") * lax.axis_size("member")
    return lax.ppermute(value, AXES, [(i, i ^ distance) for i in range(count)])


def in_hbm(value):
    return pltpu.with_memory_space_constraint(value, pltpu.HBM)


def dense_shards(tokens, grad_out, route_token, route_count, route_prob, w_gate, w_up, w_down):
    features = tokens.shape[1]
    units = w_gate.shape[1]
    chunks = features // LANES
    groups, members = lax.axis_size("group"), lax.axis_size("member")
    count = groups * members
    half = count // 2
    rows = round_up(2 * chunks + 1, 16)
    sent_rows = round_up(chunks, 16)
    arguments = (tokens, grad_out, route_token, jnp.swapaxes(route_count, 1, 2), route_prob)
    spaces = (pltpu.VMEM, pltpu.VMEM, pltpu.SMEM, pltpu.SMEM, pltpu.SMEM)
    piece = pl.pallas_call(
        functools.partial(pack_kernel, chunks),
        out_shape=pltpu.VMEM((1, rows, LANES), jnp.bfloat16),
        in_specs=[HBM] * 5,
        out_specs=VMEM,
        scratch_shapes=[pltpu.VMEM((rows, LANES), jnp.float32)]
        + [space(value.shape, value.dtype) for space, value in zip(spaces, arguments)]
        + [pltpu.SemaphoreType.DMA((5,))],
        compiler_params=pltpu.CompilerParams(vmem_limit_bytes=1024 * 1024),
        name="pack_rows",
    )(*[in_hbm(value) for value in arguments])
    loaded = [
        pl.pallas_call(
            load_kernel,
            out_shape=pltpu.VMEM(weight.shape, jnp.bfloat16),
            in_specs=[HBM],
            out_specs=VMEM,
            scratch_shapes=[pltpu.SemaphoreType.DMA((PIECES,))],
            compiler_params=pltpu.CompilerParams(vmem_limit_bytes=4 * 1024 * 1024),
            cost_estimate=pl.CostEstimate(
                flops=0, bytes_accessed=2 * units * features, transcendentals=0
            ),
            name="load_weight",
        )(in_hbm(weight))
        for weight in (w_gate, w_up, w_down)
    ]
    distance = members
    while distance < count:
        came = exchange(piece, distance)
        ready = loaded[min(1, distance // members // 2)]
        piece = pl.pallas_call(
            join_kernel,
            out_shape=pltpu.VMEM((2 * piece.shape[0], rows, LANES), jnp.bfloat16),
            in_specs=[VMEM, VMEM, pl.BlockSpec(memory_space=pl.ANY)],
            out_specs=VMEM,
            compiler_params=pltpu.CompilerParams(vmem_limit_bytes=1024 * 1024),
            name="join_rows",
        )(piece, came, ready)
        distance *= 2
    cores = [list(range(c, members, 2)) for c in range(2)]
    mine = lax.all_gather(piece, "member", axis=0, tiled=True, axis_index_groups=cores)
    other = exchange(mine, 1)
    keep, give, both, acts = pl.pallas_call(
        functools.partial(partial_kernel, chunks),
        out_shape=(
            pltpu.VMEM((half, sent_rows, LANES), jnp.float32),
            pltpu.VMEM((half, sent_rows, LANES), jnp.bfloat16),
            pltpu.VMEM((count, 2 * features), jnp.bfloat16),
            pltpu.VMEM((3, count, units), jnp.bfloat16),
        ),
        in_specs=[VMEM] * 5,
        out_specs=(VMEM,) * 4,
        scratch_shapes=[
            pltpu.VMEM((half * rows, LANES), jnp.float32),
            pltpu.VMEM((count * sent_rows, LANES), jnp.float32),
        ],
        compiler_params=pltpu.CompilerParams(vmem_limit_bytes=16 * 1024 * 1024),
        name="partial_rows",
    )(mine, other, *loaded)
    got = exchange(give, 1)
    grad_shape = jax.ShapeDtypeStruct((1, units, features), jnp.bfloat16)
    grad_gate, grad_up, grad_down, done = pl.pallas_call(
        functools.partial(grads_kernel, features),
        out_shape=(grad_shape,) * 3 + (pltpu.VMEM((8, LANES), jnp.float32),),
        in_specs=[VMEM] * 2,
        out_specs=(VMEM,) * 4,
        compiler_params=pltpu.CompilerParams(vmem_limit_bytes=16 * 1024 * 1024),
        cost_estimate=pl.CostEstimate(
            flops=6 * count * units * features,
            bytes_accessed=6 * units * features,
            transcendentals=0,
        ),
        name="weight_grads",
    )(both, acts)
    sent = pl.pallas_call(
        functools.partial(add_kernel, groups),
        out_shape=pltpu.VMEM((half, sent_rows, LANES), jnp.bfloat16),
        in_specs=[VMEM] * 3,
        out_specs=VMEM,
        compiler_params=pltpu.CompilerParams(vmem_limit_bytes=4 * 1024 * 1024),
        name="add_cores",
    )(keep, got, done)
    pairs = [list(range(c, count, 2)) for c in range(2)]
    back = lax.all_to_all(sent, AXES, 0, 0, tiled=True, axis_index_groups=pairs)
    grad_tokens = pl.pallas_call(
        functools.partial(sum_kernel, chunks),
        out_shape=jax.ShapeDtypeStruct((1, features), jnp.bfloat16),
        in_specs=[VMEM],
        out_specs=VMEM,
        scratch_shapes=[pltpu.VMEM((sent_rows, LANES), jnp.float32)],
        compiler_params=pltpu.CompilerParams(vmem_limit_bytes=4 * 1024 * 1024),
        name="sum_rows",
    )(back)
    return grad_tokens, grad_gate, grad_up, grad_down


def slice_backward(rows_x, rows_scaled, gate_weight, up_weight, down_weight):
    gate_value = jnp.dot(rows_x, gate_weight.T, preferred_element_type=jnp.float32)
    up_value = jnp.dot(rows_x, up_weight.T, preferred_element_type=jnp.float32)
    sigma_gate = jax.nn.sigmoid(gate_value)
    active = gate_value * sigma_gate
    hidden = (active * up_value).astype(jnp.bfloat16)
    d_hidden = jnp.dot(rows_scaled, down_weight.T, preferred_element_type=jnp.float32)
    d_gate = (d_hidden * up_value * sigma_gate * (1.0 + gate_value * (1.0 - sigma_gate))).astype(
        jnp.bfloat16
    )
    d_up = (d_hidden * active).astype(jnp.bfloat16)
    grad_down = jnp.dot(hidden.T, rows_scaled, preferred_element_type=jnp.float32).astype(
        jnp.bfloat16
    )
    grad_gate = jnp.dot(d_gate.T, rows_x, preferred_element_type=jnp.float32).astype(jnp.bfloat16)
    grad_up = jnp.dot(d_up.T, rows_x, preferred_element_type=jnp.float32).astype(jnp.bfloat16)
    partial_rows = jnp.dot(d_gate, gate_weight, preferred_element_type=jnp.float32)
    partial_rows = partial_rows + jnp.dot(d_up, up_weight, preferred_element_type=jnp.float32)
    return (grad_gate, grad_up, grad_down, partial_rows)


def routed_shards(tokens, grad_out, route_token, route_count, route_prob, w_gate, w_up, w_down):
    groups = route_token.shape[1]
    capacity = route_token.shape[3]
    features = tokens.shape[1]
    block_rows = groups * capacity
    split_count = max(8, lax.axis_size("member") // 8)
    expert_local = lax.axis_index("member") // split_count
    slot_tokens = lax.dynamic_index_in_dim(route_token[0], expert_local, 1, keepdims=False)
    slot_counts = lax.dynamic_index_in_dim(route_count[0], expert_local, 1, keepdims=False)
    slot_probs = lax.dynamic_index_in_dim(route_prob[0], expert_local, 1, keepdims=False)
    slot_index = jnp.arange(capacity, dtype=jnp.int32)[None, :]
    live = (slot_index < slot_counts[:, None]).astype(jnp.float32)
    slot_weights = (slot_probs * live).reshape(-1)
    flat_slots = slot_tokens.reshape(-1)
    group_x, group_dy = (
        lax.all_gather(tokens, "member", axis=0, tiled=True),
        lax.all_gather(grad_out, "member", axis=0, tiled=True),
    )
    picked_x = jnp.take(group_x, flat_slots, axis=0)
    picked_dy = jnp.take(group_dy, flat_slots, axis=0)
    scaled = (slot_weights[:, None] * picked_dy.astype(jnp.float32)).astype(jnp.bfloat16)
    send_x = picked_x.reshape(groups, capacity, features)
    send_scaled = scaled.reshape(groups, capacity, features)
    rows_x, rows_scaled = (
        lax.all_to_all(send_x, "group", split_axis=0, concat_axis=0, tiled=True),
        lax.all_to_all(send_scaled, "group", split_axis=0, concat_axis=0, tiled=True),
    )
    grad_gate, grad_up, grad_down, partial_rows = slice_backward(
        rows_x.reshape(block_rows, features),
        rows_scaled.reshape(block_rows, features),
        w_gate[0],
        w_up[0],
        w_down[0],
    )
    returned = lax.all_to_all(
        partial_rows.reshape(groups, capacity, features),
        "group",
        split_axis=0,
        concat_axis=0,
        tiled=True,
    )
    returned = returned.reshape(block_rows, features)
    row_numbers = jnp.arange(tokens.shape[0] * lax.axis_size("member"), dtype=jnp.int32)
    selector = (row_numbers[:, None] == flat_slots[None, :]).astype(jnp.float32)
    summed = lax.psum_scatter(
        jnp.dot(
            selector, returned, precision=lax.Precision.HIGHEST, preferred_element_type=jnp.float32
        ),
        "member",
        scatter_dimension=0,
        tiled=True,
    )
    return (summed.astype(jnp.bfloat16), grad_gate[None], grad_up[None], grad_down[None])


def shards(tokens, grad_out, route_token, *rest):
    devices = lax.axis_size("group") * lax.axis_size("member")
    _, groups, experts, capacity = route_token.shape
    dense = devices * tokens.shape[0] <= groups * capacity and experts == 1 and groups <= 32
    paired = tokens.shape[0] == 1 and devices & (devices - 1) == 0
    body = dense_shards if dense and paired else routed_shards
    return body(tokens, grad_out, route_token, *rest)


def solution(mesh):
    placed = (
        P(("group", "member"), None),
        P(("group", "member"), None),
        P("group", None, None, None),
        P("group", None, None),
        P("group", None, None, None),
        P(("group", "member"), None, None),
        P(("group", "member"), None, None),
        P(("group", "member"), None, None),
    )
    return jax.shard_map(
        shards,
        mesh=mesh,
        in_specs=placed,
        out_specs=(
            P(("group", "member"), None),
            P(("group", "member"), None, None),
            P(("group", "member"), None, None),
            P(("group", "member"), None, None),
        ),
        check_vma=False,
    )
```

```python
import functools

import jax
import jax.numpy as jnp
from jax import lax
from jax.experimental import pallas as pl
from jax.experimental.pallas import tpu as pltpu
from jax.sharding import PartitionSpec as P

LANES = 128
PIECES = 4
AXES = ("group", "member")
VMEM = pl.BlockSpec(memory_space=pltpu.VMEM)
HBM = pl.BlockSpec(memory_space=pltpu.HBM)
SMEM = pl.BlockSpec(memory_space=pltpu.SMEM)
NT = (((1,), (1,)), ((), ()))
TN = (((0,), (0,)), ((), ()))


def round_up(value, step):
    return (value + step - 1) // step * step


def pack_kernel(
    chunks,
    tokens_hbm,
    grad_hbm,
    token_hbm,
    count_hbm,
    prob_hbm,
    out_ref,
    rows_ref,
    tokens_ref,
    grad_ref,
    token_ref,
    count_ref,
    prob_ref,
    sems,
):
    pairs = (
        (token_hbm, token_ref),
        (count_hbm, count_ref),
        (prob_hbm, prob_ref),
        (tokens_hbm, tokens_ref),
        (grad_hbm, grad_ref),
    )
    copies = [pltpu.make_async_copy(*pair, sems.at[n]) for n, pair in enumerate(pairs)]
    for copy in copies:
        copy.start()
    for copy in copies:
        copy.wait()
    me = lax.axis_index("member")
    groups, _, capacity = token_ref.shape[1:]
    token_row = tokens_ref[...].astype(jnp.float32)
    grad_row = grad_ref[...].astype(jnp.float32)
    for k in range(chunks):
        part = slice(k * LANES, (k + 1) * LANES)
        rows_ref[k : k + 1, :] = token_row[:, part]
        rows_ref[chunks + k : chunks + k + 1, :] = grad_row[:, part]
    rows = rows_ref[...]
    is_token = lax.broadcasted_iota(jnp.int32, rows.shape, 0) < chunks
    places = out_ref.shape[0] // groups
    for g in range(groups):
        weight = jnp.float32(0)
        for p in range(capacity):
            live = (token_ref[0, g, 0, p] == me) & (p < count_ref[0, 0, g])
            weight = weight + jnp.where(live, prob_ref[0, g, 0, p], 0.0)
        packed = jnp.where(is_token, rows, rows * weight).astype(jnp.bfloat16)
        for n in range(places):
            out_ref[g * places + n] = packed


def load_kernel(gate_ref, up_ref, down_ref, gate_out, up_out, down_out, sems):
    copies = []
    for n, (source, target) in enumerate(
        ((gate_ref, gate_out), (up_ref, up_out), (down_ref, down_out))
    ):
        height = source.shape[1] // PIECES
        for k in range(PIECES):
            part = pl.ds(k * height, height)
            copies.append(
                pltpu.make_async_copy(
                    source.at[:, part], target.at[:, part], sems.at[n * PIECES + k]
                )
            )
    for copy in copies:
        copy.start()
    for copy in copies:
        copy.wait()


def unpack_rows(chunks, packed_ref, wide_ref, rows_ref):
    tokens, rows, _ = packed_ref.shape
    wide_ref[...] = packed_ref[...].astype(jnp.float32).reshape(tokens * rows, LANES)
    for k in range(rows):
        column = wide_ref[pl.ds(k, tokens, stride=rows), :]
        rows_ref[:, k * LANES : (k + 1) * LANES] = column.astype(jnp.bfloat16)


def activations(x, scaled, gate, up, down):
    gate_value = lax.dot_general(x, gate, NT, preferred_element_type=jnp.float32)
    up_value = lax.dot_general(x, up, NT, preferred_element_type=jnp.float32)
    d_hidden = lax.dot_general(scaled, down, NT, preferred_element_type=jnp.float32)
    sigma_gate = jax.nn.sigmoid(gate_value)
    active = gate_value * sigma_gate
    hidden = (active * up_value).astype(jnp.bfloat16)
    d_gate = (d_hidden * up_value * sigma_gate * (1.0 + gate_value * (1.0 - sigma_gate))).astype(
        jnp.bfloat16
    )
    d_up = (d_hidden * active).astype(jnp.bfloat16)
    return d_gate, d_up, hidden


def partial_kernel(
    chunks,
    mine_ref,
    other_ref,
    gate_ref,
    up_ref,
    down_ref,
    keep_ref,
    give_ref,
    rows_ref,
    acts_ref,
    wide_ref,
    spread_ref,
):
    count = mine_ref.shape[0]
    tokens = 2 * count
    features = chunks * LANES
    for n, ref in enumerate((mine_ref, other_ref)):
        unpack_rows(chunks, ref, wide_ref, rows_ref.at[pl.ds(n * count, count)])
    x, scaled = rows_ref[:, :features], rows_ref[:, features:]
    acts = activations(x, scaled, gate_ref[0], up_ref[0], down_ref[0])
    for k, value in enumerate(acts):
        acts_ref[k] = value
    partial = jnp.dot(acts[0], gate_ref[0], preferred_element_type=jnp.float32)
    partial = partial + jnp.dot(acts[1], up_ref[0], preferred_element_type=jnp.float32)
    sent_rows = keep_ref.shape[1]
    for k in range(chunks):
        spread_ref[pl.ds(k, tokens, stride=sent_rows), :] = partial[:, k * LANES : (k + 1) * LANES]
    for k in range(chunks, sent_rows):
        spread_ref[pl.ds(k, tokens, stride=sent_rows), :] = jnp.zeros((tokens, LANES), jnp.float32)
    half = count * sent_rows
    keep_ref[...] = spread_ref[:half, :].reshape(keep_ref.shape)
    give_ref[...] = spread_ref[half:, :].reshape(give_ref.shape).astype(jnp.bfloat16)


def grads_kernel(features, rows_ref, acts_ref, gate_out, up_out, down_out):
    for k, (out, first) in enumerate(((gate_out, 0), (up_out, 0), (down_out, features))):
        out[0] = lax.dot_general(
            acts_ref[k], rows_ref[:, first : first + features], TN, preferred_element_type=jnp.float32
        ).astype(jnp.bfloat16)


def add_kernel(keep_ref, got_ref, sent_ref):
    sent_ref[...] = (keep_ref[...] + got_ref[...].astype(jnp.float32)).astype(jnp.bfloat16)


def sum_kernel(chunks, back_ref, out_ref, total_ref):
    total_ref[...] = jnp.sum(back_ref[...].astype(jnp.float32), axis=0)
    for k in range(chunks):
        out_ref[:, k * LANES : (k + 1) * LANES] = total_ref[k : k + 1, :].astype(jnp.bfloat16)


def exchange(value, distance):
    count = lax.axis_size("group") * lax.axis_size("member")
    return lax.ppermute(value, AXES, [(i, i ^ distance) for i in range(count)])


def in_hbm(value):
    return pltpu.with_memory_space_constraint(value, pltpu.HBM)


def dense_shards(tokens, grad_out, route_token, route_count, route_prob, w_gate, w_up, w_down):
    features = tokens.shape[1]
    units = w_gate.shape[1]
    chunks = features // LANES
    count = lax.axis_size("group") * lax.axis_size("member")
    half = count // 2
    rows = 2 * chunks
    sent_rows = round_up(chunks, 16)
    arguments = (tokens, grad_out, route_token, jnp.swapaxes(route_count, 1, 2), route_prob)
    spaces = (pltpu.VMEM, pltpu.VMEM, pltpu.SMEM, pltpu.SMEM, pltpu.SMEM)
    copies = pl.pallas_call(
        functools.partial(pack_kernel, chunks),
        out_shape=jax.ShapeDtypeStruct((half, rows, LANES), jnp.bfloat16),
        in_specs=[HBM] * 5,
        out_specs=VMEM,
        scratch_shapes=[pltpu.VMEM((rows, LANES), jnp.float32)]
        + [space(value.shape, value.dtype) for space, value in zip(spaces, arguments)]
        + [pltpu.SemaphoreType.DMA((5,))],
        compiler_params=pltpu.CompilerParams(vmem_limit_bytes=4 * 1024 * 1024),
        name="pack_rows",
    )(*[in_hbm(value) for value in arguments])
    loaded = pl.pallas_call(
        load_kernel,
        out_shape=(pltpu.VMEM(w_gate.shape, jnp.bfloat16),) * 3,
        in_specs=[HBM] * 3,
        out_specs=(VMEM,) * 3,
        scratch_shapes=[pltpu.SemaphoreType.DMA((3 * PIECES,))],
        compiler_params=pltpu.CompilerParams(vmem_limit_bytes=8 * 1024 * 1024),
        cost_estimate=pl.CostEstimate(
            flops=0, bytes_accessed=6 * units * features, transcendentals=0
        ),
        name="load_weights",
    )(*[in_hbm(w) for w in (w_gate, w_up, w_down)])
    cores = [list(range(c, count, 2)) for c in range(2)]
    trade = functools.partial(
        lax.all_to_all,
        axis_name=AXES,
        split_axis=0,
        concat_axis=0,
        tiled=True,
        axis_index_groups=cores,
    )
    mine = trade(copies)
    other = exchange(mine, 1)
    keep, give, both, acts = pl.pallas_call(
        functools.partial(partial_kernel, chunks),
        out_shape=(
            pltpu.VMEM((half, sent_rows, LANES), jnp.float32),
            pltpu.VMEM((half, sent_rows, LANES), jnp.bfloat16),
            pltpu.VMEM((count, 2 * features), jnp.bfloat16),
            pltpu.VMEM((3, count, units), jnp.bfloat16),
        ),
        in_specs=[VMEM] * 5,
        out_specs=(VMEM,) * 4,
        scratch_shapes=[
            pltpu.VMEM((half * rows, LANES), jnp.float32),
            pltpu.VMEM((count * sent_rows, LANES), jnp.float32),
        ],
        compiler_params=pltpu.CompilerParams(vmem_limit_bytes=16 * 1024 * 1024),
        name="partial_rows",
    )(mine, other, *loaded)
    got = exchange(give, 1)
    grad_shape = jax.ShapeDtypeStruct((1, units, features), jnp.bfloat16)
    grad_gate, grad_up, grad_down = pl.pallas_call(
        functools.partial(grads_kernel, features),
        out_shape=(grad_shape,) * 3,
        in_specs=[VMEM] * 2,
        out_specs=(VMEM,) * 3,
        compiler_params=pltpu.CompilerParams(vmem_limit_bytes=16 * 1024 * 1024),
        cost_estimate=pl.CostEstimate(
            flops=6 * count * units * features,
            bytes_accessed=6 * units * features,
            transcendentals=0,
        ),
        name="weight_grads",
    )(both, acts)
    sent = pl.pallas_call(
        add_kernel,
        out_shape=pltpu.VMEM((half, sent_rows, LANES), jnp.bfloat16),
        in_specs=[VMEM] * 2,
        out_specs=VMEM,
        compiler_params=pltpu.CompilerParams(vmem_limit_bytes=4 * 1024 * 1024),
        name="add_cores",
    )(keep, got)
    back = trade(sent)
    grad_tokens = pl.pallas_call(
        functools.partial(sum_kernel, chunks),
        out_shape=jax.ShapeDtypeStruct((1, features), jnp.bfloat16),
        in_specs=[VMEM],
        out_specs=VMEM,
        scratch_shapes=[pltpu.VMEM((sent_rows, LANES), jnp.float32)],
        compiler_params=pltpu.CompilerParams(vmem_limit_bytes=4 * 1024 * 1024),
        name="sum_rows",
    )(back)
    return grad_tokens, grad_gate, grad_up, grad_down


def slice_backward(rows_x, rows_scaled, gate_weight, up_weight, down_weight):
    gate_value = jnp.dot(rows_x, gate_weight.T, preferred_element_type=jnp.float32)
    up_value = jnp.dot(rows_x, up_weight.T, preferred_element_type=jnp.float32)
    sigma_gate = jax.nn.sigmoid(gate_value)
    active = gate_value * sigma_gate
    hidden = (active * up_value).astype(jnp.bfloat16)
    d_hidden = jnp.dot(rows_scaled, down_weight.T, preferred_element_type=jnp.float32)
    d_gate = (d_hidden * up_value * sigma_gate * (1.0 + gate_value * (1.0 - sigma_gate))).astype(
        jnp.bfloat16
    )
    d_up = (d_hidden * active).astype(jnp.bfloat16)
    grad_down = jnp.dot(hidden.T, rows_scaled, preferred_element_type=jnp.float32).astype(
        jnp.bfloat16
    )
    grad_gate = jnp.dot(d_gate.T, rows_x, preferred_element_type=jnp.float32).astype(jnp.bfloat16)
    grad_up = jnp.dot(d_up.T, rows_x, preferred_element_type=jnp.float32).astype(jnp.bfloat16)
    partial_rows = jnp.dot(d_gate, gate_weight, preferred_element_type=jnp.float32)
    partial_rows = partial_rows + jnp.dot(d_up, up_weight, preferred_element_type=jnp.float32)
    return (grad_gate, grad_up, grad_down, partial_rows)


def routed_shards(tokens, grad_out, route_token, route_count, route_prob, w_gate, w_up, w_down):
    groups = route_token.shape[1]
    capacity = route_token.shape[3]
    features = tokens.shape[1]
    block_rows = groups * capacity
    split_count = max(8, lax.axis_size("member") // 8)
    expert_local = lax.axis_index("member") // split_count
    slot_tokens = lax.dynamic_index_in_dim(route_token[0], expert_local, 1, keepdims=False)
    slot_counts = lax.dynamic_index_in_dim(route_count[0], expert_local, 1, keepdims=False)
    slot_probs = lax.dynamic_index_in_dim(route_prob[0], expert_local, 1, keepdims=False)
    slot_index = jnp.arange(capacity, dtype=jnp.int32)[None, :]
    live = (slot_index < slot_counts[:, None]).astype(jnp.float32)
    slot_weights = (slot_probs * live).reshape(-1)
    flat_slots = slot_tokens.reshape(-1)
    group_x, group_dy = (
        lax.all_gather(tokens, "member", axis=0, tiled=True),
        lax.all_gather(grad_out, "member", axis=0, tiled=True),
    )
    picked_x = jnp.take(group_x, flat_slots, axis=0)
    picked_dy = jnp.take(group_dy, flat_slots, axis=0)
    scaled = (slot_weights[:, None] * picked_dy.astype(jnp.float32)).astype(jnp.bfloat16)
    send_x = picked_x.reshape(groups, capacity, features)
    send_scaled = scaled.reshape(groups, capacity, features)
    rows_x, rows_scaled = (
        lax.all_to_all(send_x, "group", split_axis=0, concat_axis=0, tiled=True),
        lax.all_to_all(send_scaled, "group", split_axis=0, concat_axis=0, tiled=True),
    )
    grad_gate, grad_up, grad_down, partial_rows = slice_backward(
        rows_x.reshape(block_rows, features),
        rows_scaled.reshape(block_rows, features),
        w_gate[0],
        w_up[0],
        w_down[0],
    )
    returned = lax.all_to_all(
        partial_rows.reshape(groups, capacity, features),
        "group",
        split_axis=0,
        concat_axis=0,
        tiled=True,
    )
    returned = returned.reshape(block_rows, features)
    row_numbers = jnp.arange(tokens.shape[0] * lax.axis_size("member"), dtype=jnp.int32)
    selector = (row_numbers[:, None] == flat_slots[None, :]).astype(jnp.float32)
    summed = lax.psum_scatter(
        jnp.dot(
            selector, returned, precision=lax.Precision.HIGHEST, preferred_element_type=jnp.float32
        ),
        "member",
        scatter_dimension=0,
        tiled=True,
    )
    return (summed.astype(jnp.bfloat16), grad_gate[None], grad_up[None], grad_down[None])


def shards(tokens, grad_out, route_token, *rest):
    devices = lax.axis_size("group") * lax.axis_size("member")
    _, groups, experts, capacity = route_token.shape
    dense = devices * tokens.shape[0] <= groups * capacity and experts == 1
    paired = tokens.shape[0] == 1 and devices & (devices - 1) == 0
    body = dense_shards if dense and paired else routed_shards
    return body(tokens, grad_out, route_token, *rest)


def solution(mesh):
    placed = (
        P(("group", "member"), None),
        P(("group", "member"), None),
        P("group", None, None, None),
        P("group", None, None),
        P("group", None, None, None),
        P(("group", "member"), None, None),
        P(("group", "member"), None, None),
        P(("group", "member"), None, None),
    )
    return jax.shard_map(
        shards,
        mesh=mesh,
        in_specs=placed,
        out_specs=(
            P(("group", "member"), None),
            P(("group", "member"), None, None),
            P(("group", "member"), None, None),
            P(("group", "member"), None, None),
        ),
        check_vma=False,
    )
```

```python
import functools

import jax
import jax.numpy as jnp
from jax import lax
from jax.experimental import pallas as pl
from jax.experimental.pallas import tpu as pltpu
from jax.sharding import PartitionSpec as P

LANES = 128
PIECES = 4
AXES = ("group", "member")
VMEM = pl.BlockSpec(memory_space=pltpu.VMEM)
HBM = pl.BlockSpec(memory_space=pltpu.HBM)
SMEM = pl.BlockSpec(memory_space=pltpu.SMEM)
NT = (((1,), (1,)), ((), ()))
TN = (((0,), (0,)), ((), ()))


def round_up(value, step):
    return (value + step - 1) // step * step


def pack_kernel(
    chunks,
    tokens_hbm,
    grad_hbm,
    token_hbm,
    count_hbm,
    prob_hbm,
    out_ref,
    rows_ref,
    tokens_ref,
    grad_ref,
    token_ref,
    count_ref,
    prob_ref,
    sems,
):
    pairs = (
        (token_hbm, token_ref),
        (count_hbm, count_ref),
        (prob_hbm, prob_ref),
        (tokens_hbm, tokens_ref),
        (grad_hbm, grad_ref),
    )
    copies = [pltpu.make_async_copy(*pair, sems.at[n]) for n, pair in enumerate(pairs)]
    for copy in copies:
        copy.start()
    for copy in copies:
        copy.wait()
    me = lax.axis_index("member")
    groups, _, capacity = token_ref.shape[1:]
    token_row = tokens_ref[...].astype(jnp.float32)
    grad_row = grad_ref[...].astype(jnp.float32)
    for k in range(chunks):
        part = slice(k * LANES, (k + 1) * LANES)
        rows_ref[k : k + 1, :] = token_row[:, part]
        rows_ref[chunks + k : chunks + k + 1, :] = grad_row[:, part]
    rows = rows_ref[...]
    is_token = lax.broadcasted_iota(jnp.int32, rows.shape, 0) < chunks
    places = out_ref.shape[0] // groups
    for g in range(groups):
        weight = jnp.float32(0)
        for p in range(capacity):
            live = (token_ref[0, g, 0, p] == me) & (p < count_ref[0, 0, g])
            weight = weight + jnp.where(live, prob_ref[0, g, 0, p], 0.0)
        packed = jnp.where(is_token, rows, rows * weight).astype(jnp.bfloat16)
        for n in range(places):
            out_ref[g * places + n] = packed


def load_kernel(gate_ref, up_ref, down_ref, out_ref, sems):
    copies = []
    for n, source in enumerate((gate_ref, up_ref, down_ref)):
        height = source.shape[1] // PIECES
        for k in range(PIECES):
            part = pl.ds(k * height, height)
            copies.append(
                pltpu.make_async_copy(source.at[0, part], out_ref.at[n, part], sems.at[n * PIECES + k])
            )
    for copy in copies:
        copy.start()
    for copy in copies:
        copy.wait()


def relay_kernel(value_ref, after_ref, out_ref):
    del after_ref
    out_ref[...] = value_ref[...]


def unpack_rows(chunks, packed_ref, wide_ref, rows_ref):
    tokens, rows, _ = packed_ref.shape
    wide_ref[...] = packed_ref[...].astype(jnp.float32).reshape(tokens * rows, LANES)
    for k in range(rows):
        column = wide_ref[pl.ds(k, tokens, stride=rows), :]
        rows_ref[:, k * LANES : (k + 1) * LANES] = column.astype(jnp.bfloat16)


def partial_kernel(
    chunks,
    mine_ref,
    other_ref,
    weights_ref,
    keep_ref,
    give_ref,
    rows_ref,
    acts_ref,
    wide_ref,
    spread_ref,
):
    count = mine_ref.shape[0]
    tokens = 2 * count
    features = chunks * LANES
    units = weights_ref.shape[1]
    for n, ref in enumerate((mine_ref, other_ref)):
        unpack_rows(chunks, ref, wide_ref, rows_ref.at[pl.ds(n * count, count)])
    x, scaled = rows_ref[:, :features], rows_ref[:, features:]
    both = weights_ref[:2].reshape(2 * units, features)
    values = lax.dot_general(both, x, NT, preferred_element_type=jnp.float32)
    gate_value, up_value = values[:units], values[units:]
    d_hidden = lax.dot_general(weights_ref[2], scaled, NT, preferred_element_type=jnp.float32)
    sigma_gate = jax.nn.sigmoid(gate_value)
    active = gate_value * sigma_gate
    d_gate = d_hidden * up_value * sigma_gate * (1.0 + gate_value * (1.0 - sigma_gate))
    acts_ref[0:units] = d_gate.astype(jnp.bfloat16)
    acts_ref[units : 2 * units] = (d_hidden * active).astype(jnp.bfloat16)
    acts_ref[2 * units :] = (active * up_value).astype(jnp.bfloat16)
    partial = lax.dot_general(
        acts_ref[: 2 * units], both, TN, preferred_element_type=jnp.float32
    )
    sent_rows = keep_ref.shape[1]
    for k in range(chunks):
        spread_ref[pl.ds(k, tokens, stride=sent_rows), :] = partial[:, k * LANES : (k + 1) * LANES]
    for k in range(chunks, sent_rows):
        spread_ref[pl.ds(k, tokens, stride=sent_rows), :] = jnp.zeros((tokens, LANES), jnp.float32)
    half = count * sent_rows
    keep_ref[...] = spread_ref[:half, :].reshape(keep_ref.shape)
    give_ref[...] = spread_ref[half:, :].reshape(give_ref.shape).astype(jnp.bfloat16)


def grads_kernel(
    features, rows_ref, acts_ref, gate_out, up_out, down_out, done_ref, held_ref, sems
):
    units = held_ref.shape[1]
    height = units // 2
    copies = []
    for n, (out, first) in enumerate(((gate_out, 0), (up_out, 0), (down_out, features))):
        right = rows_ref[:, first : first + features]
        for k in range(2):
            left = acts_ref[n * units + k * height : n * units + (k + 1) * height, :]
            held_ref[n, k * height : (k + 1) * height] = jnp.dot(
                left, right, preferred_element_type=jnp.float32
            ).astype(jnp.bfloat16)
            part = pl.ds(k * height, height)
            copies.append(
                pltpu.make_async_copy(held_ref.at[n, part], out.at[0, part], sems.at[2 * n + k])
            )
            copies[-1].start()
    done_ref[...] = jnp.zeros_like(done_ref)
    for copy in copies:
        copy.wait()


def add_kernel(keep_ref, got_ref, after_ref, sent_ref):
    del after_ref
    sent_ref[...] = (keep_ref[...] + got_ref[...].astype(jnp.float32)).astype(jnp.bfloat16)


def sum_kernel(chunks, back_ref, out_ref, total_ref):
    total_ref[...] = jnp.sum(back_ref[...].astype(jnp.float32), axis=0)
    for k in range(chunks):
        out_ref[:, k * LANES : (k + 1) * LANES] = total_ref[k : k + 1, :].astype(jnp.bfloat16)


def exchange(value, distance):
    count = lax.axis_size("group") * lax.axis_size("member")
    return lax.ppermute(value, AXES, [(i, i ^ distance) for i in range(count)])


def in_hbm(value):
    return pltpu.with_memory_space_constraint(value, pltpu.HBM)


def dense_shards(tokens, grad_out, route_token, route_count, route_prob, w_gate, w_up, w_down):
    features = tokens.shape[1]
    units = w_gate.shape[1]
    chunks = features // LANES
    count = lax.axis_size("group") * lax.axis_size("member")
    half = count // 2
    rows = 2 * chunks
    sent_rows = round_up(chunks, 16)
    arguments = (tokens, grad_out, route_token, jnp.swapaxes(route_count, 1, 2), route_prob)
    spaces = (pltpu.VMEM, pltpu.VMEM, pltpu.SMEM, pltpu.SMEM, pltpu.SMEM)
    copies = pl.pallas_call(
        functools.partial(pack_kernel, chunks),
        out_shape=jax.ShapeDtypeStruct((half, rows, LANES), jnp.bfloat16),
        in_specs=[HBM] * 5,
        out_specs=VMEM,
        scratch_shapes=[pltpu.VMEM((rows, LANES), jnp.float32)]
        + [space(value.shape, value.dtype) for space, value in zip(spaces, arguments)]
        + [pltpu.SemaphoreType.DMA((5,))],
        compiler_params=pltpu.CompilerParams(vmem_limit_bytes=4 * 1024 * 1024),
        name="pack_rows",
    )(*[in_hbm(value) for value in arguments])
    loaded = pl.pallas_call(
        load_kernel,
        out_shape=pltpu.VMEM((3, units, features), jnp.bfloat16),
        in_specs=[HBM] * 3,
        out_specs=VMEM,
        scratch_shapes=[pltpu.SemaphoreType.DMA((3 * PIECES,))],
        compiler_params=pltpu.CompilerParams(vmem_limit_bytes=8 * 1024 * 1024),
        cost_estimate=pl.CostEstimate(
            flops=0, bytes_accessed=6 * units * features, transcendentals=0
        ),
        name="load_weights",
    )(*[in_hbm(w) for w in (w_gate, w_up, w_down)])
    cores = [list(range(c, count, 2)) for c in range(2)]
    trade = functools.partial(
        lax.all_to_all,
        axis_name=AXES,
        split_axis=0,
        concat_axis=0,
        tiled=True,
        axis_index_groups=cores,
    )
    mine = trade(copies)
    relayed = pl.pallas_call(
        relay_kernel,
        out_shape=pltpu.VMEM((half, rows, LANES), jnp.bfloat16),
        in_specs=[VMEM, pl.BlockSpec(memory_space=pl.ANY)],
        out_specs=VMEM,
        compiler_params=pltpu.CompilerParams(vmem_limit_bytes=2 * 1024 * 1024),
        name="relay_rows",
    )(mine, loaded)
    other = exchange(relayed, 1)
    keep, give, both, acts = pl.pallas_call(
        functools.partial(partial_kernel, chunks),
        out_shape=(
            pltpu.VMEM((half, sent_rows, LANES), jnp.float32),
            pltpu.VMEM((half, sent_rows, LANES), jnp.bfloat16),
            pltpu.VMEM((count, 2 * features), jnp.bfloat16),
            pltpu.VMEM((3 * units, count), jnp.bfloat16),
        ),
        in_specs=[VMEM] * 3,
        out_specs=(VMEM,) * 4,
        scratch_shapes=[
            pltpu.VMEM((half * rows, LANES), jnp.float32),
            pltpu.VMEM((count * sent_rows, LANES), jnp.float32),
        ],
        compiler_params=pltpu.CompilerParams(vmem_limit_bytes=16 * 1024 * 1024),
        name="partial_rows",
    )(relayed, other, loaded)
    got = exchange(give, 1)
    grad_shape = jax.ShapeDtypeStruct((1, units, features), jnp.bfloat16)
    grad_gate, grad_up, grad_down, done = pl.pallas_call(
        functools.partial(grads_kernel, features),
        out_shape=(grad_shape,) * 3 + (pltpu.VMEM((8, LANES), jnp.float32),),
        in_specs=[VMEM] * 2,
        out_specs=(HBM, HBM, HBM, VMEM),
        scratch_shapes=[
            pltpu.VMEM((3, units, features), jnp.bfloat16),
            pltpu.SemaphoreType.DMA((6,)),
        ],
        compiler_params=pltpu.CompilerParams(vmem_limit_bytes=16 * 1024 * 1024),
        cost_estimate=pl.CostEstimate(
            flops=6 * count * units * features,
            bytes_accessed=6 * units * features,
            transcendentals=0,
        ),
        name="weight_grads",
    )(both, acts)
    sent = pl.pallas_call(
        add_kernel,
        out_shape=pltpu.VMEM((half, sent_rows, LANES), jnp.bfloat16),
        in_specs=[VMEM] * 3,
        out_specs=VMEM,
        compiler_params=pltpu.CompilerParams(vmem_limit_bytes=4 * 1024 * 1024),
        name="add_cores",
    )(keep, got, done)
    back = trade(sent)
    grad_tokens = pl.pallas_call(
        functools.partial(sum_kernel, chunks),
        out_shape=jax.ShapeDtypeStruct((1, features), jnp.bfloat16),
        in_specs=[VMEM],
        out_specs=VMEM,
        scratch_shapes=[pltpu.VMEM((sent_rows, LANES), jnp.float32)],
        compiler_params=pltpu.CompilerParams(vmem_limit_bytes=4 * 1024 * 1024),
        name="sum_rows",
    )(back)
    return grad_tokens, grad_gate, grad_up, grad_down


def slice_backward(rows_x, rows_scaled, gate_weight, up_weight, down_weight):
    gate_value = jnp.dot(rows_x, gate_weight.T, preferred_element_type=jnp.float32)
    up_value = jnp.dot(rows_x, up_weight.T, preferred_element_type=jnp.float32)
    sigma_gate = jax.nn.sigmoid(gate_value)
    active = gate_value * sigma_gate
    hidden = (active * up_value).astype(jnp.bfloat16)
    d_hidden = jnp.dot(rows_scaled, down_weight.T, preferred_element_type=jnp.float32)
    d_gate = (d_hidden * up_value * sigma_gate * (1.0 + gate_value * (1.0 - sigma_gate))).astype(
        jnp.bfloat16
    )
    d_up = (d_hidden * active).astype(jnp.bfloat16)
    grad_down = jnp.dot(hidden.T, rows_scaled, preferred_element_type=jnp.float32).astype(
        jnp.bfloat16
    )
    grad_gate = jnp.dot(d_gate.T, rows_x, preferred_element_type=jnp.float32).astype(jnp.bfloat16)
    grad_up = jnp.dot(d_up.T, rows_x, preferred_element_type=jnp.float32).astype(jnp.bfloat16)
    partial_rows = jnp.dot(d_gate, gate_weight, preferred_element_type=jnp.float32)
    partial_rows = partial_rows + jnp.dot(d_up, up_weight, preferred_element_type=jnp.float32)
    return (grad_gate, grad_up, grad_down, partial_rows)


def routed_shards(tokens, grad_out, route_token, route_count, route_prob, w_gate, w_up, w_down):
    groups = route_token.shape[1]
    capacity = route_token.shape[3]
    features = tokens.shape[1]
    block_rows = groups * capacity
    split_count = max(8, lax.axis_size("member") // 8)
    expert_local = lax.axis_index("member") // split_count
    slot_tokens = lax.dynamic_index_in_dim(route_token[0], expert_local, 1, keepdims=False)
    slot_counts = lax.dynamic_index_in_dim(route_count[0], expert_local, 1, keepdims=False)
    slot_probs = lax.dynamic_index_in_dim(route_prob[0], expert_local, 1, keepdims=False)
    slot_index = jnp.arange(capacity, dtype=jnp.int32)[None, :]
    live = (slot_index < slot_counts[:, None]).astype(jnp.float32)
    slot_weights = (slot_probs * live).reshape(-1)
    flat_slots = slot_tokens.reshape(-1)
    group_x, group_dy = (
        lax.all_gather(tokens, "member", axis=0, tiled=True),
        lax.all_gather(grad_out, "member", axis=0, tiled=True),
    )
    picked_x = jnp.take(group_x, flat_slots, axis=0)
    picked_dy = jnp.take(group_dy, flat_slots, axis=0)
    scaled = (slot_weights[:, None] * picked_dy.astype(jnp.float32)).astype(jnp.bfloat16)
    send_x = picked_x.reshape(groups, capacity, features)
    send_scaled = scaled.reshape(groups, capacity, features)
    rows_x, rows_scaled = (
        lax.all_to_all(send_x, "group", split_axis=0, concat_axis=0, tiled=True),
        lax.all_to_all(send_scaled, "group", split_axis=0, concat_axis=0, tiled=True),
    )
    grad_gate, grad_up, grad_down, partial_rows = slice_backward(
        rows_x.reshape(block_rows, features),
        rows_scaled.reshape(block_rows, features),
        w_gate[0],
        w_up[0],
        w_down[0],
    )
    returned = lax.all_to_all(
        partial_rows.reshape(groups, capacity, features),
        "group",
        split_axis=0,
        concat_axis=0,
        tiled=True,
    )
    returned = returned.reshape(block_rows, features)
    row_numbers = jnp.arange(tokens.shape[0] * lax.axis_size("member"), dtype=jnp.int32)
    selector = (row_numbers[:, None] == flat_slots[None, :]).astype(jnp.float32)
    summed = lax.psum_scatter(
        jnp.dot(
            selector, returned, precision=lax.Precision.HIGHEST, preferred_element_type=jnp.float32
        ),
        "member",
        scatter_dimension=0,
        tiled=True,
    )
    return (summed.astype(jnp.bfloat16), grad_gate[None], grad_up[None], grad_down[None])


def shards(tokens, grad_out, route_token, *rest):
    devices = lax.axis_size("group") * lax.axis_size("member")
    _, groups, experts, capacity = route_token.shape
    dense = devices * tokens.shape[0] <= groups * capacity and experts == 1
    paired = tokens.shape[0] == 1 and devices & (devices - 1) == 0
    body = dense_shards if dense and paired else routed_shards
    return body(tokens, grad_out, route_token, *rest)


def solution(mesh):
    placed = (
        P(("group", "member"), None),
        P(("group", "member"), None),
        P("group", None, None, None),
        P("group", None, None),
        P("group", None, None, None),
        P(("group", "member"), None, None),
        P(("group", "member"), None, None),
        P(("group", "member"), None, None),
    )
    return jax.shard_map(
        shards,
        mesh=mesh,
        in_specs=placed,
        out_specs=(
            P(("group", "member"), None),
            P(("group", "member"), None, None),
            P(("group", "member"), None, None),
            P(("group", "member"), None, None),
        ),
        check_vma=False,
    )
```

```python
import functools

import jax
import jax.numpy as jnp
from jax import lax
from jax.experimental import pallas as pl
from jax.experimental.pallas import tpu as pltpu
from jax.sharding import PartitionSpec as P

LANES = 128
PIECES = 4
AXES = ("group", "member")
VMEM = pl.BlockSpec(memory_space=pltpu.VMEM)
HBM = pl.BlockSpec(memory_space=pltpu.HBM)
SMEM = pl.BlockSpec(memory_space=pltpu.SMEM)
NT = (((1,), (1,)), ((), ()))
TN = (((0,), (0,)), ((), ()))


def round_up(value, step):
    return (value + step - 1) // step * step


def pack_kernel(chunks, groups, tokens_hbm, grad_hbm, token_hbm, count_hbm, prob_hbm, *refs):
    out_refs, refs = refs[:groups], refs[groups:]
    rows_ref, tokens_ref, grad_ref, token_ref, count_ref, prob_ref, sems = refs
    pairs = (
        (token_hbm, token_ref),
        (count_hbm, count_ref),
        (prob_hbm, prob_ref),
        (tokens_hbm, tokens_ref),
        (grad_hbm, grad_ref),
    )
    copies = [pltpu.make_async_copy(*pair, sems.at[n]) for n, pair in enumerate(pairs)]
    for copy in copies:
        copy.start()
    for copy in copies:
        copy.wait()
    me = lax.axis_index("member")
    capacity = token_ref.shape[3]
    token_row = tokens_ref[...].astype(jnp.float32)
    grad_row = grad_ref[...].astype(jnp.float32)
    for k in range(chunks):
        part = slice(k * LANES, (k + 1) * LANES)
        rows_ref[k : k + 1, :] = token_row[:, part]
        rows_ref[chunks + k : chunks + k + 1, :] = grad_row[:, part]
    rows = rows_ref[...]
    is_token = lax.broadcasted_iota(jnp.int32, rows.shape, 0) < chunks
    for z, out_ref in enumerate(out_refs):
        g = lax.axis_index("group") ^ z
        weight = jnp.float32(0)
        for p in range(capacity):
            live = (token_ref[0, g, 0, p] == me) & (p < count_ref[0, 0, g])
            weight = weight + jnp.where(live, prob_ref[0, g, 0, p], 0.0)
        out_ref[...] = jnp.where(is_token, rows, rows * weight).astype(jnp.bfloat16)


def load_kernel(gate_ref, up_ref, down_ref, out_ref, sems):
    copies = []
    for n, source in enumerate((gate_ref, up_ref, down_ref)):
        height = source.shape[1] // PIECES
        for k in range(PIECES):
            part = pl.ds(k * height, height)
            copies.append(
                pltpu.make_async_copy(source.at[0, part], out_ref.at[n, part], sems.at[n * PIECES + k])
            )
    for copy in copies:
        copy.start()
    for copy in copies:
        copy.wait()


def join_kernel(*refs):
    for z, ref in enumerate(refs[:-1]):
        refs[-1][z] = ref[...]


def split_kernel(value_ref, *out_refs):
    for z, ref in enumerate(out_refs):
        ref[...] = value_ref[z]


def unpack_rows(chunks, packed_ref, wide_ref, rows_ref):
    tokens, rows, _ = packed_ref.shape
    wide_ref[...] = packed_ref[...].astype(jnp.float32).reshape(tokens * rows, LANES)
    for k in range(rows):
        column = wide_ref[pl.ds(k, tokens, stride=rows), :]
        rows_ref[:, k * LANES : (k + 1) * LANES] = column.astype(jnp.bfloat16)


def partial_kernel(
    chunks,
    mine_ref,
    other_ref,
    weights_ref,
    keep_ref,
    give_ref,
    rows_ref,
    acts_ref,
    wide_ref,
    spread_ref,
):
    count = mine_ref.shape[0]
    tokens = 2 * count
    features = chunks * LANES
    units = weights_ref.shape[1]
    for n, ref in enumerate((mine_ref, other_ref)):
        unpack_rows(chunks, ref, wide_ref, rows_ref.at[pl.ds(n * count, count)])
    x, scaled = rows_ref[:, :features], rows_ref[:, features:]
    both = weights_ref[:2].reshape(2 * units, features)
    values = lax.dot_general(both, x, NT, preferred_element_type=jnp.float32)
    gate_value, up_value = values[:units], values[units:]
    d_hidden = lax.dot_general(weights_ref[2], scaled, NT, preferred_element_type=jnp.float32)
    sigma_gate = jax.nn.sigmoid(gate_value)
    active = gate_value * sigma_gate
    d_gate = d_hidden * up_value * sigma_gate * (1.0 + gate_value * (1.0 - sigma_gate))
    acts_ref[0:units] = d_gate.astype(jnp.bfloat16)
    acts_ref[units : 2 * units] = (d_hidden * active).astype(jnp.bfloat16)
    acts_ref[2 * units :] = (active * up_value).astype(jnp.bfloat16)
    partial = lax.dot_general(
        acts_ref[: 2 * units], both, TN, preferred_element_type=jnp.float32
    )
    sent_rows = keep_ref.shape[1]
    for k in range(chunks):
        spread_ref[pl.ds(k, tokens, stride=sent_rows), :] = partial[:, k * LANES : (k + 1) * LANES]
    for k in range(chunks, sent_rows):
        spread_ref[pl.ds(k, tokens, stride=sent_rows), :] = jnp.zeros((tokens, LANES), jnp.float32)
    half = count * sent_rows
    keep_ref[...] = spread_ref[:half, :].reshape(keep_ref.shape)
    give_ref[...] = spread_ref[half:, :].reshape(give_ref.shape).astype(jnp.bfloat16)


def grads_kernel(
    features, rows_ref, acts_ref, gate_out, up_out, down_out, done_ref, held_ref, sems
):
    units = held_ref.shape[1]
    height = units // 2
    copies = []
    for n, (out, first) in enumerate(((gate_out, 0), (up_out, 0), (down_out, features))):
        right = rows_ref[:, first : first + features]
        for k in range(2):
            left = acts_ref[n * units + k * height : n * units + (k + 1) * height, :]
            held_ref[n, k * height : (k + 1) * height] = jnp.dot(
                left, right, preferred_element_type=jnp.float32
            ).astype(jnp.bfloat16)
            part = pl.ds(k * height, height)
            copies.append(
                pltpu.make_async_copy(held_ref.at[n, part], out.at[0, part], sems.at[2 * n + k])
            )
            copies[-1].start()
    done_ref[...] = jnp.zeros_like(done_ref)
    for copy in copies:
        copy.wait()


def add_kernel(keep_ref, got_ref, after_ref, sent_ref):
    del after_ref
    sent_ref[...] = (keep_ref[...] + got_ref[...].astype(jnp.float32)).astype(jnp.bfloat16)


def sum_kernel(chunks, *refs):
    *back_refs, out_ref, total_ref = refs
    total = back_refs[0][...].astype(jnp.float32)
    for ref in back_refs[1:]:
        total = total + ref[...].astype(jnp.float32)
    total_ref[...] = total
    for k in range(chunks):
        out_ref[:, k * LANES : (k + 1) * LANES] = total_ref[k : k + 1, :].astype(jnp.bfloat16)


def exchange(value, distance):
    count = lax.axis_size("group") * lax.axis_size("member")
    return lax.ppermute(value, AXES, [(i, i ^ distance) for i in range(count)])


def in_hbm(value):
    return pltpu.with_memory_space_constraint(value, pltpu.HBM)


def dense_shards(tokens, grad_out, route_token, route_count, route_prob, w_gate, w_up, w_down):
    features = tokens.shape[1]
    units = w_gate.shape[1]
    chunks = features // LANES
    groups, members = lax.axis_size("group"), lax.axis_size("member")
    count = groups * members
    half = count // 2
    rows = 2 * chunks
    sent_rows = round_up(chunks, 16)
    arguments = (tokens, grad_out, route_token, jnp.swapaxes(route_count, 1, 2), route_prob)
    spaces = (pltpu.VMEM, pltpu.VMEM, pltpu.SMEM, pltpu.SMEM, pltpu.SMEM)
    copies = pl.pallas_call(
        functools.partial(pack_kernel, chunks, groups),
        out_shape=(pltpu.VMEM((rows, LANES), jnp.bfloat16),) * groups,
        in_specs=[HBM] * 5,
        out_specs=(VMEM,) * groups,
        scratch_shapes=[pltpu.VMEM((rows, LANES), jnp.float32)]
        + [space(value.shape, value.dtype) for space, value in zip(spaces, arguments)]
        + [pltpu.SemaphoreType.DMA((5,))],
        compiler_params=pltpu.CompilerParams(vmem_limit_bytes=4 * 1024 * 1024),
        name="pack_rows",
    )(*[in_hbm(value) for value in arguments])
    loaded = pl.pallas_call(
        load_kernel,
        out_shape=pltpu.VMEM((3, units, features), jnp.bfloat16),
        in_specs=[HBM] * 3,
        out_specs=VMEM,
        scratch_shapes=[pltpu.SemaphoreType.DMA((3 * PIECES,))],
        compiler_params=pltpu.CompilerParams(vmem_limit_bytes=8 * 1024 * 1024),
        cost_estimate=pl.CostEstimate(
            flops=0, bytes_accessed=6 * units * features, transcendentals=0
        ),
        name="load_weights",
    )(*[in_hbm(w) for w in (w_gate, w_up, w_down)])
    cores = [list(range(c, members, 2)) for c in range(2)]
    came = [exchange(copies[z], z * members) for z in range(1, groups)]
    column = pl.pallas_call(
        join_kernel,
        out_shape=pltpu.VMEM((groups, rows, LANES), jnp.bfloat16),
        in_specs=[VMEM] * groups,
        out_specs=VMEM,
        compiler_params=pltpu.CompilerParams(vmem_limit_bytes=1024 * 1024),
        name="join_rows",
    )(copies[0], *came)
    mine = lax.all_gather(column, "member", axis=0, tiled=True, axis_index_groups=cores)
    other = exchange(mine, 1)
    keep, give, both, acts = pl.pallas_call(
        functools.partial(partial_kernel, chunks),
        out_shape=(
            pltpu.VMEM((half, sent_rows, LANES), jnp.float32),
            pltpu.VMEM((half, sent_rows, LANES), jnp.bfloat16),
            pltpu.VMEM((count, 2 * features), jnp.bfloat16),
            pltpu.VMEM((3 * units, count), jnp.bfloat16),
        ),
        in_specs=[VMEM] * 3,
        out_specs=(VMEM,) * 4,
        scratch_shapes=[
            pltpu.VMEM((half * rows, LANES), jnp.float32),
            pltpu.VMEM((count * sent_rows, LANES), jnp.float32),
        ],
        compiler_params=pltpu.CompilerParams(vmem_limit_bytes=16 * 1024 * 1024),
        name="partial_rows",
    )(mine, other, loaded)
    got = exchange(give, 1)
    grad_shape = jax.ShapeDtypeStruct((1, units, features), jnp.bfloat16)
    grad_gate, grad_up, grad_down, done = pl.pallas_call(
        functools.partial(grads_kernel, features),
        out_shape=(grad_shape,) * 3 + (pltpu.VMEM((8, LANES), jnp.float32),),
        in_specs=[VMEM] * 2,
        out_specs=(HBM, HBM, HBM, VMEM),
        scratch_shapes=[
            pltpu.VMEM((3, units, features), jnp.bfloat16),
            pltpu.SemaphoreType.DMA((6,)),
        ],
        compiler_params=pltpu.CompilerParams(vmem_limit_bytes=16 * 1024 * 1024),
        cost_estimate=pl.CostEstimate(
            flops=6 * count * units * features,
            bytes_accessed=6 * units * features,
            transcendentals=0,
        ),
        name="weight_grads",
    )(both, acts)
    sent = pl.pallas_call(
        add_kernel,
        out_shape=pltpu.VMEM((half, sent_rows, LANES), jnp.bfloat16),
        in_specs=[VMEM] * 3,
        out_specs=VMEM,
        compiler_params=pltpu.CompilerParams(vmem_limit_bytes=4 * 1024 * 1024),
        name="add_cores",
    )(keep, got, done)
    summed = lax.psum_scatter(
        sent.reshape(members // 2, groups, sent_rows, LANES),
        "member",
        scatter_dimension=0,
        axis_index_groups=cores,
        tiled=False,
    )
    split = pl.pallas_call(
        split_kernel,
        out_shape=(pltpu.VMEM((sent_rows, LANES), jnp.bfloat16),) * groups,
        in_specs=[VMEM],
        out_specs=(VMEM,) * groups,
        compiler_params=pltpu.CompilerParams(vmem_limit_bytes=1024 * 1024),
        name="split_rows",
    )(summed)
    back = [split[0]] + [exchange(split[z], z * members) for z in range(1, groups)]
    grad_tokens = pl.pallas_call(
        functools.partial(sum_kernel, chunks),
        out_shape=jax.ShapeDtypeStruct((1, features), jnp.bfloat16),
        in_specs=[VMEM] * groups,
        out_specs=VMEM,
        scratch_shapes=[pltpu.VMEM((sent_rows, LANES), jnp.float32)],
        compiler_params=pltpu.CompilerParams(vmem_limit_bytes=1024 * 1024),
        name="sum_rows",
    )(*back)
    return grad_tokens, grad_gate, grad_up, grad_down


def slice_backward(rows_x, rows_scaled, gate_weight, up_weight, down_weight):
    gate_value = jnp.dot(rows_x, gate_weight.T, preferred_element_type=jnp.float32)
    up_value = jnp.dot(rows_x, up_weight.T, preferred_element_type=jnp.float32)
    sigma_gate = jax.nn.sigmoid(gate_value)
    active = gate_value * sigma_gate
    hidden = (active * up_value).astype(jnp.bfloat16)
    d_hidden = jnp.dot(rows_scaled, down_weight.T, preferred_element_type=jnp.float32)
    d_gate = (d_hidden * up_value * sigma_gate * (1.0 + gate_value * (1.0 - sigma_gate))).astype(
        jnp.bfloat16
    )
    d_up = (d_hidden * active).astype(jnp.bfloat16)
    grad_down = jnp.dot(hidden.T, rows_scaled, preferred_element_type=jnp.float32).astype(
        jnp.bfloat16
    )
    grad_gate = jnp.dot(d_gate.T, rows_x, preferred_element_type=jnp.float32).astype(jnp.bfloat16)
    grad_up = jnp.dot(d_up.T, rows_x, preferred_element_type=jnp.float32).astype(jnp.bfloat16)
    partial_rows = jnp.dot(d_gate, gate_weight, preferred_element_type=jnp.float32)
    partial_rows = partial_rows + jnp.dot(d_up, up_weight, preferred_element_type=jnp.float32)
    return (grad_gate, grad_up, grad_down, partial_rows)


def routed_shards(tokens, grad_out, route_token, route_count, route_prob, w_gate, w_up, w_down):
    groups = route_token.shape[1]
    capacity = route_token.shape[3]
    features = tokens.shape[1]
    block_rows = groups * capacity
    split_count = max(8, lax.axis_size("member") // 8)
    expert_local = lax.axis_index("member") // split_count
    slot_tokens = lax.dynamic_index_in_dim(route_token[0], expert_local, 1, keepdims=False)
    slot_counts = lax.dynamic_index_in_dim(route_count[0], expert_local, 1, keepdims=False)
    slot_probs = lax.dynamic_index_in_dim(route_prob[0], expert_local, 1, keepdims=False)
    slot_index = jnp.arange(capacity, dtype=jnp.int32)[None, :]
    live = (slot_index < slot_counts[:, None]).astype(jnp.float32)
    slot_weights = (slot_probs * live).reshape(-1)
    flat_slots = slot_tokens.reshape(-1)
    group_x, group_dy = (
        lax.all_gather(tokens, "member", axis=0, tiled=True),
        lax.all_gather(grad_out, "member", axis=0, tiled=True),
    )
    picked_x = jnp.take(group_x, flat_slots, axis=0)
    picked_dy = jnp.take(group_dy, flat_slots, axis=0)
    scaled = (slot_weights[:, None] * picked_dy.astype(jnp.float32)).astype(jnp.bfloat16)
    send_x = picked_x.reshape(groups, capacity, features)
    send_scaled = scaled.reshape(groups, capacity, features)
    rows_x, rows_scaled = (
        lax.all_to_all(send_x, "group", split_axis=0, concat_axis=0, tiled=True),
        lax.all_to_all(send_scaled, "group", split_axis=0, concat_axis=0, tiled=True),
    )
    grad_gate, grad_up, grad_down, partial_rows = slice_backward(
        rows_x.reshape(block_rows, features),
        rows_scaled.reshape(block_rows, features),
        w_gate[0],
        w_up[0],
        w_down[0],
    )
    returned = lax.all_to_all(
        partial_rows.reshape(groups, capacity, features),
        "group",
        split_axis=0,
        concat_axis=0,
        tiled=True,
    )
    returned = returned.reshape(block_rows, features)
    row_numbers = jnp.arange(tokens.shape[0] * lax.axis_size("member"), dtype=jnp.int32)
    selector = (row_numbers[:, None] == flat_slots[None, :]).astype(jnp.float32)
    summed = lax.psum_scatter(
        jnp.dot(
            selector, returned, precision=lax.Precision.HIGHEST, preferred_element_type=jnp.float32
        ),
        "member",
        scatter_dimension=0,
        tiled=True,
    )
    return (summed.astype(jnp.bfloat16), grad_gate[None], grad_up[None], grad_down[None])


def shards(tokens, grad_out, route_token, *rest):
    devices = lax.axis_size("group") * lax.axis_size("member")
    _, groups, experts, capacity = route_token.shape
    dense = devices * tokens.shape[0] <= groups * capacity and experts == 1
    paired = tokens.shape[0] == 1 and devices & (devices - 1) == 0
    body = dense_shards if dense and paired else routed_shards
    return body(tokens, grad_out, route_token, *rest)


def solution(mesh):
    placed = (
        P(("group", "member"), None),
        P(("group", "member"), None),
        P("group", None, None, None),
        P("group", None, None),
        P("group", None, None, None),
        P(("group", "member"), None, None),
        P(("group", "member"), None, None),
        P(("group", "member"), None, None),
    )
    return jax.shard_map(
        shards,
        mesh=mesh,
        in_specs=placed,
        out_specs=(
            P(("group", "member"), None),
            P(("group", "member"), None, None),
            P(("group", "member"), None, None),
            P(("group", "member"), None, None),
        ),
        check_vma=False,
    )
```

```python
import functools

import jax
import jax.numpy as jnp
from jax import lax
from jax.experimental import pallas as pl
from jax.experimental.pallas import tpu as pltpu
from jax.sharding import PartitionSpec as P

LANES = 128
PIECES = 8
PARTS = 4
AXES = ("group", "member")
VMEM = pl.BlockSpec(memory_space=pltpu.VMEM)
HBM = pl.BlockSpec(memory_space=pltpu.HBM)
SMEM = pl.BlockSpec(memory_space=pltpu.SMEM)
NT = (((1,), (1,)), ((), ()))
TN = (((0,), (0,)), ((), ()))


def round_up(value, step):
    return (value + step - 1) // step * step


def pack_kernel(
    chunks,
    tokens_hbm,
    grad_hbm,
    token_hbm,
    count_hbm,
    prob_hbm,
    out_ref,
    rows_ref,
    tokens_ref,
    grad_ref,
    token_ref,
    count_ref,
    prob_ref,
    sems,
):
    pairs = (
        (token_hbm, token_ref),
        (count_hbm, count_ref),
        (prob_hbm, prob_ref),
        (tokens_hbm, tokens_ref),
        (grad_hbm, grad_ref),
    )
    copies = [pltpu.make_async_copy(*pair, sems.at[n]) for n, pair in enumerate(pairs)]
    for copy in copies:
        copy.start()
    for copy in copies:
        copy.wait()
    me = lax.axis_index("member")
    groups, _, capacity = token_ref.shape[1:]
    token_row = tokens_ref[...].astype(jnp.float32)
    grad_row = grad_ref[...].astype(jnp.float32)
    for k in range(chunks):
        part = slice(k * LANES, (k + 1) * LANES)
        rows_ref[k : k + 1, :] = token_row[:, part]
        rows_ref[chunks + k : chunks + k + 1, :] = grad_row[:, part]
    rows = rows_ref[...]
    is_token = lax.broadcasted_iota(jnp.int32, rows.shape, 0) < chunks
    places = out_ref.shape[0] // groups
    for g in range(groups):
        weight = jnp.float32(0)
        for p in range(capacity):
            live = (token_ref[0, g, 0, p] == me) & (p < count_ref[0, 0, g])
            weight = weight + jnp.where(live, prob_ref[0, g, 0, p], 0.0)
        packed = jnp.where(is_token, rows, rows * weight).astype(jnp.bfloat16)
        for n in range(places):
            out_ref[g * places + n] = packed


def unpack_rows(chunks, packed_ref, wide_ref, rows_ref):
    tokens, rows, _ = packed_ref.shape
    wide_ref[...] = packed_ref[...].astype(jnp.float32).reshape(tokens * rows, LANES)
    for k in range(rows):
        column = wide_ref[pl.ds(k, tokens, stride=rows), :]
        rows_ref[:, k * LANES : (k + 1) * LANES] = column.astype(jnp.bfloat16)


def load_kernel(chunks, mine_ref, gate_ref, up_ref, down_ref, out_ref, rows_ref, wide_ref, sems):
    copies = []
    for n, source in enumerate((gate_ref, up_ref, down_ref)):
        height = source.shape[1] // PIECES
        for k in range(PIECES):
            part = pl.ds(k * height, height)
            copies.append(
                pltpu.make_async_copy(source.at[0, part], out_ref.at[n, part], sems.at[n * PIECES + k])
            )
    for copy in copies:
        copy.start()
    unpack_rows(chunks, mine_ref, wide_ref, rows_ref)
    for copy in copies:
        copy.wait()


def partial_kernel(
    chunks,
    mine_ref,
    other_ref,
    weights_ref,
    keep_ref,
    give_ref,
    rows_ref,
    acts_ref,
    wide_ref,
    spread_ref,
):
    count = mine_ref.shape[0]
    tokens = 2 * count
    features = chunks * LANES
    units = weights_ref.shape[1]
    rows_ref[:count] = mine_ref[...]
    unpack_rows(chunks, other_ref, wide_ref, rows_ref.at[pl.ds(count, count)])
    x, scaled = rows_ref[:, :features], rows_ref[:, features:]
    both = weights_ref[:2].reshape(2 * units, features)
    values = lax.dot_general(both, x, NT, preferred_element_type=jnp.float32)
    gate_value, up_value = values[:units], values[units:]
    d_hidden = lax.dot_general(weights_ref[2], scaled, NT, preferred_element_type=jnp.float32)
    sigma_gate = jax.nn.sigmoid(gate_value)
    active = gate_value * sigma_gate
    d_gate = d_hidden * up_value * sigma_gate * (1.0 + gate_value * (1.0 - sigma_gate))
    acts_ref[0:units] = d_gate.astype(jnp.bfloat16)
    acts_ref[units : 2 * units] = (d_hidden * active).astype(jnp.bfloat16)
    acts_ref[2 * units :] = (active * up_value).astype(jnp.bfloat16)
    partial = lax.dot_general(
        acts_ref[: 2 * units], both, TN, preferred_element_type=jnp.float32
    )
    sent_rows = keep_ref.shape[1]
    for k in range(chunks):
        spread_ref[pl.ds(k, tokens, stride=sent_rows), :] = partial[:, k * LANES : (k + 1) * LANES]
    for k in range(chunks, sent_rows):
        spread_ref[pl.ds(k, tokens, stride=sent_rows), :] = jnp.zeros((tokens, LANES), jnp.float32)
    half = count * sent_rows
    keep_ref[...] = spread_ref[:half, :].reshape(keep_ref.shape)
    give_ref[...] = spread_ref[half:, :].reshape(give_ref.shape).astype(jnp.bfloat16)


def grads_kernel(
    features, rows_ref, acts_ref, gate_out, up_out, down_out, done_ref, held_ref, sems
):
    units = held_ref.shape[1]
    height = units // PARTS
    copies = []
    for n, (out, first) in enumerate(((gate_out, 0), (up_out, 0), (down_out, features))):
        right = rows_ref[:, first : first + features]
        for k in range(PARTS):
            left = acts_ref[n * units + k * height : n * units + (k + 1) * height, :]
            held_ref[n, k * height : (k + 1) * height] = jnp.dot(
                left, right, preferred_element_type=jnp.float32
            ).astype(jnp.bfloat16)
            part = pl.ds(k * height, height)
            copies.append(
                pltpu.make_async_copy(held_ref.at[n, part], out.at[0, part], sems.at[PARTS * n + k])
            )
            copies[-1].start()
    done_ref[...] = jnp.zeros_like(done_ref)
    for copy in copies:
        copy.wait()


def add_kernel(keep_ref, got_ref, after_ref, sent_ref):
    del after_ref
    count, blocks, height, _ = sent_ref.shape
    for n in range(count):
        value = keep_ref[n] + got_ref[n].astype(jnp.float32)
        for k in range(blocks):
            sent_ref[n, k] = value[k * height : (k + 1) * height].astype(jnp.bfloat16)


def sum_kernel(back_ref, out_ref):
    count, blocks, height, _ = back_ref.shape
    for k in range(blocks):
        total = back_ref[0, k].astype(jnp.float32)
        for n in range(1, count):
            total = total + back_ref[n, k].astype(jnp.float32)
        for r in range(height):
            part = pl.ds((k * height + r) * LANES, LANES)
            out_ref[:, part] = total[r : r + 1, :].astype(jnp.bfloat16)


def exchange(value, distance):
    count = lax.axis_size("group") * lax.axis_size("member")
    return lax.ppermute(value, AXES, [(i, i ^ distance) for i in range(count)])


def in_hbm(value):
    return pltpu.with_memory_space_constraint(value, pltpu.HBM)


def dense_shards(tokens, grad_out, route_token, route_count, route_prob, w_gate, w_up, w_down):
    features = tokens.shape[1]
    units = w_gate.shape[1]
    chunks = features // LANES
    count = lax.axis_size("group") * lax.axis_size("member")
    half = count // 2
    rows = 2 * chunks
    sent_rows = round_up(chunks, 16)
    arguments = (tokens, grad_out, route_token, jnp.swapaxes(route_count, 1, 2), route_prob)
    spaces = (pltpu.VMEM, pltpu.VMEM, pltpu.SMEM, pltpu.SMEM, pltpu.SMEM)
    copies = pl.pallas_call(
        functools.partial(pack_kernel, chunks),
        out_shape=pltpu.VMEM((half, rows, LANES), jnp.bfloat16),
        in_specs=[HBM] * 5,
        out_specs=VMEM,
        scratch_shapes=[pltpu.VMEM((rows, LANES), jnp.float32)]
        + [space(value.shape, value.dtype) for space, value in zip(spaces, arguments)]
        + [pltpu.SemaphoreType.DMA((5,))],
        compiler_params=pltpu.CompilerParams(vmem_limit_bytes=4 * 1024 * 1024),
        name="pack_rows",
    )(*[in_hbm(value) for value in arguments])
    cores = [list(range(c, count, 2)) for c in range(2)]
    trade = functools.partial(
        lax.all_to_all,
        axis_name=AXES,
        split_axis=0,
        concat_axis=0,
        tiled=True,
        axis_index_groups=cores,
    )
    mine = trade(copies)
    other = exchange(mine, 1)
    wide = pltpu.VMEM((half * rows, LANES), jnp.float32)
    loaded, unpacked = pl.pallas_call(
        functools.partial(load_kernel, chunks),
        out_shape=(
            pltpu.VMEM((3, units, features), jnp.bfloat16),
            pltpu.VMEM((half, 2 * features), jnp.bfloat16),
        ),
        in_specs=[VMEM] + [HBM] * 3,
        out_specs=(VMEM,) * 2,
        scratch_shapes=[wide, pltpu.SemaphoreType.DMA((3 * PIECES,))],
        compiler_params=pltpu.CompilerParams(vmem_limit_bytes=8 * 1024 * 1024),
        cost_estimate=pl.CostEstimate(
            flops=0, bytes_accessed=6 * units * features, transcendentals=0
        ),
        name="load_weights",
    )(mine, *[in_hbm(w) for w in (w_gate, w_up, w_down)])
    keep, give, both, acts = pl.pallas_call(
        functools.partial(partial_kernel, chunks),
        out_shape=(
            pltpu.VMEM((half, sent_rows, LANES), jnp.float32),
            pltpu.VMEM((half, sent_rows, LANES), jnp.bfloat16),
            pltpu.VMEM((count, 2 * features), jnp.bfloat16),
            pltpu.VMEM((3 * units, count), jnp.bfloat16),
        ),
        in_specs=[VMEM] * 3,
        out_specs=(VMEM,) * 4,
        scratch_shapes=[wide, pltpu.VMEM((count * sent_rows, LANES), jnp.float32)],
        compiler_params=pltpu.CompilerParams(vmem_limit_bytes=16 * 1024 * 1024),
        name="partial_rows",
    )(unpacked, other, loaded)
    got = exchange(give, 1)
    grad_shape = jax.ShapeDtypeStruct((1, units, features), jnp.bfloat16)
    grad_gate, grad_up, grad_down, done = pl.pallas_call(
        functools.partial(grads_kernel, features),
        out_shape=(grad_shape,) * 3 + (pltpu.VMEM((8, LANES), jnp.float32),),
        in_specs=[VMEM] * 2,
        out_specs=(HBM, HBM, HBM, VMEM),
        scratch_shapes=[
            pltpu.VMEM((3, units, features), jnp.bfloat16),
            pltpu.SemaphoreType.DMA((3 * PARTS,)),
        ],
        compiler_params=pltpu.CompilerParams(vmem_limit_bytes=16 * 1024 * 1024),
        cost_estimate=pl.CostEstimate(
            flops=6 * count * units * features,
            bytes_accessed=6 * units * features,
            transcendentals=0,
        ),
        name="weight_grads",
    )(both, acts)
    sent = pl.pallas_call(
        add_kernel,
        out_shape=pltpu.VMEM((half, chunks // 4, 4, LANES), jnp.bfloat16),
        in_specs=[VMEM] * 3,
        out_specs=VMEM,
        compiler_params=pltpu.CompilerParams(vmem_limit_bytes=4 * 1024 * 1024),
        name="add_cores",
    )(keep, got, done)
    back = trade(sent)
    grad_tokens = pl.pallas_call(
        sum_kernel,
        out_shape=jax.ShapeDtypeStruct((1, features), jnp.bfloat16),
        in_specs=[VMEM],
        out_specs=VMEM,
        compiler_params=pltpu.CompilerParams(vmem_limit_bytes=4 * 1024 * 1024),
        name="sum_rows",
    )(back)
    return grad_tokens, grad_gate, grad_up, grad_down


def slice_backward(rows_x, rows_scaled, gate_weight, up_weight, down_weight):
    gate_value = jnp.dot(rows_x, gate_weight.T, preferred_element_type=jnp.float32)
    up_value = jnp.dot(rows_x, up_weight.T, preferred_element_type=jnp.float32)
    sigma_gate = jax.nn.sigmoid(gate_value)
    active = gate_value * sigma_gate
    hidden = (active * up_value).astype(jnp.bfloat16)
    d_hidden = jnp.dot(rows_scaled, down_weight.T, preferred_element_type=jnp.float32)
    d_gate = (d_hidden * up_value * sigma_gate * (1.0 + gate_value * (1.0 - sigma_gate))).astype(
        jnp.bfloat16
    )
    d_up = (d_hidden * active).astype(jnp.bfloat16)
    grad_down = jnp.dot(hidden.T, rows_scaled, preferred_element_type=jnp.float32).astype(
        jnp.bfloat16
    )
    grad_gate = jnp.dot(d_gate.T, rows_x, preferred_element_type=jnp.float32).astype(jnp.bfloat16)
    grad_up = jnp.dot(d_up.T, rows_x, preferred_element_type=jnp.float32).astype(jnp.bfloat16)
    partial_rows = jnp.dot(d_gate, gate_weight, preferred_element_type=jnp.float32)
    partial_rows = partial_rows + jnp.dot(d_up, up_weight, preferred_element_type=jnp.float32)
    return (grad_gate, grad_up, grad_down, partial_rows)


def routed_shards(tokens, grad_out, route_token, route_count, route_prob, w_gate, w_up, w_down):
    groups = route_token.shape[1]
    capacity = route_token.shape[3]
    features = tokens.shape[1]
    block_rows = groups * capacity
    split_count = max(8, lax.axis_size("member") // 8)
    expert_local = lax.axis_index("member") // split_count
    slot_tokens = lax.dynamic_index_in_dim(route_token[0], expert_local, 1, keepdims=False)
    slot_counts = lax.dynamic_index_in_dim(route_count[0], expert_local, 1, keepdims=False)
    slot_probs = lax.dynamic_index_in_dim(route_prob[0], expert_local, 1, keepdims=False)
    slot_index = jnp.arange(capacity, dtype=jnp.int32)[None, :]
    live = (slot_index < slot_counts[:, None]).astype(jnp.float32)
    slot_weights = (slot_probs * live).reshape(-1)
    flat_slots = slot_tokens.reshape(-1)
    group_x, group_dy = (
        lax.all_gather(tokens, "member", axis=0, tiled=True),
        lax.all_gather(grad_out, "member", axis=0, tiled=True),
    )
    picked_x = jnp.take(group_x, flat_slots, axis=0)
    picked_dy = jnp.take(group_dy, flat_slots, axis=0)
    scaled = (slot_weights[:, None] * picked_dy.astype(jnp.float32)).astype(jnp.bfloat16)
    send_x = picked_x.reshape(groups, capacity, features)
    send_scaled = scaled.reshape(groups, capacity, features)
    rows_x, rows_scaled = (
        lax.all_to_all(send_x, "group", split_axis=0, concat_axis=0, tiled=True),
        lax.all_to_all(send_scaled, "group", split_axis=0, concat_axis=0, tiled=True),
    )
    grad_gate, grad_up, grad_down, partial_rows = slice_backward(
        rows_x.reshape(block_rows, features),
        rows_scaled.reshape(block_rows, features),
        w_gate[0],
        w_up[0],
        w_down[0],
    )
    returned = lax.all_to_all(
        partial_rows.reshape(groups, capacity, features),
        "group",
        split_axis=0,
        concat_axis=0,
        tiled=True,
    )
    returned = returned.reshape(block_rows, features)
    row_numbers = jnp.arange(tokens.shape[0] * lax.axis_size("member"), dtype=jnp.int32)
    selector = (row_numbers[:, None] == flat_slots[None, :]).astype(jnp.float32)
    summed = lax.psum_scatter(
        jnp.dot(
            selector, returned, precision=lax.Precision.HIGHEST, preferred_element_type=jnp.float32
        ),
        "member",
        scatter_dimension=0,
        tiled=True,
    )
    return (summed.astype(jnp.bfloat16), grad_gate[None], grad_up[None], grad_down[None])


def shards(tokens, grad_out, route_token, *rest):
    devices = lax.axis_size("group") * lax.axis_size("member")
    _, groups, experts, capacity = route_token.shape
    dense = devices * tokens.shape[0] <= groups * capacity and experts == 1
    paired = tokens.shape[0] == 1 and devices & (devices - 1) == 0
    body = dense_shards if dense and paired else routed_shards
    return body(tokens, grad_out, route_token, *rest)


def solution(mesh):
    placed = (
        P(("group", "member"), None),
        P(("group", "member"), None),
        P("group", None, None, None),
        P("group", None, None),
        P("group", None, None, None),
        P(("group", "member"), None, None),
        P(("group", "member"), None, None),
        P(("group", "member"), None, None),
    )
    return jax.shard_map(
        shards,
        mesh=mesh,
        in_specs=placed,
        out_specs=(
            P(("group", "member"), None),
            P(("group", "member"), None, None),
            P(("group", "member"), None, None),
            P(("group", "member"), None, None),
        ),
        check_vma=False,
    )
```

```python
import functools

import jax
import jax.numpy as jnp
from jax import lax
from jax.experimental import pallas as pl
from jax.experimental.pallas import tpu as pltpu
from jax.sharding import PartitionSpec as P

LANES = 128
PARTS = 4
AXES = ("group", "member")
VMEM = pl.BlockSpec(memory_space=pltpu.VMEM)
HBM = pl.BlockSpec(memory_space=pltpu.HBM)
SMEM = pl.BlockSpec(memory_space=pltpu.SMEM)
NT = (((1,), (1,)), ((), ()))
TN = (((0,), (0,)), ((), ()))


def round_up(value, step):
    return (value + step - 1) // step * step


def pack_kernel(
    chunks,
    tokens_hbm,
    grad_hbm,
    token_hbm,
    count_hbm,
    prob_hbm,
    out_ref,
    rows_ref,
    tokens_ref,
    grad_ref,
    token_ref,
    count_ref,
    prob_ref,
    sems,
):
    pairs = (
        (token_hbm, token_ref),
        (count_hbm, count_ref),
        (prob_hbm, prob_ref),
        (tokens_hbm, tokens_ref),
        (grad_hbm, grad_ref),
    )
    copies = [pltpu.make_async_copy(*pair, sems.at[n]) for n, pair in enumerate(pairs)]
    for copy in copies:
        copy.start()
    for copy in copies:
        copy.wait()
    me = lax.axis_index("member")
    groups, _, capacity = token_ref.shape[1:]
    token_row = tokens_ref[...].astype(jnp.float32)
    grad_row = grad_ref[...].astype(jnp.float32)
    for k in range(chunks):
        part = slice(k * LANES, (k + 1) * LANES)
        rows_ref[k : k + 1, :] = token_row[:, part]
        rows_ref[chunks + k : chunks + k + 1, :] = grad_row[:, part]
    rows = rows_ref[...]
    is_token = lax.broadcasted_iota(jnp.int32, rows.shape, 0) < chunks
    places = out_ref.shape[0] // groups
    for g in range(groups):
        weight = jnp.float32(0)
        for p in range(capacity):
            live = (token_ref[0, g, 0, p] == me) & (p < count_ref[0, 0, g])
            weight = weight + jnp.where(live, prob_ref[0, g, 0, p], 0.0)
        packed = jnp.where(is_token, rows, rows * weight).astype(jnp.bfloat16)
        for n in range(places):
            out_ref[g * places + n] = packed


def unpack_rows(chunks, packed_ref, wide_ref, rows_ref):
    tokens, rows, _ = packed_ref.shape
    wide_ref[...] = packed_ref[...].astype(jnp.float32).reshape(tokens * rows, LANES)
    for k in range(rows):
        column = wide_ref[pl.ds(k, tokens, stride=rows), :]
        rows_ref[:, k * LANES : (k + 1) * LANES] = column.astype(jnp.bfloat16)


def unpack_kernel(chunks, mine_ref, rows_ref, wide_ref):
    unpack_rows(chunks, mine_ref, wide_ref, rows_ref)


def partial_kernel(
    chunks,
    mine_ref,
    other_ref,
    gate_ref,
    up_ref,
    down_ref,
    keep_ref,
    give_ref,
    rows_ref,
    acts_ref,
    wide_ref,
    spread_ref,
):
    count = mine_ref.shape[0]
    tokens = 2 * count
    features = chunks * LANES
    units = gate_ref.shape[1]
    rows_ref[:count] = mine_ref[...]
    unpack_rows(chunks, other_ref, wide_ref, rows_ref.at[pl.ds(count, count)])
    x, scaled = rows_ref[:, :features], rows_ref[:, features:]
    gate_value = lax.dot_general(gate_ref[0], x, NT, preferred_element_type=jnp.float32)
    up_value = lax.dot_general(up_ref[0], x, NT, preferred_element_type=jnp.float32)
    d_hidden = lax.dot_general(down_ref[0], scaled, NT, preferred_element_type=jnp.float32)
    sigma_gate = jax.nn.sigmoid(gate_value)
    active = gate_value * sigma_gate
    d_gate = d_hidden * up_value * sigma_gate * (1.0 + gate_value * (1.0 - sigma_gate))
    acts_ref[0:units] = d_gate.astype(jnp.bfloat16)
    acts_ref[units : 2 * units] = (d_hidden * active).astype(jnp.bfloat16)
    acts_ref[2 * units :] = (active * up_value).astype(jnp.bfloat16)
    partial = lax.dot_general(
        acts_ref[:units], gate_ref[0], TN, preferred_element_type=jnp.float32
    ) + lax.dot_general(
        acts_ref[units : 2 * units], up_ref[0], TN, preferred_element_type=jnp.float32
    )
    sent_rows = keep_ref.shape[1]
    for k in range(chunks):
        spread_ref[pl.ds(k, tokens, stride=sent_rows), :] = partial[:, k * LANES : (k + 1) * LANES]
    for k in range(chunks, sent_rows):
        spread_ref[pl.ds(k, tokens, stride=sent_rows), :] = jnp.zeros((tokens, LANES), jnp.float32)
    half = count * sent_rows
    keep_ref[...] = spread_ref[:half, :].reshape(keep_ref.shape)
    give_ref[...] = spread_ref[half:, :].reshape(give_ref.shape).astype(jnp.bfloat16)


def grads_kernel(
    features, rows_ref, acts_ref, gate_out, up_out, down_out, done_ref, held_ref, sems
):
    units = held_ref.shape[1]
    height = units // PARTS
    copies = []
    for n, (out, first) in enumerate(((gate_out, 0), (up_out, 0), (down_out, features))):
        right = rows_ref[:, first : first + features]
        for k in range(PARTS):
            left = acts_ref[n * units + k * height : n * units + (k + 1) * height, :]
            held_ref[n, k * height : (k + 1) * height] = jnp.dot(
                left, right, preferred_element_type=jnp.float32
            ).astype(jnp.bfloat16)
            part = pl.ds(k * height, height)
            copies.append(
                pltpu.make_async_copy(held_ref.at[n, part], out.at[0, part], sems.at[PARTS * n + k])
            )
            copies[-1].start()
    done_ref[...] = jnp.zeros_like(done_ref)
    for copy in copies:
        copy.wait()


def add_kernel(keep_ref, got_ref, after_ref, sent_ref):
    del after_ref
    count, blocks, height, _ = sent_ref.shape
    for n in range(count):
        value = keep_ref[n] + got_ref[n].astype(jnp.float32)
        for k in range(blocks):
            sent_ref[n, k] = value[k * height : (k + 1) * height].astype(jnp.bfloat16)


def sum_kernel(back_ref, out_ref):
    count, blocks, height, _ = back_ref.shape
    for k in range(blocks):
        total = back_ref[0, k].astype(jnp.float32)
        for n in range(1, count):
            total = total + back_ref[n, k].astype(jnp.float32)
        for r in range(height):
            part = pl.ds((k * height + r) * LANES, LANES)
            out_ref[:, part] = total[r : r + 1, :].astype(jnp.bfloat16)


def exchange(value, distance):
    count = lax.axis_size("group") * lax.axis_size("member")
    return lax.ppermute(value, AXES, [(i, i ^ distance) for i in range(count)])


def in_hbm(value):
    return pltpu.with_memory_space_constraint(value, pltpu.HBM)


def dense_shards(tokens, grad_out, route_token, route_count, route_prob, w_gate, w_up, w_down):
    features = tokens.shape[1]
    units = w_gate.shape[1]
    chunks = features // LANES
    count = lax.axis_size("group") * lax.axis_size("member")
    half = count // 2
    rows = 2 * chunks
    sent_rows = round_up(chunks, 16)
    loaded = [exchange(w, 0) for w in (w_gate, w_up, w_down)]
    arguments = (tokens, grad_out, route_token, jnp.swapaxes(route_count, 1, 2), route_prob)
    spaces = (pltpu.VMEM, pltpu.VMEM, pltpu.SMEM, pltpu.SMEM, pltpu.SMEM)
    copies = pl.pallas_call(
        functools.partial(pack_kernel, chunks),
        out_shape=pltpu.VMEM((half, rows, LANES), jnp.bfloat16),
        in_specs=[HBM] * 5,
        out_specs=VMEM,
        scratch_shapes=[pltpu.VMEM((rows, LANES), jnp.float32)]
        + [space(value.shape, value.dtype) for space, value in zip(spaces, arguments)]
        + [pltpu.SemaphoreType.DMA((5,))],
        compiler_params=pltpu.CompilerParams(vmem_limit_bytes=4 * 1024 * 1024),
        name="pack_rows",
    )(*[in_hbm(value) for value in arguments])
    cores = [list(range(c, count, 2)) for c in range(2)]
    trade = functools.partial(
        lax.all_to_all,
        axis_name=AXES,
        split_axis=0,
        concat_axis=0,
        tiled=True,
        axis_index_groups=cores,
    )
    mine = trade(copies)
    other = exchange(mine, 1)
    wide = pltpu.VMEM((half * rows, LANES), jnp.float32)
    unpacked = pl.pallas_call(
        functools.partial(unpack_kernel, chunks),
        out_shape=pltpu.VMEM((half, 2 * features), jnp.bfloat16),
        in_specs=[VMEM],
        out_specs=VMEM,
        scratch_shapes=[wide],
        compiler_params=pltpu.CompilerParams(vmem_limit_bytes=2 * 1024 * 1024),
        name="unpack_rows",
    )(mine)
    keep, give, both, acts = pl.pallas_call(
        functools.partial(partial_kernel, chunks),
        out_shape=(
            pltpu.VMEM((half, sent_rows, LANES), jnp.float32),
            pltpu.VMEM((half, sent_rows, LANES), jnp.bfloat16),
            pltpu.VMEM((count, 2 * features), jnp.bfloat16),
            pltpu.VMEM((3 * units, count), jnp.bfloat16),
        ),
        in_specs=[VMEM] * 5,
        out_specs=(VMEM,) * 4,
        scratch_shapes=[wide, pltpu.VMEM((count * sent_rows, LANES), jnp.float32)],
        compiler_params=pltpu.CompilerParams(vmem_limit_bytes=16 * 1024 * 1024),
        name="partial_rows",
    )(unpacked, other, *loaded)
    got = exchange(give, 1)
    grad_shape = jax.ShapeDtypeStruct((1, units, features), jnp.bfloat16)
    grad_gate, grad_up, grad_down, done = pl.pallas_call(
        functools.partial(grads_kernel, features),
        out_shape=(grad_shape,) * 3 + (pltpu.VMEM((8, LANES), jnp.float32),),
        in_specs=[VMEM] * 2,
        out_specs=(HBM, HBM, HBM, VMEM),
        scratch_shapes=[
            pltpu.VMEM((3, units, features), jnp.bfloat16),
            pltpu.SemaphoreType.DMA((3 * PARTS,)),
        ],
        compiler_params=pltpu.CompilerParams(vmem_limit_bytes=16 * 1024 * 1024),
        cost_estimate=pl.CostEstimate(
            flops=6 * count * units * features,
            bytes_accessed=6 * units * features,
            transcendentals=0,
        ),
        name="weight_grads",
    )(both, acts)
    sent = pl.pallas_call(
        add_kernel,
        out_shape=pltpu.VMEM((half, chunks // 4, 4, LANES), jnp.bfloat16),
        in_specs=[VMEM] * 3,
        out_specs=VMEM,
        compiler_params=pltpu.CompilerParams(vmem_limit_bytes=4 * 1024 * 1024),
        name="add_cores",
    )(keep, got, done)
    back = trade(sent)
    grad_tokens = pl.pallas_call(
        sum_kernel,
        out_shape=jax.ShapeDtypeStruct((1, features), jnp.bfloat16),
        in_specs=[VMEM],
        out_specs=VMEM,
        compiler_params=pltpu.CompilerParams(vmem_limit_bytes=4 * 1024 * 1024),
        name="sum_rows",
    )(back)
    return grad_tokens, grad_gate, grad_up, grad_down


def slice_backward(rows_x, rows_scaled, gate_weight, up_weight, down_weight):
    gate_value = jnp.dot(rows_x, gate_weight.T, preferred_element_type=jnp.float32)
    up_value = jnp.dot(rows_x, up_weight.T, preferred_element_type=jnp.float32)
    sigma_gate = jax.nn.sigmoid(gate_value)
    active = gate_value * sigma_gate
    hidden = (active * up_value).astype(jnp.bfloat16)
    d_hidden = jnp.dot(rows_scaled, down_weight.T, preferred_element_type=jnp.float32)
    d_gate = (d_hidden * up_value * sigma_gate * (1.0 + gate_value * (1.0 - sigma_gate))).astype(
        jnp.bfloat16
    )
    d_up = (d_hidden * active).astype(jnp.bfloat16)
    grad_down = jnp.dot(hidden.T, rows_scaled, preferred_element_type=jnp.float32).astype(
        jnp.bfloat16
    )
    grad_gate = jnp.dot(d_gate.T, rows_x, preferred_element_type=jnp.float32).astype(jnp.bfloat16)
    grad_up = jnp.dot(d_up.T, rows_x, preferred_element_type=jnp.float32).astype(jnp.bfloat16)
    partial_rows = jnp.dot(d_gate, gate_weight, preferred_element_type=jnp.float32)
    partial_rows = partial_rows + jnp.dot(d_up, up_weight, preferred_element_type=jnp.float32)
    return (grad_gate, grad_up, grad_down, partial_rows)


def routed_shards(tokens, grad_out, route_token, route_count, route_prob, w_gate, w_up, w_down):
    groups = route_token.shape[1]
    capacity = route_token.shape[3]
    features = tokens.shape[1]
    block_rows = groups * capacity
    split_count = max(8, lax.axis_size("member") // 8)
    expert_local = lax.axis_index("member") // split_count
    slot_tokens = lax.dynamic_index_in_dim(route_token[0], expert_local, 1, keepdims=False)
    slot_counts = lax.dynamic_index_in_dim(route_count[0], expert_local, 1, keepdims=False)
    slot_probs = lax.dynamic_index_in_dim(route_prob[0], expert_local, 1, keepdims=False)
    slot_index = jnp.arange(capacity, dtype=jnp.int32)[None, :]
    live = (slot_index < slot_counts[:, None]).astype(jnp.float32)
    slot_weights = (slot_probs * live).reshape(-1)
    flat_slots = slot_tokens.reshape(-1)
    group_x, group_dy = (
        lax.all_gather(tokens, "member", axis=0, tiled=True),
        lax.all_gather(grad_out, "member", axis=0, tiled=True),
    )
    picked_x = jnp.take(group_x, flat_slots, axis=0)
    picked_dy = jnp.take(group_dy, flat_slots, axis=0)
    scaled = (slot_weights[:, None] * picked_dy.astype(jnp.float32)).astype(jnp.bfloat16)
    send_x = picked_x.reshape(groups, capacity, features)
    send_scaled = scaled.reshape(groups, capacity, features)
    rows_x, rows_scaled = (
        lax.all_to_all(send_x, "group", split_axis=0, concat_axis=0, tiled=True),
        lax.all_to_all(send_scaled, "group", split_axis=0, concat_axis=0, tiled=True),
    )
    grad_gate, grad_up, grad_down, partial_rows = slice_backward(
        rows_x.reshape(block_rows, features),
        rows_scaled.reshape(block_rows, features),
        w_gate[0],
        w_up[0],
        w_down[0],
    )
    returned = lax.all_to_all(
        partial_rows.reshape(groups, capacity, features),
        "group",
        split_axis=0,
        concat_axis=0,
        tiled=True,
    )
    returned = returned.reshape(block_rows, features)
    row_numbers = jnp.arange(tokens.shape[0] * lax.axis_size("member"), dtype=jnp.int32)
    selector = (row_numbers[:, None] == flat_slots[None, :]).astype(jnp.float32)
    summed = lax.psum_scatter(
        jnp.dot(
            selector, returned, precision=lax.Precision.HIGHEST, preferred_element_type=jnp.float32
        ),
        "member",
        scatter_dimension=0,
        tiled=True,
    )
    return (summed.astype(jnp.bfloat16), grad_gate[None], grad_up[None], grad_down[None])


def shards(tokens, grad_out, route_token, *rest):
    devices = lax.axis_size("group") * lax.axis_size("member")
    _, groups, experts, capacity = route_token.shape
    dense = devices * tokens.shape[0] <= groups * capacity and experts == 1
    paired = tokens.shape[0] == 1 and devices & (devices - 1) == 0
    body = dense_shards if dense and paired else routed_shards
    return body(tokens, grad_out, route_token, *rest)


def solution(mesh):
    placed = (
        P(("group", "member"), None),
        P(("group", "member"), None),
        P("group", None, None, None),
        P("group", None, None),
        P("group", None, None, None),
        P(("group", "member"), None, None),
        P(("group", "member"), None, None),
        P(("group", "member"), None, None),
    )
    return jax.shard_map(
        shards,
        mesh=mesh,
        in_specs=placed,
        out_specs=(
            P(("group", "member"), None),
            P(("group", "member"), None, None),
            P(("group", "member"), None, None),
            P(("group", "member"), None, None),
        ),
        check_vma=False,
    )
```

```python
import functools

import jax
import jax.numpy as jnp
from jax import lax
from jax.experimental import pallas as pl
from jax.experimental.pallas import tpu as pltpu
from jax.sharding import PartitionSpec as P

LANES = 128
PARTS = 4
AXES = ("group", "member")
VMEM = pl.BlockSpec(memory_space=pltpu.VMEM)
HBM = pl.BlockSpec(memory_space=pltpu.HBM)
SMEM = pl.BlockSpec(memory_space=pltpu.SMEM)
NT = (((1,), (1,)), ((), ()))
TN = (((0,), (0,)), ((), ()))


def round_up(value, step):
    return (value + step - 1) // step * step


def pack_kernel(
    chunks,
    tokens_hbm,
    grad_hbm,
    token_hbm,
    count_hbm,
    prob_hbm,
    out_ref,
    rows_ref,
    tokens_ref,
    grad_ref,
    token_ref,
    count_ref,
    prob_ref,
    sems,
):
    pairs = (
        (token_hbm, token_ref),
        (count_hbm, count_ref),
        (prob_hbm, prob_ref),
        (tokens_hbm, tokens_ref),
        (grad_hbm, grad_ref),
    )
    copies = [pltpu.make_async_copy(*pair, sems.at[n]) for n, pair in enumerate(pairs)]
    for copy in copies:
        copy.start()
    for copy in copies:
        copy.wait()
    me = lax.axis_index("member")
    groups, _, capacity = token_ref.shape[1:]
    token_row = tokens_ref[...].astype(jnp.float32)
    grad_row = grad_ref[...].astype(jnp.float32)
    for k in range(chunks):
        part = slice(k * LANES, (k + 1) * LANES)
        rows_ref[k : k + 1, :] = token_row[:, part]
        rows_ref[chunks + k : chunks + k + 1, :] = grad_row[:, part]
    rows = rows_ref[...]
    is_token = lax.broadcasted_iota(jnp.int32, rows.shape, 0) < chunks
    places = out_ref.shape[0] // groups
    for g in range(groups):
        weight = jnp.float32(0)
        for p in range(capacity):
            live = (token_ref[0, g, 0, p] == me) & (p < count_ref[0, 0, g])
            weight = weight + jnp.where(live, prob_ref[0, g, 0, p], 0.0)
        packed = jnp.where(is_token, rows, rows * weight).astype(jnp.bfloat16)
        for n in range(places):
            out_ref[g * places + n] = packed


def unpack_rows(chunks, packed_ref, wide_ref, rows_ref):
    tokens, rows, _ = packed_ref.shape
    wide_ref[...] = packed_ref[...].astype(jnp.float32).reshape(tokens * rows, LANES)
    for k in range(rows):
        column = wide_ref[pl.ds(k, tokens, stride=rows), :]
        rows_ref[:, k * LANES : (k + 1) * LANES] = column.astype(jnp.bfloat16)


def unpack_kernel(chunks, mine_ref, rows_ref, wide_ref):
    unpack_rows(chunks, mine_ref, wide_ref, rows_ref)


def partial_kernel(
    chunks,
    mine_ref,
    other_ref,
    gate_ref,
    up_ref,
    down_ref,
    keep_ref,
    give_ref,
    rows_ref,
    acts_ref,
    wide_ref,
    spread_ref,
):
    count = mine_ref.shape[0]
    tokens = 2 * count
    features = chunks * LANES
    units = gate_ref.shape[1]
    rows_ref[:count] = mine_ref[...]
    unpack_rows(chunks, other_ref, wide_ref, rows_ref.at[pl.ds(count, count)])
    x, scaled = rows_ref[:, :features], rows_ref[:, features:]
    gate_value = lax.dot_general(gate_ref[0], x, NT, preferred_element_type=jnp.float32)
    up_value = lax.dot_general(up_ref[0], x, NT, preferred_element_type=jnp.float32)
    d_hidden = lax.dot_general(down_ref[0], scaled, NT, preferred_element_type=jnp.float32)
    sigma_gate = jax.nn.sigmoid(gate_value)
    active = gate_value * sigma_gate
    d_gate = d_hidden * up_value * sigma_gate * (1.0 + gate_value * (1.0 - sigma_gate))
    acts_ref[0:units] = d_gate.astype(jnp.bfloat16)
    acts_ref[units : 2 * units] = (d_hidden * active).astype(jnp.bfloat16)
    acts_ref[2 * units :] = (active * up_value).astype(jnp.bfloat16)
    partial = lax.dot_general(
        acts_ref[:units], gate_ref[0], TN, preferred_element_type=jnp.float32
    ) + lax.dot_general(
        acts_ref[units : 2 * units], up_ref[0], TN, preferred_element_type=jnp.float32
    )
    sent_rows = keep_ref.shape[1]
    for k in range(chunks):
        spread_ref[pl.ds(k, tokens, stride=sent_rows), :] = partial[:, k * LANES : (k + 1) * LANES]
    for k in range(chunks, sent_rows):
        spread_ref[pl.ds(k, tokens, stride=sent_rows), :] = jnp.zeros((tokens, LANES), jnp.float32)
    half = count * sent_rows
    keep_ref[...] = spread_ref[:half, :].reshape(keep_ref.shape)
    give_ref[...] = spread_ref[half:, :].reshape(give_ref.shape).astype(jnp.bfloat16)


def grads_kernel(
    features, rows_ref, acts_ref, gate_out, up_out, down_out, done_ref, held_ref, sems
):
    units = held_ref.shape[1]
    height = units // PARTS
    copies = []
    for n, (out, first) in enumerate(((gate_out, 0), (up_out, 0), (down_out, features))):
        right = rows_ref[:, first : first + features]
        for k in range(PARTS):
            left = acts_ref[n * units + k * height : n * units + (k + 1) * height, :]
            held_ref[n, k * height : (k + 1) * height] = jnp.dot(
                left, right, preferred_element_type=jnp.float32
            ).astype(jnp.bfloat16)
            part = pl.ds(k * height, height)
            copies.append(
                pltpu.make_async_copy(held_ref.at[n, part], out.at[0, part], sems.at[PARTS * n + k])
            )
            copies[-1].start()
    done_ref[...] = jnp.zeros_like(done_ref)
    for copy in copies:
        copy.wait()


def add_kernel(keep_ref, got_ref, after_ref, sent_ref):
    del after_ref
    count, blocks, height, _ = sent_ref.shape
    for n in range(count):
        value = keep_ref[n] + got_ref[n].astype(jnp.float32)
        for k in range(blocks):
            sent_ref[n, k] = value[k * height : (k + 1) * height].astype(jnp.bfloat16)


def sum_kernel(back_ref, out_ref):
    count, blocks, height, _ = back_ref.shape
    for k in range(blocks):
        total = back_ref[0, k].astype(jnp.float32)
        for n in range(1, count):
            total = total + back_ref[n, k].astype(jnp.float32)
        for r in range(height):
            part = pl.ds((k * height + r) * LANES, LANES)
            out_ref[:, part] = total[r : r + 1, :].astype(jnp.bfloat16)


def exchange(value, distance):
    count = lax.axis_size("group") * lax.axis_size("member")
    return lax.ppermute(value, AXES, [(i, i ^ distance) for i in range(count)])


def in_hbm(value):
    return pltpu.with_memory_space_constraint(value, pltpu.HBM)


def dense_shards(tokens, grad_out, route_token, route_count, route_prob, w_gate, w_up, w_down):
    features = tokens.shape[1]
    units = w_gate.shape[1]
    chunks = features // LANES
    count = lax.axis_size("group") * lax.axis_size("member")
    half = count // 2
    rows = 2 * chunks
    sent_rows = round_up(chunks, 16)
    arguments = (tokens, grad_out, route_token, jnp.swapaxes(route_count, 1, 2), route_prob)
    spaces = (pltpu.VMEM, pltpu.VMEM, pltpu.SMEM, pltpu.SMEM, pltpu.SMEM)
    copies = pl.pallas_call(
        functools.partial(pack_kernel, chunks),
        out_shape=pltpu.VMEM((half, rows, LANES), jnp.bfloat16),
        in_specs=[HBM] * 5,
        out_specs=VMEM,
        scratch_shapes=[pltpu.VMEM((rows, LANES), jnp.float32)]
        + [space(value.shape, value.dtype) for space, value in zip(spaces, arguments)]
        + [pltpu.SemaphoreType.DMA((5,))],
        compiler_params=pltpu.CompilerParams(vmem_limit_bytes=4 * 1024 * 1024),
        cost_estimate=pl.CostEstimate(
            flops=40000 * units * features,
            bytes_accessed=16 * units * features,
            transcendentals=0,
        ),
        name="pack_rows",
    )(*[in_hbm(value) for value in arguments])
    cores = [list(range(c, count, 2)) for c in range(2)]
    trade = functools.partial(
        lax.all_to_all,
        axis_name=AXES,
        split_axis=0,
        concat_axis=0,
        tiled=True,
        axis_index_groups=cores,
    )
    mine = trade(copies)
    other = exchange(mine, 1)
    wide = pltpu.VMEM((half * rows, LANES), jnp.float32)
    unpacked = pl.pallas_call(
        functools.partial(unpack_kernel, chunks),
        out_shape=pltpu.VMEM((half, 2 * features), jnp.bfloat16),
        in_specs=[VMEM],
        out_specs=VMEM,
        scratch_shapes=[wide],
        compiler_params=pltpu.CompilerParams(vmem_limit_bytes=2 * 1024 * 1024),
        name="unpack_rows",
    )(mine)
    keep, give, both, acts = pl.pallas_call(
        functools.partial(partial_kernel, chunks),
        out_shape=(
            pltpu.VMEM((half, sent_rows, LANES), jnp.float32),
            pltpu.VMEM((half, sent_rows, LANES), jnp.bfloat16),
            pltpu.VMEM((count, 2 * features), jnp.bfloat16),
            pltpu.VMEM((3 * units, count), jnp.bfloat16),
        ),
        in_specs=[VMEM] * 5,
        out_specs=(VMEM,) * 4,
        scratch_shapes=[wide, pltpu.VMEM((count * sent_rows, LANES), jnp.float32)],
        compiler_params=pltpu.CompilerParams(vmem_limit_bytes=16 * 1024 * 1024),
        name="partial_rows",
    )(unpacked, other, w_gate, w_up, w_down)
    got = exchange(give, 1)
    grad_shape = jax.ShapeDtypeStruct((1, units, features), jnp.bfloat16)
    grad_gate, grad_up, grad_down, done = pl.pallas_call(
        functools.partial(grads_kernel, features),
        out_shape=(grad_shape,) * 3 + (pltpu.VMEM((8, LANES), jnp.float32),),
        in_specs=[VMEM] * 2,
        out_specs=(HBM, HBM, HBM, VMEM),
        scratch_shapes=[
            pltpu.VMEM((3, units, features), jnp.bfloat16),
            pltpu.SemaphoreType.DMA((3 * PARTS,)),
        ],
        compiler_params=pltpu.CompilerParams(vmem_limit_bytes=16 * 1024 * 1024),
        cost_estimate=pl.CostEstimate(
            flops=6 * count * units * features,
            bytes_accessed=6 * units * features,
            transcendentals=0,
        ),
        name="weight_grads",
    )(both, acts)
    sent = pl.pallas_call(
        add_kernel,
        out_shape=pltpu.VMEM((half, chunks // 4, 4, LANES), jnp.bfloat16),
        in_specs=[VMEM] * 3,
        out_specs=VMEM,
        compiler_params=pltpu.CompilerParams(vmem_limit_bytes=4 * 1024 * 1024),
        name="add_cores",
    )(keep, got, done)
    back = trade(sent)
    grad_tokens = pl.pallas_call(
        sum_kernel,
        out_shape=jax.ShapeDtypeStruct((1, features), jnp.bfloat16),
        in_specs=[VMEM],
        out_specs=VMEM,
        compiler_params=pltpu.CompilerParams(vmem_limit_bytes=4 * 1024 * 1024),
        name="sum_rows",
    )(back)
    return grad_tokens, grad_gate, grad_up, grad_down


def slice_backward(rows_x, rows_scaled, gate_weight, up_weight, down_weight):
    gate_value = jnp.dot(rows_x, gate_weight.T, preferred_element_type=jnp.float32)
    up_value = jnp.dot(rows_x, up_weight.T, preferred_element_type=jnp.float32)
    sigma_gate = jax.nn.sigmoid(gate_value)
    active = gate_value * sigma_gate
    hidden = (active * up_value).astype(jnp.bfloat16)
    d_hidden = jnp.dot(rows_scaled, down_weight.T, preferred_element_type=jnp.float32)
    d_gate = (d_hidden * up_value * sigma_gate * (1.0 + gate_value * (1.0 - sigma_gate))).astype(
        jnp.bfloat16
    )
    d_up = (d_hidden * active).astype(jnp.bfloat16)
    grad_down = jnp.dot(hidden.T, rows_scaled, preferred_element_type=jnp.float32).astype(
        jnp.bfloat16
    )
    grad_gate = jnp.dot(d_gate.T, rows_x, preferred_element_type=jnp.float32).astype(jnp.bfloat16)
    grad_up = jnp.dot(d_up.T, rows_x, preferred_element_type=jnp.float32).astype(jnp.bfloat16)
    partial_rows = jnp.dot(d_gate, gate_weight, preferred_element_type=jnp.float32)
    partial_rows = partial_rows + jnp.dot(d_up, up_weight, preferred_element_type=jnp.float32)
    return (grad_gate, grad_up, grad_down, partial_rows)


def routed_shards(tokens, grad_out, route_token, route_count, route_prob, w_gate, w_up, w_down):
    groups = route_token.shape[1]
    capacity = route_token.shape[3]
    features = tokens.shape[1]
    block_rows = groups * capacity
    split_count = max(8, lax.axis_size("member") // 8)
    expert_local = lax.axis_index("member") // split_count
    slot_tokens = lax.dynamic_index_in_dim(route_token[0], expert_local, 1, keepdims=False)
    slot_counts = lax.dynamic_index_in_dim(route_count[0], expert_local, 1, keepdims=False)
    slot_probs = lax.dynamic_index_in_dim(route_prob[0], expert_local, 1, keepdims=False)
    slot_index = jnp.arange(capacity, dtype=jnp.int32)[None, :]
    live = (slot_index < slot_counts[:, None]).astype(jnp.float32)
    slot_weights = (slot_probs * live).reshape(-1)
    flat_slots = slot_tokens.reshape(-1)
    group_x, group_dy = (
        lax.all_gather(tokens, "member", axis=0, tiled=True),
        lax.all_gather(grad_out, "member", axis=0, tiled=True),
    )
    picked_x = jnp.take(group_x, flat_slots, axis=0)
    picked_dy = jnp.take(group_dy, flat_slots, axis=0)
    scaled = (slot_weights[:, None] * picked_dy.astype(jnp.float32)).astype(jnp.bfloat16)
    send_x = picked_x.reshape(groups, capacity, features)
    send_scaled = scaled.reshape(groups, capacity, features)
    rows_x, rows_scaled = (
        lax.all_to_all(send_x, "group", split_axis=0, concat_axis=0, tiled=True),
        lax.all_to_all(send_scaled, "group", split_axis=0, concat_axis=0, tiled=True),
    )
    grad_gate, grad_up, grad_down, partial_rows = slice_backward(
        rows_x.reshape(block_rows, features),
        rows_scaled.reshape(block_rows, features),
        w_gate[0],
        w_up[0],
        w_down[0],
    )
    returned = lax.all_to_all(
        partial_rows.reshape(groups, capacity, features),
        "group",
        split_axis=0,
        concat_axis=0,
        tiled=True,
    )
    returned = returned.reshape(block_rows, features)
    row_numbers = jnp.arange(tokens.shape[0] * lax.axis_size("member"), dtype=jnp.int32)
    selector = (row_numbers[:, None] == flat_slots[None, :]).astype(jnp.float32)
    summed = lax.psum_scatter(
        jnp.dot(
            selector, returned, precision=lax.Precision.HIGHEST, preferred_element_type=jnp.float32
        ),
        "member",
        scatter_dimension=0,
        tiled=True,
    )
    return (summed.astype(jnp.bfloat16), grad_gate[None], grad_up[None], grad_down[None])


def shards(tokens, grad_out, route_token, *rest):
    devices = lax.axis_size("group") * lax.axis_size("member")
    _, groups, experts, capacity = route_token.shape
    dense = devices * tokens.shape[0] <= groups * capacity and experts == 1
    paired = tokens.shape[0] == 1 and devices & (devices - 1) == 0
    body = dense_shards if dense and paired else routed_shards
    return body(tokens, grad_out, route_token, *rest)


def solution(mesh):
    placed = (
        P(("group", "member"), None),
        P(("group", "member"), None),
        P("group", None, None, None),
        P("group", None, None),
        P("group", None, None, None),
        P(("group", "member"), None, None),
        P(("group", "member"), None, None),
        P(("group", "member"), None, None),
    )
    return jax.shard_map(
        shards,
        mesh=mesh,
        in_specs=placed,
        out_specs=(
            P(("group", "member"), None),
            P(("group", "member"), None, None),
            P(("group", "member"), None, None),
            P(("group", "member"), None, None),
        ),
        check_vma=False,
    )
```

```python
import functools

import jax
import jax.numpy as jnp
from jax import lax
from jax.experimental import pallas as pl
from jax.experimental.pallas import tpu as pltpu
from jax.sharding import PartitionSpec as P

LANES = 128
PARTS = 4
AXES = ("group", "member")
VMEM = pl.BlockSpec(memory_space=pltpu.VMEM)
HBM = pl.BlockSpec(memory_space=pltpu.HBM)
SMEM = pl.BlockSpec(memory_space=pltpu.SMEM)
NT = (((1,), (1,)), ((), ()))
TN = (((0,), (0,)), ((), ()))


def round_up(value, step):
    return (value + step - 1) // step * step


def pack_kernel(
    chunks,
    tokens_hbm,
    grad_hbm,
    token_hbm,
    count_hbm,
    prob_hbm,
    out_ref,
    rows_ref,
    tokens_ref,
    grad_ref,
    token_ref,
    count_ref,
    prob_ref,
    sems,
):
    pairs = (
        (token_hbm, token_ref),
        (count_hbm, count_ref),
        (prob_hbm, prob_ref),
        (tokens_hbm, tokens_ref),
        (grad_hbm, grad_ref),
    )
    copies = [pltpu.make_async_copy(*pair, sems.at[n]) for n, pair in enumerate(pairs)]
    for copy in copies:
        copy.start()
    for copy in copies:
        copy.wait()
    me = lax.axis_index("member")
    groups, _, capacity = token_ref.shape[1:]
    token_row = tokens_ref[...].astype(jnp.float32)
    grad_row = grad_ref[...].astype(jnp.float32)
    for k in range(chunks):
        part = slice(k * LANES, (k + 1) * LANES)
        rows_ref[k : k + 1, :] = token_row[:, part]
        rows_ref[chunks + k : chunks + k + 1, :] = grad_row[:, part]
    rows = rows_ref[...]
    is_token = lax.broadcasted_iota(jnp.int32, rows.shape, 0) < chunks
    places = out_ref.shape[0] // groups
    for g in range(groups):
        weight = jnp.float32(0)
        for p in range(capacity):
            live = (token_ref[0, g, 0, p] == me) & (p < count_ref[0, 0, g])
            weight = weight + jnp.where(live, prob_ref[0, g, 0, p], 0.0)
        packed = jnp.where(is_token, rows, rows * weight).astype(jnp.bfloat16)
        for n in range(places):
            out_ref[g * places + n] = packed


def unpack_rows(chunks, packed_ref, wide_ref, rows_ref):
    tokens, rows, _ = packed_ref.shape
    wide_ref[...] = packed_ref[...].astype(jnp.float32).reshape(tokens * rows, LANES)
    for k in range(rows):
        column = wide_ref[pl.ds(k, tokens, stride=rows), :]
        rows_ref[:, k * LANES : (k + 1) * LANES] = column.astype(jnp.bfloat16)


def partial_kernel(
    chunks,
    packed_ref,
    gate_ref,
    up_ref,
    down_ref,
    partial_ref,
    rows_ref,
    acts_ref,
    wide_ref,
    spread_ref,
):
    tokens = packed_ref.shape[0]
    features = chunks * LANES
    units = gate_ref.shape[1]
    unpack_rows(chunks, packed_ref, wide_ref, rows_ref)
    x, scaled = rows_ref[:, :features], rows_ref[:, features:]
    gate_value = lax.dot_general(gate_ref[0], x, NT, preferred_element_type=jnp.float32)
    up_value = lax.dot_general(up_ref[0], x, NT, preferred_element_type=jnp.float32)
    d_hidden = lax.dot_general(down_ref[0], scaled, NT, preferred_element_type=jnp.float32)
    sigma_gate = jax.nn.sigmoid(gate_value)
    active = gate_value * sigma_gate
    d_gate = d_hidden * up_value * sigma_gate * (1.0 + gate_value * (1.0 - sigma_gate))
    acts_ref[0:units] = d_gate.astype(jnp.bfloat16)
    acts_ref[units : 2 * units] = (d_hidden * active).astype(jnp.bfloat16)
    acts_ref[2 * units :] = (active * up_value).astype(jnp.bfloat16)
    partial = lax.dot_general(
        acts_ref[:units], gate_ref[0], TN, preferred_element_type=jnp.float32
    ) + lax.dot_general(
        acts_ref[units : 2 * units], up_ref[0], TN, preferred_element_type=jnp.float32
    )
    sent_rows = partial_ref.shape[1]
    for k in range(chunks):
        spread_ref[pl.ds(k, tokens, stride=sent_rows), :] = partial[:, k * LANES : (k + 1) * LANES]
    for k in range(chunks, sent_rows):
        spread_ref[pl.ds(k, tokens, stride=sent_rows), :] = jnp.zeros((tokens, LANES), jnp.float32)
    partial_ref[...] = spread_ref[...].reshape(partial_ref.shape).astype(partial_ref.dtype)


def grads_kernel(
    features,
    mine_ref,
    mine_acts_ref,
    other_ref,
    other_acts_ref,
    gate_out,
    up_out,
    down_out,
    done_ref,
    held_ref,
    sems,
):
    units = held_ref.shape[1]
    height = units // PARTS
    copies = []
    for n, (out, first) in enumerate(((gate_out, 0), (up_out, 0), (down_out, features))):
        part = slice(first, first + features)
        right = jnp.concatenate([mine_ref[:, part], other_ref[:, part]], axis=0)
        for k in range(PARTS):
            part = slice(n * units + k * height, n * units + (k + 1) * height)
            left = jnp.concatenate([mine_acts_ref[part], other_acts_ref[part]], axis=1)
            held_ref[n, k * height : (k + 1) * height] = jnp.dot(
                left, right, preferred_element_type=jnp.float32
            ).astype(jnp.bfloat16)
            part = pl.ds(k * height, height)
            copies.append(
                pltpu.make_async_copy(held_ref.at[n, part], out.at[0, part], sems.at[PARTS * n + k])
            )
            copies[-1].start(priority=k % 2)
    done_ref[...] = jnp.zeros_like(done_ref)
    for copy in copies:
        copy.wait()


def add_kernel(keep_ref, got_ref, after_ref, sent_ref):
    del after_ref
    count, blocks, height, _ = sent_ref.shape
    for n in range(count):
        value = keep_ref[n] + got_ref[n].astype(jnp.float32)
        for k in range(blocks):
            sent_ref[n, k] = value[k * height : (k + 1) * height].astype(jnp.bfloat16)


def sum_kernel(back_ref, out_ref):
    count, blocks, height, _ = back_ref.shape
    for k in range(blocks):
        total = back_ref[0, k].astype(jnp.float32)
        for n in range(1, count):
            total = total + back_ref[n, k].astype(jnp.float32)
        for r in range(height):
            part = pl.ds((k * height + r) * LANES, LANES)
            out_ref[:, part] = total[r : r + 1, :].astype(jnp.bfloat16)


def exchange(value, distance):
    count = lax.axis_size("group") * lax.axis_size("member")
    return lax.ppermute(value, AXES, [(i, i ^ distance) for i in range(count)])


def in_hbm(value):
    return pltpu.with_memory_space_constraint(value, pltpu.HBM)


def dense_shards(tokens, grad_out, route_token, route_count, route_prob, w_gate, w_up, w_down):
    features = tokens.shape[1]
    units = w_gate.shape[1]
    chunks = features // LANES
    count = lax.axis_size("group") * lax.axis_size("member")
    half = count // 2
    rows = 2 * chunks
    sent_rows = round_up(chunks, 16)
    arguments = (tokens, grad_out, route_token, jnp.swapaxes(route_count, 1, 2), route_prob)
    spaces = (pltpu.VMEM, pltpu.VMEM, pltpu.SMEM, pltpu.SMEM, pltpu.SMEM)
    copies = pl.pallas_call(
        functools.partial(pack_kernel, chunks),
        out_shape=pltpu.VMEM((half, rows, LANES), jnp.bfloat16),
        in_specs=[HBM] * 5,
        out_specs=VMEM,
        scratch_shapes=[pltpu.VMEM((rows, LANES), jnp.float32)]
        + [space(value.shape, value.dtype) for space, value in zip(spaces, arguments)]
        + [pltpu.SemaphoreType.DMA((5,))],
        compiler_params=pltpu.CompilerParams(vmem_limit_bytes=4 * 1024 * 1024),
        cost_estimate=pl.CostEstimate(
            flops=40000 * units * features,
            bytes_accessed=16 * units * features,
            transcendentals=0,
        ),
        name="pack_rows",
    )(*[in_hbm(value) for value in arguments])
    cores = [list(range(c, count, 2)) for c in range(2)]
    trade = functools.partial(
        lax.all_to_all,
        axis_name=AXES,
        split_axis=0,
        concat_axis=0,
        tiled=True,
        axis_index_groups=cores,
    )
    mine = trade(copies)
    other = exchange(mine, 1)
    work = lambda dtype: pl.pallas_call(
        functools.partial(partial_kernel, chunks),
        out_shape=(
            pltpu.VMEM((half, sent_rows, LANES), dtype),
            pltpu.VMEM((half, 2 * features), jnp.bfloat16),
            pltpu.VMEM((3 * units, half), jnp.bfloat16),
        ),
        in_specs=[VMEM] * 4,
        out_specs=(VMEM,) * 3,
        scratch_shapes=[
            pltpu.VMEM((half * rows, LANES), jnp.float32),
            pltpu.VMEM((half * sent_rows, LANES), jnp.float32),
        ],
        compiler_params=pltpu.CompilerParams(vmem_limit_bytes=16 * 1024 * 1024),
        name="partial_rows",
    )
    keep, mine_rows, mine_acts = work(jnp.float32)(mine, w_gate, w_up, w_down)
    give, other_rows, other_acts = work(jnp.bfloat16)(other, w_gate, w_up, w_down)
    got = exchange(give, 1)
    grad_shape = jax.ShapeDtypeStruct((1, units, features), jnp.bfloat16)
    grad_gate, grad_up, grad_down, done = pl.pallas_call(
        functools.partial(grads_kernel, features),
        out_shape=(grad_shape,) * 3 + (pltpu.VMEM((8, LANES), jnp.float32),),
        in_specs=[VMEM] * 4,
        out_specs=(HBM, HBM, HBM, VMEM),
        scratch_shapes=[
            pltpu.VMEM((3, units, features), jnp.bfloat16),
            pltpu.SemaphoreType.DMA((3 * PARTS,)),
        ],
        compiler_params=pltpu.CompilerParams(vmem_limit_bytes=16 * 1024 * 1024),
        cost_estimate=pl.CostEstimate(
            flops=6 * count * units * features,
            bytes_accessed=6 * units * features,
            transcendentals=0,
        ),
        name="weight_grads",
    )(mine_rows, mine_acts, other_rows, other_acts)
    sent = pl.pallas_call(
        add_kernel,
        out_shape=pltpu.VMEM((half, chunks // 4, 4, LANES), jnp.bfloat16),
        in_specs=[VMEM] * 3,
        out_specs=VMEM,
        compiler_params=pltpu.CompilerParams(vmem_limit_bytes=4 * 1024 * 1024),
        name="add_cores",
    )(keep, got, done)
    back = trade(sent)
    grad_tokens = pl.pallas_call(
        sum_kernel,
        out_shape=jax.ShapeDtypeStruct((1, features), jnp.bfloat16),
        in_specs=[VMEM],
        out_specs=VMEM,
        compiler_params=pltpu.CompilerParams(vmem_limit_bytes=4 * 1024 * 1024),
        name="sum_rows",
    )(back)
    return grad_tokens, grad_gate, grad_up, grad_down


def slice_backward(rows_x, rows_scaled, gate_weight, up_weight, down_weight):
    gate_value = jnp.dot(rows_x, gate_weight.T, preferred_element_type=jnp.float32)
    up_value = jnp.dot(rows_x, up_weight.T, preferred_element_type=jnp.float32)
    sigma_gate = jax.nn.sigmoid(gate_value)
    active = gate_value * sigma_gate
    hidden = (active * up_value).astype(jnp.bfloat16)
    d_hidden = jnp.dot(rows_scaled, down_weight.T, preferred_element_type=jnp.float32)
    d_gate = (d_hidden * up_value * sigma_gate * (1.0 + gate_value * (1.0 - sigma_gate))).astype(
        jnp.bfloat16
    )
    d_up = (d_hidden * active).astype(jnp.bfloat16)
    grad_down = jnp.dot(hidden.T, rows_scaled, preferred_element_type=jnp.float32).astype(
        jnp.bfloat16
    )
    grad_gate = jnp.dot(d_gate.T, rows_x, preferred_element_type=jnp.float32).astype(jnp.bfloat16)
    grad_up = jnp.dot(d_up.T, rows_x, preferred_element_type=jnp.float32).astype(jnp.bfloat16)
    partial_rows = jnp.dot(d_gate, gate_weight, preferred_element_type=jnp.float32)
    partial_rows = partial_rows + jnp.dot(d_up, up_weight, preferred_element_type=jnp.float32)
    return (grad_gate, grad_up, grad_down, partial_rows)


def routed_shards(tokens, grad_out, route_token, route_count, route_prob, w_gate, w_up, w_down):
    groups = route_token.shape[1]
    capacity = route_token.shape[3]
    features = tokens.shape[1]
    block_rows = groups * capacity
    split_count = max(8, lax.axis_size("member") // 8)
    expert_local = lax.axis_index("member") // split_count
    slot_tokens = lax.dynamic_index_in_dim(route_token[0], expert_local, 1, keepdims=False)
    slot_counts = lax.dynamic_index_in_dim(route_count[0], expert_local, 1, keepdims=False)
    slot_probs = lax.dynamic_index_in_dim(route_prob[0], expert_local, 1, keepdims=False)
    slot_index = jnp.arange(capacity, dtype=jnp.int32)[None, :]
    live = (slot_index < slot_counts[:, None]).astype(jnp.float32)
    slot_weights = (slot_probs * live).reshape(-1)
    flat_slots = slot_tokens.reshape(-1)
    group_x, group_dy = (
        lax.all_gather(tokens, "member", axis=0, tiled=True),
        lax.all_gather(grad_out, "member", axis=0, tiled=True),
    )
    picked_x = jnp.take(group_x, flat_slots, axis=0)
    picked_dy = jnp.take(group_dy, flat_slots, axis=0)
    scaled = (slot_weights[:, None] * picked_dy.astype(jnp.float32)).astype(jnp.bfloat16)
    send_x = picked_x.reshape(groups, capacity, features)
    send_scaled = scaled.reshape(groups, capacity, features)
    rows_x, rows_scaled = (
        lax.all_to_all(send_x, "group", split_axis=0, concat_axis=0, tiled=True),
        lax.all_to_all(send_scaled, "group", split_axis=0, concat_axis=0, tiled=True),
    )
    grad_gate, grad_up, grad_down, partial_rows = slice_backward(
        rows_x.reshape(block_rows, features),
        rows_scaled.reshape(block_rows, features),
        w_gate[0],
        w_up[0],
        w_down[0],
    )
    returned = lax.all_to_all(
        partial_rows.reshape(groups, capacity, features),
        "group",
        split_axis=0,
        concat_axis=0,
        tiled=True,
    )
    returned = returned.reshape(block_rows, features)
    row_numbers = jnp.arange(tokens.shape[0] * lax.axis_size("member"), dtype=jnp.int32)
    selector = (row_numbers[:, None] == flat_slots[None, :]).astype(jnp.float32)
    summed = lax.psum_scatter(
        jnp.dot(
            selector, returned, precision=lax.Precision.HIGHEST, preferred_element_type=jnp.float32
        ),
        "member",
        scatter_dimension=0,
        tiled=True,
    )
    return (summed.astype(jnp.bfloat16), grad_gate[None], grad_up[None], grad_down[None])


def shards(tokens, grad_out, route_token, *rest):
    devices = lax.axis_size("group") * lax.axis_size("member")
    _, groups, experts, capacity = route_token.shape
    dense = devices * tokens.shape[0] <= groups * capacity and experts == 1
    paired = tokens.shape[0] == 1 and devices & (devices - 1) == 0
    body = dense_shards if dense and paired else routed_shards
    return body(tokens, grad_out, route_token, *rest)


def solution(mesh):
    placed = (
        P(("group", "member"), None),
        P(("group", "member"), None),
        P("group", None, None, None),
        P("group", None, None),
        P("group", None, None, None),
        P(("group", "member"), None, None),
        P(("group", "member"), None, None),
        P(("group", "member"), None, None),
    )
    return jax.shard_map(
        shards,
        mesh=mesh,
        in_specs=placed,
        out_specs=(
            P(("group", "member"), None),
            P(("group", "member"), None, None),
            P(("group", "member"), None, None),
            P(("group", "member"), None, None),
        ),
        check_vma=False,
    )
```

```python
import functools

import jax
import jax.numpy as jnp
from jax import lax
from jax.experimental import pallas as pl
from jax.experimental.pallas import tpu as pltpu
from jax.sharding import PartitionSpec as P

LANES = 128
PARTS = 4
AXES = ("group", "member")
VMEM = pl.BlockSpec(memory_space=pltpu.VMEM)
HBM = pl.BlockSpec(memory_space=pltpu.HBM)
SMEM = pl.BlockSpec(memory_space=pltpu.SMEM)
NT = (((1,), (1,)), ((), ()))
TN = (((0,), (0,)), ((), ()))


def round_up(value, step):
    return (value + step - 1) // step * step


def pack_kernel(
    chunks,
    tokens_hbm,
    grad_hbm,
    token_hbm,
    count_hbm,
    prob_hbm,
    out_ref,
    rows_ref,
    tokens_ref,
    grad_ref,
    token_ref,
    count_ref,
    prob_ref,
    sems,
):
    pairs = (
        (token_hbm, token_ref),
        (count_hbm, count_ref),
        (prob_hbm, prob_ref),
        (tokens_hbm, tokens_ref),
        (grad_hbm, grad_ref),
    )
    copies = [pltpu.make_async_copy(*pair, sems.at[n]) for n, pair in enumerate(pairs)]
    for copy in copies:
        copy.start()
    for copy in copies:
        copy.wait()
    me = lax.axis_index("member")
    groups, experts, capacity = token_ref.shape[1:]
    token_row = tokens_ref[...].astype(jnp.float32)
    grad_row = grad_ref[...].astype(jnp.float32)
    for k in range(chunks):
        part = slice(k * LANES, (k + 1) * LANES)
        rows_ref[k : k + 1, :] = token_row[:, part]
        rows_ref[chunks + k : chunks + k + 1, :] = grad_row[:, part]
    lane = lax.broadcasted_iota(jnp.int32, (1, LANES), 1)
    third = lax.rem(lane, 32)
    weights = jnp.zeros((1, LANES), jnp.float32)
    for g in range(groups):
        for j in range(experts):
            weight = jnp.float32(0)
            for p in range(capacity):
                live = (token_ref[0, g, j, p] == me) & (p < count_ref[0, j, g])
                weight = weight + jnp.where(live, prob_ref[0, g, j, p], 0.0)
            weights = jnp.where(third == g * experts + j, weight, weights)
    high = weights.astype(jnp.bfloat16).astype(jnp.float32)
    middle = (weights - high).astype(jnp.bfloat16).astype(jnp.float32)
    low = weights - high - middle
    parts = jnp.where(lane < 32, high, jnp.where(lane < 64, middle, jnp.where(lane < 96, low, 0.0)))
    rows_ref[2 * chunks : 2 * chunks + 1, :] = parts
    used = 2 * chunks + 1
    rows_ref[used:, :] = jnp.zeros((rows_ref.shape[0] - used, LANES), jnp.float32)
    out_ref[0] = rows_ref[...].astype(jnp.bfloat16)


def unpack_rows(chunks, packed_ref, wide_ref, rows_ref):
    tokens, rows, _ = packed_ref.shape
    features = chunks * LANES
    wide_ref[...] = packed_ref[...].astype(jnp.float32).reshape(tokens * rows, LANES)

    def column(k):
        return wide_ref[pl.ds(k, tokens, stride=rows), :]

    lane = lax.broadcasted_iota(jnp.int32, (tokens, LANES), 1)
    mine = (lane < 96) & (lax.rem(lane, 32) == lax.axis_index("group"))
    weight = jnp.sum(jnp.where(mine, column(2 * chunks), 0.0), axis=1, keepdims=True)
    for k in range(chunks):
        rows_ref[:, k * LANES : (k + 1) * LANES] = column(k).astype(jnp.bfloat16)
        rows_ref[:, features + k * LANES : features + (k + 1) * LANES] = (
            weight * column(chunks + k)
        ).astype(jnp.bfloat16)


def unpack_kernel(chunks, mine_ref, rows_ref, wide_ref):
    unpack_rows(chunks, mine_ref, wide_ref, rows_ref)


def partial_kernel(
    chunks,
    mine_ref,
    other_ref,
    gate_ref,
    up_ref,
    down_ref,
    keep_ref,
    give_ref,
    rows_ref,
    acts_ref,
    wide_ref,
    spread_ref,
):
    count = mine_ref.shape[0]
    tokens = 2 * count
    features = chunks * LANES
    units = gate_ref.shape[1]
    rows_ref[:count] = mine_ref[...]
    unpack_rows(chunks, other_ref, wide_ref, rows_ref.at[pl.ds(count, count)])
    x, scaled = rows_ref[:, :features], rows_ref[:, features:]
    gate_value = lax.dot_general(gate_ref[0], x, NT, preferred_element_type=jnp.float32)
    up_value = lax.dot_general(up_ref[0], x, NT, preferred_element_type=jnp.float32)
    d_hidden = lax.dot_general(down_ref[0], scaled, NT, preferred_element_type=jnp.float32)
    sigma_gate = jax.nn.sigmoid(gate_value)
    active = gate_value * sigma_gate
    d_gate = d_hidden * up_value * sigma_gate * (1.0 + gate_value * (1.0 - sigma_gate))
    acts_ref[0:units] = d_gate.astype(jnp.bfloat16)
    acts_ref[units : 2 * units] = (d_hidden * active).astype(jnp.bfloat16)
    acts_ref[2 * units :] = (active * up_value).astype(jnp.bfloat16)
    partial = lax.dot_general(
        acts_ref[:units], gate_ref[0], TN, preferred_element_type=jnp.float32
    ) + lax.dot_general(
        acts_ref[units : 2 * units], up_ref[0], TN, preferred_element_type=jnp.float32
    )
    sent_rows = keep_ref.shape[1]
    for k in range(chunks):
        spread_ref[pl.ds(k, tokens, stride=sent_rows), :] = partial[:, k * LANES : (k + 1) * LANES]
    for k in range(chunks, sent_rows):
        spread_ref[pl.ds(k, tokens, stride=sent_rows), :] = jnp.zeros((tokens, LANES), jnp.float32)
    half = count * sent_rows
    keep_ref[...] = spread_ref[:half, :].reshape(keep_ref.shape)
    give_ref[...] = spread_ref[half:, :].reshape(give_ref.shape).astype(jnp.bfloat16)


def grads_kernel(
    features, rows_ref, acts_ref, gate_out, up_out, down_out, done_ref, held_ref, sems
):
    units = held_ref.shape[1]
    height = units // PARTS
    copies = []
    for n, (out, first) in enumerate(((gate_out, 0), (up_out, 0), (down_out, features))):
        right = rows_ref[:, first : first + features]
        for k in range(PARTS):
            left = acts_ref[n * units + k * height : n * units + (k + 1) * height, :]
            held_ref[n, k * height : (k + 1) * height] = jnp.dot(
                left, right, preferred_element_type=jnp.float32
            ).astype(jnp.bfloat16)
            part = pl.ds(k * height, height)
            copies.append(
                pltpu.make_async_copy(held_ref.at[n, part], out.at[0, part], sems.at[PARTS * n + k])
            )
            copies[-1].start()
    done_ref[...] = jnp.zeros_like(done_ref)
    for copy in copies:
        copy.wait()


def add_kernel(keep_ref, got_ref, after_ref, sent_ref):
    del after_ref
    count, blocks, height, _ = sent_ref.shape
    for n in range(count):
        value = keep_ref[n] + got_ref[n].astype(jnp.float32)
        for k in range(blocks):
            sent_ref[n, k] = value[k * height : (k + 1) * height].astype(jnp.bfloat16)


def sum_kernel(back_ref, out_ref):
    count, blocks, height, _ = back_ref.shape
    for k in range(blocks):
        total = back_ref[0, k].astype(jnp.float32)
        for n in range(1, count):
            total = total + back_ref[n, k].astype(jnp.float32)
        for r in range(height):
            part = pl.ds((k * height + r) * LANES, LANES)
            out_ref[:, part] = total[r : r + 1, :].astype(jnp.bfloat16)


def exchange(value, distance):
    count = lax.axis_size("group") * lax.axis_size("member")
    return lax.ppermute(value, AXES, [(i, i ^ distance) for i in range(count)])


def in_hbm(value):
    return pltpu.with_memory_space_constraint(value, pltpu.HBM)


def dense_shards(tokens, grad_out, route_token, route_count, route_prob, w_gate, w_up, w_down):
    features = tokens.shape[1]
    units = w_gate.shape[1]
    chunks = features // LANES
    count = lax.axis_size("group") * lax.axis_size("member")
    half = count // 2
    rows = round_up(2 * chunks + 1, 16)
    sent_rows = round_up(chunks, 16)
    arguments = (tokens, grad_out, route_token, jnp.swapaxes(route_count, 1, 2), route_prob)
    spaces = (pltpu.VMEM, pltpu.VMEM, pltpu.SMEM, pltpu.SMEM, pltpu.SMEM)
    copies = pl.pallas_call(
        functools.partial(pack_kernel, chunks),
        out_shape=pltpu.VMEM((1, rows, LANES), jnp.bfloat16),
        in_specs=[HBM] * 5,
        out_specs=VMEM,
        scratch_shapes=[pltpu.VMEM((rows, LANES), jnp.float32)]
        + [space(value.shape, value.dtype) for space, value in zip(spaces, arguments)]
        + [pltpu.SemaphoreType.DMA((5,))],
        compiler_params=pltpu.CompilerParams(vmem_limit_bytes=4 * 1024 * 1024),
        cost_estimate=pl.CostEstimate(
            flops=40000 * units * features,
            bytes_accessed=16 * units * features,
            transcendentals=0,
        ),
        name="pack_rows",
    )(*[in_hbm(value) for value in arguments])
    cores = [list(range(c, count, 2)) for c in range(2)]
    trade = functools.partial(
        lax.all_to_all,
        axis_name=AXES,
        split_axis=0,
        concat_axis=0,
        tiled=True,
        axis_index_groups=cores,
    )
    mine = lax.all_gather(copies, AXES, axis=0, tiled=True, axis_index_groups=cores)
    other = exchange(mine, 1)
    wide = pltpu.VMEM((half * rows, LANES), jnp.float32)
    unpacked = pl.pallas_call(
        functools.partial(unpack_kernel, chunks),
        out_shape=pltpu.VMEM((half, 2 * features), jnp.bfloat16),
        in_specs=[VMEM],
        out_specs=VMEM,
        scratch_shapes=[wide],
        compiler_params=pltpu.CompilerParams(vmem_limit_bytes=2 * 1024 * 1024),
        name="unpack_rows",
    )(mine)
    keep, give, both, acts = pl.pallas_call(
        functools.partial(partial_kernel, chunks),
        out_shape=(
            pltpu.VMEM((half, sent_rows, LANES), jnp.float32),
            pltpu.VMEM((half, sent_rows, LANES), jnp.bfloat16),
            pltpu.VMEM((count, 2 * features), jnp.bfloat16),
            pltpu.VMEM((3 * units, count), jnp.bfloat16),
        ),
        in_specs=[VMEM] * 5,
        out_specs=(VMEM,) * 4,
        scratch_shapes=[wide, pltpu.VMEM((count * sent_rows, LANES), jnp.float32)],
        compiler_params=pltpu.CompilerParams(vmem_limit_bytes=16 * 1024 * 1024),
        name="partial_rows",
    )(unpacked, other, w_gate, w_up, w_down)
    got = exchange(give, 1)
    grad_shape = jax.ShapeDtypeStruct((1, units, features), jnp.bfloat16)
    grad_gate, grad_up, grad_down, done = pl.pallas_call(
        functools.partial(grads_kernel, features),
        out_shape=(grad_shape,) * 3 + (pltpu.VMEM((8, LANES), jnp.float32),),
        in_specs=[VMEM] * 2,
        out_specs=(HBM, HBM, HBM, VMEM),
        scratch_shapes=[
            pltpu.VMEM((3, units, features), jnp.bfloat16),
            pltpu.SemaphoreType.DMA((3 * PARTS,)),
        ],
        compiler_params=pltpu.CompilerParams(vmem_limit_bytes=16 * 1024 * 1024),
        cost_estimate=pl.CostEstimate(
            flops=6 * count * units * features,
            bytes_accessed=6 * units * features,
            transcendentals=0,
        ),
        name="weight_grads",
    )(both, acts)
    sent = pl.pallas_call(
        add_kernel,
        out_shape=pltpu.VMEM((half, chunks // 4, 4, LANES), jnp.bfloat16),
        in_specs=[VMEM] * 3,
        out_specs=VMEM,
        compiler_params=pltpu.CompilerParams(vmem_limit_bytes=4 * 1024 * 1024),
        name="add_cores",
    )(keep, got, done)
    back = trade(sent)
    grad_tokens = pl.pallas_call(
        sum_kernel,
        out_shape=jax.ShapeDtypeStruct((1, features), jnp.bfloat16),
        in_specs=[VMEM],
        out_specs=VMEM,
        compiler_params=pltpu.CompilerParams(vmem_limit_bytes=4 * 1024 * 1024),
        name="sum_rows",
    )(back)
    return grad_tokens, grad_gate, grad_up, grad_down


def slice_backward(rows_x, rows_scaled, gate_weight, up_weight, down_weight):
    gate_value = jnp.dot(rows_x, gate_weight.T, preferred_element_type=jnp.float32)
    up_value = jnp.dot(rows_x, up_weight.T, preferred_element_type=jnp.float32)
    sigma_gate = jax.nn.sigmoid(gate_value)
    active = gate_value * sigma_gate
    hidden = (active * up_value).astype(jnp.bfloat16)
    d_hidden = jnp.dot(rows_scaled, down_weight.T, preferred_element_type=jnp.float32)
    d_gate = (d_hidden * up_value * sigma_gate * (1.0 + gate_value * (1.0 - sigma_gate))).astype(
        jnp.bfloat16
    )
    d_up = (d_hidden * active).astype(jnp.bfloat16)
    grad_down = jnp.dot(hidden.T, rows_scaled, preferred_element_type=jnp.float32).astype(
        jnp.bfloat16
    )
    grad_gate = jnp.dot(d_gate.T, rows_x, preferred_element_type=jnp.float32).astype(jnp.bfloat16)
    grad_up = jnp.dot(d_up.T, rows_x, preferred_element_type=jnp.float32).astype(jnp.bfloat16)
    partial_rows = jnp.dot(d_gate, gate_weight, preferred_element_type=jnp.float32)
    partial_rows = partial_rows + jnp.dot(d_up, up_weight, preferred_element_type=jnp.float32)
    return (grad_gate, grad_up, grad_down, partial_rows)


def routed_shards(tokens, grad_out, route_token, route_count, route_prob, w_gate, w_up, w_down):
    groups = route_token.shape[1]
    capacity = route_token.shape[3]
    features = tokens.shape[1]
    block_rows = groups * capacity
    split_count = max(8, lax.axis_size("member") // 8)
    expert_local = lax.axis_index("member") // split_count
    slot_tokens = lax.dynamic_index_in_dim(route_token[0], expert_local, 1, keepdims=False)
    slot_counts = lax.dynamic_index_in_dim(route_count[0], expert_local, 1, keepdims=False)
    slot_probs = lax.dynamic_index_in_dim(route_prob[0], expert_local, 1, keepdims=False)
    slot_index = jnp.arange(capacity, dtype=jnp.int32)[None, :]
    live = (slot_index < slot_counts[:, None]).astype(jnp.float32)
    slot_weights = (slot_probs * live).reshape(-1)
    flat_slots = slot_tokens.reshape(-1)
    group_x, group_dy = (
        lax.all_gather(tokens, "member", axis=0, tiled=True),
        lax.all_gather(grad_out, "member", axis=0, tiled=True),
    )
    picked_x = jnp.take(group_x, flat_slots, axis=0)
    picked_dy = jnp.take(group_dy, flat_slots, axis=0)
    scaled = (slot_weights[:, None] * picked_dy.astype(jnp.float32)).astype(jnp.bfloat16)
    send_x = picked_x.reshape(groups, capacity, features)
    send_scaled = scaled.reshape(groups, capacity, features)
    rows_x, rows_scaled = (
        lax.all_to_all(send_x, "group", split_axis=0, concat_axis=0, tiled=True),
        lax.all_to_all(send_scaled, "group", split_axis=0, concat_axis=0, tiled=True),
    )
    grad_gate, grad_up, grad_down, partial_rows = slice_backward(
        rows_x.reshape(block_rows, features),
        rows_scaled.reshape(block_rows, features),
        w_gate[0],
        w_up[0],
        w_down[0],
    )
    returned = lax.all_to_all(
        partial_rows.reshape(groups, capacity, features),
        "group",
        split_axis=0,
        concat_axis=0,
        tiled=True,
    )
    returned = returned.reshape(block_rows, features)
    row_numbers = jnp.arange(tokens.shape[0] * lax.axis_size("member"), dtype=jnp.int32)
    selector = (row_numbers[:, None] == flat_slots[None, :]).astype(jnp.float32)
    summed = lax.psum_scatter(
        jnp.dot(
            selector, returned, precision=lax.Precision.HIGHEST, preferred_element_type=jnp.float32
        ),
        "member",
        scatter_dimension=0,
        tiled=True,
    )
    return (summed.astype(jnp.bfloat16), grad_gate[None], grad_up[None], grad_down[None])


def shards(tokens, grad_out, route_token, *rest):
    devices = lax.axis_size("group") * lax.axis_size("member")
    _, groups, experts, capacity = route_token.shape
    dense = devices * tokens.shape[0] <= groups * capacity and experts == 1 and groups <= 32
    paired = tokens.shape[0] == 1 and devices & (devices - 1) == 0
    body = dense_shards if dense and paired else routed_shards
    return body(tokens, grad_out, route_token, *rest)


def solution(mesh):
    placed = (
        P(("group", "member"), None),
        P(("group", "member"), None),
        P("group", None, None, None),
        P("group", None, None),
        P("group", None, None, None),
        P(("group", "member"), None, None),
        P(("group", "member"), None, None),
        P(("group", "member"), None, None),
    )
    return jax.shard_map(
        shards,
        mesh=mesh,
        in_specs=placed,
        out_specs=(
            P(("group", "member"), None),
            P(("group", "member"), None, None),
            P(("group", "member"), None, None),
            P(("group", "member"), None, None),
        ),
        check_vma=False,
    )
```

```python
import functools

import jax
import jax.numpy as jnp
from jax import lax
from jax.experimental import pallas as pl
from jax.experimental.pallas import tpu as pltpu
from jax.sharding import PartitionSpec as P

LANES = 128
PARTS = 4
AXES = ("group", "member")
VMEM = pl.BlockSpec(memory_space=pltpu.VMEM)
HBM = pl.BlockSpec(memory_space=pltpu.HBM)
SMEM = pl.BlockSpec(memory_space=pltpu.SMEM)
NT = (((1,), (1,)), ((), ()))
TN = (((0,), (0,)), ((), ()))


def round_up(value, step):
    return (value + step - 1) // step * step


def pack_kernel(
    chunks,
    tokens_hbm,
    grad_hbm,
    token_hbm,
    count_hbm,
    prob_hbm,
    out_ref,
    rows_ref,
    tokens_ref,
    grad_ref,
    token_ref,
    count_ref,
    prob_ref,
    sems,
):
    pairs = (
        (token_hbm, token_ref),
        (count_hbm, count_ref),
        (prob_hbm, prob_ref),
        (tokens_hbm, tokens_ref),
        (grad_hbm, grad_ref),
    )
    copies = [pltpu.make_async_copy(*pair, sems.at[n]) for n, pair in enumerate(pairs)]
    for copy in copies:
        copy.start()
    for copy in copies:
        copy.wait()
    me = lax.axis_index("member")
    groups, _, capacity = token_ref.shape[1:]
    token_row = tokens_ref[...].astype(jnp.float32)
    grad_row = grad_ref[...].astype(jnp.float32)
    for k in range(chunks):
        part = slice(k * LANES, (k + 1) * LANES)
        rows_ref[k : k + 1, :] = token_row[:, part]
        rows_ref[chunks + k : chunks + k + 1, :] = grad_row[:, part]
    rows = rows_ref[...]
    is_token = lax.broadcasted_iota(jnp.int32, rows.shape, 0) < chunks
    places = out_ref.shape[0] // groups
    for g in range(groups):
        weight = jnp.float32(0)
        for p in range(capacity):
            live = (token_ref[0, g, 0, p] == me) & (p < count_ref[0, 0, g])
            weight = weight + jnp.where(live, prob_ref[0, g, 0, p], 0.0)
        packed = jnp.where(is_token, rows, rows * weight).astype(jnp.bfloat16)
        for n in range(places):
            out_ref[g * places + n] = packed


def unpack_rows(chunks, packed_ref, wide_ref, rows_ref):
    tokens, rows, _ = packed_ref.shape
    wide_ref[...] = packed_ref[...].astype(jnp.float32).reshape(tokens * rows, LANES)
    for k in range(rows):
        column = wide_ref[pl.ds(k, tokens, stride=rows), :]
        rows_ref[:, k * LANES : (k + 1) * LANES] = column.astype(jnp.bfloat16)


def unpack_kernel(chunks, mine_ref, rows_ref, wide_ref):
    unpack_rows(chunks, mine_ref, wide_ref, rows_ref)


def partial_kernel(
    chunks,
    mine_ref,
    other_ref,
    gate_ref,
    up_ref,
    down_ref,
    keep_ref,
    give_ref,
    rows_ref,
    acts_ref,
    wide_ref,
    spread_ref,
):
    count = mine_ref.shape[0]
    tokens = 2 * count
    features = chunks * LANES
    units = gate_ref.shape[1]
    rows_ref[:count] = mine_ref[...]
    unpack_rows(chunks, other_ref, wide_ref, rows_ref.at[pl.ds(count, count)])
    x, scaled = rows_ref[:, :features], rows_ref[:, features:]
    both = jnp.concatenate([gate_ref[0], up_ref[0]], axis=0)
    values = lax.dot_general(x, both, NT, preferred_element_type=jnp.float32)
    gate_value, up_value = values[:, :units], values[:, units:]
    d_hidden = lax.dot_general(scaled, down_ref[0], NT, preferred_element_type=jnp.float32)
    sigma_gate = jax.nn.sigmoid(gate_value)
    active = gate_value * sigma_gate
    d_gate = d_hidden * up_value * sigma_gate * (1.0 + gate_value * (1.0 - sigma_gate))
    acts_ref[:, :units] = d_gate.astype(jnp.bfloat16)
    acts_ref[:, units : 2 * units] = (d_hidden * active).astype(jnp.bfloat16)
    acts_ref[:, 2 * units :] = (active * up_value).astype(jnp.bfloat16)
    partial = jnp.dot(acts_ref[:, : 2 * units], both, preferred_element_type=jnp.float32)
    sent_rows = keep_ref.shape[1]
    for k in range(chunks):
        spread_ref[pl.ds(k, tokens, stride=sent_rows), :] = partial[:, k * LANES : (k + 1) * LANES]
    for k in range(chunks, sent_rows):
        spread_ref[pl.ds(k, tokens, stride=sent_rows), :] = jnp.zeros((tokens, LANES), jnp.float32)
    half = count * sent_rows
    keep_ref[...] = spread_ref[:half, :].reshape(keep_ref.shape)
    give_ref[...] = spread_ref[half:, :].reshape(give_ref.shape).astype(jnp.bfloat16)


def grads_kernel(
    features, rows_ref, acts_ref, gate_out, up_out, down_out, done_ref, held_ref, sems
):
    units = held_ref.shape[1]
    height = units // PARTS
    copies = []
    for n, (out, first) in enumerate(((gate_out, 0), (up_out, 0), (down_out, features))):
        left = acts_ref[:, n * units : (n + 1) * units].astype(jnp.float32).T.astype(jnp.bfloat16)
        right = rows_ref[:, first : first + features]
        for k in range(PARTS):
            held_ref[n, k * height : (k + 1) * height] = jnp.dot(
                left[k * height : (k + 1) * height], right, preferred_element_type=jnp.float32
            ).astype(jnp.bfloat16)
            part = pl.ds(k * height, height)
            copies.append(
                pltpu.make_async_copy(held_ref.at[n, part], out.at[0, part], sems.at[PARTS * n + k])
            )
            copies[-1].start()
    done_ref[...] = jnp.zeros_like(done_ref)
    for copy in copies:
        copy.wait()


def add_kernel(keep_ref, got_ref, after_ref, sent_ref):
    del after_ref
    count, blocks, height, _ = sent_ref.shape
    for n in range(count):
        value = keep_ref[n] + got_ref[n].astype(jnp.float32)
        for k in range(blocks):
            sent_ref[n, k] = value[k * height : (k + 1) * height].astype(jnp.bfloat16)


def sum_kernel(back_ref, out_ref):
    count, blocks, height, _ = back_ref.shape
    for k in range(blocks):
        total = back_ref[0, k].astype(jnp.float32)
        for n in range(1, count):
            total = total + back_ref[n, k].astype(jnp.float32)
        for r in range(height):
            part = pl.ds((k * height + r) * LANES, LANES)
            out_ref[:, part] = total[r : r + 1, :].astype(jnp.bfloat16)


def exchange(value, distance):
    count = lax.axis_size("group") * lax.axis_size("member")
    return lax.ppermute(value, AXES, [(i, i ^ distance) for i in range(count)])


def in_hbm(value):
    return pltpu.with_memory_space_constraint(value, pltpu.HBM)


def dense_shards(tokens, grad_out, route_token, route_count, route_prob, w_gate, w_up, w_down):
    features = tokens.shape[1]
    units = w_gate.shape[1]
    chunks = features // LANES
    count = lax.axis_size("group") * lax.axis_size("member")
    half = count // 2
    rows = 2 * chunks
    sent_rows = round_up(chunks, 16)
    arguments = (tokens, grad_out, route_token, jnp.swapaxes(route_count, 1, 2), route_prob)
    spaces = (pltpu.VMEM, pltpu.VMEM, pltpu.SMEM, pltpu.SMEM, pltpu.SMEM)
    copies = pl.pallas_call(
        functools.partial(pack_kernel, chunks),
        out_shape=pltpu.VMEM((half, rows, LANES), jnp.bfloat16),
        in_specs=[HBM] * 5,
        out_specs=VMEM,
        scratch_shapes=[pltpu.VMEM((rows, LANES), jnp.float32)]
        + [space(value.shape, value.dtype) for space, value in zip(spaces, arguments)]
        + [pltpu.SemaphoreType.DMA((5,))],
        compiler_params=pltpu.CompilerParams(vmem_limit_bytes=4 * 1024 * 1024),
        cost_estimate=pl.CostEstimate(
            flops=40000 * units * features,
            bytes_accessed=16 * units * features,
            transcendentals=0,
        ),
        name="pack_rows",
    )(*[in_hbm(value) for value in arguments])
    cores = [list(range(c, count, 2)) for c in range(2)]
    trade = functools.partial(
        lax.all_to_all,
        axis_name=AXES,
        split_axis=0,
        concat_axis=0,
        tiled=True,
        axis_index_groups=cores,
    )
    mine = trade(copies)
    other = exchange(mine, 1)
    wide = pltpu.VMEM((half * rows, LANES), jnp.float32)
    unpacked = pl.pallas_call(
        functools.partial(unpack_kernel, chunks),
        out_shape=pltpu.VMEM((half, 2 * features), jnp.bfloat16),
        in_specs=[VMEM],
        out_specs=VMEM,
        scratch_shapes=[wide],
        compiler_params=pltpu.CompilerParams(vmem_limit_bytes=2 * 1024 * 1024),
        name="unpack_rows",
    )(mine)
    keep, give, both, acts = pl.pallas_call(
        functools.partial(partial_kernel, chunks),
        out_shape=(
            pltpu.VMEM((half, sent_rows, LANES), jnp.float32),
            pltpu.VMEM((half, sent_rows, LANES), jnp.bfloat16),
            pltpu.VMEM((count, 2 * features), jnp.bfloat16),
            pltpu.VMEM((count, 3 * units), jnp.bfloat16),
        ),
        in_specs=[VMEM] * 5,
        out_specs=(VMEM,) * 4,
        scratch_shapes=[wide, pltpu.VMEM((count * sent_rows, LANES), jnp.float32)],
        compiler_params=pltpu.CompilerParams(vmem_limit_bytes=16 * 1024 * 1024),
        name="partial_rows",
    )(unpacked, other, w_gate, w_up, w_down)
    got = exchange(give, 1)
    grad_shape = jax.ShapeDtypeStruct((1, units, features), jnp.bfloat16)
    grad_gate, grad_up, grad_down, done = pl.pallas_call(
        functools.partial(grads_kernel, features),
        out_shape=(grad_shape,) * 3 + (pltpu.VMEM((8, LANES), jnp.float32),),
        in_specs=[VMEM] * 2,
        out_specs=(HBM, HBM, HBM, VMEM),
        scratch_shapes=[
            pltpu.VMEM((3, units, features), jnp.bfloat16),
            pltpu.SemaphoreType.DMA((3 * PARTS,)),
        ],
        compiler_params=pltpu.CompilerParams(vmem_limit_bytes=16 * 1024 * 1024),
        cost_estimate=pl.CostEstimate(
            flops=6 * count * units * features,
            bytes_accessed=6 * units * features,
            transcendentals=0,
        ),
        name="weight_grads",
    )(both, acts)
    sent = pl.pallas_call(
        add_kernel,
        out_shape=pltpu.VMEM((half, chunks // 4, 4, LANES), jnp.bfloat16),
        in_specs=[VMEM] * 3,
        out_specs=VMEM,
        compiler_params=pltpu.CompilerParams(vmem_limit_bytes=4 * 1024 * 1024),
        name="add_cores",
    )(keep, got, done)
    back = trade(sent)
    grad_tokens = pl.pallas_call(
        sum_kernel,
        out_shape=jax.ShapeDtypeStruct((1, features), jnp.bfloat16),
        in_specs=[VMEM],
        out_specs=VMEM,
        compiler_params=pltpu.CompilerParams(vmem_limit_bytes=4 * 1024 * 1024),
        name="sum_rows",
    )(back)
    return grad_tokens, grad_gate, grad_up, grad_down


def slice_backward(rows_x, rows_scaled, gate_weight, up_weight, down_weight):
    gate_value = jnp.dot(rows_x, gate_weight.T, preferred_element_type=jnp.float32)
    up_value = jnp.dot(rows_x, up_weight.T, preferred_element_type=jnp.float32)
    sigma_gate = jax.nn.sigmoid(gate_value)
    active = gate_value * sigma_gate
    hidden = (active * up_value).astype(jnp.bfloat16)
    d_hidden = jnp.dot(rows_scaled, down_weight.T, preferred_element_type=jnp.float32)
    d_gate = (d_hidden * up_value * sigma_gate * (1.0 + gate_value * (1.0 - sigma_gate))).astype(
        jnp.bfloat16
    )
    d_up = (d_hidden * active).astype(jnp.bfloat16)
    grad_down = jnp.dot(hidden.T, rows_scaled, preferred_element_type=jnp.float32).astype(
        jnp.bfloat16
    )
    grad_gate = jnp.dot(d_gate.T, rows_x, preferred_element_type=jnp.float32).astype(jnp.bfloat16)
    grad_up = jnp.dot(d_up.T, rows_x, preferred_element_type=jnp.float32).astype(jnp.bfloat16)
    partial_rows = jnp.dot(d_gate, gate_weight, preferred_element_type=jnp.float32)
    partial_rows = partial_rows + jnp.dot(d_up, up_weight, preferred_element_type=jnp.float32)
    return (grad_gate, grad_up, grad_down, partial_rows)


def routed_shards(tokens, grad_out, route_token, route_count, route_prob, w_gate, w_up, w_down):
    groups = route_token.shape[1]
    capacity = route_token.shape[3]
    features = tokens.shape[1]
    block_rows = groups * capacity
    split_count = max(8, lax.axis_size("member") // 8)
    expert_local = lax.axis_index("member") // split_count
    slot_tokens = lax.dynamic_index_in_dim(route_token[0], expert_local, 1, keepdims=False)
    slot_counts = lax.dynamic_index_in_dim(route_count[0], expert_local, 1, keepdims=False)
    slot_probs = lax.dynamic_index_in_dim(route_prob[0], expert_local, 1, keepdims=False)
    slot_index = jnp.arange(capacity, dtype=jnp.int32)[None, :]
    live = (slot_index < slot_counts[:, None]).astype(jnp.float32)
    slot_weights = (slot_probs * live).reshape(-1)
    flat_slots = slot_tokens.reshape(-1)
    group_x, group_dy = (
        lax.all_gather(tokens, "member", axis=0, tiled=True),
        lax.all_gather(grad_out, "member", axis=0, tiled=True),
    )
    picked_x = jnp.take(group_x, flat_slots, axis=0)
    picked_dy = jnp.take(group_dy, flat_slots, axis=0)
    scaled = (slot_weights[:, None] * picked_dy.astype(jnp.float32)).astype(jnp.bfloat16)
    send_x = picked_x.reshape(groups, capacity, features)
    send_scaled = scaled.reshape(groups, capacity, features)
    rows_x, rows_scaled = (
        lax.all_to_all(send_x, "group", split_axis=0, concat_axis=0, tiled=True),
        lax.all_to_all(send_scaled, "group", split_axis=0, concat_axis=0, tiled=True),
    )
    grad_gate, grad_up, grad_down, partial_rows = slice_backward(
        rows_x.reshape(block_rows, features),
        rows_scaled.reshape(block_rows, features),
        w_gate[0],
        w_up[0],
        w_down[0],
    )
    returned = lax.all_to_all(
        partial_rows.reshape(groups, capacity, features),
        "group",
        split_axis=0,
        concat_axis=0,
        tiled=True,
    )
    returned = returned.reshape(block_rows, features)
    row_numbers = jnp.arange(tokens.shape[0] * lax.axis_size("member"), dtype=jnp.int32)
    selector = (row_numbers[:, None] == flat_slots[None, :]).astype(jnp.float32)
    summed = lax.psum_scatter(
        jnp.dot(
            selector, returned, precision=lax.Precision.HIGHEST, preferred_element_type=jnp.float32
        ),
        "member",
        scatter_dimension=0,
        tiled=True,
    )
    return (summed.astype(jnp.bfloat16), grad_gate[None], grad_up[None], grad_down[None])


def shards(tokens, grad_out, route_token, *rest):
    devices = lax.axis_size("group") * lax.axis_size("member")
    _, groups, experts, capacity = route_token.shape
    dense = devices * tokens.shape[0] <= groups * capacity and experts == 1
    paired = tokens.shape[0] == 1 and devices & (devices - 1) == 0
    body = dense_shards if dense and paired else routed_shards
    return body(tokens, grad_out, route_token, *rest)


def solution(mesh):
    placed = (
        P(("group", "member"), None),
        P(("group", "member"), None),
        P("group", None, None, None),
        P("group", None, None),
        P("group", None, None, None),
        P(("group", "member"), None, None),
        P(("group", "member"), None, None),
        P(("group", "member"), None, None),
    )
    return jax.shard_map(
        shards,
        mesh=mesh,
        in_specs=placed,
        out_specs=(
            P(("group", "member"), None),
            P(("group", "member"), None, None),
            P(("group", "member"), None, None),
            P(("group", "member"), None, None),
        ),
        check_vma=False,
    )
```

```python
import functools

import jax
import jax.numpy as jnp
from jax import lax
from jax.experimental import pallas as pl
from jax.experimental.pallas import tpu as pltpu
from jax.sharding import PartitionSpec as P

LANES = 128
PARTS = 4
AXES = ("group", "member")
VMEM = pl.BlockSpec(memory_space=pltpu.VMEM)
HBM = pl.BlockSpec(memory_space=pltpu.HBM)
SMEM = pl.BlockSpec(memory_space=pltpu.SMEM)
NT = (((1,), (1,)), ((), ()))
TN = (((0,), (0,)), ((), ()))


def pack_kernel(
    chunks,
    tokens_hbm,
    grad_hbm,
    token_hbm,
    count_hbm,
    prob_hbm,
    out_ref,
    rows_ref,
    tokens_ref,
    grad_ref,
    token_ref,
    count_ref,
    prob_ref,
    sems,
):
    pairs = (
        (token_hbm, token_ref),
        (count_hbm, count_ref),
        (prob_hbm, prob_ref),
        (tokens_hbm, tokens_ref),
        (grad_hbm, grad_ref),
    )
    copies = [pltpu.make_async_copy(*pair, sems.at[n]) for n, pair in enumerate(pairs)]
    for copy in copies:
        copy.start()
    for copy in copies:
        copy.wait()
    me = lax.axis_index("member")
    groups, _, capacity = token_ref.shape[1:]
    token_row = tokens_ref[...].astype(jnp.float32)
    grad_row = grad_ref[...].astype(jnp.float32)
    for k in range(chunks):
        part = slice(k * LANES, (k + 1) * LANES)
        rows_ref[k : k + 1, :] = token_row[:, part]
        rows_ref[chunks + k : chunks + k + 1, :] = grad_row[:, part]
    rows = rows_ref[...]
    is_token = lax.broadcasted_iota(jnp.int32, rows.shape, 0) < chunks
    places = out_ref.shape[0] // groups
    for g in range(groups):
        weight = jnp.float32(0)
        for p in range(capacity):
            live = (token_ref[0, g, 0, p] == me) & (p < count_ref[0, 0, g])
            weight = weight + jnp.where(live, prob_ref[0, g, 0, p], 0.0)
        packed = jnp.where(is_token, rows, rows * weight).astype(jnp.bfloat16)
        for n in range(places):
            out_ref[g * places + n] = packed


def unpack_rows(chunks, packed_ref, wide_ref, rows_ref):
    tokens, rows, _ = packed_ref.shape
    wide_ref[...] = packed_ref[...].astype(jnp.float32).reshape(tokens * rows, LANES)
    for k in range(rows):
        column = wide_ref[pl.ds(k, tokens, stride=rows), :]
        rows_ref[:, k * LANES : (k + 1) * LANES] = column.astype(jnp.bfloat16)


def unpack_kernel(chunks, mine_ref, rows_ref, wide_ref):
    unpack_rows(chunks, mine_ref, wide_ref, rows_ref)


def partial_kernel(
    chunks,
    mine_ref,
    other_ref,
    gate_ref,
    up_ref,
    down_ref,
    sent_ref,
    rows_ref,
    acts_ref,
    wide_ref,
    spread_ref,
):
    count = mine_ref.shape[0]
    tokens = 2 * count
    features = chunks * LANES
    units = gate_ref.shape[1]
    rows_ref[:count] = mine_ref[...]
    unpack_rows(chunks, other_ref, wide_ref, rows_ref.at[pl.ds(count, count)])
    x, scaled = rows_ref[:, :features], rows_ref[:, features:]
    both = jnp.concatenate([gate_ref[0], up_ref[0]], axis=0)
    values = lax.dot_general(both, x, NT, preferred_element_type=jnp.float32)
    gate_value, up_value = values[:units], values[units:]
    d_hidden = lax.dot_general(down_ref[0], scaled, NT, preferred_element_type=jnp.float32)
    sigma_gate = jax.nn.sigmoid(gate_value)
    active = gate_value * sigma_gate
    d_gate = d_hidden * up_value * sigma_gate * (1.0 + gate_value * (1.0 - sigma_gate))
    acts_ref[0:units] = d_gate.astype(jnp.bfloat16)
    acts_ref[units : 2 * units] = (d_hidden * active).astype(jnp.bfloat16)
    acts_ref[2 * units :] = (active * up_value).astype(jnp.bfloat16)
    partial = lax.dot_general(
        acts_ref[: 2 * units], both, TN, preferred_element_type=jnp.float32
    )
    blocks, height = sent_ref.shape[2:4]
    sent_rows = blocks * height
    for k in range(chunks):
        spread_ref[pl.ds(k, tokens, stride=sent_rows), :] = partial[:, k * LANES : (k + 1) * LANES]
    core = lax.rem(lax.axis_index("member"), 2)
    for n in range(2):
        for i in range(count):
            for k in range(blocks):
                first = (n * count + i) * sent_rows + k * height
                sent_ref[i, core ^ n, k] = spread_ref[first : first + height, :].astype(jnp.bfloat16)


def grads_kernel(
    features, rows_ref, acts_ref, gate_out, up_out, down_out, held_ref, sems
):
    units = held_ref.shape[1]
    height = units // PARTS
    copies = []
    for n, (out, first) in enumerate(((gate_out, 0), (up_out, 0), (down_out, features))):
        right = rows_ref[:, first : first + features]
        for k in range(PARTS):
            left = acts_ref[n * units + k * height : n * units + (k + 1) * height, :]
            held_ref[n, k * height : (k + 1) * height] = jnp.dot(
                left, right, preferred_element_type=jnp.float32
            ).astype(jnp.bfloat16)
            part = pl.ds(k * height, height)
            copies.append(
                pltpu.make_async_copy(held_ref.at[n, part], out.at[0, part], sems.at[PARTS * n + k])
            )
            copies[-1].start()
    for copy in copies:
        copy.wait()


def sum_kernel(back_ref, out_ref):
    count, blocks, height, _ = back_ref.shape
    for k in range(blocks):
        total = back_ref[0, k].astype(jnp.float32)
        for n in range(1, count):
            total = total + back_ref[n, k].astype(jnp.float32)
        for r in range(height):
            part = pl.ds((k * height + r) * LANES, LANES)
            out_ref[:, part] = total[r : r + 1, :].astype(jnp.bfloat16)


def exchange(value, distance):
    count = lax.axis_size("group") * lax.axis_size("member")
    return lax.ppermute(value, AXES, [(i, i ^ distance) for i in range(count)])


def in_hbm(value):
    return pltpu.with_memory_space_constraint(value, pltpu.HBM)


def dense_shards(tokens, grad_out, route_token, route_count, route_prob, w_gate, w_up, w_down):
    features = tokens.shape[1]
    units = w_gate.shape[1]
    chunks = features // LANES
    count = lax.axis_size("group") * lax.axis_size("member")
    half = count // 2
    rows = 2 * chunks
    arguments = (tokens, grad_out, route_token, jnp.swapaxes(route_count, 1, 2), route_prob)
    spaces = (pltpu.VMEM, pltpu.VMEM, pltpu.SMEM, pltpu.SMEM, pltpu.SMEM)
    copies = pl.pallas_call(
        functools.partial(pack_kernel, chunks),
        out_shape=pltpu.VMEM((half, rows, LANES), jnp.bfloat16),
        in_specs=[HBM] * 5,
        out_specs=VMEM,
        scratch_shapes=[pltpu.VMEM((rows, LANES), jnp.float32)]
        + [space(value.shape, value.dtype) for space, value in zip(spaces, arguments)]
        + [pltpu.SemaphoreType.DMA((5,))],
        compiler_params=pltpu.CompilerParams(vmem_limit_bytes=4 * 1024 * 1024),
        cost_estimate=pl.CostEstimate(
            flops=40000 * units * features,
            bytes_accessed=16 * units * features,
            transcendentals=0,
        ),
        name="pack_rows",
    )(*[in_hbm(value) for value in arguments])
    cores = [list(range(c, count, 2)) for c in range(2)]
    trade = functools.partial(
        lax.all_to_all,
        axis_name=AXES,
        split_axis=0,
        concat_axis=0,
        tiled=True,
        axis_index_groups=cores,
    )
    mine = trade(copies)
    other = exchange(mine, 1)
    wide = pltpu.VMEM((half * rows, LANES), jnp.float32)
    unpacked = pl.pallas_call(
        functools.partial(unpack_kernel, chunks),
        out_shape=pltpu.VMEM((half, 2 * features), jnp.bfloat16),
        in_specs=[VMEM],
        out_specs=VMEM,
        scratch_shapes=[wide],
        compiler_params=pltpu.CompilerParams(vmem_limit_bytes=2 * 1024 * 1024),
        name="unpack_rows",
    )(mine)
    sent, both, acts = pl.pallas_call(
        functools.partial(partial_kernel, chunks),
        out_shape=(
            jax.ShapeDtypeStruct((half, 2, chunks // 4, 4, LANES), jnp.bfloat16),
            pltpu.VMEM((count, 2 * features), jnp.bfloat16),
            pltpu.VMEM((3 * units, count), jnp.bfloat16),
        ),
        in_specs=[VMEM] * 5,
        out_specs=(VMEM,) * 3,
        scratch_shapes=[wide, pltpu.VMEM((count * chunks, LANES), jnp.float32)],
        compiler_params=pltpu.CompilerParams(vmem_limit_bytes=16 * 1024 * 1024),
        name="partial_rows",
    )(unpacked, other, w_gate, w_up, w_down)
    grad_shape = jax.ShapeDtypeStruct((1, units, features), jnp.bfloat16)
    grad_gate, grad_up, grad_down = pl.pallas_call(
        functools.partial(grads_kernel, features),
        out_shape=(grad_shape,) * 3,
        in_specs=[VMEM] * 2,
        out_specs=(HBM, HBM, HBM),
        scratch_shapes=[
            pltpu.VMEM((3, units, features), jnp.bfloat16),
            pltpu.SemaphoreType.DMA((3 * PARTS,)),
        ],
        compiler_params=pltpu.CompilerParams(vmem_limit_bytes=16 * 1024 * 1024),
        cost_estimate=pl.CostEstimate(
            flops=6 * count * units * features,
            bytes_accessed=6 * units * features,
            transcendentals=0,
        ),
        name="weight_grads",
    )(both, acts)
    back = lax.all_to_all(
        sent.reshape(count, chunks // 4, 4, LANES), AXES, 0, 0, tiled=True
    )
    grad_tokens = pl.pallas_call(
        sum_kernel,
        out_shape=jax.ShapeDtypeStruct((1, features), jnp.bfloat16),
        in_specs=[VMEM],
        out_specs=VMEM,
        compiler_params=pltpu.CompilerParams(vmem_limit_bytes=4 * 1024 * 1024),
        name="sum_rows",
    )(back)
    return grad_tokens, grad_gate, grad_up, grad_down


def slice_backward(rows_x, rows_scaled, gate_weight, up_weight, down_weight):
    gate_value = jnp.dot(rows_x, gate_weight.T, preferred_element_type=jnp.float32)
    up_value = jnp.dot(rows_x, up_weight.T, preferred_element_type=jnp.float32)
    sigma_gate = jax.nn.sigmoid(gate_value)
    active = gate_value * sigma_gate
    hidden = (active * up_value).astype(jnp.bfloat16)
    d_hidden = jnp.dot(rows_scaled, down_weight.T, preferred_element_type=jnp.float32)
    d_gate = (d_hidden * up_value * sigma_gate * (1.0 + gate_value * (1.0 - sigma_gate))).astype(
        jnp.bfloat16
    )
    d_up = (d_hidden * active).astype(jnp.bfloat16)
    grad_down = jnp.dot(hidden.T, rows_scaled, preferred_element_type=jnp.float32).astype(
        jnp.bfloat16
    )
    grad_gate = jnp.dot(d_gate.T, rows_x, preferred_element_type=jnp.float32).astype(jnp.bfloat16)
    grad_up = jnp.dot(d_up.T, rows_x, preferred_element_type=jnp.float32).astype(jnp.bfloat16)
    partial_rows = jnp.dot(d_gate, gate_weight, preferred_element_type=jnp.float32)
    partial_rows = partial_rows + jnp.dot(d_up, up_weight, preferred_element_type=jnp.float32)
    return (grad_gate, grad_up, grad_down, partial_rows)


def routed_shards(tokens, grad_out, route_token, route_count, route_prob, w_gate, w_up, w_down):
    groups = route_token.shape[1]
    capacity = route_token.shape[3]
    features = tokens.shape[1]
    block_rows = groups * capacity
    split_count = max(8, lax.axis_size("member") // 8)
    expert_local = lax.axis_index("member") // split_count
    slot_tokens = lax.dynamic_index_in_dim(route_token[0], expert_local, 1, keepdims=False)
    slot_counts = lax.dynamic_index_in_dim(route_count[0], expert_local, 1, keepdims=False)
    slot_probs = lax.dynamic_index_in_dim(route_prob[0], expert_local, 1, keepdims=False)
    slot_index = jnp.arange(capacity, dtype=jnp.int32)[None, :]
    live = (slot_index < slot_counts[:, None]).astype(jnp.float32)
    slot_weights = (slot_probs * live).reshape(-1)
    flat_slots = slot_tokens.reshape(-1)
    group_x, group_dy = (
        lax.all_gather(tokens, "member", axis=0, tiled=True),
        lax.all_gather(grad_out, "member", axis=0, tiled=True),
    )
    picked_x = jnp.take(group_x, flat_slots, axis=0)
    picked_dy = jnp.take(group_dy, flat_slots, axis=0)
    scaled = (slot_weights[:, None] * picked_dy.astype(jnp.float32)).astype(jnp.bfloat16)
    send_x = picked_x.reshape(groups, capacity, features)
    send_scaled = scaled.reshape(groups, capacity, features)
    rows_x, rows_scaled = (
        lax.all_to_all(send_x, "group", split_axis=0, concat_axis=0, tiled=True),
        lax.all_to_all(send_scaled, "group", split_axis=0, concat_axis=0, tiled=True),
    )
    grad_gate, grad_up, grad_down, partial_rows = slice_backward(
        rows_x.reshape(block_rows, features),
        rows_scaled.reshape(block_rows, features),
        w_gate[0],
        w_up[0],
        w_down[0],
    )
    returned = lax.all_to_all(
        partial_rows.reshape(groups, capacity, features),
        "group",
        split_axis=0,
        concat_axis=0,
        tiled=True,
    )
    returned = returned.reshape(block_rows, features)
    row_numbers = jnp.arange(tokens.shape[0] * lax.axis_size("member"), dtype=jnp.int32)
    selector = (row_numbers[:, None] == flat_slots[None, :]).astype(jnp.float32)
    summed = lax.psum_scatter(
        jnp.dot(
            selector, returned, precision=lax.Precision.HIGHEST, preferred_element_type=jnp.float32
        ),
        "member",
        scatter_dimension=0,
        tiled=True,
    )
    return (summed.astype(jnp.bfloat16), grad_gate[None], grad_up[None], grad_down[None])


def shards(tokens, grad_out, route_token, *rest):
    devices = lax.axis_size("group") * lax.axis_size("member")
    _, groups, experts, capacity = route_token.shape
    dense = devices * tokens.shape[0] <= groups * capacity and experts == 1
    paired = tokens.shape[0] == 1 and devices & (devices - 1) == 0
    body = dense_shards if dense and paired else routed_shards
    return body(tokens, grad_out, route_token, *rest)


def solution(mesh):
    placed = (
        P(("group", "member"), None),
        P(("group", "member"), None),
        P("group", None, None, None),
        P("group", None, None),
        P("group", None, None, None),
        P(("group", "member"), None, None),
        P(("group", "member"), None, None),
        P(("group", "member"), None, None),
    )
    return jax.shard_map(
        shards,
        mesh=mesh,
        in_specs=placed,
        out_specs=(
            P(("group", "member"), None),
            P(("group", "member"), None, None),
            P(("group", "member"), None, None),
            P(("group", "member"), None, None),
        ),
        check_vma=False,
    )
```

```python
import functools

import jax
import jax.numpy as jnp
from jax import lax
from jax.experimental import pallas as pl
from jax.experimental.pallas import tpu as pltpu
from jax.sharding import PartitionSpec as P

LANES = 128
PARTS = 4
AXES = ("group", "member")
VMEM = pl.BlockSpec(memory_space=pltpu.VMEM)
HBM = pl.BlockSpec(memory_space=pltpu.HBM)
SMEM = pl.BlockSpec(memory_space=pltpu.SMEM)
NT = (((1,), (1,)), ((), ()))
TN = (((0,), (0,)), ((), ()))


def pack_kernel(
    chunks,
    tokens_hbm,
    grad_hbm,
    token_hbm,
    count_hbm,
    prob_hbm,
    out_ref,
    rows_ref,
    tokens_ref,
    grad_ref,
    token_ref,
    count_ref,
    prob_ref,
    sems,
):
    pairs = (
        (token_hbm, token_ref),
        (count_hbm, count_ref),
        (prob_hbm, prob_ref),
        (tokens_hbm, tokens_ref),
        (grad_hbm, grad_ref),
    )
    copies = [pltpu.make_async_copy(*pair, sems.at[n]) for n, pair in enumerate(pairs)]
    for copy in copies:
        copy.start()
    for copy in copies:
        copy.wait()
    me = lax.axis_index("member")
    groups, _, capacity = token_ref.shape[1:]
    token_row = tokens_ref[...].astype(jnp.float32)
    grad_row = grad_ref[...].astype(jnp.float32)
    for k in range(chunks):
        part = slice(k * LANES, (k + 1) * LANES)
        rows_ref[k : k + 1, :] = token_row[:, part]
        rows_ref[chunks + k : chunks + k + 1, :] = grad_row[:, part]
    rows = rows_ref[...]
    is_token = lax.broadcasted_iota(jnp.int32, rows.shape, 0) < chunks
    places = out_ref.shape[0] // groups
    for g in range(groups):
        weight = jnp.float32(0)
        for p in range(capacity):
            live = (token_ref[0, g, 0, p] == me) & (p < count_ref[0, 0, g])
            weight = weight + jnp.where(live, prob_ref[0, g, 0, p], 0.0)
        packed = jnp.where(is_token, rows, rows * weight).astype(jnp.bfloat16)
        for n in range(places):
            out_ref[g * places + n] = packed


def unpack_kernel(chunks, packed_ref, x_ref, scaled_ref, wide_ref):
    tokens, rows, _ = packed_ref.shape
    wide_ref[...] = packed_ref[...].astype(jnp.float32).reshape(tokens * rows, LANES)
    for n, out_ref in enumerate((x_ref, scaled_ref)):
        for k in range(chunks):
            column = wide_ref[pl.ds(n * chunks + k, tokens, stride=rows), :]
            out_ref[:, k * LANES : (k + 1) * LANES] = column.astype(jnp.bfloat16)


def first_kernel(mine_ref, other_ref, gate_ref, up_ref, values_ref):
    x = jnp.concatenate([mine_ref[...], other_ref[...]], axis=0)
    both = jnp.concatenate([gate_ref[0], up_ref[0]], axis=0)
    values_ref[...] = lax.dot_general(both, x, NT, preferred_element_type=jnp.float32)


def partial_kernel(
    chunks,
    values_ref,
    mine_ref,
    other_ref,
    gate_ref,
    up_ref,
    down_ref,
    sent_ref,
    acts_ref,
    spread_ref,
):
    count = mine_ref.shape[0]
    tokens = 2 * count
    units = gate_ref.shape[1]
    scaled = jnp.concatenate([mine_ref[...], other_ref[...]], axis=0)
    d_hidden = lax.dot_general(down_ref[0], scaled, NT, preferred_element_type=jnp.float32)
    gate_value, up_value = values_ref[:units], values_ref[units:]
    sigma_gate = jax.nn.sigmoid(gate_value)
    active = gate_value * sigma_gate
    d_gate = d_hidden * up_value * sigma_gate * (1.0 + gate_value * (1.0 - sigma_gate))
    acts_ref[0:units] = d_gate.astype(jnp.bfloat16)
    acts_ref[units : 2 * units] = (d_hidden * active).astype(jnp.bfloat16)
    acts_ref[2 * units :] = (active * up_value).astype(jnp.bfloat16)
    both = jnp.concatenate([gate_ref[0], up_ref[0]], axis=0)
    partial = lax.dot_general(
        acts_ref[: 2 * units], both, TN, preferred_element_type=jnp.float32
    )
    blocks, height = sent_ref.shape[2:4]
    sent_rows = blocks * height
    for k in range(chunks):
        spread_ref[pl.ds(k, tokens, stride=sent_rows), :] = partial[:, k * LANES : (k + 1) * LANES]
    core = lax.rem(lax.axis_index("member"), 2)
    for n in range(2):
        for i in range(count):
            for k in range(blocks):
                first = (n * count + i) * sent_rows + k * height
                sent_ref[i, core ^ n, k] = spread_ref[first : first + height, :].astype(jnp.bfloat16)


def grads_kernel(
    mine_x_ref,
    other_x_ref,
    mine_scaled_ref,
    other_scaled_ref,
    acts_ref,
    gate_out,
    up_out,
    down_out,
    held_ref,
    sems,
):
    units = held_ref.shape[1]
    height = units // PARTS
    x = jnp.concatenate([mine_x_ref[...], other_x_ref[...]], axis=0)
    scaled = jnp.concatenate([mine_scaled_ref[...], other_scaled_ref[...]], axis=0)
    copies = []
    for n, (out, right) in enumerate(((gate_out, x), (up_out, x), (down_out, scaled))):
        for k in range(PARTS):
            left = acts_ref[n * units + k * height : n * units + (k + 1) * height, :]
            held_ref[n, k * height : (k + 1) * height] = jnp.dot(
                left, right, preferred_element_type=jnp.float32
            ).astype(jnp.bfloat16)
            part = pl.ds(k * height, height)
            copies.append(
                pltpu.make_async_copy(held_ref.at[n, part], out.at[0, part], sems.at[PARTS * n + k])
            )
            copies[-1].start()
    for copy in copies:
        copy.wait()


def sum_kernel(back_ref, out_ref):
    count, blocks, height, _ = back_ref.shape
    for k in range(blocks):
        total = back_ref[0, k].astype(jnp.float32)
        for n in range(1, count):
            total = total + back_ref[n, k].astype(jnp.float32)
        for r in range(height):
            part = pl.ds((k * height + r) * LANES, LANES)
            out_ref[:, part] = total[r : r + 1, :].astype(jnp.bfloat16)


def exchange(value, distance):
    count = lax.axis_size("group") * lax.axis_size("member")
    return lax.ppermute(value, AXES, [(i, i ^ distance) for i in range(count)])


def in_hbm(value):
    return pltpu.with_memory_space_constraint(value, pltpu.HBM)


def dense_shards(tokens, grad_out, route_token, route_count, route_prob, w_gate, w_up, w_down):
    features = tokens.shape[1]
    units = w_gate.shape[1]
    chunks = features // LANES
    count = lax.axis_size("group") * lax.axis_size("member")
    half = count // 2
    rows = 2 * chunks
    arguments = (tokens, grad_out, route_token, jnp.swapaxes(route_count, 1, 2), route_prob)
    spaces = (pltpu.VMEM, pltpu.VMEM, pltpu.SMEM, pltpu.SMEM, pltpu.SMEM)
    copies = pl.pallas_call(
        functools.partial(pack_kernel, chunks),
        out_shape=pltpu.VMEM((half, rows, LANES), jnp.bfloat16),
        in_specs=[HBM] * 5,
        out_specs=VMEM,
        scratch_shapes=[pltpu.VMEM((rows, LANES), jnp.float32)]
        + [space(value.shape, value.dtype) for space, value in zip(spaces, arguments)]
        + [pltpu.SemaphoreType.DMA((5,))],
        compiler_params=pltpu.CompilerParams(vmem_limit_bytes=4 * 1024 * 1024),
        cost_estimate=pl.CostEstimate(
            flops=40000 * units * features,
            bytes_accessed=16 * units * features,
            transcendentals=0,
        ),
        name="pack_rows",
    )(*[in_hbm(value) for value in arguments])
    cores = [list(range(c, count, 2)) for c in range(2)]
    trade = functools.partial(
        lax.all_to_all,
        axis_name=AXES,
        split_axis=0,
        concat_axis=0,
        tiled=True,
        axis_index_groups=cores,
    )
    mine = trade(copies)
    half_rows = pltpu.VMEM((half, features), jnp.bfloat16)
    mine_x, mine_scaled = pl.pallas_call(
        functools.partial(unpack_kernel, chunks),
        out_shape=(half_rows,) * 2,
        in_specs=[VMEM],
        out_specs=(VMEM,) * 2,
        scratch_shapes=[pltpu.VMEM((half * rows, LANES), jnp.float32)],
        compiler_params=pltpu.CompilerParams(vmem_limit_bytes=2 * 1024 * 1024),
        name="unpack_rows",
    )(mine)
    other_x = exchange(mine_x, 1)
    other_scaled = exchange(mine_scaled, 1)
    values = pl.pallas_call(
        first_kernel,
        out_shape=pltpu.VMEM((2 * units, count), jnp.float32),
        in_specs=[VMEM] * 4,
        out_specs=VMEM,
        compiler_params=pltpu.CompilerParams(vmem_limit_bytes=8 * 1024 * 1024),
        name="gate_up",
    )(mine_x, other_x, w_gate, w_up)
    sent, acts = pl.pallas_call(
        functools.partial(partial_kernel, chunks),
        out_shape=(
            jax.ShapeDtypeStruct((half, 2, chunks // 4, 4, LANES), jnp.bfloat16),
            pltpu.VMEM((3 * units, count), jnp.bfloat16),
        ),
        in_specs=[VMEM] * 6,
        out_specs=(VMEM,) * 2,
        scratch_shapes=[pltpu.VMEM((count * chunks, LANES), jnp.float32)],
        compiler_params=pltpu.CompilerParams(vmem_limit_bytes=16 * 1024 * 1024),
        name="partial_rows",
    )(values, mine_scaled, other_scaled, w_gate, w_up, w_down)
    grad_shape = jax.ShapeDtypeStruct((1, units, features), jnp.bfloat16)
    grad_gate, grad_up, grad_down = pl.pallas_call(
        grads_kernel,
        out_shape=(grad_shape,) * 3,
        in_specs=[VMEM] * 5,
        out_specs=(HBM, HBM, HBM),
        scratch_shapes=[
            pltpu.VMEM((3, units, features), jnp.bfloat16),
            pltpu.SemaphoreType.DMA((3 * PARTS,)),
        ],
        compiler_params=pltpu.CompilerParams(vmem_limit_bytes=16 * 1024 * 1024),
        cost_estimate=pl.CostEstimate(
            flops=6 * count * units * features,
            bytes_accessed=6 * units * features,
            transcendentals=0,
        ),
        name="weight_grads",
    )(mine_x, other_x, mine_scaled, other_scaled, acts)
    back = lax.all_to_all(
        sent.reshape(count, chunks // 4, 4, LANES), AXES, 0, 0, tiled=True
    )
    grad_tokens = pl.pallas_call(
        sum_kernel,
        out_shape=jax.ShapeDtypeStruct((1, features), jnp.bfloat16),
        in_specs=[VMEM],
        out_specs=VMEM,
        compiler_params=pltpu.CompilerParams(vmem_limit_bytes=4 * 1024 * 1024),
        name="sum_rows",
    )(back)
    return grad_tokens, grad_gate, grad_up, grad_down


def slice_backward(rows_x, rows_scaled, gate_weight, up_weight, down_weight):
    gate_value = jnp.dot(rows_x, gate_weight.T, preferred_element_type=jnp.float32)
    up_value = jnp.dot(rows_x, up_weight.T, preferred_element_type=jnp.float32)
    sigma_gate = jax.nn.sigmoid(gate_value)
    active = gate_value * sigma_gate
    hidden = (active * up_value).astype(jnp.bfloat16)
    d_hidden = jnp.dot(rows_scaled, down_weight.T, preferred_element_type=jnp.float32)
    d_gate = (d_hidden * up_value * sigma_gate * (1.0 + gate_value * (1.0 - sigma_gate))).astype(
        jnp.bfloat16
    )
    d_up = (d_hidden * active).astype(jnp.bfloat16)
    grad_down = jnp.dot(hidden.T, rows_scaled, preferred_element_type=jnp.float32).astype(
        jnp.bfloat16
    )
    grad_gate = jnp.dot(d_gate.T, rows_x, preferred_element_type=jnp.float32).astype(jnp.bfloat16)
    grad_up = jnp.dot(d_up.T, rows_x, preferred_element_type=jnp.float32).astype(jnp.bfloat16)
    partial_rows = jnp.dot(d_gate, gate_weight, preferred_element_type=jnp.float32)
    partial_rows = partial_rows + jnp.dot(d_up, up_weight, preferred_element_type=jnp.float32)
    return (grad_gate, grad_up, grad_down, partial_rows)


def routed_shards(tokens, grad_out, route_token, route_count, route_prob, w_gate, w_up, w_down):
    groups = route_token.shape[1]
    capacity = route_token.shape[3]
    features = tokens.shape[1]
    block_rows = groups * capacity
    split_count = max(8, lax.axis_size("member") // 8)
    expert_local = lax.axis_index("member") // split_count
    slot_tokens = lax.dynamic_index_in_dim(route_token[0], expert_local, 1, keepdims=False)
    slot_counts = lax.dynamic_index_in_dim(route_count[0], expert_local, 1, keepdims=False)
    slot_probs = lax.dynamic_index_in_dim(route_prob[0], expert_local, 1, keepdims=False)
    slot_index = jnp.arange(capacity, dtype=jnp.int32)[None, :]
    live = (slot_index < slot_counts[:, None]).astype(jnp.float32)
    slot_weights = (slot_probs * live).reshape(-1)
    flat_slots = slot_tokens.reshape(-1)
    group_x, group_dy = (
        lax.all_gather(tokens, "member", axis=0, tiled=True),
        lax.all_gather(grad_out, "member", axis=0, tiled=True),
    )
    picked_x = jnp.take(group_x, flat_slots, axis=0)
    picked_dy = jnp.take(group_dy, flat_slots, axis=0)
    scaled = (slot_weights[:, None] * picked_dy.astype(jnp.float32)).astype(jnp.bfloat16)
    send_x = picked_x.reshape(groups, capacity, features)
    send_scaled = scaled.reshape(groups, capacity, features)
    rows_x, rows_scaled = (
        lax.all_to_all(send_x, "group", split_axis=0, concat_axis=0, tiled=True),
        lax.all_to_all(send_scaled, "group", split_axis=0, concat_axis=0, tiled=True),
    )
    grad_gate, grad_up, grad_down, partial_rows = slice_backward(
        rows_x.reshape(block_rows, features),
        rows_scaled.reshape(block_rows, features),
        w_gate[0],
        w_up[0],
        w_down[0],
    )
    returned = lax.all_to_all(
        partial_rows.reshape(groups, capacity, features),
        "group",
        split_axis=0,
        concat_axis=0,
        tiled=True,
    )
    returned = returned.reshape(block_rows, features)
    row_numbers = jnp.arange(tokens.shape[0] * lax.axis_size("member"), dtype=jnp.int32)
    selector = (row_numbers[:, None] == flat_slots[None, :]).astype(jnp.float32)
    summed = lax.psum_scatter(
        jnp.dot(
            selector, returned, precision=lax.Precision.HIGHEST, preferred_element_type=jnp.float32
        ),
        "member",
        scatter_dimension=0,
        tiled=True,
    )
    return (summed.astype(jnp.bfloat16), grad_gate[None], grad_up[None], grad_down[None])


def shards(tokens, grad_out, route_token, *rest):
    devices = lax.axis_size("group") * lax.axis_size("member")
    _, groups, experts, capacity = route_token.shape
    dense = devices * tokens.shape[0] <= groups * capacity and experts == 1
    paired = tokens.shape[0] == 1 and devices & (devices - 1) == 0
    body = dense_shards if dense and paired else routed_shards
    return body(tokens, grad_out, route_token, *rest)


def solution(mesh):
    placed = (
        P(("group", "member"), None),
        P(("group", "member"), None),
        P("group", None, None, None),
        P("group", None, None),
        P("group", None, None, None),
        P(("group", "member"), None, None),
        P(("group", "member"), None, None),
        P(("group", "member"), None, None),
    )
    return jax.shard_map(
        shards,
        mesh=mesh,
        in_specs=placed,
        out_specs=(
            P(("group", "member"), None),
            P(("group", "member"), None, None),
            P(("group", "member"), None, None),
            P(("group", "member"), None, None),
        ),
        check_vma=False,
    )
```

```python
import functools

import jax
import jax.numpy as jnp
from jax import lax
from jax.experimental import pallas as pl
from jax.experimental.pallas import tpu as pltpu
from jax.sharding import PartitionSpec as P

LANES = 128
PARTS = 4
AXES = ("group", "member")
VMEM = pl.BlockSpec(memory_space=pltpu.VMEM)
HBM = pl.BlockSpec(memory_space=pltpu.HBM)
SMEM = pl.BlockSpec(memory_space=pltpu.SMEM)
NT = (((1,), (1,)), ((), ()))
TN = (((0,), (0,)), ((), ()))


def pack_kernel(
    chunks,
    tokens_hbm,
    grad_hbm,
    token_hbm,
    count_hbm,
    prob_hbm,
    out_ref,
    rows_ref,
    tokens_ref,
    grad_ref,
    token_ref,
    count_ref,
    prob_ref,
    sems,
):
    pairs = (
        (token_hbm, token_ref),
        (count_hbm, count_ref),
        (prob_hbm, prob_ref),
        (tokens_hbm, tokens_ref),
        (grad_hbm, grad_ref),
    )
    copies = [pltpu.make_async_copy(*pair, sems.at[n]) for n, pair in enumerate(pairs)]
    for copy in copies:
        copy.start()
    for copy in copies:
        copy.wait()
    me = lax.axis_index("member")
    groups, _, capacity = token_ref.shape[1:]
    token_row = tokens_ref[...].astype(jnp.float32)
    grad_row = grad_ref[...].astype(jnp.float32)
    for k in range(chunks):
        part = slice(k * LANES, (k + 1) * LANES)
        rows_ref[k : k + 1, :] = token_row[:, part]
        rows_ref[chunks + k : chunks + k + 1, :] = grad_row[:, part]
    rows = rows_ref[...]
    is_token = lax.broadcasted_iota(jnp.int32, rows.shape, 0) < chunks
    places = out_ref.shape[0] // groups
    for g in range(groups):
        weight = jnp.float32(0)
        for p in range(capacity):
            live = (token_ref[0, g, 0, p] == me) & (p < count_ref[0, 0, g])
            weight = weight + jnp.where(live, prob_ref[0, g, 0, p], 0.0)
        packed = jnp.where(is_token, rows, rows * weight).astype(jnp.bfloat16)
        for n in range(places):
            out_ref[g * places + n] = packed


def unpack_rows(chunks, packed_ref, wide_ref, rows_ref):
    tokens, rows, _ = packed_ref.shape
    wide_ref[...] = packed_ref[...].astype(jnp.float32).reshape(tokens * rows, LANES)
    for k in range(rows):
        column = wide_ref[pl.ds(k, tokens, stride=rows), :]
        rows_ref[:, k * LANES : (k + 1) * LANES] = column.astype(jnp.bfloat16)


def unpack_kernel(chunks, mine_ref, rows_ref, wide_ref):
    unpack_rows(chunks, mine_ref, wide_ref, rows_ref)


def partial_kernel(
    chunks,
    mine_ref,
    other_ref,
    gate_ref,
    up_ref,
    down_ref,
    sent_ref,
    rows_ref,
    acts_ref,
    wide_ref,
    spread_ref,
):
    count = mine_ref.shape[0]
    tokens = 2 * count
    features = chunks * LANES
    units = gate_ref.shape[1]
    rows_ref[:count] = mine_ref[...]
    unpack_rows(chunks, other_ref, wide_ref, rows_ref.at[pl.ds(count, count)])
    x, scaled = rows_ref[:, :features], rows_ref[:, features:]
    both = jnp.concatenate([gate_ref[0], up_ref[0]], axis=0)
    values = lax.dot_general(both, x, NT, preferred_element_type=jnp.float32)
    gate_value, up_value = values[:units], values[units:]
    d_hidden = lax.dot_general(down_ref[0], scaled, NT, preferred_element_type=jnp.float32)
    sigma_gate = jax.nn.sigmoid(gate_value)
    active = gate_value * sigma_gate
    d_gate = d_hidden * up_value * sigma_gate * (1.0 + gate_value * (1.0 - sigma_gate))
    acts_ref[0:units] = d_gate.astype(jnp.bfloat16)
    acts_ref[units : 2 * units] = (d_hidden * active).astype(jnp.bfloat16)
    acts_ref[2 * units :] = (active * up_value).astype(jnp.bfloat16)
    partial = lax.dot_general(
        acts_ref[: 2 * units], both, TN, preferred_element_type=jnp.float32
    )
    blocks, height = sent_ref.shape[2:4]
    sent_rows = blocks * height
    for k in range(chunks):
        spread_ref[pl.ds(k, tokens, stride=sent_rows), :] = partial[:, k * LANES : (k + 1) * LANES]
    core = lax.rem(lax.axis_index("member"), 2)
    for n in range(2):
        for i in range(count):
            for k in range(blocks):
                first = (n * count + i) * sent_rows + k * height
                sent_ref[i, core ^ n, k] = spread_ref[first : first + height, :].astype(jnp.bfloat16)


def grads_kernel(
    features, rows_ref, acts_ref, gate_out, up_out, down_out, held_ref, sems
):
    units = held_ref.shape[1]
    height = units // PARTS
    copies = []
    for n, (out, first) in enumerate(((gate_out, 0), (up_out, 0), (down_out, features))):
        right = rows_ref[:, first : first + features]
        for k in range(PARTS):
            left = acts_ref[n * units + k * height : n * units + (k + 1) * height, :]
            held_ref[n, k * height : (k + 1) * height] = jnp.dot(
                left, right, preferred_element_type=jnp.float32
            ).astype(jnp.bfloat16)
            part = pl.ds(k * height, height)
            copies.append(
                pltpu.make_async_copy(held_ref.at[n, part], out.at[0, part], sems.at[PARTS * n + k])
            )
            copies[-1].start()
    for copy in copies:
        copy.wait()


def sum_kernel(back_ref, out_ref):
    count, blocks, height, _ = back_ref.shape
    for k in range(blocks):
        total = back_ref[0, k].astype(jnp.float32)
        for n in range(1, count):
            total = total + back_ref[n, k].astype(jnp.float32)
        for r in range(height):
            part = pl.ds((k * height + r) * LANES, LANES)
            out_ref[:, part] = total[r : r + 1, :].astype(jnp.bfloat16)


def exchange(value, distance):
    count = lax.axis_size("group") * lax.axis_size("member")
    return lax.ppermute(value, AXES, [(i, i ^ distance) for i in range(count)])


def in_hbm(value):
    return pltpu.with_memory_space_constraint(value, pltpu.HBM)


def dense_shards(tokens, grad_out, route_token, route_count, route_prob, w_gate, w_up, w_down):
    features = tokens.shape[1]
    units = w_gate.shape[1]
    chunks = features // LANES
    count = lax.axis_size("group") * lax.axis_size("member")
    half = count // 2
    rows = 2 * chunks
    arguments = (tokens, grad_out, route_token, jnp.swapaxes(route_count, 1, 2), route_prob)
    spaces = (pltpu.VMEM, pltpu.VMEM, pltpu.SMEM, pltpu.SMEM, pltpu.SMEM)
    copies = pl.pallas_call(
        functools.partial(pack_kernel, chunks),
        out_shape=pltpu.VMEM((half, rows, LANES), jnp.bfloat16),
        in_specs=[HBM] * 5,
        out_specs=VMEM,
        scratch_shapes=[pltpu.VMEM((rows, LANES), jnp.float32)]
        + [space(value.shape, value.dtype) for space, value in zip(spaces, arguments)]
        + [pltpu.SemaphoreType.DMA((5,))],
        compiler_params=pltpu.CompilerParams(vmem_limit_bytes=4 * 1024 * 1024),
        cost_estimate=pl.CostEstimate(
            flops=40000 * units * features,
            bytes_accessed=16 * units * features,
            transcendentals=0,
        ),
        name="pack_rows",
    )(*[in_hbm(value) for value in arguments])
    cores = [list(range(c, count, 2)) for c in range(2)]
    trade = functools.partial(
        lax.all_to_all,
        axis_name=AXES,
        split_axis=0,
        concat_axis=0,
        tiled=True,
        axis_index_groups=cores,
    )
    mine = trade(copies)
    other = exchange(mine, 1)
    wide = pltpu.VMEM((half * rows, LANES), jnp.float32)
    unpacked = pl.pallas_call(
        functools.partial(unpack_kernel, chunks),
        out_shape=pltpu.VMEM((half, 2 * features), jnp.bfloat16),
        in_specs=[VMEM],
        out_specs=VMEM,
        scratch_shapes=[wide],
        compiler_params=pltpu.CompilerParams(vmem_limit_bytes=2 * 1024 * 1024),
        name="unpack_rows",
    )(mine)
    sent, both, acts = pl.pallas_call(
        functools.partial(partial_kernel, chunks),
        out_shape=(
            pltpu.VMEM((half, 2, chunks // 4, 4, LANES), jnp.bfloat16),
            pltpu.VMEM((count, 2 * features), jnp.bfloat16),
            pltpu.VMEM((3 * units, count), jnp.bfloat16),
        ),
        in_specs=[VMEM] * 5,
        out_specs=(VMEM,) * 3,
        scratch_shapes=[wide, pltpu.VMEM((count * chunks, LANES), jnp.float32)],
        compiler_params=pltpu.CompilerParams(vmem_limit_bytes=16 * 1024 * 1024),
        name="partial_rows",
    )(unpacked, other, w_gate, w_up, w_down)
    grad_shape = jax.ShapeDtypeStruct((1, units, features), jnp.bfloat16)
    grad_gate, grad_up, grad_down = pl.pallas_call(
        functools.partial(grads_kernel, features),
        out_shape=(grad_shape,) * 3,
        in_specs=[VMEM] * 2,
        out_specs=(HBM, HBM, HBM),
        scratch_shapes=[
            pltpu.VMEM((3, units, features), jnp.bfloat16),
            pltpu.SemaphoreType.DMA((3 * PARTS,)),
        ],
        compiler_params=pltpu.CompilerParams(vmem_limit_bytes=16 * 1024 * 1024),
        cost_estimate=pl.CostEstimate(
            flops=6 * count * units * features,
            bytes_accessed=6 * units * features,
            transcendentals=0,
        ),
        name="weight_grads",
    )(both, acts)
    back = lax.all_to_all(
        sent.reshape(count, chunks // 4, 4, LANES), AXES, 0, 0, tiled=True
    )
    grad_tokens = pl.pallas_call(
        sum_kernel,
        out_shape=jax.ShapeDtypeStruct((1, features), jnp.bfloat16),
        in_specs=[VMEM],
        out_specs=VMEM,
        compiler_params=pltpu.CompilerParams(vmem_limit_bytes=4 * 1024 * 1024),
        name="sum_rows",
    )(back)
    return grad_tokens, grad_gate, grad_up, grad_down


def slice_backward(rows_x, rows_scaled, gate_weight, up_weight, down_weight):
    gate_value = jnp.dot(rows_x, gate_weight.T, preferred_element_type=jnp.float32)
    up_value = jnp.dot(rows_x, up_weight.T, preferred_element_type=jnp.float32)
    sigma_gate = jax.nn.sigmoid(gate_value)
    active = gate_value * sigma_gate
    hidden = (active * up_value).astype(jnp.bfloat16)
    d_hidden = jnp.dot(rows_scaled, down_weight.T, preferred_element_type=jnp.float32)
    d_gate = (d_hidden * up_value * sigma_gate * (1.0 + gate_value * (1.0 - sigma_gate))).astype(
        jnp.bfloat16
    )
    d_up = (d_hidden * active).astype(jnp.bfloat16)
    grad_down = jnp.dot(hidden.T, rows_scaled, preferred_element_type=jnp.float32).astype(
        jnp.bfloat16
    )
    grad_gate = jnp.dot(d_gate.T, rows_x, preferred_element_type=jnp.float32).astype(jnp.bfloat16)
    grad_up = jnp.dot(d_up.T, rows_x, preferred_element_type=jnp.float32).astype(jnp.bfloat16)
    partial_rows = jnp.dot(d_gate, gate_weight, preferred_element_type=jnp.float32)
    partial_rows = partial_rows + jnp.dot(d_up, up_weight, preferred_element_type=jnp.float32)
    return (grad_gate, grad_up, grad_down, partial_rows)


def routed_shards(tokens, grad_out, route_token, route_count, route_prob, w_gate, w_up, w_down):
    groups = route_token.shape[1]
    capacity = route_token.shape[3]
    features = tokens.shape[1]
    block_rows = groups * capacity
    split_count = max(8, lax.axis_size("member") // 8)
    expert_local = lax.axis_index("member") // split_count
    slot_tokens = lax.dynamic_index_in_dim(route_token[0], expert_local, 1, keepdims=False)
    slot_counts = lax.dynamic_index_in_dim(route_count[0], expert_local, 1, keepdims=False)
    slot_probs = lax.dynamic_index_in_dim(route_prob[0], expert_local, 1, keepdims=False)
    slot_index = jnp.arange(capacity, dtype=jnp.int32)[None, :]
    live = (slot_index < slot_counts[:, None]).astype(jnp.float32)
    slot_weights = (slot_probs * live).reshape(-1)
    flat_slots = slot_tokens.reshape(-1)
    group_x, group_dy = (
        lax.all_gather(tokens, "member", axis=0, tiled=True),
        lax.all_gather(grad_out, "member", axis=0, tiled=True),
    )
    picked_x = jnp.take(group_x, flat_slots, axis=0)
    picked_dy = jnp.take(group_dy, flat_slots, axis=0)
    scaled = (slot_weights[:, None] * picked_dy.astype(jnp.float32)).astype(jnp.bfloat16)
    send_x = picked_x.reshape(groups, capacity, features)
    send_scaled = scaled.reshape(groups, capacity, features)
    rows_x, rows_scaled = (
        lax.all_to_all(send_x, "group", split_axis=0, concat_axis=0, tiled=True),
        lax.all_to_all(send_scaled, "group", split_axis=0, concat_axis=0, tiled=True),
    )
    grad_gate, grad_up, grad_down, partial_rows = slice_backward(
        rows_x.reshape(block_rows, features),
        rows_scaled.reshape(block_rows, features),
        w_gate[0],
        w_up[0],
        w_down[0],
    )
    returned = lax.all_to_all(
        partial_rows.reshape(groups, capacity, features),
        "group",
        split_axis=0,
        concat_axis=0,
        tiled=True,
    )
    returned = returned.reshape(block_rows, features)
    row_numbers = jnp.arange(tokens.shape[0] * lax.axis_size("member"), dtype=jnp.int32)
    selector = (row_numbers[:, None] == flat_slots[None, :]).astype(jnp.float32)
    summed = lax.psum_scatter(
        jnp.dot(
            selector, returned, precision=lax.Precision.HIGHEST, preferred_element_type=jnp.float32
        ),
        "member",
        scatter_dimension=0,
        tiled=True,
    )
    return (summed.astype(jnp.bfloat16), grad_gate[None], grad_up[None], grad_down[None])


def shards(tokens, grad_out, route_token, *rest):
    devices = lax.axis_size("group") * lax.axis_size("member")
    _, groups, experts, capacity = route_token.shape
    dense = devices * tokens.shape[0] <= groups * capacity and experts == 1
    paired = tokens.shape[0] == 1 and devices & (devices - 1) == 0
    body = dense_shards if dense and paired else routed_shards
    return body(tokens, grad_out, route_token, *rest)


def solution(mesh):
    placed = (
        P(("group", "member"), None),
        P(("group", "member"), None),
        P("group", None, None, None),
        P("group", None, None),
        P("group", None, None, None),
        P(("group", "member"), None, None),
        P(("group", "member"), None, None),
        P(("group", "member"), None, None),
    )
    return jax.shard_map(
        shards,
        mesh=mesh,
        in_specs=placed,
        out_specs=(
            P(("group", "member"), None),
            P(("group", "member"), None, None),
            P(("group", "member"), None, None),
            P(("group", "member"), None, None),
        ),
        check_vma=False,
    )
```

```python
import functools

import jax
import jax.numpy as jnp
from jax import lax
from jax.experimental import pallas as pl
from jax.experimental.pallas import tpu as pltpu
from jax.sharding import PartitionSpec as P

LANES = 128
PARTS = 4
AXES = ("group", "member")
VMEM = pl.BlockSpec(memory_space=pltpu.VMEM)
HBM = pl.BlockSpec(memory_space=pltpu.HBM)
SMEM = pl.BlockSpec(memory_space=pltpu.SMEM)
NT = (((1,), (1,)), ((), ()))
TN = (((0,), (0,)), ((), ()))


def pack_kernel(
    chunks,
    tokens_hbm,
    grad_hbm,
    token_hbm,
    count_hbm,
    prob_hbm,
    out_ref,
    rows_ref,
    tokens_ref,
    grad_ref,
    token_ref,
    count_ref,
    prob_ref,
    sems,
):
    pairs = (
        (token_hbm, token_ref),
        (count_hbm, count_ref),
        (prob_hbm, prob_ref),
        (tokens_hbm, tokens_ref),
        (grad_hbm, grad_ref),
    )
    copies = [pltpu.make_async_copy(*pair, sems.at[n]) for n, pair in enumerate(pairs)]
    for copy in copies:
        copy.start()
    for copy in copies:
        copy.wait()
    me = lax.axis_index("member")
    groups, _, capacity = token_ref.shape[1:]
    token_row = tokens_ref[...].astype(jnp.float32)
    grad_row = grad_ref[...].astype(jnp.float32)
    for k in range(chunks):
        part = slice(k * LANES, (k + 1) * LANES)
        rows_ref[k : k + 1, :] = token_row[:, part]
        rows_ref[chunks + k : chunks + k + 1, :] = grad_row[:, part]
    rows = rows_ref[...]
    is_token = lax.broadcasted_iota(jnp.int32, rows.shape, 0) < chunks
    places = out_ref.shape[0] // groups
    for g in range(groups):
        weight = jnp.float32(0)
        for p in range(capacity):
            live = (token_ref[0, g, 0, p] == me) & (p < count_ref[0, 0, g])
            weight = weight + jnp.where(live, prob_ref[0, g, 0, p], 0.0)
        packed = jnp.where(is_token, rows, rows * weight).astype(jnp.bfloat16)
        for n in range(places):
            out_ref[g * places + n] = packed


def unpack_rows(chunks, packed_ref, wide_ref, rows_ref):
    tokens, rows, _ = packed_ref.shape
    wide_ref[...] = packed_ref[...].astype(jnp.float32).reshape(tokens * rows, LANES)
    for k in range(rows):
        column = wide_ref[pl.ds(k, tokens, stride=rows), :]
        rows_ref[:, k * LANES : (k + 1) * LANES] = column.astype(jnp.bfloat16)


def unpack_kernel(chunks, mine_ref, rows_ref, wide_ref):
    unpack_rows(chunks, mine_ref, wide_ref, rows_ref)


def partial_kernel(
    chunks,
    mine_ref,
    other_ref,
    gate_ref,
    up_ref,
    down_ref,
    sent_ref,
    rows_ref,
    acts_ref,
    wide_ref,
    spread_ref,
):
    count = mine_ref.shape[0]
    tokens = 2 * count
    features = chunks * LANES
    units = gate_ref.shape[1]
    rows_ref[:count] = mine_ref[...]
    unpack_rows(chunks, other_ref, wide_ref, rows_ref.at[pl.ds(count, count)])
    x, scaled = rows_ref[:, :features], rows_ref[:, features:]
    both = jnp.concatenate([gate_ref[0], up_ref[0]], axis=0)
    values = lax.dot_general(both, x, NT, preferred_element_type=jnp.float32)
    gate_value, up_value = values[:units], values[units:]
    d_hidden = lax.dot_general(down_ref[0], scaled, NT, preferred_element_type=jnp.float32)
    sigma_gate = jax.nn.sigmoid(gate_value)
    active = gate_value * sigma_gate
    d_gate = d_hidden * up_value * sigma_gate * (1.0 + gate_value * (1.0 - sigma_gate))
    acts_ref[0:units] = d_gate.astype(jnp.bfloat16)
    acts_ref[units : 2 * units] = (d_hidden * active).astype(jnp.bfloat16)
    acts_ref[2 * units :] = (active * up_value).astype(jnp.bfloat16)
    partial = lax.dot_general(
        acts_ref[: 2 * units], both, TN, preferred_element_type=jnp.float32
    )
    core = lax.rem(lax.axis_index("member"), 2)
    for k in range(chunks):
        column = partial[:, k * LANES : (k + 1) * LANES]
        for n in range(2):
            place = pl.ds((core ^ n) * chunks + k, count, stride=2 * chunks)
            spread_ref[place, :] = column[n * count : (n + 1) * count]
    sent_ref[...] = spread_ref[...].astype(jnp.bfloat16)


def grads_kernel(
    features, rows_ref, acts_ref, gate_out, up_out, down_out, held_ref, sems
):
    units = held_ref.shape[1]
    height = units // PARTS
    copies = []
    for n, (out, first) in enumerate(((gate_out, 0), (up_out, 0), (down_out, features))):
        right = rows_ref[:, first : first + features]
        for k in range(PARTS):
            left = acts_ref[n * units + k * height : n * units + (k + 1) * height, :]
            held_ref[n, k * height : (k + 1) * height] = jnp.dot(
                left, right, preferred_element_type=jnp.float32
            ).astype(jnp.bfloat16)
            part = pl.ds(k * height, height)
            copies.append(
                pltpu.make_async_copy(held_ref.at[n, part], out.at[0, part], sems.at[PARTS * n + k])
            )
            copies[-1].start()
    for copy in copies:
        copy.wait()


def sum_kernel(back_ref, out_ref):
    count, blocks, height, _ = back_ref.shape
    for k in range(blocks):
        total = back_ref[0, k].astype(jnp.float32)
        for n in range(1, count):
            total = total + back_ref[n, k].astype(jnp.float32)
        for r in range(height):
            part = pl.ds((k * height + r) * LANES, LANES)
            out_ref[:, part] = total[r : r + 1, :].astype(jnp.bfloat16)


def exchange(value, distance):
    count = lax.axis_size("group") * lax.axis_size("member")
    return lax.ppermute(value, AXES, [(i, i ^ distance) for i in range(count)])


def in_hbm(value):
    return pltpu.with_memory_space_constraint(value, pltpu.HBM)


def dense_shards(tokens, grad_out, route_token, route_count, route_prob, w_gate, w_up, w_down):
    features = tokens.shape[1]
    units = w_gate.shape[1]
    chunks = features // LANES
    count = lax.axis_size("group") * lax.axis_size("member")
    half = count // 2
    rows = 2 * chunks
    arguments = (tokens, grad_out, route_token, jnp.swapaxes(route_count, 1, 2), route_prob)
    spaces = (pltpu.VMEM, pltpu.VMEM, pltpu.SMEM, pltpu.SMEM, pltpu.SMEM)
    copies = pl.pallas_call(
        functools.partial(pack_kernel, chunks),
        out_shape=pltpu.VMEM((half, rows, LANES), jnp.bfloat16),
        in_specs=[HBM] * 5,
        out_specs=VMEM,
        scratch_shapes=[pltpu.VMEM((rows, LANES), jnp.float32)]
        + [space(value.shape, value.dtype) for space, value in zip(spaces, arguments)]
        + [pltpu.SemaphoreType.DMA((5,))],
        compiler_params=pltpu.CompilerParams(vmem_limit_bytes=4 * 1024 * 1024),
        cost_estimate=pl.CostEstimate(
            flops=40000 * units * features,
            bytes_accessed=16 * units * features,
            transcendentals=0,
        ),
        name="pack_rows",
    )(*[in_hbm(value) for value in arguments])
    cores = [list(range(c, count, 2)) for c in range(2)]
    trade = functools.partial(
        lax.all_to_all,
        axis_name=AXES,
        split_axis=0,
        concat_axis=0,
        tiled=True,
        axis_index_groups=cores,
    )
    mine = trade(copies)
    other = exchange(mine, 1)
    wide = pltpu.VMEM((half * rows, LANES), jnp.float32)
    unpacked = pl.pallas_call(
        functools.partial(unpack_kernel, chunks),
        out_shape=pltpu.VMEM((half, 2 * features), jnp.bfloat16),
        in_specs=[VMEM],
        out_specs=VMEM,
        scratch_shapes=[wide],
        compiler_params=pltpu.CompilerParams(vmem_limit_bytes=2 * 1024 * 1024),
        name="unpack_rows",
    )(mine)
    sent, both, acts = pl.pallas_call(
        functools.partial(partial_kernel, chunks),
        out_shape=(
            pltpu.VMEM((count * chunks, LANES), jnp.bfloat16),
            pltpu.VMEM((count, 2 * features), jnp.bfloat16),
            pltpu.VMEM((3 * units, count), jnp.bfloat16),
        ),
        in_specs=[VMEM] * 5,
        out_specs=(VMEM,) * 3,
        scratch_shapes=[wide, pltpu.VMEM((count * chunks, LANES), jnp.float32)],
        compiler_params=pltpu.CompilerParams(vmem_limit_bytes=16 * 1024 * 1024),
        name="partial_rows",
    )(unpacked, other, w_gate, w_up, w_down)
    grad_shape = jax.ShapeDtypeStruct((1, units, features), jnp.bfloat16)
    grad_gate, grad_up, grad_down = pl.pallas_call(
        functools.partial(grads_kernel, features),
        out_shape=(grad_shape,) * 3,
        in_specs=[VMEM] * 2,
        out_specs=(HBM, HBM, HBM),
        scratch_shapes=[
            pltpu.VMEM((3, units, features), jnp.bfloat16),
            pltpu.SemaphoreType.DMA((3 * PARTS,)),
        ],
        compiler_params=pltpu.CompilerParams(vmem_limit_bytes=16 * 1024 * 1024),
        cost_estimate=pl.CostEstimate(
            flops=6 * count * units * features,
            bytes_accessed=6 * units * features,
            transcendentals=0,
        ),
        name="weight_grads",
    )(both, acts)
    back = lax.all_to_all(
        sent.reshape(count, chunks // 4, 4, LANES), AXES, 0, 0, tiled=True
    )
    grad_tokens = pl.pallas_call(
        sum_kernel,
        out_shape=jax.ShapeDtypeStruct((1, features), jnp.bfloat16),
        in_specs=[VMEM],
        out_specs=VMEM,
        compiler_params=pltpu.CompilerParams(vmem_limit_bytes=4 * 1024 * 1024),
        name="sum_rows",
    )(back)
    return grad_tokens, grad_gate, grad_up, grad_down


def slice_backward(rows_x, rows_scaled, gate_weight, up_weight, down_weight):
    gate_value = jnp.dot(rows_x, gate_weight.T, preferred_element_type=jnp.float32)
    up_value = jnp.dot(rows_x, up_weight.T, preferred_element_type=jnp.float32)
    sigma_gate = jax.nn.sigmoid(gate_value)
    active = gate_value * sigma_gate
    hidden = (active * up_value).astype(jnp.bfloat16)
    d_hidden = jnp.dot(rows_scaled, down_weight.T, preferred_element_type=jnp.float32)
    d_gate = (d_hidden * up_value * sigma_gate * (1.0 + gate_value * (1.0 - sigma_gate))).astype(
        jnp.bfloat16
    )
    d_up = (d_hidden * active).astype(jnp.bfloat16)
    grad_down = jnp.dot(hidden.T, rows_scaled, preferred_element_type=jnp.float32).astype(
        jnp.bfloat16
    )
    grad_gate = jnp.dot(d_gate.T, rows_x, preferred_element_type=jnp.float32).astype(jnp.bfloat16)
    grad_up = jnp.dot(d_up.T, rows_x, preferred_element_type=jnp.float32).astype(jnp.bfloat16)
    partial_rows = jnp.dot(d_gate, gate_weight, preferred_element_type=jnp.float32)
    partial_rows = partial_rows + jnp.dot(d_up, up_weight, preferred_element_type=jnp.float32)
    return (grad_gate, grad_up, grad_down, partial_rows)


def routed_shards(tokens, grad_out, route_token, route_count, route_prob, w_gate, w_up, w_down):
    groups = route_token.shape[1]
    capacity = route_token.shape[3]
    features = tokens.shape[1]
    block_rows = groups * capacity
    split_count = max(8, lax.axis_size("member") // 8)
    expert_local = lax.axis_index("member") // split_count
    slot_tokens = lax.dynamic_index_in_dim(route_token[0], expert_local, 1, keepdims=False)
    slot_counts = lax.dynamic_index_in_dim(route_count[0], expert_local, 1, keepdims=False)
    slot_probs = lax.dynamic_index_in_dim(route_prob[0], expert_local, 1, keepdims=False)
    slot_index = jnp.arange(capacity, dtype=jnp.int32)[None, :]
    live = (slot_index < slot_counts[:, None]).astype(jnp.float32)
    slot_weights = (slot_probs * live).reshape(-1)
    flat_slots = slot_tokens.reshape(-1)
    group_x, group_dy = (
        lax.all_gather(tokens, "member", axis=0, tiled=True),
        lax.all_gather(grad_out, "member", axis=0, tiled=True),
    )
    picked_x = jnp.take(group_x, flat_slots, axis=0)
    picked_dy = jnp.take(group_dy, flat_slots, axis=0)
    scaled = (slot_weights[:, None] * picked_dy.astype(jnp.float32)).astype(jnp.bfloat16)
    send_x = picked_x.reshape(groups, capacity, features)
    send_scaled = scaled.reshape(groups, capacity, features)
    rows_x, rows_scaled = (
        lax.all_to_all(send_x, "group", split_axis=0, concat_axis=0, tiled=True),
        lax.all_to_all(send_scaled, "group", split_axis=0, concat_axis=0, tiled=True),
    )
    grad_gate, grad_up, grad_down, partial_rows = slice_backward(
        rows_x.reshape(block_rows, features),
        rows_scaled.reshape(block_rows, features),
        w_gate[0],
        w_up[0],
        w_down[0],
    )
    returned = lax.all_to_all(
        partial_rows.reshape(groups, capacity, features),
        "group",
        split_axis=0,
        concat_axis=0,
        tiled=True,
    )
    returned = returned.reshape(block_rows, features)
    row_numbers = jnp.arange(tokens.shape[0] * lax.axis_size("member"), dtype=jnp.int32)
    selector = (row_numbers[:, None] == flat_slots[None, :]).astype(jnp.float32)
    summed = lax.psum_scatter(
        jnp.dot(
            selector, returned, precision=lax.Precision.HIGHEST, preferred_element_type=jnp.float32
        ),
        "member",
        scatter_dimension=0,
        tiled=True,
    )
    return (summed.astype(jnp.bfloat16), grad_gate[None], grad_up[None], grad_down[None])


def shards(tokens, grad_out, route_token, *rest):
    devices = lax.axis_size("group") * lax.axis_size("member")
    _, groups, experts, capacity = route_token.shape
    dense = devices * tokens.shape[0] <= groups * capacity and experts == 1
    paired = tokens.shape[0] == 1 and devices & (devices - 1) == 0
    body = dense_shards if dense and paired else routed_shards
    return body(tokens, grad_out, route_token, *rest)


def solution(mesh):
    placed = (
        P(("group", "member"), None),
        P(("group", "member"), None),
        P("group", None, None, None),
        P("group", None, None),
        P("group", None, None, None),
        P(("group", "member"), None, None),
        P(("group", "member"), None, None),
        P(("group", "member"), None, None),
    )
    return jax.shard_map(
        shards,
        mesh=mesh,
        in_specs=placed,
        out_specs=(
            P(("group", "member"), None),
            P(("group", "member"), None, None),
            P(("group", "member"), None, None),
            P(("group", "member"), None, None),
        ),
        check_vma=False,
    )
```

```python
import functools

import jax
import jax.numpy as jnp
from jax import lax
from jax.experimental import pallas as pl
from jax.experimental.pallas import tpu as pltpu
from jax.sharding import PartitionSpec as P

LANES = 128
PARTS = 4
AXES = ("group", "member")
VMEM = pl.BlockSpec(memory_space=pltpu.VMEM)
HBM = pl.BlockSpec(memory_space=pltpu.HBM)
SMEM = pl.BlockSpec(memory_space=pltpu.SMEM)
NT = (((1,), (1,)), ((), ()))
TN = (((0,), (0,)), ((), ()))


def pack_kernel(
    chunks,
    tokens_hbm,
    grad_hbm,
    token_hbm,
    count_hbm,
    prob_hbm,
    out_ref,
    rows_ref,
    tokens_ref,
    grad_ref,
    token_ref,
    count_ref,
    prob_ref,
    sems,
):
    pairs = (
        (token_hbm, token_ref),
        (count_hbm, count_ref),
        (prob_hbm, prob_ref),
        (tokens_hbm, tokens_ref),
        (grad_hbm, grad_ref),
    )
    copies = [pltpu.make_async_copy(*pair, sems.at[n]) for n, pair in enumerate(pairs)]
    for copy in copies:
        copy.start()
    for copy in copies:
        copy.wait()
    me = lax.axis_index("member")
    groups, _, capacity = token_ref.shape[1:]
    token_row = tokens_ref[...].astype(jnp.float32)
    grad_row = grad_ref[...].astype(jnp.float32)
    for k in range(chunks):
        part = slice(k * LANES, (k + 1) * LANES)
        rows_ref[k : k + 1, :] = token_row[:, part]
        rows_ref[chunks + k : chunks + k + 1, :] = grad_row[:, part]
    rows = rows_ref[...]
    is_token = lax.broadcasted_iota(jnp.int32, rows.shape, 0) < chunks
    places = out_ref.shape[0] // groups
    for g in range(groups):
        weight = jnp.float32(0)
        for p in range(capacity):
            live = (token_ref[0, g, 0, p] == me) & (p < count_ref[0, 0, g])
            weight = weight + jnp.where(live, prob_ref[0, g, 0, p], 0.0)
        packed = jnp.where(is_token, rows, rows * weight).astype(jnp.bfloat16)
        for n in range(places):
            out_ref[g * places + n] = packed


def unpack_rows(chunks, packed_ref, wide_ref, rows_ref):
    tokens, rows, _ = packed_ref.shape
    wide_ref[...] = packed_ref[...].astype(jnp.float32).reshape(tokens * rows, LANES)
    for k in range(rows):
        column = wide_ref[pl.ds(k, tokens, stride=rows), :]
        rows_ref[:, k * LANES : (k + 1) * LANES] = column.astype(jnp.bfloat16)


def unpack_kernel(chunks, mine_ref, rows_ref, wide_ref):
    unpack_rows(chunks, mine_ref, wide_ref, rows_ref)


def partial_kernel(
    chunks,
    mine_ref,
    other_ref,
    gate_ref,
    up_ref,
    down_ref,
    sent_ref,
    rows_ref,
    acts_ref,
    wide_ref,
    spread_ref,
):
    count = mine_ref.shape[0]
    tokens = 2 * count
    features = chunks * LANES
    units = gate_ref.shape[1]
    rows_ref[:count] = mine_ref[...]
    unpack_rows(chunks, other_ref, wide_ref, rows_ref.at[pl.ds(count, count)])
    x, scaled = rows_ref[:, :features], rows_ref[:, features:]
    both = jnp.concatenate([gate_ref[0], up_ref[0]], axis=0)
    values = lax.dot_general(both, x, NT, preferred_element_type=jnp.float32)
    gate_value, up_value = values[:units], values[units:]
    d_hidden = lax.dot_general(down_ref[0], scaled, NT, preferred_element_type=jnp.float32)
    sigma_gate = jax.nn.sigmoid(gate_value)
    active = gate_value * sigma_gate
    d_gate = d_hidden * up_value * sigma_gate * (1.0 + gate_value * (1.0 - sigma_gate))
    d_up = d_hidden * active
    acts_ref[0:units] = d_gate.astype(jnp.bfloat16)
    acts_ref[units : 2 * units] = d_up.astype(jnp.bfloat16)
    acts_ref[2 * units :] = (active * up_value).astype(jnp.bfloat16)
    turned = jnp.concatenate([d_gate.T, d_up.T], axis=1).astype(jnp.bfloat16)
    partial = jnp.dot(turned, both, preferred_element_type=jnp.float32)
    core = lax.rem(lax.axis_index("member"), 2)
    for k in range(chunks):
        column = partial[:, k * LANES : (k + 1) * LANES]
        for n in range(2):
            place = pl.ds((core ^ n) * chunks + k, count, stride=2 * chunks)
            spread_ref[place, :] = column[n * count : (n + 1) * count]
    sent_ref[...] = spread_ref[...].astype(jnp.bfloat16)


def grads_kernel(
    features, rows_ref, acts_ref, gate_out, up_out, down_out, held_ref, sems
):
    units = held_ref.shape[1]
    height = units // PARTS
    copies = []
    for n, (out, first) in enumerate(((gate_out, 0), (up_out, 0), (down_out, features))):
        right = rows_ref[:, first : first + features]
        for k in range(PARTS):
            left = acts_ref[n * units + k * height : n * units + (k + 1) * height, :]
            held_ref[n, k * height : (k + 1) * height] = jnp.dot(
                left, right, preferred_element_type=jnp.float32
            ).astype(jnp.bfloat16)
            part = pl.ds(k * height, height)
            copies.append(
                pltpu.make_async_copy(held_ref.at[n, part], out.at[0, part], sems.at[PARTS * n + k])
            )
            copies[-1].start()
    for copy in copies:
        copy.wait()


def sum_kernel(back_ref, out_ref):
    count, blocks, height, _ = back_ref.shape
    for k in range(blocks):
        total = back_ref[0, k].astype(jnp.float32)
        for n in range(1, count):
            total = total + back_ref[n, k].astype(jnp.float32)
        for r in range(height):
            part = pl.ds((k * height + r) * LANES, LANES)
            out_ref[:, part] = total[r : r + 1, :].astype(jnp.bfloat16)


def exchange(value, distance):
    count = lax.axis_size("group") * lax.axis_size("member")
    return lax.ppermute(value, AXES, [(i, i ^ distance) for i in range(count)])


def in_hbm(value):
    return pltpu.with_memory_space_constraint(value, pltpu.HBM)


def dense_shards(tokens, grad_out, route_token, route_count, route_prob, w_gate, w_up, w_down):
    features = tokens.shape[1]
    units = w_gate.shape[1]
    chunks = features // LANES
    count = lax.axis_size("group") * lax.axis_size("member")
    half = count // 2
    rows = 2 * chunks
    arguments = (tokens, grad_out, route_token, jnp.swapaxes(route_count, 1, 2), route_prob)
    spaces = (pltpu.VMEM, pltpu.VMEM, pltpu.SMEM, pltpu.SMEM, pltpu.SMEM)
    copies = pl.pallas_call(
        functools.partial(pack_kernel, chunks),
        out_shape=pltpu.VMEM((half, rows, LANES), jnp.bfloat16),
        in_specs=[HBM] * 5,
        out_specs=VMEM,
        scratch_shapes=[pltpu.VMEM((rows, LANES), jnp.float32)]
        + [space(value.shape, value.dtype) for space, value in zip(spaces, arguments)]
        + [pltpu.SemaphoreType.DMA((5,))],
        compiler_params=pltpu.CompilerParams(vmem_limit_bytes=4 * 1024 * 1024),
        cost_estimate=pl.CostEstimate(
            flops=40000 * units * features,
            bytes_accessed=16 * units * features,
            transcendentals=0,
        ),
        name="pack_rows",
    )(*[in_hbm(value) for value in arguments])
    cores = [list(range(c, count, 2)) for c in range(2)]
    trade = functools.partial(
        lax.all_to_all,
        axis_name=AXES,
        split_axis=0,
        concat_axis=0,
        tiled=True,
        axis_index_groups=cores,
    )
    mine = trade(copies)
    other = exchange(mine, 1)
    wide = pltpu.VMEM((half * rows, LANES), jnp.float32)
    unpacked = pl.pallas_call(
        functools.partial(unpack_kernel, chunks),
        out_shape=pltpu.VMEM((half, 2 * features), jnp.bfloat16),
        in_specs=[VMEM],
        out_specs=VMEM,
        scratch_shapes=[wide],
        compiler_params=pltpu.CompilerParams(vmem_limit_bytes=2 * 1024 * 1024),
        name="unpack_rows",
    )(mine)
    sent, both, acts = pl.pallas_call(
        functools.partial(partial_kernel, chunks),
        out_shape=(
            pltpu.VMEM((count * chunks, LANES), jnp.bfloat16),
            pltpu.VMEM((count, 2 * features), jnp.bfloat16),
            pltpu.VMEM((3 * units, count), jnp.bfloat16),
        ),
        in_specs=[VMEM] * 5,
        out_specs=(VMEM,) * 3,
        scratch_shapes=[wide, pltpu.VMEM((count * chunks, LANES), jnp.float32)],
        compiler_params=pltpu.CompilerParams(vmem_limit_bytes=16 * 1024 * 1024),
        name="partial_rows",
    )(unpacked, other, w_gate, w_up, w_down)
    grad_shape = jax.ShapeDtypeStruct((1, units, features), jnp.bfloat16)
    grad_gate, grad_up, grad_down = pl.pallas_call(
        functools.partial(grads_kernel, features),
        out_shape=(grad_shape,) * 3,
        in_specs=[VMEM] * 2,
        out_specs=(HBM, HBM, HBM),
        scratch_shapes=[
            pltpu.VMEM((3, units, features), jnp.bfloat16),
            pltpu.SemaphoreType.DMA((3 * PARTS,)),
        ],
        compiler_params=pltpu.CompilerParams(vmem_limit_bytes=16 * 1024 * 1024),
        cost_estimate=pl.CostEstimate(
            flops=6 * count * units * features,
            bytes_accessed=6 * units * features,
            transcendentals=0,
        ),
        name="weight_grads",
    )(both, acts)
    back = lax.all_to_all(
        sent.reshape(count, chunks // 4, 4, LANES), AXES, 0, 0, tiled=True
    )
    grad_tokens = pl.pallas_call(
        sum_kernel,
        out_shape=jax.ShapeDtypeStruct((1, features), jnp.bfloat16),
        in_specs=[VMEM],
        out_specs=VMEM,
        compiler_params=pltpu.CompilerParams(vmem_limit_bytes=4 * 1024 * 1024),
        name="sum_rows",
    )(back)
    return grad_tokens, grad_gate, grad_up, grad_down


def slice_backward(rows_x, rows_scaled, gate_weight, up_weight, down_weight):
    gate_value = jnp.dot(rows_x, gate_weight.T, preferred_element_type=jnp.float32)
    up_value = jnp.dot(rows_x, up_weight.T, preferred_element_type=jnp.float32)
    sigma_gate = jax.nn.sigmoid(gate_value)
    active = gate_value * sigma_gate
    hidden = (active * up_value).astype(jnp.bfloat16)
    d_hidden = jnp.dot(rows_scaled, down_weight.T, preferred_element_type=jnp.float32)
    d_gate = (d_hidden * up_value * sigma_gate * (1.0 + gate_value * (1.0 - sigma_gate))).astype(
        jnp.bfloat16
    )
    d_up = (d_hidden * active).astype(jnp.bfloat16)
    grad_down = jnp.dot(hidden.T, rows_scaled, preferred_element_type=jnp.float32).astype(
        jnp.bfloat16
    )
    grad_gate = jnp.dot(d_gate.T, rows_x, preferred_element_type=jnp.float32).astype(jnp.bfloat16)
    grad_up = jnp.dot(d_up.T, rows_x, preferred_element_type=jnp.float32).astype(jnp.bfloat16)
    partial_rows = jnp.dot(d_gate, gate_weight, preferred_element_type=jnp.float32)
    partial_rows = partial_rows + jnp.dot(d_up, up_weight, preferred_element_type=jnp.float32)
    return (grad_gate, grad_up, grad_down, partial_rows)


def routed_shards(tokens, grad_out, route_token, route_count, route_prob, w_gate, w_up, w_down):
    groups = route_token.shape[1]
    capacity = route_token.shape[3]
    features = tokens.shape[1]
    block_rows = groups * capacity
    split_count = max(8, lax.axis_size("member") // 8)
    expert_local = lax.axis_index("member") // split_count
    slot_tokens = lax.dynamic_index_in_dim(route_token[0], expert_local, 1, keepdims=False)
    slot_counts = lax.dynamic_index_in_dim(route_count[0], expert_local, 1, keepdims=False)
    slot_probs = lax.dynamic_index_in_dim(route_prob[0], expert_local, 1, keepdims=False)
    slot_index = jnp.arange(capacity, dtype=jnp.int32)[None, :]
    live = (slot_index < slot_counts[:, None]).astype(jnp.float32)
    slot_weights = (slot_probs * live).reshape(-1)
    flat_slots = slot_tokens.reshape(-1)
    group_x, group_dy = (
        lax.all_gather(tokens, "member", axis=0, tiled=True),
        lax.all_gather(grad_out, "member", axis=0, tiled=True),
    )
    picked_x = jnp.take(group_x, flat_slots, axis=0)
    picked_dy = jnp.take(group_dy, flat_slots, axis=0)
    scaled = (slot_weights[:, None] * picked_dy.astype(jnp.float32)).astype(jnp.bfloat16)
    send_x = picked_x.reshape(groups, capacity, features)
    send_scaled = scaled.reshape(groups, capacity, features)
    rows_x, rows_scaled = (
        lax.all_to_all(send_x, "group", split_axis=0, concat_axis=0, tiled=True),
        lax.all_to_all(send_scaled, "group", split_axis=0, concat_axis=0, tiled=True),
    )
    grad_gate, grad_up, grad_down, partial_rows = slice_backward(
        rows_x.reshape(block_rows, features),
        rows_scaled.reshape(block_rows, features),
        w_gate[0],
        w_up[0],
        w_down[0],
    )
    returned = lax.all_to_all(
        partial_rows.reshape(groups, capacity, features),
        "group",
        split_axis=0,
        concat_axis=0,
        tiled=True,
    )
    returned = returned.reshape(block_rows, features)
    row_numbers = jnp.arange(tokens.shape[0] * lax.axis_size("member"), dtype=jnp.int32)
    selector = (row_numbers[:, None] == flat_slots[None, :]).astype(jnp.float32)
    summed = lax.psum_scatter(
        jnp.dot(
            selector, returned, precision=lax.Precision.HIGHEST, preferred_element_type=jnp.float32
        ),
        "member",
        scatter_dimension=0,
        tiled=True,
    )
    return (summed.astype(jnp.bfloat16), grad_gate[None], grad_up[None], grad_down[None])


def shards(tokens, grad_out, route_token, *rest):
    devices = lax.axis_size("group") * lax.axis_size("member")
    _, groups, experts, capacity = route_token.shape
    dense = devices * tokens.shape[0] <= groups * capacity and experts == 1
    paired = tokens.shape[0] == 1 and devices & (devices - 1) == 0
    body = dense_shards if dense and paired else routed_shards
    return body(tokens, grad_out, route_token, *rest)


def solution(mesh):
    placed = (
        P(("group", "member"), None),
        P(("group", "member"), None),
        P("group", None, None, None),
        P("group", None, None),
        P("group", None, None, None),
        P(("group", "member"), None, None),
        P(("group", "member"), None, None),
        P(("group", "member"), None, None),
    )
    return jax.shard_map(
        shards,
        mesh=mesh,
        in_specs=placed,
        out_specs=(
            P(("group", "member"), None),
            P(("group", "member"), None, None),
            P(("group", "member"), None, None),
            P(("group", "member"), None, None),
        ),
        check_vma=False,
    )
```

```python
import functools

import jax
import jax.numpy as jnp
from jax import lax
from jax.experimental import pallas as pl
from jax.experimental.pallas import tpu as pltpu
from jax.sharding import PartitionSpec as P

LANES = 128
PARTS = 4
AXES = ("group", "member")
VMEM = pl.BlockSpec(memory_space=pltpu.VMEM)
HBM = pl.BlockSpec(memory_space=pltpu.HBM)
SMEM = pl.BlockSpec(memory_space=pltpu.SMEM)
NT = (((1,), (1,)), ((), ()))
TN = (((0,), (0,)), ((), ()))


def pack_kernel(
    chunks,
    tokens_hbm,
    grad_hbm,
    token_hbm,
    count_hbm,
    prob_hbm,
    out_ref,
    rows_ref,
    tokens_ref,
    grad_ref,
    token_ref,
    count_ref,
    prob_ref,
    sems,
):
    pairs = (
        (token_hbm, token_ref),
        (count_hbm, count_ref),
        (prob_hbm, prob_ref),
        (tokens_hbm, tokens_ref),
        (grad_hbm, grad_ref),
    )
    copies = [pltpu.make_async_copy(*pair, sems.at[n]) for n, pair in enumerate(pairs)]
    for copy in copies:
        copy.start()
    for copy in copies:
        copy.wait()
    me = lax.axis_index("member")
    groups, _, capacity = token_ref.shape[1:]
    token_row = tokens_ref[...].astype(jnp.float32)
    grad_row = grad_ref[...].astype(jnp.float32)
    for k in range(chunks):
        part = slice(k * LANES, (k + 1) * LANES)
        rows_ref[k : k + 1, :] = token_row[:, part]
        rows_ref[chunks + k : chunks + k + 1, :] = grad_row[:, part]
    rows = rows_ref[...]
    is_token = lax.broadcasted_iota(jnp.int32, rows.shape, 0) < chunks
    places = out_ref.shape[0] // groups
    for g in range(groups):
        weight = jnp.float32(0)
        for p in range(capacity):
            live = (token_ref[0, g, 0, p] == me) & (p < count_ref[0, 0, g])
            weight = weight + jnp.where(live, prob_ref[0, g, 0, p], 0.0)
        packed = jnp.where(is_token, rows, rows * weight).astype(jnp.bfloat16)
        for n in range(places):
            out_ref[g * places + n] = packed


def unpack_rows(chunks, packed_ref, wide_ref, rows_ref):
    tokens, rows, _ = packed_ref.shape
    wide_ref[...] = packed_ref[...].astype(jnp.float32).reshape(tokens * rows, LANES)
    for k in range(rows):
        column = wide_ref[pl.ds(k, tokens, stride=rows), :]
        rows_ref[:, k * LANES : (k + 1) * LANES] = column.astype(jnp.bfloat16)


def unpack_kernel(chunks, mine_ref, rows_ref, wide_ref):
    unpack_rows(chunks, mine_ref, wide_ref, rows_ref)


def partial_kernel(
    chunks,
    mine_ref,
    other_ref,
    gate_ref,
    up_ref,
    down_ref,
    sent_ref,
    rows_ref,
    acts_ref,
    wide_ref,
    spread_ref,
):
    count = mine_ref.shape[0]
    tokens = 2 * count
    features = chunks * LANES
    units = gate_ref.shape[1]
    rows_ref[:count] = mine_ref[...]
    unpack_rows(chunks, other_ref, wide_ref, rows_ref.at[pl.ds(count, count)])
    x, scaled = rows_ref[:, :features], rows_ref[:, features:]
    both = jnp.concatenate([gate_ref[0], up_ref[0]], axis=0)
    values = lax.dot_general(x, both, NT, preferred_element_type=jnp.float32)
    gate_value, up_value = values[:, :units], values[:, units:]
    d_hidden = lax.dot_general(scaled, down_ref[0], NT, preferred_element_type=jnp.float32)
    sigma_gate = jax.nn.sigmoid(gate_value)
    active = gate_value * sigma_gate
    d_gate = d_hidden * up_value * sigma_gate * (1.0 + gate_value * (1.0 - sigma_gate))
    acts_ref[:, :units] = d_gate.astype(jnp.bfloat16)
    acts_ref[:, units : 2 * units] = (d_hidden * active).astype(jnp.bfloat16)
    acts_ref[:, 2 * units :] = (active * up_value).astype(jnp.bfloat16)
    partial = jnp.dot(acts_ref[:, : 2 * units], both, preferred_element_type=jnp.float32)
    core = lax.rem(lax.axis_index("member"), 2)
    for k in range(chunks):
        column = partial[:, k * LANES : (k + 1) * LANES]
        for n in range(2):
            place = pl.ds((core ^ n) * chunks + k, count, stride=2 * chunks)
            spread_ref[place, :] = column[n * count : (n + 1) * count]
    sent_ref[...] = spread_ref[...].astype(jnp.bfloat16)


def grads_kernel(
    features, rows_ref, acts_ref, gate_out, up_out, down_out, held_ref, sems
):
    units = held_ref.shape[1]
    height = units // PARTS
    copies = []
    for n, (out, first) in enumerate(((gate_out, 0), (up_out, 0), (down_out, features))):
        left = acts_ref[:, n * units : (n + 1) * units].astype(jnp.float32).T.astype(jnp.bfloat16)
        right = rows_ref[:, first : first + features]
        for k in range(PARTS):
            held_ref[n, k * height : (k + 1) * height] = jnp.dot(
                left[k * height : (k + 1) * height], right, preferred_element_type=jnp.float32
            ).astype(jnp.bfloat16)
            part = pl.ds(k * height, height)
            copies.append(
                pltpu.make_async_copy(held_ref.at[n, part], out.at[0, part], sems.at[PARTS * n + k])
            )
            copies[-1].start()
    for copy in copies:
        copy.wait()


def sum_kernel(back_ref, out_ref):
    count, blocks, height, _ = back_ref.shape
    for k in range(blocks):
        total = back_ref[0, k].astype(jnp.float32)
        for n in range(1, count):
            total = total + back_ref[n, k].astype(jnp.float32)
        for r in range(height):
            part = pl.ds((k * height + r) * LANES, LANES)
            out_ref[:, part] = total[r : r + 1, :].astype(jnp.bfloat16)


def exchange(value, distance):
    count = lax.axis_size("group") * lax.axis_size("member")
    return lax.ppermute(value, AXES, [(i, i ^ distance) for i in range(count)])


def in_hbm(value):
    return pltpu.with_memory_space_constraint(value, pltpu.HBM)


def dense_shards(tokens, grad_out, route_token, route_count, route_prob, w_gate, w_up, w_down):
    features = tokens.shape[1]
    units = w_gate.shape[1]
    chunks = features // LANES
    count = lax.axis_size("group") * lax.axis_size("member")
    half = count // 2
    rows = 2 * chunks
    arguments = (tokens, grad_out, route_token, jnp.swapaxes(route_count, 1, 2), route_prob)
    spaces = (pltpu.VMEM, pltpu.VMEM, pltpu.SMEM, pltpu.SMEM, pltpu.SMEM)
    copies = pl.pallas_call(
        functools.partial(pack_kernel, chunks),
        out_shape=pltpu.VMEM((half, rows, LANES), jnp.bfloat16),
        in_specs=[HBM] * 5,
        out_specs=VMEM,
        scratch_shapes=[pltpu.VMEM((rows, LANES), jnp.float32)]
        + [space(value.shape, value.dtype) for space, value in zip(spaces, arguments)]
        + [pltpu.SemaphoreType.DMA((5,))],
        compiler_params=pltpu.CompilerParams(vmem_limit_bytes=4 * 1024 * 1024),
        cost_estimate=pl.CostEstimate(
            flops=40000 * units * features,
            bytes_accessed=16 * units * features,
            transcendentals=0,
        ),
        name="pack_rows",
    )(*[in_hbm(value) for value in arguments])
    cores = [list(range(c, count, 2)) for c in range(2)]
    trade = functools.partial(
        lax.all_to_all,
        axis_name=AXES,
        split_axis=0,
        concat_axis=0,
        tiled=True,
        axis_index_groups=cores,
    )
    mine = trade(copies)
    other = exchange(mine, 1)
    wide = pltpu.VMEM((half * rows, LANES), jnp.float32)
    unpacked = pl.pallas_call(
        functools.partial(unpack_kernel, chunks),
        out_shape=pltpu.VMEM((half, 2 * features), jnp.bfloat16),
        in_specs=[VMEM],
        out_specs=VMEM,
        scratch_shapes=[wide],
        compiler_params=pltpu.CompilerParams(vmem_limit_bytes=2 * 1024 * 1024),
        name="unpack_rows",
    )(mine)
    sent, both, acts = pl.pallas_call(
        functools.partial(partial_kernel, chunks),
        out_shape=(
            pltpu.VMEM((count * chunks, LANES), jnp.bfloat16),
            pltpu.VMEM((count, 2 * features), jnp.bfloat16),
            pltpu.VMEM((count, 3 * units), jnp.bfloat16),
        ),
        in_specs=[VMEM] * 5,
        out_specs=(VMEM,) * 3,
        scratch_shapes=[wide, pltpu.VMEM((count * chunks, LANES), jnp.float32)],
        compiler_params=pltpu.CompilerParams(vmem_limit_bytes=16 * 1024 * 1024),
        name="partial_rows",
    )(unpacked, other, w_gate, w_up, w_down)
    grad_shape = jax.ShapeDtypeStruct((1, units, features), jnp.bfloat16)
    grad_gate, grad_up, grad_down = pl.pallas_call(
        functools.partial(grads_kernel, features),
        out_shape=(grad_shape,) * 3,
        in_specs=[VMEM] * 2,
        out_specs=(HBM, HBM, HBM),
        scratch_shapes=[
            pltpu.VMEM((3, units, features), jnp.bfloat16),
            pltpu.SemaphoreType.DMA((3 * PARTS,)),
        ],
        compiler_params=pltpu.CompilerParams(vmem_limit_bytes=16 * 1024 * 1024),
        cost_estimate=pl.CostEstimate(
            flops=6 * count * units * features,
            bytes_accessed=6 * units * features,
            transcendentals=0,
        ),
        name="weight_grads",
    )(both, acts)
    back = lax.all_to_all(
        sent.reshape(count, chunks // 4, 4, LANES), AXES, 0, 0, tiled=True
    )
    grad_tokens = pl.pallas_call(
        sum_kernel,
        out_shape=jax.ShapeDtypeStruct((1, features), jnp.bfloat16),
        in_specs=[VMEM],
        out_specs=VMEM,
        compiler_params=pltpu.CompilerParams(vmem_limit_bytes=4 * 1024 * 1024),
        name="sum_rows",
    )(back)
    return grad_tokens, grad_gate, grad_up, grad_down


def slice_backward(rows_x, rows_scaled, gate_weight, up_weight, down_weight):
    gate_value = jnp.dot(rows_x, gate_weight.T, preferred_element_type=jnp.float32)
    up_value = jnp.dot(rows_x, up_weight.T, preferred_element_type=jnp.float32)
    sigma_gate = jax.nn.sigmoid(gate_value)
    active = gate_value * sigma_gate
    hidden = (active * up_value).astype(jnp.bfloat16)
    d_hidden = jnp.dot(rows_scaled, down_weight.T, preferred_element_type=jnp.float32)
    d_gate = (d_hidden * up_value * sigma_gate * (1.0 + gate_value * (1.0 - sigma_gate))).astype(
        jnp.bfloat16
    )
    d_up = (d_hidden * active).astype(jnp.bfloat16)
    grad_down = jnp.dot(hidden.T, rows_scaled, preferred_element_type=jnp.float32).astype(
        jnp.bfloat16
    )
    grad_gate = jnp.dot(d_gate.T, rows_x, preferred_element_type=jnp.float32).astype(jnp.bfloat16)
    grad_up = jnp.dot(d_up.T, rows_x, preferred_element_type=jnp.float32).astype(jnp.bfloat16)
    partial_rows = jnp.dot(d_gate, gate_weight, preferred_element_type=jnp.float32)
    partial_rows = partial_rows + jnp.dot(d_up, up_weight, preferred_element_type=jnp.float32)
    return (grad_gate, grad_up, grad_down, partial_rows)


def routed_shards(tokens, grad_out, route_token, route_count, route_prob, w_gate, w_up, w_down):
    groups = route_token.shape[1]
    capacity = route_token.shape[3]
    features = tokens.shape[1]
    block_rows = groups * capacity
    split_count = max(8, lax.axis_size("member") // 8)
    expert_local = lax.axis_index("member") // split_count
    slot_tokens = lax.dynamic_index_in_dim(route_token[0], expert_local, 1, keepdims=False)
    slot_counts = lax.dynamic_index_in_dim(route_count[0], expert_local, 1, keepdims=False)
    slot_probs = lax.dynamic_index_in_dim(route_prob[0], expert_local, 1, keepdims=False)
    slot_index = jnp.arange(capacity, dtype=jnp.int32)[None, :]
    live = (slot_index < slot_counts[:, None]).astype(jnp.float32)
    slot_weights = (slot_probs * live).reshape(-1)
    flat_slots = slot_tokens.reshape(-1)
    group_x, group_dy = (
        lax.all_gather(tokens, "member", axis=0, tiled=True),
        lax.all_gather(grad_out, "member", axis=0, tiled=True),
    )
    picked_x = jnp.take(group_x, flat_slots, axis=0)
    picked_dy = jnp.take(group_dy, flat_slots, axis=0)
    scaled = (slot_weights[:, None] * picked_dy.astype(jnp.float32)).astype(jnp.bfloat16)
    send_x = picked_x.reshape(groups, capacity, features)
    send_scaled = scaled.reshape(groups, capacity, features)
    rows_x, rows_scaled = (
        lax.all_to_all(send_x, "group", split_axis=0, concat_axis=0, tiled=True),
        lax.all_to_all(send_scaled, "group", split_axis=0, concat_axis=0, tiled=True),
    )
    grad_gate, grad_up, grad_down, partial_rows = slice_backward(
        rows_x.reshape(block_rows, features),
        rows_scaled.reshape(block_rows, features),
        w_gate[0],
        w_up[0],
        w_down[0],
    )
    returned = lax.all_to_all(
        partial_rows.reshape(groups, capacity, features),
        "group",
        split_axis=0,
        concat_axis=0,
        tiled=True,
    )
    returned = returned.reshape(block_rows, features)
    row_numbers = jnp.arange(tokens.shape[0] * lax.axis_size("member"), dtype=jnp.int32)
    selector = (row_numbers[:, None] == flat_slots[None, :]).astype(jnp.float32)
    summed = lax.psum_scatter(
        jnp.dot(
            selector, returned, precision=lax.Precision.HIGHEST, preferred_element_type=jnp.float32
        ),
        "member",
        scatter_dimension=0,
        tiled=True,
    )
    return (summed.astype(jnp.bfloat16), grad_gate[None], grad_up[None], grad_down[None])


def shards(tokens, grad_out, route_token, *rest):
    devices = lax.axis_size("group") * lax.axis_size("member")
    _, groups, experts, capacity = route_token.shape
    dense = devices * tokens.shape[0] <= groups * capacity and experts == 1
    paired = tokens.shape[0] == 1 and devices & (devices - 1) == 0
    body = dense_shards if dense and paired else routed_shards
    return body(tokens, grad_out, route_token, *rest)


def solution(mesh):
    placed = (
        P(("group", "member"), None),
        P(("group", "member"), None),
        P("group", None, None, None),
        P("group", None, None),
        P("group", None, None, None),
        P(("group", "member"), None, None),
        P(("group", "member"), None, None),
        P(("group", "member"), None, None),
    )
    return jax.shard_map(
        shards,
        mesh=mesh,
        in_specs=placed,
        out_specs=(
            P(("group", "member"), None),
            P(("group", "member"), None, None),
            P(("group", "member"), None, None),
            P(("group", "member"), None, None),
        ),
        check_vma=False,
    )
```

```python
import functools

import jax
import jax.numpy as jnp
from jax import lax
from jax.experimental import pallas as pl
from jax.experimental.pallas import tpu as pltpu
from jax.sharding import PartitionSpec as P

LANES = 128
PARTS = 4
AXES = ("group", "member")
VMEM = pl.BlockSpec(memory_space=pltpu.VMEM)
HBM = pl.BlockSpec(memory_space=pltpu.HBM)
SMEM = pl.BlockSpec(memory_space=pltpu.SMEM)
NT = (((1,), (1,)), ((), ()))
TN = (((0,), (0,)), ((), ()))


def pack_kernel(
    chunks,
    tokens_hbm,
    grad_hbm,
    token_hbm,
    count_hbm,
    prob_hbm,
    out_ref,
    rows_ref,
    tokens_ref,
    grad_ref,
    token_ref,
    count_ref,
    prob_ref,
    sems,
):
    pairs = (
        (token_hbm, token_ref),
        (count_hbm, count_ref),
        (prob_hbm, prob_ref),
        (tokens_hbm, tokens_ref),
        (grad_hbm, grad_ref),
    )
    copies = [pltpu.make_async_copy(*pair, sems.at[n]) for n, pair in enumerate(pairs)]
    for copy in copies:
        copy.start()
    for copy in copies:
        copy.wait()
    me = lax.axis_index("member")
    groups, _, capacity = token_ref.shape[1:]
    token_row = tokens_ref[...].astype(jnp.float32)
    grad_row = grad_ref[...].astype(jnp.float32)
    for k in range(chunks):
        part = slice(k * LANES, (k + 1) * LANES)
        rows_ref[k : k + 1, :] = token_row[:, part]
        rows_ref[chunks + k : chunks + k + 1, :] = grad_row[:, part]
    rows = rows_ref[...]
    is_token = lax.broadcasted_iota(jnp.int32, rows.shape, 0) < chunks
    places = out_ref.shape[0] // groups
    for g in range(groups):
        weight = jnp.float32(0)
        for p in range(capacity):
            live = (token_ref[0, g, 0, p] == me) & (p < count_ref[0, 0, g])
            weight = weight + jnp.where(live, prob_ref[0, g, 0, p], 0.0)
        packed = jnp.where(is_token, rows, rows * weight).astype(jnp.bfloat16)
        for n in range(places):
            out_ref[g * places + n] = packed


def unpack_rows(chunks, packed_ref, wide_ref, rows_ref):
    tokens, rows, _ = packed_ref.shape
    wide_ref[...] = packed_ref[...].astype(jnp.float32).reshape(tokens * rows, LANES)
    for k in range(rows):
        column = wide_ref[pl.ds(k, tokens, stride=rows), :]
        rows_ref[:, k * LANES : (k + 1) * LANES] = column.astype(jnp.bfloat16)


def unpack_kernel(chunks, mine_ref, rows_ref, wide_ref):
    unpack_rows(chunks, mine_ref, wide_ref, rows_ref)


def partial_kernel(
    chunks,
    mine_ref,
    other_ref,
    gate_ref,
    up_ref,
    down_ref,
    sent_ref,
    rows_ref,
    acts_ref,
    wide_ref,
    spread_ref,
):
    count = mine_ref.shape[0]
    tokens = 2 * count
    features = chunks * LANES
    units = gate_ref.shape[1]
    rows_ref[:count] = mine_ref[...]
    unpack_rows(chunks, other_ref, wide_ref, rows_ref.at[pl.ds(count, count)])
    x, scaled = rows_ref[:, :features], rows_ref[:, features:]
    both = jnp.concatenate([gate_ref[0], up_ref[0]], axis=0)
    values = lax.dot_general(both, x, NT, preferred_element_type=jnp.float32)
    gate_value, up_value = values[:units], values[units:]
    d_hidden = lax.dot_general(down_ref[0], scaled, NT, preferred_element_type=jnp.float32)
    sigma_gate = jax.nn.sigmoid(gate_value)
    active = gate_value * sigma_gate
    d_gate = d_hidden * up_value * sigma_gate * (1.0 + gate_value * (1.0 - sigma_gate))
    acts_ref[0:units] = d_gate.astype(jnp.bfloat16)
    acts_ref[units : 2 * units] = (d_hidden * active).astype(jnp.bfloat16)
    acts_ref[2 * units :] = (active * up_value).astype(jnp.bfloat16)
    partial = lax.dot_general(
        acts_ref[: 2 * units], both, TN, preferred_element_type=jnp.float32
    )
    core = lax.rem(lax.axis_index("member"), 2)
    for k in range(chunks):
        column = partial[:, k * LANES : (k + 1) * LANES]
        for n in range(2):
            place = pl.ds((core ^ n) * chunks + k, count, stride=2 * chunks)
            spread_ref[place, :] = column[n * count : (n + 1) * count]
    owners, blocks, height, _ = sent_ref.shape
    for owner in range(owners):
        for k in range(blocks):
            first = owner * chunks + k * height
            sent_ref[owner, k] = spread_ref[first : first + height, :].astype(jnp.bfloat16)


def grads_kernel(
    features, rows_ref, acts_ref, gate_out, up_out, down_out, held_ref, sems
):
    units = held_ref.shape[1]
    height = units // PARTS
    copies = []
    for n, (out, first) in enumerate(((gate_out, 0), (up_out, 0), (down_out, features))):
        right = rows_ref[:, first : first + features]
        for k in range(PARTS):
            left = acts_ref[n * units + k * height : n * units + (k + 1) * height, :]
            held_ref[n, k * height : (k + 1) * height] = jnp.dot(
                left, right, preferred_element_type=jnp.float32
            ).astype(jnp.bfloat16)
            part = pl.ds(k * height, height)
            copies.append(
                pltpu.make_async_copy(held_ref.at[n, part], out.at[0, part], sems.at[PARTS * n + k])
            )
            copies[-1].start()
    for copy in copies:
        copy.wait()


def sum_kernel(back_ref, out_ref):
    count, blocks, height, _ = back_ref.shape
    for k in range(blocks):
        total = back_ref[0, k].astype(jnp.float32)
        for n in range(1, count):
            total = total + back_ref[n, k].astype(jnp.float32)
        for r in range(height):
            part = pl.ds((k * height + r) * LANES, LANES)
            out_ref[:, part] = total[r : r + 1, :].astype(jnp.bfloat16)


def exchange(value, distance):
    count = lax.axis_size("group") * lax.axis_size("member")
    return lax.ppermute(value, AXES, [(i, i ^ distance) for i in range(count)])


def in_hbm(value):
    return pltpu.with_memory_space_constraint(value, pltpu.HBM)


def dense_shards(tokens, grad_out, route_token, route_count, route_prob, w_gate, w_up, w_down):
    features = tokens.shape[1]
    units = w_gate.shape[1]
    chunks = features // LANES
    count = lax.axis_size("group") * lax.axis_size("member")
    half = count // 2
    rows = 2 * chunks
    arguments = (tokens, grad_out, route_token, jnp.swapaxes(route_count, 1, 2), route_prob)
    spaces = (pltpu.VMEM, pltpu.VMEM, pltpu.SMEM, pltpu.SMEM, pltpu.SMEM)
    copies = pl.pallas_call(
        functools.partial(pack_kernel, chunks),
        out_shape=pltpu.VMEM((half, rows, LANES), jnp.bfloat16),
        in_specs=[HBM] * 5,
        out_specs=VMEM,
        scratch_shapes=[pltpu.VMEM((rows, LANES), jnp.float32)]
        + [space(value.shape, value.dtype) for space, value in zip(spaces, arguments)]
        + [pltpu.SemaphoreType.DMA((5,))],
        compiler_params=pltpu.CompilerParams(vmem_limit_bytes=4 * 1024 * 1024),
        cost_estimate=pl.CostEstimate(
            flops=40000 * units * features,
            bytes_accessed=16 * units * features,
            transcendentals=0,
        ),
        name="pack_rows",
    )(*[in_hbm(value) for value in arguments])
    cores = [list(range(c, count, 2)) for c in range(2)]
    trade = functools.partial(
        lax.all_to_all,
        axis_name=AXES,
        split_axis=0,
        concat_axis=0,
        tiled=True,
        axis_index_groups=cores,
    )
    mine = trade(copies)
    other = exchange(mine, 1)
    wide = pltpu.VMEM((half * rows, LANES), jnp.float32)
    unpacked = pl.pallas_call(
        functools.partial(unpack_kernel, chunks),
        out_shape=pltpu.VMEM((half, 2 * features), jnp.bfloat16),
        in_specs=[VMEM],
        out_specs=VMEM,
        scratch_shapes=[wide],
        compiler_params=pltpu.CompilerParams(vmem_limit_bytes=2 * 1024 * 1024),
        name="unpack_rows",
    )(mine)
    sent, both, acts = pl.pallas_call(
        functools.partial(partial_kernel, chunks),
        out_shape=(
            pltpu.VMEM((count, chunks // 4, 4, LANES), jnp.bfloat16),
            pltpu.VMEM((count, 2 * features), jnp.bfloat16),
            pltpu.VMEM((3 * units, count), jnp.bfloat16),
        ),
        in_specs=[VMEM] * 5,
        out_specs=(VMEM,) * 3,
        scratch_shapes=[wide, pltpu.VMEM((count * chunks, LANES), jnp.float32)],
        compiler_params=pltpu.CompilerParams(vmem_limit_bytes=16 * 1024 * 1024),
        name="partial_rows",
    )(unpacked, other, w_gate, w_up, w_down)
    grad_shape = jax.ShapeDtypeStruct((1, units, features), jnp.bfloat16)
    grad_gate, grad_up, grad_down = pl.pallas_call(
        functools.partial(grads_kernel, features),
        out_shape=(grad_shape,) * 3,
        in_specs=[VMEM] * 2,
        out_specs=(HBM, HBM, HBM),
        scratch_shapes=[
            pltpu.VMEM((3, units, features), jnp.bfloat16),
            pltpu.SemaphoreType.DMA((3 * PARTS,)),
        ],
        compiler_params=pltpu.CompilerParams(vmem_limit_bytes=16 * 1024 * 1024),
        cost_estimate=pl.CostEstimate(
            flops=6 * count * units * features,
            bytes_accessed=6 * units * features,
            transcendentals=0,
        ),
        name="weight_grads",
    )(both, acts)
    back = lax.all_to_all(sent, AXES, 0, 0, tiled=True)
    grad_tokens = pl.pallas_call(
        sum_kernel,
        out_shape=jax.ShapeDtypeStruct((1, features), jnp.bfloat16),
        in_specs=[VMEM],
        out_specs=VMEM,
        compiler_params=pltpu.CompilerParams(vmem_limit_bytes=4 * 1024 * 1024),
        name="sum_rows",
    )(back)
    return grad_tokens, grad_gate, grad_up, grad_down


def slice_backward(rows_x, rows_scaled, gate_weight, up_weight, down_weight):
    gate_value = jnp.dot(rows_x, gate_weight.T, preferred_element_type=jnp.float32)
    up_value = jnp.dot(rows_x, up_weight.T, preferred_element_type=jnp.float32)
    sigma_gate = jax.nn.sigmoid(gate_value)
    active = gate_value * sigma_gate
    hidden = (active * up_value).astype(jnp.bfloat16)
    d_hidden = jnp.dot(rows_scaled, down_weight.T, preferred_element_type=jnp.float32)
    d_gate = (d_hidden * up_value * sigma_gate * (1.0 + gate_value * (1.0 - sigma_gate))).astype(
        jnp.bfloat16
    )
    d_up = (d_hidden * active).astype(jnp.bfloat16)
    grad_down = jnp.dot(hidden.T, rows_scaled, preferred_element_type=jnp.float32).astype(
        jnp.bfloat16
    )
    grad_gate = jnp.dot(d_gate.T, rows_x, preferred_element_type=jnp.float32).astype(jnp.bfloat16)
    grad_up = jnp.dot(d_up.T, rows_x, preferred_element_type=jnp.float32).astype(jnp.bfloat16)
    partial_rows = jnp.dot(d_gate, gate_weight, preferred_element_type=jnp.float32)
    partial_rows = partial_rows + jnp.dot(d_up, up_weight, preferred_element_type=jnp.float32)
    return (grad_gate, grad_up, grad_down, partial_rows)


def routed_shards(tokens, grad_out, route_token, route_count, route_prob, w_gate, w_up, w_down):
    groups = route_token.shape[1]
    capacity = route_token.shape[3]
    features = tokens.shape[1]
    block_rows = groups * capacity
    split_count = max(8, lax.axis_size("member") // 8)
    expert_local = lax.axis_index("member") // split_count
    slot_tokens = lax.dynamic_index_in_dim(route_token[0], expert_local, 1, keepdims=False)
    slot_counts = lax.dynamic_index_in_dim(route_count[0], expert_local, 1, keepdims=False)
    slot_probs = lax.dynamic_index_in_dim(route_prob[0], expert_local, 1, keepdims=False)
    slot_index = jnp.arange(capacity, dtype=jnp.int32)[None, :]
    live = (slot_index < slot_counts[:, None]).astype(jnp.float32)
    slot_weights = (slot_probs * live).reshape(-1)
    flat_slots = slot_tokens.reshape(-1)
    group_x, group_dy = (
        lax.all_gather(tokens, "member", axis=0, tiled=True),
        lax.all_gather(grad_out, "member", axis=0, tiled=True),
    )
    picked_x = jnp.take(group_x, flat_slots, axis=0)
    picked_dy = jnp.take(group_dy, flat_slots, axis=0)
    scaled = (slot_weights[:, None] * picked_dy.astype(jnp.float32)).astype(jnp.bfloat16)
    send_x = picked_x.reshape(groups, capacity, features)
    send_scaled = scaled.reshape(groups, capacity, features)
    rows_x, rows_scaled = (
        lax.all_to_all(send_x, "group", split_axis=0, concat_axis=0, tiled=True),
        lax.all_to_all(send_scaled, "group", split_axis=0, concat_axis=0, tiled=True),
    )
    grad_gate, grad_up, grad_down, partial_rows = slice_backward(
        rows_x.reshape(block_rows, features),
        rows_scaled.reshape(block_rows, features),
        w_gate[0],
        w_up[0],
        w_down[0],
    )
    returned = lax.all_to_all(
        partial_rows.reshape(groups, capacity, features),
        "group",
        split_axis=0,
        concat_axis=0,
        tiled=True,
    )
    returned = returned.reshape(block_rows, features)
    row_numbers = jnp.arange(tokens.shape[0] * lax.axis_size("member"), dtype=jnp.int32)
    selector = (row_numbers[:, None] == flat_slots[None, :]).astype(jnp.float32)
    summed = lax.psum_scatter(
        jnp.dot(
            selector, returned, precision=lax.Precision.HIGHEST, preferred_element_type=jnp.float32
        ),
        "member",
        scatter_dimension=0,
        tiled=True,
    )
    return (summed.astype(jnp.bfloat16), grad_gate[None], grad_up[None], grad_down[None])


def shards(tokens, grad_out, route_token, *rest):
    devices = lax.axis_size("group") * lax.axis_size("member")
    _, groups, experts, capacity = route_token.shape
    dense = devices * tokens.shape[0] <= groups * capacity and experts == 1
    paired = tokens.shape[0] == 1 and devices & (devices - 1) == 0
    body = dense_shards if dense and paired else routed_shards
    return body(tokens, grad_out, route_token, *rest)


def solution(mesh):
    placed = (
        P(("group", "member"), None),
        P(("group", "member"), None),
        P("group", None, None, None),
        P("group", None, None),
        P("group", None, None, None),
        P(("group", "member"), None, None),
        P(("group", "member"), None, None),
        P(("group", "member"), None, None),
    )
    return jax.shard_map(
        shards,
        mesh=mesh,
        in_specs=placed,
        out_specs=(
            P(("group", "member"), None),
            P(("group", "member"), None, None),
            P(("group", "member"), None, None),
            P(("group", "member"), None, None),
        ),
        check_vma=False,
    )
```

```python
import functools

import jax
import jax.numpy as jnp
from jax import lax
from jax.experimental import pallas as pl
from jax.experimental.pallas import tpu as pltpu
from jax.sharding import PartitionSpec as P

LANES = 128
PARTS = 4
AXES = ("group", "member")
VMEM = pl.BlockSpec(memory_space=pltpu.VMEM)
HBM = pl.BlockSpec(memory_space=pltpu.HBM)
SMEM = pl.BlockSpec(memory_space=pltpu.SMEM)
NT = (((1,), (1,)), ((), ()))
TN = (((0,), (0,)), ((), ()))


def pack_kernel(
    chunks,
    tokens_hbm,
    grad_hbm,
    token_hbm,
    count_hbm,
    prob_hbm,
    out_ref,
    rows_ref,
    tokens_ref,
    grad_ref,
    token_ref,
    count_ref,
    prob_ref,
    sems,
):
    pairs = (
        (token_hbm, token_ref),
        (count_hbm, count_ref),
        (prob_hbm, prob_ref),
        (tokens_hbm, tokens_ref),
        (grad_hbm, grad_ref),
    )
    copies = [pltpu.make_async_copy(*pair, sems.at[n]) for n, pair in enumerate(pairs)]
    for copy in copies:
        copy.start()
    for copy in copies:
        copy.wait()
    me = lax.axis_index("member")
    groups, _, capacity = token_ref.shape[1:]
    token_row = tokens_ref[...].astype(jnp.float32)
    grad_row = grad_ref[...].astype(jnp.float32)
    for k in range(chunks):
        part = slice(k * LANES, (k + 1) * LANES)
        rows_ref[k : k + 1, :] = token_row[:, part]
        rows_ref[chunks + k : chunks + k + 1, :] = grad_row[:, part]
    rows = rows_ref[...]
    is_token = lax.broadcasted_iota(jnp.int32, rows.shape, 0) < chunks
    places = out_ref.shape[0] // groups
    for g in range(groups):
        weight = jnp.float32(0)
        for p in range(capacity):
            live = (token_ref[0, g, 0, p] == me) & (p < count_ref[0, 0, g])
            weight = weight + jnp.where(live, prob_ref[0, g, 0, p], 0.0)
        packed = jnp.where(is_token, rows, rows * weight).astype(jnp.bfloat16)
        for n in range(places):
            out_ref[g * places + n] = packed


def unpack_rows(chunks, packed_ref, wide_ref, rows_ref):
    tokens, rows, _ = packed_ref.shape
    wide_ref[...] = packed_ref[...].astype(jnp.float32).reshape(tokens * rows, LANES)
    for k in range(rows):
        column = wide_ref[pl.ds(k, tokens, stride=rows), :]
        rows_ref[:, k * LANES : (k + 1) * LANES] = column.astype(jnp.bfloat16)


def unpack_kernel(chunks, mine_ref, rows_ref, wide_ref):
    unpack_rows(chunks, mine_ref, wide_ref, rows_ref)


def partial_kernel(
    chunks,
    mine_ref,
    other_ref,
    gate_ref,
    up_ref,
    down_ref,
    sent_hbm,
    rows_ref,
    acts_ref,
    wide_ref,
    spread_ref,
    held_ref,
    sems,
):
    count = mine_ref.shape[0]
    tokens = 2 * count
    features = chunks * LANES
    units = gate_ref.shape[1]
    rows_ref[:count] = mine_ref[...]
    unpack_rows(chunks, other_ref, wide_ref, rows_ref.at[pl.ds(count, count)])
    x, scaled = rows_ref[:, :features], rows_ref[:, features:]
    gate_value = lax.dot_general(gate_ref[0], x, NT, preferred_element_type=jnp.float32)
    up_value = lax.dot_general(up_ref[0], x, NT, preferred_element_type=jnp.float32)
    d_hidden = lax.dot_general(down_ref[0], scaled, NT, preferred_element_type=jnp.float32)
    sigma_gate = jax.nn.sigmoid(gate_value)
    active = gate_value * sigma_gate
    d_gate = d_hidden * up_value * sigma_gate * (1.0 + gate_value * (1.0 - sigma_gate))
    acts_ref[0:units] = d_gate.astype(jnp.bfloat16)
    acts_ref[units : 2 * units] = (d_hidden * active).astype(jnp.bfloat16)
    acts_ref[2 * units :] = (active * up_value).astype(jnp.bfloat16)
    core = lax.rem(lax.axis_index("member"), 2)
    blocks, owners, height, _ = held_ref.shape
    copies = []
    for k in range(blocks):
        part = slice(k * height * LANES, (k + 1) * height * LANES)
        partial = lax.dot_general(
            acts_ref[:units], gate_ref[0, :, part], TN, preferred_element_type=jnp.float32
        ) + lax.dot_general(
            acts_ref[units : 2 * units], up_ref[0, :, part], TN, preferred_element_type=jnp.float32
        )
        for r in range(height):
            column = partial[:, r * LANES : (r + 1) * LANES]
            for n in range(2):
                place = pl.ds(k * owners * height + (core ^ n) * height + r, count, stride=2 * height)
                spread_ref[place, :] = column[n * count : (n + 1) * count]
        for owner in range(owners):
            first = (k * owners + owner) * height
            held_ref[k, owner] = spread_ref[first : first + height, :].astype(jnp.bfloat16)
        copies.append(pltpu.make_async_copy(held_ref.at[k], sent_hbm.at[:, k], sems.at[k]))
        copies[-1].start()
    for copy in copies:
        copy.wait()


def grads_kernel(
    features, rows_ref, acts_ref, gate_out, up_out, down_out, held_ref, sems
):
    units = held_ref.shape[1]
    height = units // PARTS
    copies = []
    for n, (out, first) in enumerate(((gate_out, 0), (up_out, 0), (down_out, features))):
        right = rows_ref[:, first : first + features]
        for k in range(PARTS):
            left = acts_ref[n * units + k * height : n * units + (k + 1) * height, :]
            held_ref[n, k * height : (k + 1) * height] = jnp.dot(
                left, right, preferred_element_type=jnp.float32
            ).astype(jnp.bfloat16)
            part = pl.ds(k * height, height)
            copies.append(
                pltpu.make_async_copy(held_ref.at[n, part], out.at[0, part], sems.at[PARTS * n + k])
            )
            copies[-1].start()
    for copy in copies:
        copy.wait()


def sum_kernel(back_ref, out_ref):
    count, blocks, height, _ = back_ref.shape
    for k in range(blocks):
        total = back_ref[0, k].astype(jnp.float32)
        for n in range(1, count):
            total = total + back_ref[n, k].astype(jnp.float32)
        for r in range(height):
            part = pl.ds((k * height + r) * LANES, LANES)
            out_ref[:, part] = total[r : r + 1, :].astype(jnp.bfloat16)


def exchange(value, distance):
    count = lax.axis_size("group") * lax.axis_size("member")
    return lax.ppermute(value, AXES, [(i, i ^ distance) for i in range(count)])


def in_hbm(value):
    return pltpu.with_memory_space_constraint(value, pltpu.HBM)


def dense_shards(tokens, grad_out, route_token, route_count, route_prob, w_gate, w_up, w_down):
    features = tokens.shape[1]
    units = w_gate.shape[1]
    chunks = features // LANES
    count = lax.axis_size("group") * lax.axis_size("member")
    half = count // 2
    rows = 2 * chunks
    arguments = (tokens, grad_out, route_token, jnp.swapaxes(route_count, 1, 2), route_prob)
    spaces = (pltpu.VMEM, pltpu.VMEM, pltpu.SMEM, pltpu.SMEM, pltpu.SMEM)
    copies = pl.pallas_call(
        functools.partial(pack_kernel, chunks),
        out_shape=pltpu.VMEM((half, rows, LANES), jnp.bfloat16),
        in_specs=[HBM] * 5,
        out_specs=VMEM,
        scratch_shapes=[pltpu.VMEM((rows, LANES), jnp.float32)]
        + [space(value.shape, value.dtype) for space, value in zip(spaces, arguments)]
        + [pltpu.SemaphoreType.DMA((5,))],
        compiler_params=pltpu.CompilerParams(vmem_limit_bytes=4 * 1024 * 1024),
        cost_estimate=pl.CostEstimate(
            flops=40000 * units * features,
            bytes_accessed=16 * units * features,
            transcendentals=0,
        ),
        name="pack_rows",
    )(*[in_hbm(value) for value in arguments])
    cores = [list(range(c, count, 2)) for c in range(2)]
    trade = functools.partial(
        lax.all_to_all,
        axis_name=AXES,
        split_axis=0,
        concat_axis=0,
        tiled=True,
        axis_index_groups=cores,
    )
    mine = trade(copies)
    other = exchange(mine, 1)
    wide = pltpu.VMEM((half * rows, LANES), jnp.float32)
    unpacked = pl.pallas_call(
        functools.partial(unpack_kernel, chunks),
        out_shape=pltpu.VMEM((half, 2 * features), jnp.bfloat16),
        in_specs=[VMEM],
        out_specs=VMEM,
        scratch_shapes=[wide],
        compiler_params=pltpu.CompilerParams(vmem_limit_bytes=2 * 1024 * 1024),
        name="unpack_rows",
    )(mine)
    sent, both, acts = pl.pallas_call(
        functools.partial(partial_kernel, chunks),
        out_shape=(
            jax.ShapeDtypeStruct((count, chunks // 4, 4, LANES), jnp.bfloat16),
            pltpu.VMEM((count, 2 * features), jnp.bfloat16),
            pltpu.VMEM((3 * units, count), jnp.bfloat16),
        ),
        in_specs=[VMEM] * 5,
        out_specs=(HBM, VMEM, VMEM),
        scratch_shapes=[
            wide,
            pltpu.VMEM((count * chunks, LANES), jnp.float32),
            pltpu.VMEM((chunks // 4, count, 4, LANES), jnp.bfloat16),
            pltpu.SemaphoreType.DMA((chunks // 4,)),
        ],
        compiler_params=pltpu.CompilerParams(vmem_limit_bytes=16 * 1024 * 1024),
        name="partial_rows",
    )(unpacked, other, w_gate, w_up, w_down)
    grad_shape = jax.ShapeDtypeStruct((1, units, features), jnp.bfloat16)
    grad_gate, grad_up, grad_down = pl.pallas_call(
        functools.partial(grads_kernel, features),
        out_shape=(grad_shape,) * 3,
        in_specs=[VMEM] * 2,
        out_specs=(HBM, HBM, HBM),
        scratch_shapes=[
            pltpu.VMEM((3, units, features), jnp.bfloat16),
            pltpu.SemaphoreType.DMA((3 * PARTS,)),
        ],
        compiler_params=pltpu.CompilerParams(vmem_limit_bytes=16 * 1024 * 1024),
        cost_estimate=pl.CostEstimate(
            flops=6 * count * units * features,
            bytes_accessed=6 * units * features,
            transcendentals=0,
        ),
        name="weight_grads",
    )(both, acts)
    back = lax.all_to_all(sent, AXES, 0, 0, tiled=True)
    grad_tokens = pl.pallas_call(
        sum_kernel,
        out_shape=jax.ShapeDtypeStruct((1, features), jnp.bfloat16),
        in_specs=[VMEM],
        out_specs=VMEM,
        compiler_params=pltpu.CompilerParams(vmem_limit_bytes=4 * 1024 * 1024),
        name="sum_rows",
    )(back)
    return grad_tokens, grad_gate, grad_up, grad_down


def slice_backward(rows_x, rows_scaled, gate_weight, up_weight, down_weight):
    gate_value = jnp.dot(rows_x, gate_weight.T, preferred_element_type=jnp.float32)
    up_value = jnp.dot(rows_x, up_weight.T, preferred_element_type=jnp.float32)
    sigma_gate = jax.nn.sigmoid(gate_value)
    active = gate_value * sigma_gate
    hidden = (active * up_value).astype(jnp.bfloat16)
    d_hidden = jnp.dot(rows_scaled, down_weight.T, preferred_element_type=jnp.float32)
    d_gate = (d_hidden * up_value * sigma_gate * (1.0 + gate_value * (1.0 - sigma_gate))).astype(
        jnp.bfloat16
    )
    d_up = (d_hidden * active).astype(jnp.bfloat16)
    grad_down = jnp.dot(hidden.T, rows_scaled, preferred_element_type=jnp.float32).astype(
        jnp.bfloat16
    )
    grad_gate = jnp.dot(d_gate.T, rows_x, preferred_element_type=jnp.float32).astype(jnp.bfloat16)
    grad_up = jnp.dot(d_up.T, rows_x, preferred_element_type=jnp.float32).astype(jnp.bfloat16)
    partial_rows = jnp.dot(d_gate, gate_weight, preferred_element_type=jnp.float32)
    partial_rows = partial_rows + jnp.dot(d_up, up_weight, preferred_element_type=jnp.float32)
    return (grad_gate, grad_up, grad_down, partial_rows)


def routed_shards(tokens, grad_out, route_token, route_count, route_prob, w_gate, w_up, w_down):
    groups = route_token.shape[1]
    capacity = route_token.shape[3]
    features = tokens.shape[1]
    block_rows = groups * capacity
    split_count = max(8, lax.axis_size("member") // 8)
    expert_local = lax.axis_index("member") // split_count
    slot_tokens = lax.dynamic_index_in_dim(route_token[0], expert_local, 1, keepdims=False)
    slot_counts = lax.dynamic_index_in_dim(route_count[0], expert_local, 1, keepdims=False)
    slot_probs = lax.dynamic_index_in_dim(route_prob[0], expert_local, 1, keepdims=False)
    slot_index = jnp.arange(capacity, dtype=jnp.int32)[None, :]
    live = (slot_index < slot_counts[:, None]).astype(jnp.float32)
    slot_weights = (slot_probs * live).reshape(-1)
    flat_slots = slot_tokens.reshape(-1)
    group_x, group_dy = (
        lax.all_gather(tokens, "member", axis=0, tiled=True),
        lax.all_gather(grad_out, "member", axis=0, tiled=True),
    )
    picked_x = jnp.take(group_x, flat_slots, axis=0)
    picked_dy = jnp.take(group_dy, flat_slots, axis=0)
    scaled = (slot_weights[:, None] * picked_dy.astype(jnp.float32)).astype(jnp.bfloat16)
    send_x = picked_x.reshape(groups, capacity, features)
    send_scaled = scaled.reshape(groups, capacity, features)
    rows_x, rows_scaled = (
        lax.all_to_all(send_x, "group", split_axis=0, concat_axis=0, tiled=True),
        lax.all_to_all(send_scaled, "group", split_axis=0, concat_axis=0, tiled=True),
    )
    grad_gate, grad_up, grad_down, partial_rows = slice_backward(
        rows_x.reshape(block_rows, features),
        rows_scaled.reshape(block_rows, features),
        w_gate[0],
        w_up[0],
        w_down[0],
    )
    returned = lax.all_to_all(
        partial_rows.reshape(groups, capacity, features),
        "group",
        split_axis=0,
        concat_axis=0,
        tiled=True,
    )
    returned = returned.reshape(block_rows, features)
    row_numbers = jnp.arange(tokens.shape[0] * lax.axis_size("member"), dtype=jnp.int32)
    selector = (row_numbers[:, None] == flat_slots[None, :]).astype(jnp.float32)
    summed = lax.psum_scatter(
        jnp.dot(
            selector, returned, precision=lax.Precision.HIGHEST, preferred_element_type=jnp.float32
        ),
        "member",
        scatter_dimension=0,
        tiled=True,
    )
    return (summed.astype(jnp.bfloat16), grad_gate[None], grad_up[None], grad_down[None])


def shards(tokens, grad_out, route_token, *rest):
    devices = lax.axis_size("group") * lax.axis_size("member")
    _, groups, experts, capacity = route_token.shape
    dense = devices * tokens.shape[0] <= groups * capacity and experts == 1
    paired = tokens.shape[0] == 1 and devices & (devices - 1) == 0
    body = dense_shards if dense and paired else routed_shards
    return body(tokens, grad_out, route_token, *rest)


def solution(mesh):
    placed = (
        P(("group", "member"), None),
        P(("group", "member"), None),
        P("group", None, None, None),
        P("group", None, None),
        P("group", None, None, None),
        P(("group", "member"), None, None),
        P(("group", "member"), None, None),
        P(("group", "member"), None, None),
    )
    return jax.shard_map(
        shards,
        mesh=mesh,
        in_specs=placed,
        out_specs=(
            P(("group", "member"), None),
            P(("group", "member"), None, None),
            P(("group", "member"), None, None),
            P(("group", "member"), None, None),
        ),
        check_vma=False,
    )
```

```python
import functools

import jax
import jax.numpy as jnp
from jax import lax
from jax.experimental import pallas as pl
from jax.experimental.pallas import tpu as pltpu
from jax.sharding import PartitionSpec as P

LANES = 128
PARTS = 4
AXES = ("group", "member")
VMEM = pl.BlockSpec(memory_space=pltpu.VMEM)
HBM = pl.BlockSpec(memory_space=pltpu.HBM)
SMEM = pl.BlockSpec(memory_space=pltpu.SMEM)
NT = (((1,), (1,)), ((), ()))
TN = (((0,), (0,)), ((), ()))


def pack_kernel(
    chunks,
    tokens_hbm,
    grad_hbm,
    token_hbm,
    count_hbm,
    prob_hbm,
    out_ref,
    rows_ref,
    tokens_ref,
    grad_ref,
    token_ref,
    count_ref,
    prob_ref,
    sems,
):
    pairs = (
        (token_hbm, token_ref),
        (count_hbm, count_ref),
        (prob_hbm, prob_ref),
        (tokens_hbm, tokens_ref),
        (grad_hbm, grad_ref),
    )
    copies = [pltpu.make_async_copy(*pair, sems.at[n]) for n, pair in enumerate(pairs)]
    for copy in copies:
        copy.start()
    for copy in copies:
        copy.wait()
    me = lax.axis_index("member")
    groups, _, capacity = token_ref.shape[1:]
    token_row = tokens_ref[...].astype(jnp.float32)
    grad_row = grad_ref[...].astype(jnp.float32)
    for k in range(chunks):
        part = slice(k * LANES, (k + 1) * LANES)
        rows_ref[k : k + 1, :] = token_row[:, part]
        rows_ref[chunks + k : chunks + k + 1, :] = grad_row[:, part]
    rows = rows_ref[...]
    is_token = lax.broadcasted_iota(jnp.int32, rows.shape, 0) < chunks
    places = out_ref.shape[0] // groups
    for g in range(groups):
        weight = jnp.float32(0)
        for p in range(capacity):
            live = (token_ref[0, g, 0, p] == me) & (p < count_ref[0, 0, g])
            weight = weight + jnp.where(live, prob_ref[0, g, 0, p], 0.0)
        packed = jnp.where(is_token, rows, rows * weight).astype(jnp.bfloat16)
        for n in range(places):
            out_ref[g * places + n] = packed


def unpack_rows(chunks, packed_ref, wide_ref, rows_ref):
    tokens, rows, _ = packed_ref.shape
    wide_ref[...] = packed_ref[...].astype(jnp.float32).reshape(tokens * rows, LANES)
    for k in range(rows):
        column = wide_ref[pl.ds(k, tokens, stride=rows), :]
        rows_ref[:, k * LANES : (k + 1) * LANES] = column.astype(jnp.bfloat16)


def unpack_kernel(chunks, mine_ref, rows_ref, wide_ref):
    unpack_rows(chunks, mine_ref, wide_ref, rows_ref)


def partial_kernel(
    chunks,
    mine_ref,
    other_ref,
    gate_ref,
    up_ref,
    down_ref,
    sent_ref,
    rows_ref,
    acts_ref,
    wide_ref,
    spread_ref,
):
    count = mine_ref.shape[0]
    tokens = 2 * count
    features = chunks * LANES
    units = gate_ref.shape[1]
    rows_ref[:count] = mine_ref[...]
    unpack_rows(chunks, other_ref, wide_ref, rows_ref.at[pl.ds(count, count)])
    x, scaled = rows_ref[:, :features], rows_ref[:, features:]
    both = jnp.concatenate([gate_ref[0], up_ref[0]], axis=0)
    values = lax.dot_general(both, x, NT, preferred_element_type=jnp.float32)
    gate_value, up_value = values[:units], values[units:]
    d_hidden = lax.dot_general(down_ref[0], scaled, NT, preferred_element_type=jnp.float32)
    sigma_gate = jax.nn.sigmoid(gate_value)
    active = gate_value * sigma_gate
    d_gate = d_hidden * up_value * sigma_gate * (1.0 + gate_value * (1.0 - sigma_gate))
    acts_ref[0:units] = d_gate.astype(jnp.bfloat16)
    acts_ref[units : 2 * units] = (d_hidden * active).astype(jnp.bfloat16)
    acts_ref[2 * units :] = (active * up_value).astype(jnp.bfloat16)
    partial = lax.dot_general(
        acts_ref[: 2 * units], both, TN, preferred_element_type=jnp.float32
    )
    core = lax.rem(lax.axis_index("member"), 2)
    for k in range(chunks):
        column = partial[:, k * LANES : (k + 1) * LANES]
        for n in range(2):
            place = pl.ds((core ^ n) * chunks + k, count, stride=2 * chunks)
            spread_ref[place, :] = column[n * count : (n + 1) * count]
    sent_ref[...] = spread_ref[: tokens * chunks, :].astype(jnp.bfloat16)


def grads_kernel(
    features, rows_ref, acts_ref, gate_out, up_out, down_out, held_ref, sems
):
    units = held_ref.shape[1]
    height = units // PARTS
    copies = []
    for n, (out, first) in enumerate(((gate_out, 0), (up_out, 0), (down_out, features))):
        right = rows_ref[:, first : first + features]
        for k in range(PARTS):
            left = acts_ref[n * units + k * height : n * units + (k + 1) * height, :]
            held_ref[n, k * height : (k + 1) * height] = jnp.dot(
                left, right, preferred_element_type=jnp.float32
            ).astype(jnp.bfloat16)
            part = pl.ds(k * height, height)
            copies.append(
                pltpu.make_async_copy(held_ref.at[n, part], out.at[0, part], sems.at[PARTS * n + k])
            )
            copies[-1].start()
    for copy in copies:
        copy.wait()


def sum_kernel(back_ref, out_ref):
    count, blocks, height, _ = back_ref.shape
    for k in range(blocks):
        total = back_ref[0, k].astype(jnp.float32)
        for n in range(1, count):
            total = total + back_ref[n, k].astype(jnp.float32)
        for r in range(height):
            part = pl.ds((k * height + r) * LANES, LANES)
            out_ref[:, part] = total[r : r + 1, :].astype(jnp.bfloat16)


def exchange(value, distance):
    count = lax.axis_size("group") * lax.axis_size("member")
    return lax.ppermute(value, AXES, [(i, i ^ distance) for i in range(count)])


def in_hbm(value):
    return pltpu.with_memory_space_constraint(value, pltpu.HBM)


def dense_shards(tokens, grad_out, route_token, route_count, route_prob, w_gate, w_up, w_down):
    features = tokens.shape[1]
    units = w_gate.shape[1]
    chunks = features // LANES
    count = lax.axis_size("group") * lax.axis_size("member")
    half = count // 2
    rows = 2 * chunks
    arguments = (tokens, grad_out, route_token, jnp.swapaxes(route_count, 1, 2), route_prob)
    spaces = (pltpu.VMEM, pltpu.VMEM, pltpu.SMEM, pltpu.SMEM, pltpu.SMEM)
    copies = pl.pallas_call(
        functools.partial(pack_kernel, chunks),
        out_shape=pltpu.VMEM((half, rows, LANES), jnp.bfloat16),
        in_specs=[HBM] * 5,
        out_specs=VMEM,
        scratch_shapes=[pltpu.VMEM((rows, LANES), jnp.float32)]
        + [space(value.shape, value.dtype) for space, value in zip(spaces, arguments)]
        + [pltpu.SemaphoreType.DMA((5,))],
        compiler_params=pltpu.CompilerParams(vmem_limit_bytes=4 * 1024 * 1024),
        cost_estimate=pl.CostEstimate(
            flops=40000 * units * features,
            bytes_accessed=16 * units * features,
            transcendentals=0,
        ),
        name="pack_rows",
    )(*[in_hbm(value) for value in arguments])
    cores = [list(range(c, count, 2)) for c in range(2)]
    trade = functools.partial(
        lax.all_to_all,
        axis_name=AXES,
        split_axis=0,
        concat_axis=0,
        tiled=True,
        axis_index_groups=cores,
    )
    mine = trade(copies)
    other = exchange(mine, 1)
    wide = pltpu.VMEM((half * rows, LANES), jnp.float32)
    unpacked = pl.pallas_call(
        functools.partial(unpack_kernel, chunks),
        out_shape=pltpu.VMEM((half, 2 * features), jnp.bfloat16),
        in_specs=[VMEM],
        out_specs=VMEM,
        scratch_shapes=[wide],
        compiler_params=pltpu.CompilerParams(vmem_limit_bytes=2 * 1024 * 1024),
        name="unpack_rows",
    )(mine)
    sent, both, acts = pl.pallas_call(
        functools.partial(partial_kernel, chunks),
        out_shape=(
            pltpu.VMEM((count * chunks, LANES), jnp.bfloat16),
            pltpu.VMEM((count, 2 * features), jnp.bfloat16),
            pltpu.VMEM((3 * units, count), jnp.bfloat16),
        ),
        in_specs=[VMEM] * 5,
        out_specs=(VMEM,) * 3,
        scratch_shapes=[wide, pltpu.VMEM(((count + 2) * chunks, LANES), jnp.float32)],
        compiler_params=pltpu.CompilerParams(vmem_limit_bytes=16 * 1024 * 1024),
        name="partial_rows",
    )(unpacked, other, w_gate, w_up, w_down)
    grad_shape = jax.ShapeDtypeStruct((1, units, features), jnp.bfloat16)
    grad_gate, grad_up, grad_down = pl.pallas_call(
        functools.partial(grads_kernel, features),
        out_shape=(grad_shape,) * 3,
        in_specs=[VMEM] * 2,
        out_specs=(HBM, HBM, HBM),
        scratch_shapes=[
            pltpu.VMEM((3, units, features), jnp.bfloat16),
            pltpu.SemaphoreType.DMA((3 * PARTS,)),
        ],
        compiler_params=pltpu.CompilerParams(vmem_limit_bytes=16 * 1024 * 1024),
        cost_estimate=pl.CostEstimate(
            flops=6 * count * units * features,
            bytes_accessed=6 * units * features,
            transcendentals=0,
        ),
        name="weight_grads",
    )(both, acts)
    back = lax.all_to_all(
        sent.reshape(count, chunks // 4, 4, LANES), AXES, 0, 0, tiled=True
    )
    grad_tokens = pl.pallas_call(
        sum_kernel,
        out_shape=jax.ShapeDtypeStruct((1, features), jnp.bfloat16),
        in_specs=[VMEM],
        out_specs=VMEM,
        compiler_params=pltpu.CompilerParams(vmem_limit_bytes=4 * 1024 * 1024),
        name="sum_rows",
    )(back)
    return grad_tokens, grad_gate, grad_up, grad_down


def slice_backward(rows_x, rows_scaled, gate_weight, up_weight, down_weight):
    gate_value = jnp.dot(rows_x, gate_weight.T, preferred_element_type=jnp.float32)
    up_value = jnp.dot(rows_x, up_weight.T, preferred_element_type=jnp.float32)
    sigma_gate = jax.nn.sigmoid(gate_value)
    active = gate_value * sigma_gate
    hidden = (active * up_value).astype(jnp.bfloat16)
    d_hidden = jnp.dot(rows_scaled, down_weight.T, preferred_element_type=jnp.float32)
    d_gate = (d_hidden * up_value * sigma_gate * (1.0 + gate_value * (1.0 - sigma_gate))).astype(
        jnp.bfloat16
    )
    d_up = (d_hidden * active).astype(jnp.bfloat16)
    grad_down = jnp.dot(hidden.T, rows_scaled, preferred_element_type=jnp.float32).astype(
        jnp.bfloat16
    )
    grad_gate = jnp.dot(d_gate.T, rows_x, preferred_element_type=jnp.float32).astype(jnp.bfloat16)
    grad_up = jnp.dot(d_up.T, rows_x, preferred_element_type=jnp.float32).astype(jnp.bfloat16)
    partial_rows = jnp.dot(d_gate, gate_weight, preferred_element_type=jnp.float32)
    partial_rows = partial_rows + jnp.dot(d_up, up_weight, preferred_element_type=jnp.float32)
    return (grad_gate, grad_up, grad_down, partial_rows)


def routed_shards(tokens, grad_out, route_token, route_count, route_prob, w_gate, w_up, w_down):
    groups = route_token.shape[1]
    capacity = route_token.shape[3]
    features = tokens.shape[1]
    block_rows = groups * capacity
    split_count = max(8, lax.axis_size("member") // 8)
    expert_local = lax.axis_index("member") // split_count
    slot_tokens = lax.dynamic_index_in_dim(route_token[0], expert_local, 1, keepdims=False)
    slot_counts = lax.dynamic_index_in_dim(route_count[0], expert_local, 1, keepdims=False)
    slot_probs = lax.dynamic_index_in_dim(route_prob[0], expert_local, 1, keepdims=False)
    slot_index = jnp.arange(capacity, dtype=jnp.int32)[None, :]
    live = (slot_index < slot_counts[:, None]).astype(jnp.float32)
    slot_weights = (slot_probs * live).reshape(-1)
    flat_slots = slot_tokens.reshape(-1)
    group_x, group_dy = (
        lax.all_gather(tokens, "member", axis=0, tiled=True),
        lax.all_gather(grad_out, "member", axis=0, tiled=True),
    )
    picked_x = jnp.take(group_x, flat_slots, axis=0)
    picked_dy = jnp.take(group_dy, flat_slots, axis=0)
    scaled = (slot_weights[:, None] * picked_dy.astype(jnp.float32)).astype(jnp.bfloat16)
    send_x = picked_x.reshape(groups, capacity, features)
    send_scaled = scaled.reshape(groups, capacity, features)
    rows_x, rows_scaled = (
        lax.all_to_all(send_x, "group", split_axis=0, concat_axis=0, tiled=True),
        lax.all_to_all(send_scaled, "group", split_axis=0, concat_axis=0, tiled=True),
    )
    grad_gate, grad_up, grad_down, partial_rows = slice_backward(
        rows_x.reshape(block_rows, features),
        rows_scaled.reshape(block_rows, features),
        w_gate[0],
        w_up[0],
        w_down[0],
    )
    returned = lax.all_to_all(
        partial_rows.reshape(groups, capacity, features),
        "group",
        split_axis=0,
        concat_axis=0,
        tiled=True,
    )
    returned = returned.reshape(block_rows, features)
    row_numbers = jnp.arange(tokens.shape[0] * lax.axis_size("member"), dtype=jnp.int32)
    selector = (row_numbers[:, None] == flat_slots[None, :]).astype(jnp.float32)
    summed = lax.psum_scatter(
        jnp.dot(
            selector, returned, precision=lax.Precision.HIGHEST, preferred_element_type=jnp.float32
        ),
        "member",
        scatter_dimension=0,
        tiled=True,
    )
    return (summed.astype(jnp.bfloat16), grad_gate[None], grad_up[None], grad_down[None])


def shards(tokens, grad_out, route_token, *rest):
    devices = lax.axis_size("group") * lax.axis_size("member")
    _, groups, experts, capacity = route_token.shape
    dense = devices * tokens.shape[0] <= groups * capacity and experts == 1
    dense = dense and tokens.shape[1] % (4 * LANES) == 0
    paired = tokens.shape[0] == 1 and devices & (devices - 1) == 0
    body = dense_shards if dense and paired else routed_shards
    return body(tokens, grad_out, route_token, *rest)


def solution(mesh):
    placed = (
        P(("group", "member"), None),
        P(("group", "member"), None),
        P("group", None, None, None),
        P("group", None, None),
        P("group", None, None, None),
        P(("group", "member"), None, None),
        P(("group", "member"), None, None),
        P(("group", "member"), None, None),
    )
    return jax.shard_map(
        shards,
        mesh=mesh,
        in_specs=placed,
        out_specs=(
            P(("group", "member"), None),
            P(("group", "member"), None, None),
            P(("group", "member"), None, None),
            P(("group", "member"), None, None),
        ),
        check_vma=False,
    )
```

```python
import functools

import jax
import jax.numpy as jnp
from jax import lax
from jax.experimental import pallas as pl
from jax.experimental.pallas import tpu as pltpu
from jax.sharding import PartitionSpec as P

LANES = 128
PARTS = 4
AXES = ("group", "member")
VMEM = pl.BlockSpec(memory_space=pltpu.VMEM)
HBM = pl.BlockSpec(memory_space=pltpu.HBM)
SMEM = pl.BlockSpec(memory_space=pltpu.SMEM)
NT = (((1,), (1,)), ((), ()))
TN = (((0,), (0,)), ((), ()))


def pack_kernel(
    chunks,
    tokens_hbm,
    grad_hbm,
    token_hbm,
    count_hbm,
    prob_hbm,
    out_ref,
    rows_ref,
    tokens_ref,
    grad_ref,
    token_ref,
    count_ref,
    prob_ref,
    sems,
):
    pairs = (
        (token_hbm, token_ref),
        (count_hbm, count_ref),
        (prob_hbm, prob_ref),
        (tokens_hbm, tokens_ref),
        (grad_hbm, grad_ref),
    )
    copies = [pltpu.make_async_copy(*pair, sems.at[n]) for n, pair in enumerate(pairs)]
    for copy in copies:
        copy.start()
    for copy in copies[:3]:
        copy.wait()
    me = lax.axis_index("member")
    groups, _, capacity = token_ref.shape[1:]
    weights = []
    for g in range(groups):
        weight = jnp.float32(0)
        for p in range(capacity):
            live = (token_ref[0, g, 0, p] == me) & (p < count_ref[0, 0, g])
            weight = weight + jnp.where(live, prob_ref[0, g, 0, p], 0.0)
        weights.append(weight)
    for copy in copies[3:]:
        copy.wait()
    token_row = tokens_ref[...].astype(jnp.float32)
    grad_row = grad_ref[...].astype(jnp.float32)
    for k in range(chunks):
        part = slice(k * LANES, (k + 1) * LANES)
        rows_ref[k : k + 1, :] = token_row[:, part]
        rows_ref[chunks + k : chunks + k + 1, :] = grad_row[:, part]
    rows = rows_ref[...]
    is_token = lax.broadcasted_iota(jnp.int32, rows.shape, 0) < chunks
    places = out_ref.shape[0] // groups
    for g, weight in enumerate(weights):
        packed = jnp.where(is_token, rows, rows * weight).astype(jnp.bfloat16)
        for n in range(places):
            out_ref[g * places + n] = packed


def unpack_rows(chunks, packed_ref, wide_ref, rows_ref):
    tokens, rows, _ = packed_ref.shape
    wide_ref[...] = packed_ref[...].astype(jnp.float32).reshape(tokens * rows, LANES)
    for k in range(rows):
        column = wide_ref[pl.ds(k, tokens, stride=rows), :]
        rows_ref[:, k * LANES : (k + 1) * LANES] = column.astype(jnp.bfloat16)


def unpack_kernel(chunks, mine_ref, rows_ref, wide_ref):
    unpack_rows(chunks, mine_ref, wide_ref, rows_ref)


def partial_kernel(
    chunks,
    mine_ref,
    other_ref,
    gate_ref,
    up_ref,
    down_ref,
    sent_ref,
    rows_ref,
    acts_ref,
    wide_ref,
    spread_ref,
):
    count = mine_ref.shape[0]
    tokens = 2 * count
    features = chunks * LANES
    units = gate_ref.shape[1]
    rows_ref[:count] = mine_ref[...]
    unpack_rows(chunks, other_ref, wide_ref, rows_ref.at[pl.ds(count, count)])
    x, scaled = rows_ref[:, :features], rows_ref[:, features:]
    both = jnp.concatenate([gate_ref[0], up_ref[0]], axis=0)
    values = lax.dot_general(both, x, NT, preferred_element_type=jnp.float32)
    gate_value, up_value = values[:units], values[units:]
    d_hidden = lax.dot_general(down_ref[0], scaled, NT, preferred_element_type=jnp.float32)
    sigma_gate = jax.nn.sigmoid(gate_value)
    active = gate_value * sigma_gate
    d_gate = d_hidden * up_value * sigma_gate * (1.0 + gate_value * (1.0 - sigma_gate))
    acts_ref[0:units] = d_gate.astype(jnp.bfloat16)
    acts_ref[units : 2 * units] = (d_hidden * active).astype(jnp.bfloat16)
    acts_ref[2 * units :] = (active * up_value).astype(jnp.bfloat16)
    partial = lax.dot_general(
        acts_ref[: 2 * units], both, TN, preferred_element_type=jnp.float32
    )
    core = lax.rem(lax.axis_index("member"), 2)
    for k in range(chunks):
        column = partial[:, k * LANES : (k + 1) * LANES]
        for n in range(2):
            place = pl.ds((core ^ n) * chunks + k, count, stride=2 * chunks)
            spread_ref[place, :] = column[n * count : (n + 1) * count]
    sent_ref[...] = spread_ref[: tokens * chunks, :].astype(jnp.bfloat16)


def grads_kernel(
    features, rows_ref, acts_ref, gate_out, up_out, down_out, held_ref, sems
):
    units = held_ref.shape[1]
    height = units // PARTS
    copies = []
    for n, (out, first) in enumerate(((gate_out, 0), (up_out, 0), (down_out, features))):
        right = rows_ref[:, first : first + features]
        for k in range(PARTS):
            left = acts_ref[n * units + k * height : n * units + (k + 1) * height, :]
            held_ref[n, k * height : (k + 1) * height] = jnp.dot(
                left, right, preferred_element_type=jnp.float32
            ).astype(jnp.bfloat16)
            part = pl.ds(k * height, height)
            copies.append(
                pltpu.make_async_copy(held_ref.at[n, part], out.at[0, part], sems.at[PARTS * n + k])
            )
            copies[-1].start()
    for copy in copies:
        copy.wait()


def sum_kernel(back_ref, out_ref):
    count, blocks, height, _ = back_ref.shape
    for k in range(blocks):
        total = back_ref[0, k].astype(jnp.float32)
        for n in range(1, count):
            total = total + back_ref[n, k].astype(jnp.float32)
        for r in range(height):
            part = pl.ds((k * height + r) * LANES, LANES)
            out_ref[:, part] = total[r : r + 1, :].astype(jnp.bfloat16)


def exchange(value, distance):
    count = lax.axis_size("group") * lax.axis_size("member")
    return lax.ppermute(value, AXES, [(i, i ^ distance) for i in range(count)])


def in_hbm(value):
    return pltpu.with_memory_space_constraint(value, pltpu.HBM)


def dense_shards(tokens, grad_out, route_token, route_count, route_prob, w_gate, w_up, w_down):
    features = tokens.shape[1]
    units = w_gate.shape[1]
    chunks = features // LANES
    count = lax.axis_size("group") * lax.axis_size("member")
    half = count // 2
    rows = 2 * chunks
    arguments = (tokens, grad_out, route_token, jnp.swapaxes(route_count, 1, 2), route_prob)
    spaces = (pltpu.VMEM, pltpu.VMEM, pltpu.SMEM, pltpu.SMEM, pltpu.SMEM)
    copies = pl.pallas_call(
        functools.partial(pack_kernel, chunks),
        out_shape=pltpu.VMEM((half, rows, LANES), jnp.bfloat16),
        in_specs=[HBM] * 5,
        out_specs=VMEM,
        scratch_shapes=[pltpu.VMEM((rows, LANES), jnp.float32)]
        + [space(value.shape, value.dtype) for space, value in zip(spaces, arguments)]
        + [pltpu.SemaphoreType.DMA((5,))],
        compiler_params=pltpu.CompilerParams(vmem_limit_bytes=4 * 1024 * 1024),
        cost_estimate=pl.CostEstimate(
            flops=40000 * units * features,
            bytes_accessed=16 * units * features,
            transcendentals=0,
        ),
        name="pack_rows",
    )(*[in_hbm(value) for value in arguments])
    cores = [list(range(c, count, 2)) for c in range(2)]
    trade = functools.partial(
        lax.all_to_all,
        axis_name=AXES,
        split_axis=0,
        concat_axis=0,
        tiled=True,
        axis_index_groups=cores,
    )
    mine = trade(copies)
    other = exchange(mine, 1)
    wide = pltpu.VMEM((half * rows, LANES), jnp.float32)
    unpacked = pl.pallas_call(
        functools.partial(unpack_kernel, chunks),
        out_shape=pltpu.VMEM((half, 2 * features), jnp.bfloat16),
        in_specs=[VMEM],
        out_specs=VMEM,
        scratch_shapes=[wide],
        compiler_params=pltpu.CompilerParams(vmem_limit_bytes=2 * 1024 * 1024),
        name="unpack_rows",
    )(mine)
    sent, both, acts = pl.pallas_call(
        functools.partial(partial_kernel, chunks),
        out_shape=(
            pltpu.VMEM((count * chunks, LANES), jnp.bfloat16),
            pltpu.VMEM((count, 2 * features), jnp.bfloat16),
            pltpu.VMEM((3 * units, count), jnp.bfloat16),
        ),
        in_specs=[VMEM] * 5,
        out_specs=(VMEM,) * 3,
        scratch_shapes=[wide, pltpu.VMEM(((count + 2) * chunks, LANES), jnp.float32)],
        compiler_params=pltpu.CompilerParams(vmem_limit_bytes=16 * 1024 * 1024),
        name="partial_rows",
    )(unpacked, other, w_gate, w_up, w_down)
    grad_shape = jax.ShapeDtypeStruct((1, units, features), jnp.bfloat16)
    grad_gate, grad_up, grad_down = pl.pallas_call(
        functools.partial(grads_kernel, features),
        out_shape=(grad_shape,) * 3,
        in_specs=[VMEM] * 2,
        out_specs=(HBM, HBM, HBM),
        scratch_shapes=[
            pltpu.VMEM((3, units, features), jnp.bfloat16),
            pltpu.SemaphoreType.DMA((3 * PARTS,)),
        ],
        compiler_params=pltpu.CompilerParams(vmem_limit_bytes=16 * 1024 * 1024),
        cost_estimate=pl.CostEstimate(
            flops=6 * count * units * features,
            bytes_accessed=6 * units * features,
            transcendentals=0,
        ),
        name="weight_grads",
    )(both, acts)
    back = lax.all_to_all(
        sent.reshape(count, chunks // 4, 4, LANES), AXES, 0, 0, tiled=True
    )
    grad_tokens = pl.pallas_call(
        sum_kernel,
        out_shape=jax.ShapeDtypeStruct((1, features), jnp.bfloat16),
        in_specs=[VMEM],
        out_specs=VMEM,
        compiler_params=pltpu.CompilerParams(vmem_limit_bytes=4 * 1024 * 1024),
        name="sum_rows",
    )(back)
    return grad_tokens, grad_gate, grad_up, grad_down


def slice_backward(rows_x, rows_scaled, gate_weight, up_weight, down_weight):
    gate_value = jnp.dot(rows_x, gate_weight.T, preferred_element_type=jnp.float32)
    up_value = jnp.dot(rows_x, up_weight.T, preferred_element_type=jnp.float32)
    sigma_gate = jax.nn.sigmoid(gate_value)
    active = gate_value * sigma_gate
    hidden = (active * up_value).astype(jnp.bfloat16)
    d_hidden = jnp.dot(rows_scaled, down_weight.T, preferred_element_type=jnp.float32)
    d_gate = (d_hidden * up_value * sigma_gate * (1.0 + gate_value * (1.0 - sigma_gate))).astype(
        jnp.bfloat16
    )
    d_up = (d_hidden * active).astype(jnp.bfloat16)
    grad_down = jnp.dot(hidden.T, rows_scaled, preferred_element_type=jnp.float32).astype(
        jnp.bfloat16
    )
    grad_gate = jnp.dot(d_gate.T, rows_x, preferred_element_type=jnp.float32).astype(jnp.bfloat16)
    grad_up = jnp.dot(d_up.T, rows_x, preferred_element_type=jnp.float32).astype(jnp.bfloat16)
    partial_rows = jnp.dot(d_gate, gate_weight, preferred_element_type=jnp.float32)
    partial_rows = partial_rows + jnp.dot(d_up, up_weight, preferred_element_type=jnp.float32)
    return (grad_gate, grad_up, grad_down, partial_rows)


def routed_shards(tokens, grad_out, route_token, route_count, route_prob, w_gate, w_up, w_down):
    groups = route_token.shape[1]
    capacity = route_token.shape[3]
    features = tokens.shape[1]
    block_rows = groups * capacity
    split_count = max(8, lax.axis_size("member") // 8)
    expert_local = lax.axis_index("member") // split_count
    slot_tokens = lax.dynamic_index_in_dim(route_token[0], expert_local, 1, keepdims=False)
    slot_counts = lax.dynamic_index_in_dim(route_count[0], expert_local, 1, keepdims=False)
    slot_probs = lax.dynamic_index_in_dim(route_prob[0], expert_local, 1, keepdims=False)
    slot_index = jnp.arange(capacity, dtype=jnp.int32)[None, :]
    live = (slot_index < slot_counts[:, None]).astype(jnp.float32)
    slot_weights = (slot_probs * live).reshape(-1)
    flat_slots = slot_tokens.reshape(-1)
    group_x, group_dy = (
        lax.all_gather(tokens, "member", axis=0, tiled=True),
        lax.all_gather(grad_out, "member", axis=0, tiled=True),
    )
    picked_x = jnp.take(group_x, flat_slots, axis=0)
    picked_dy = jnp.take(group_dy, flat_slots, axis=0)
    scaled = (slot_weights[:, None] * picked_dy.astype(jnp.float32)).astype(jnp.bfloat16)
    send_x = picked_x.reshape(groups, capacity, features)
    send_scaled = scaled.reshape(groups, capacity, features)
    rows_x, rows_scaled = (
        lax.all_to_all(send_x, "group", split_axis=0, concat_axis=0, tiled=True),
        lax.all_to_all(send_scaled, "group", split_axis=0, concat_axis=0, tiled=True),
    )
    grad_gate, grad_up, grad_down, partial_rows = slice_backward(
        rows_x.reshape(block_rows, features),
        rows_scaled.reshape(block_rows, features),
        w_gate[0],
        w_up[0],
        w_down[0],
    )
    returned = lax.all_to_all(
        partial_rows.reshape(groups, capacity, features),
        "group",
        split_axis=0,
        concat_axis=0,
        tiled=True,
    )
    returned = returned.reshape(block_rows, features)
    row_numbers = jnp.arange(tokens.shape[0] * lax.axis_size("member"), dtype=jnp.int32)
    selector = (row_numbers[:, None] == flat_slots[None, :]).astype(jnp.float32)
    summed = lax.psum_scatter(
        jnp.dot(
            selector, returned, precision=lax.Precision.HIGHEST, preferred_element_type=jnp.float32
        ),
        "member",
        scatter_dimension=0,
        tiled=True,
    )
    return (summed.astype(jnp.bfloat16), grad_gate[None], grad_up[None], grad_down[None])


def shards(tokens, grad_out, route_token, *rest):
    devices = lax.axis_size("group") * lax.axis_size("member")
    _, groups, experts, capacity = route_token.shape
    dense = devices * tokens.shape[0] <= groups * capacity and experts == 1
    dense = dense and tokens.shape[1] % (4 * LANES) == 0
    paired = tokens.shape[0] == 1 and devices & (devices - 1) == 0
    body = dense_shards if dense and paired else routed_shards
    return body(tokens, grad_out, route_token, *rest)


def solution(mesh):
    placed = (
        P(("group", "member"), None),
        P(("group", "member"), None),
        P("group", None, None, None),
        P("group", None, None),
        P("group", None, None, None),
        P(("group", "member"), None, None),
        P(("group", "member"), None, None),
        P(("group", "member"), None, None),
    )
    return jax.shard_map(
        shards,
        mesh=mesh,
        in_specs=placed,
        out_specs=(
            P(("group", "member"), None),
            P(("group", "member"), None, None),
            P(("group", "member"), None, None),
            P(("group", "member"), None, None),
        ),
        check_vma=False,
    )
```

```python
import functools

import jax
import jax.numpy as jnp
from jax import lax
from jax.experimental import pallas as pl
from jax.experimental.pallas import tpu as pltpu
from jax.sharding import PartitionSpec as P

LANES = 128
PARTS = 4
AXES = ("group", "member")
VMEM = pl.BlockSpec(memory_space=pltpu.VMEM)
HBM = pl.BlockSpec(memory_space=pltpu.HBM)
SMEM = pl.BlockSpec(memory_space=pltpu.SMEM)
NT = (((1,), (1,)), ((), ()))
TN = (((0,), (0,)), ((), ()))


def pack_kernel(
    chunks,
    tokens_hbm,
    grad_hbm,
    token_hbm,
    count_hbm,
    prob_hbm,
    out_ref,
    rows_ref,
    tokens_ref,
    grad_ref,
    token_ref,
    count_ref,
    prob_ref,
    sems,
):
    pairs = (
        (token_hbm, token_ref),
        (count_hbm, count_ref),
        (prob_hbm, prob_ref),
        (tokens_hbm, tokens_ref),
        (grad_hbm, grad_ref),
    )
    copies = [pltpu.make_async_copy(*pair, sems.at[n]) for n, pair in enumerate(pairs)]
    for copy in copies:
        copy.start()
    for copy in copies[:3]:
        copy.wait()
    me = lax.axis_index("member")
    groups, _, capacity = token_ref.shape[1:]
    weights = []
    for g in range(groups):
        weight = jnp.float32(0)
        for p in range(capacity):
            live = (token_ref[0, g, 0, p] == me) & (p < count_ref[0, 0, g])
            weight = weight + jnp.where(live, prob_ref[0, g, 0, p], 0.0)
        weights.append(weight)
    for copy in copies[3:]:
        copy.wait()
    token_row = tokens_ref[...].astype(jnp.float32)
    grad_row = grad_ref[...].astype(jnp.float32)
    for k in range(chunks):
        part = slice(k * LANES, (k + 1) * LANES)
        rows_ref[k : k + 1, :] = token_row[:, part]
        rows_ref[chunks + k : chunks + k + 1, :] = grad_row[:, part]
    rows = rows_ref[...]
    is_token = lax.broadcasted_iota(jnp.int32, rows.shape, 0) < chunks
    places = out_ref.shape[0] // groups
    for g, weight in enumerate(weights):
        packed = jnp.where(is_token, rows, rows * weight).astype(jnp.bfloat16)
        for n in range(places):
            out_ref[g * places + n] = packed


def unpack_rows(chunks, packed_ref, wide_ref, rows_ref):
    tokens, rows, _ = packed_ref.shape
    wide_ref[...] = packed_ref[...].astype(jnp.float32).reshape(tokens * rows, LANES)
    for k in range(rows):
        column = wide_ref[pl.ds(k, tokens, stride=rows), :]
        rows_ref[:, k * LANES : (k + 1) * LANES] = column.astype(jnp.bfloat16)


def unpack_kernel(chunks, mine_ref, rows_ref, wide_ref):
    unpack_rows(chunks, mine_ref, wide_ref, rows_ref)


def partial_kernel(
    chunks,
    mine_ref,
    other_ref,
    gate_ref,
    up_ref,
    down_ref,
    sent_ref,
    rows_ref,
    acts_ref,
    wide_ref,
    spread_ref,
):
    count = mine_ref.shape[0]
    tokens = 2 * count
    features = chunks * LANES
    units = gate_ref.shape[1]
    rows_ref[:count] = mine_ref[...]
    unpack_rows(chunks, other_ref, wide_ref, rows_ref.at[pl.ds(count, count)])
    x, scaled = rows_ref[:, :features], rows_ref[:, features:]
    both = jnp.concatenate([gate_ref[0], up_ref[0]], axis=0)
    values = lax.dot_general(both, x, NT, preferred_element_type=jnp.float32)
    gate_value, up_value = values[:units], values[units:]
    d_hidden = lax.dot_general(down_ref[0], scaled, NT, preferred_element_type=jnp.float32)
    sigma_gate = jax.nn.sigmoid(gate_value)
    active = gate_value * sigma_gate
    d_gate = d_hidden * up_value * sigma_gate * (1.0 + gate_value * (1.0 - sigma_gate))
    d_up = d_hidden * active
    acts_ref[0:units] = d_gate.astype(jnp.bfloat16)
    acts_ref[units : 2 * units] = d_up.astype(jnp.bfloat16)
    acts_ref[2 * units :] = (active * up_value).astype(jnp.bfloat16)
    turned = jnp.concatenate([d_gate.T, d_up.T], axis=1).astype(jnp.bfloat16)
    partial = jnp.dot(turned, both, preferred_element_type=jnp.float32)
    core = lax.rem(lax.axis_index("member"), 2)
    for k in range(chunks):
        column = partial[:, k * LANES : (k + 1) * LANES]
        for n in range(2):
            place = pl.ds((core ^ n) * chunks + k, count, stride=2 * chunks)
            spread_ref[place, :] = column[n * count : (n + 1) * count]
    sent_ref[...] = spread_ref[: tokens * chunks, :].astype(jnp.bfloat16)


def grads_kernel(
    features, rows_ref, acts_ref, gate_out, up_out, down_out, held_ref, sems
):
    units = held_ref.shape[1]
    height = units // PARTS
    copies = []
    for n, (out, first) in enumerate(((gate_out, 0), (up_out, 0), (down_out, features))):
        right = rows_ref[:, first : first + features]
        for k in range(PARTS):
            left = acts_ref[n * units + k * height : n * units + (k + 1) * height, :]
            held_ref[n, k * height : (k + 1) * height] = jnp.dot(
                left, right, preferred_element_type=jnp.float32
            ).astype(jnp.bfloat16)
            part = pl.ds(k * height, height)
            copies.append(
                pltpu.make_async_copy(held_ref.at[n, part], out.at[0, part], sems.at[PARTS * n + k])
            )
            copies[-1].start()
    for copy in copies:
        copy.wait()


def sum_kernel(back_ref, out_ref):
    count, blocks, height, _ = back_ref.shape
    for k in range(blocks):
        total = back_ref[0, k].astype(jnp.float32)
        for n in range(1, count):
            total = total + back_ref[n, k].astype(jnp.float32)
        for r in range(height):
            part = pl.ds((k * height + r) * LANES, LANES)
            out_ref[:, part] = total[r : r + 1, :].astype(jnp.bfloat16)


def exchange(value, distance):
    count = lax.axis_size("group") * lax.axis_size("member")
    return lax.ppermute(value, AXES, [(i, i ^ distance) for i in range(count)])


def in_hbm(value):
    return pltpu.with_memory_space_constraint(value, pltpu.HBM)


def dense_shards(tokens, grad_out, route_token, route_count, route_prob, w_gate, w_up, w_down):
    features = tokens.shape[1]
    units = w_gate.shape[1]
    chunks = features // LANES
    count = lax.axis_size("group") * lax.axis_size("member")
    half = count // 2
    rows = 2 * chunks
    arguments = (tokens, grad_out, route_token, jnp.swapaxes(route_count, 1, 2), route_prob)
    spaces = (pltpu.VMEM, pltpu.VMEM, pltpu.SMEM, pltpu.SMEM, pltpu.SMEM)
    copies = pl.pallas_call(
        functools.partial(pack_kernel, chunks),
        out_shape=pltpu.VMEM((half, rows, LANES), jnp.bfloat16),
        in_specs=[HBM] * 5,
        out_specs=VMEM,
        scratch_shapes=[pltpu.VMEM((rows, LANES), jnp.float32)]
        + [space(value.shape, value.dtype) for space, value in zip(spaces, arguments)]
        + [pltpu.SemaphoreType.DMA((5,))],
        compiler_params=pltpu.CompilerParams(vmem_limit_bytes=4 * 1024 * 1024),
        cost_estimate=pl.CostEstimate(
            flops=40000 * units * features,
            bytes_accessed=16 * units * features,
            transcendentals=0,
        ),
        name="pack_rows",
    )(*[in_hbm(value) for value in arguments])
    cores = [list(range(c, count, 2)) for c in range(2)]
    trade = functools.partial(
        lax.all_to_all,
        axis_name=AXES,
        split_axis=0,
        concat_axis=0,
        tiled=True,
        axis_index_groups=cores,
    )
    mine = trade(copies)
    other = exchange(mine, 1)
    wide = pltpu.VMEM((half * rows, LANES), jnp.float32)
    unpacked = pl.pallas_call(
        functools.partial(unpack_kernel, chunks),
        out_shape=pltpu.VMEM((half, 2 * features), jnp.bfloat16),
        in_specs=[VMEM],
        out_specs=VMEM,
        scratch_shapes=[wide],
        compiler_params=pltpu.CompilerParams(vmem_limit_bytes=2 * 1024 * 1024),
        name="unpack_rows",
    )(mine)
    sent, both, acts = pl.pallas_call(
        functools.partial(partial_kernel, chunks),
        out_shape=(
            pltpu.VMEM((count * chunks, LANES), jnp.bfloat16),
            pltpu.VMEM((count, 2 * features), jnp.bfloat16),
            pltpu.VMEM((3 * units, count), jnp.bfloat16),
        ),
        in_specs=[VMEM] * 5,
        out_specs=(VMEM,) * 3,
        scratch_shapes=[wide, pltpu.VMEM(((count + 2) * chunks, LANES), jnp.float32)],
        compiler_params=pltpu.CompilerParams(vmem_limit_bytes=16 * 1024 * 1024),
        name="partial_rows",
    )(unpacked, other, w_gate, w_up, w_down)
    grad_shape = jax.ShapeDtypeStruct((1, units, features), jnp.bfloat16)
    grad_gate, grad_up, grad_down = pl.pallas_call(
        functools.partial(grads_kernel, features),
        out_shape=(grad_shape,) * 3,
        in_specs=[VMEM] * 2,
        out_specs=(HBM, HBM, HBM),
        scratch_shapes=[
            pltpu.VMEM((3, units, features), jnp.bfloat16),
            pltpu.SemaphoreType.DMA((3 * PARTS,)),
        ],
        compiler_params=pltpu.CompilerParams(vmem_limit_bytes=16 * 1024 * 1024),
        cost_estimate=pl.CostEstimate(
            flops=6 * count * units * features,
            bytes_accessed=6 * units * features,
            transcendentals=0,
        ),
        name="weight_grads",
    )(both, acts)
    back = lax.all_to_all(
        sent.reshape(count, chunks // 4, 4, LANES), AXES, 0, 0, tiled=True
    )
    grad_tokens = pl.pallas_call(
        sum_kernel,
        out_shape=jax.ShapeDtypeStruct((1, features), jnp.bfloat16),
        in_specs=[VMEM],
        out_specs=VMEM,
        compiler_params=pltpu.CompilerParams(vmem_limit_bytes=4 * 1024 * 1024),
        name="sum_rows",
    )(back)
    return grad_tokens, grad_gate, grad_up, grad_down


def slice_backward(rows_x, rows_scaled, gate_weight, up_weight, down_weight):
    gate_value = jnp.dot(rows_x, gate_weight.T, preferred_element_type=jnp.float32)
    up_value = jnp.dot(rows_x, up_weight.T, preferred_element_type=jnp.float32)
    sigma_gate = jax.nn.sigmoid(gate_value)
    active = gate_value * sigma_gate
    hidden = (active * up_value).astype(jnp.bfloat16)
    d_hidden = jnp.dot(rows_scaled, down_weight.T, preferred_element_type=jnp.float32)
    d_gate = (d_hidden * up_value * sigma_gate * (1.0 + gate_value * (1.0 - sigma_gate))).astype(
        jnp.bfloat16
    )
    d_up = (d_hidden * active).astype(jnp.bfloat16)
    grad_down = jnp.dot(hidden.T, rows_scaled, preferred_element_type=jnp.float32).astype(
        jnp.bfloat16
    )
    grad_gate = jnp.dot(d_gate.T, rows_x, preferred_element_type=jnp.float32).astype(jnp.bfloat16)
    grad_up = jnp.dot(d_up.T, rows_x, preferred_element_type=jnp.float32).astype(jnp.bfloat16)
    partial_rows = jnp.dot(d_gate, gate_weight, preferred_element_type=jnp.float32)
    partial_rows = partial_rows + jnp.dot(d_up, up_weight, preferred_element_type=jnp.float32)
    return (grad_gate, grad_up, grad_down, partial_rows)


def routed_shards(tokens, grad_out, route_token, route_count, route_prob, w_gate, w_up, w_down):
    groups = route_token.shape[1]
    capacity = route_token.shape[3]
    features = tokens.shape[1]
    block_rows = groups * capacity
    split_count = max(8, lax.axis_size("member") // 8)
    expert_local = lax.axis_index("member") // split_count
    slot_tokens = lax.dynamic_index_in_dim(route_token[0], expert_local, 1, keepdims=False)
    slot_counts = lax.dynamic_index_in_dim(route_count[0], expert_local, 1, keepdims=False)
    slot_probs = lax.dynamic_index_in_dim(route_prob[0], expert_local, 1, keepdims=False)
    slot_index = jnp.arange(capacity, dtype=jnp.int32)[None, :]
    live = (slot_index < slot_counts[:, None]).astype(jnp.float32)
    slot_weights = (slot_probs * live).reshape(-1)
    flat_slots = slot_tokens.reshape(-1)
    group_x, group_dy = (
        lax.all_gather(tokens, "member", axis=0, tiled=True),
        lax.all_gather(grad_out, "member", axis=0, tiled=True),
    )
    picked_x = jnp.take(group_x, flat_slots, axis=0)
    picked_dy = jnp.take(group_dy, flat_slots, axis=0)
    scaled = (slot_weights[:, None] * picked_dy.astype(jnp.float32)).astype(jnp.bfloat16)
    send_x = picked_x.reshape(groups, capacity, features)
    send_scaled = scaled.reshape(groups, capacity, features)
    rows_x, rows_scaled = (
        lax.all_to_all(send_x, "group", split_axis=0, concat_axis=0, tiled=True),
        lax.all_to_all(send_scaled, "group", split_axis=0, concat_axis=0, tiled=True),
    )
    grad_gate, grad_up, grad_down, partial_rows = slice_backward(
        rows_x.reshape(block_rows, features),
        rows_scaled.reshape(block_rows, features),
        w_gate[0],
        w_up[0],
        w_down[0],
    )
    returned = lax.all_to_all(
        partial_rows.reshape(groups, capacity, features),
        "group",
        split_axis=0,
        concat_axis=0,
        tiled=True,
    )
    returned = returned.reshape(block_rows, features)
    row_numbers = jnp.arange(tokens.shape[0] * lax.axis_size("member"), dtype=jnp.int32)
    selector = (row_numbers[:, None] == flat_slots[None, :]).astype(jnp.float32)
    summed = lax.psum_scatter(
        jnp.dot(
            selector, returned, precision=lax.Precision.HIGHEST, preferred_element_type=jnp.float32
        ),
        "member",
        scatter_dimension=0,
        tiled=True,
    )
    return (summed.astype(jnp.bfloat16), grad_gate[None], grad_up[None], grad_down[None])


def shards(tokens, grad_out, route_token, *rest):
    devices = lax.axis_size("group") * lax.axis_size("member")
    _, groups, experts, capacity = route_token.shape
    dense = devices * tokens.shape[0] <= groups * capacity and experts == 1
    dense = dense and tokens.shape[1] % (4 * LANES) == 0
    paired = tokens.shape[0] == 1 and devices & (devices - 1) == 0
    body = dense_shards if dense and paired else routed_shards
    return body(tokens, grad_out, route_token, *rest)


def solution(mesh):
    placed = (
        P(("group", "member"), None),
        P(("group", "member"), None),
        P("group", None, None, None),
        P("group", None, None),
        P("group", None, None, None),
        P(("group", "member"), None, None),
        P(("group", "member"), None, None),
        P(("group", "member"), None, None),
    )
    return jax.shard_map(
        shards,
        mesh=mesh,
        in_specs=placed,
        out_specs=(
            P(("group", "member"), None),
            P(("group", "member"), None, None),
            P(("group", "member"), None, None),
            P(("group", "member"), None, None),
        ),
        check_vma=False,
    )
```
